32 devices in a mesh: dp: 4 (over z), fsdp: 8 (over y, x, core).
Axes of the slice: x: 2, y: 2, z: 4, core: 2. Of those that a mesh axis runs over, the one named last changes fastest.
Arguments:
- tokens: bfloat16 [4096, 1280], P(('dp', 'fsdp')), may hold values from -6 to 6
- out_grad: bfloat16 [4096, 1280], P(('dp', 'fsdp')), may hold values from -6 to 6
- segment_ids: int32 [4096], P(('dp', 'fsdp')), may hold values from 0 to 15, never falling along the last dimension, each value on 1 to 1024 neighbouring positions
- expert_ids: int32 [4096, 7], P(('dp', 'fsdp')), may hold values from 0 to 15, all different within a row; in each aligned block of 128 rows (0 to 127, 128 to 255, ...) at most 80 rows name the same one
- attn_gain: bfloat16 [1280], P(('dp', 'fsdp')), may hold values from 0.5 to 1.5
- ffn_gain: bfloat16 [1280], P(('dp', 'fsdp')), may hold values from 0.5 to 1.5
- w_qkv: bfloat16 [1280, 3840], P(('dp', 'fsdp')), may hold values from -0.15625 to 0.15625
- w_out: bfloat16 [1280, 1280], P(('dp', 'fsdp')), may hold values from -1.25 to 1.25
- w_router: bfloat16 [1280, 16], P(('dp', 'fsdp')), may hold values from -0.078125 to 0.078125
- w_shared_up: bfloat16 [1280, 1792], P(('dp', 'fsdp')), may hold values from -0.15625 to 0.15625
- w_shared_down: bfloat16 [896, 1280], P(('dp', 'fsdp')), may hold values from -0.1875 to 0.1875
- w_expert_up: bfloat16 [16, 1280, 1792], P('fsdp', 'dp'), may hold values from -0.15625 to 0.15625
- w_expert_down: bfloat16 [16, 896, 1280], P('fsdp', 'dp'), may hold values from -0.375 to 0.375
Outputs:
- block_out: bfloat16 [4096, 1280], P(('dp', 'fsdp'))
- tokens_grad: bfloat16 [4096, 1280], P(('dp', 'fsdp'))
- grad_attn_gain: float32 [1280], P(('dp', 'fsdp'))
- grad_ffn_gain: float32 [1280], P(('dp', 'fsdp'))
- grad_w_qkv: float32 [1280, 3840], P(('dp', 'fsdp'))
- grad_w_out: float32 [1280, 1280], P(('dp', 'fsdp'))
- grad_w_router: float32 [1280, 16], P(('dp', 'fsdp'))
- grad_w_shared_up: float32 [1280, 1792], P(('dp', 'fsdp'))
- grad_w_shared_down: float32 [896, 1280], P(('dp', 'fsdp'))
- grad_w_expert_up: float32 [16, 1280, 1792], P('fsdp', 'dp')
- grad_w_expert_down: float32 [16, 896, 1280], P('fsdp', 'dp')
The draws below stay inside these ranges and needn't reach their ends.
Inputs may be any that keep to these rules, and one draw needn't show every extreme that they name: `expert_ids`: each token names 7 different routed experts. Among the tokens of one device no expert is named more than 80 times, and in every draw some expert is named exactly 80 times by one device's tokens. `segment_ids`: document numbers never fall along the tokens; a document holds 1 to 1024 tokens and one holds exactly 1024.
All inputs are finite; a program needn't handle non-finite values.
Results may differ from the reference program's by a relative error of at most 0.024.
Values may be sent and summed in bfloat16 or wider, within the bound.
A program may use at most 256 MiB of HBM per device.

```python
import math
import jax
import jax.numpy as jnp
import numpy as np
from jax import lax

D = 1280
HEADS = 10
HEAD_DIM = 128
HIDDEN_SIZE = 896
TOPK = 7
TOK_DEV = 128
SEQ = 1024
EXPERTS = 16
TOKENS = 4096
CAP = 80


def block_levels(rng, extent, cuts, smallest, high):
    level = 1.0
    for axis_at, parts in cuts:
        heights = jax.random.uniform(jax.random.fold_in(jax.random.fold_in(rng, 6), axis_at), (parts,), jnp.float32, smallest / len(cuts), high / len(cuts))
        level = level * jnp.repeat(jnp.exp(heights), extent[axis_at] // parts).reshape((-1,) + (1,) * (len(extent) - 1 - axis_at))
    return level


def profile(count, total, most, skew):
    portions = [(1 << 20) // math.isqrt(standing ** skew) + 1 for standing in range(2, count + 1)]
    rest, given = total - most - (count - 1), [1] * (count - 1)
    while rest > 0:
        movable = [i for i in range(count - 1) if given[i] < most]
        whole, budget = sum([portions[i] for i in movable]), rest
        for i in movable:
            addition = min(most - given[i], max(1, budget * portions[i] // whole), rest)
            given[i] = given[i] + addition
            rest = rest - addition
    return np.array([most] + given)


def ragged_sizes(own_key, amount, total, reach, skew):
    if amount == 2:
        one = jax.random.randint(own_key, (), max(1, total - reach), min(reach, total - 1) + 1)
        return jnp.stack([one, total - one])
    tallies = jnp.asarray(profile(amount, total, reach, skew), jnp.int32)
    pairs = (amount - 1) // 2
    source_of, taker = tallies[1:1 + 2 * pairs:2], tallies[2:2 + 2 * pairs:2]
    room = jnp.minimum(source_of - 1, reach - taker)
    moved = jax.random.randint(jax.random.fold_in(own_key, 1), (pairs,), 0, 1 << 20) % (room + 1)
    tallies = tallies.at[1:1 + 2 * pairs:2].set(source_of - moved).at[2:2 + 2 * pairs:2].set(taker + moved)
    return tallies[jax.random.permutation(jax.random.fold_in(own_key, 2), amount)]


def assign_block(own_key, own, number, rows, count, top, bound, skew):
    sequence = jax.random.permutation(own_key, count)
    packed, usual = shares(count, rows * top, bound, skew, True), shares(count, rows * top, bound, skew, False)
    places = jnp.arange(count)

    def named(tallies, offset_by):
        used = int((tallies > 0).sum())
        fixed = max(1, used // 4)
        passed = fixed + (places - fixed + offset_by * (used - fixed)) % max(1, count - fixed)
        return jnp.zeros((count,), jnp.int32).at[sequence[jnp.where(places < fixed, places, passed)]].set(jnp.asarray(tallies, jnp.int32))

    tallies = jnp.where(number % 4 == 0, named(packed, number // 4), named(usual, number - number // 4 - 1))
    mixed = jax.random.permutation(jax.random.fold_in(own, 3), count)
    source_of, sink = mixed[0:count // 2 * 2:2], mixed[1:count // 2 * 2:2]
    slack = jnp.minimum(tallies[source_of] - 1, bound - tallies[sink]) // 2
    slack = jnp.where((source_of == sequence[0]) | (sink == sequence[0]) | (tallies[sink] == 0), 0, jnp.maximum(slack, 0))
    passed = jax.random.randint(jax.random.fold_in(own, 4), (count // 2,), 0, 1 << 20) % (slack + 1)
    tallies = tallies.at[source_of].add(-passed).at[sink].add(passed)
    items = jnp.searchsorted(jnp.cumsum(tallies), jnp.arange(rows * top), side="right").astype(jnp.int32)
    listing = items.reshape(top, rows).T
    listing = listing[jax.random.permutation(jax.random.fold_in(own, 1), rows)]
    offset_by = jax.random.randint(jax.random.fold_in(own, 2), (rows, 1), 0, top)
    return jnp.take_along_axis(listing, (jnp.arange(top)[None, :] + offset_by) % top, axis=1)


def shares(number_of, total, reach, lean, full):
    portions = [(1 << 20) // math.isqrt(standing ** lean) + 1 for standing in range(1, number_of + 1)]
    largest = reach if full else min(reach, max(-(-total // number_of), total * portions[0] // sum(portions)))
    least = 1 if total - largest >= number_of - 1 else 0
    counts, surplus = [largest] + [least] * (number_of - 1), total - largest - least * (number_of - 1)
    while surplus > 0:
        candidates = [i for i in range(1, number_of) if counts[i] < largest] or [i for i in range(1, number_of) if counts[i] < reach]
        pool, budget = sum([portions[i] for i in candidates]), surplus
        for i in candidates:
            addition = min(reach - counts[i], max(1, budget * portions[i] // pool), surplus)
            counts[i] = counts[i] + addition
            surplus = surplus - addition
    return np.array(counts)


def noise(own_key, extent, width, reach, cuts=(), kind=jnp.bfloat16):
    level = block_levels(own_key, extent, cuts, -0.22, 0.18) if cuts else 1.0
    array = jax.random.normal(own_key, extent, jnp.float32) * width * level
    return jnp.minimum(jnp.maximum(array, -reach), reach).astype(kind)


def setup_inputs(seed: int = 0) -> dict:
    keys = jax.random.split(jax.random.key(seed), 14)
    tokens = noise(keys[0], (TOKENS, D), 1.0, 6.0, ((0, 32),))
    out_grad = noise(keys[1], (TOKENS, D), 1.0, 6.0, ((0, 32),))
    segment_ids = jnp.searchsorted(jnp.cumsum(ragged_sizes(keys[2], TOKENS // (SEQ // 4), TOKENS, SEQ, 2)), jnp.arange(TOKENS), side="right").astype(jnp.int32)
    expert_ids_keys = jax.random.split(jax.random.fold_in(keys[3], 1), TOKENS // TOK_DEV)
    expert_ids_turns = jax.random.permutation(jax.random.fold_in(keys[3], 3), TOKENS // TOK_DEV)
    expert_ids = jax.vmap(lambda own, number: assign_block(jax.random.fold_in(keys[3], 2), own, number, TOK_DEV, EXPERTS, TOPK, CAP, 2))(expert_ids_keys, expert_ids_turns).reshape((TOKENS, TOPK))
    attn_gain = jnp.clip(1.0 + 0.1 * jax.random.normal(keys[4], (D,), jnp.float32), 0.5, 1.5).astype(jnp.bfloat16)
    ffn_gain = jnp.clip(1.0 + 0.1 * jax.random.normal(keys[5], (D,), jnp.float32), 0.5, 1.5).astype(jnp.bfloat16)
    w_qkv = noise(keys[6], (D, 3 * D), D ** -0.5, 0.15625, ((0, 32),))
    w_out = noise(keys[7], (D, D), (D // 64) ** -0.5, 1.25, ((0, 32),))
    w_router = noise(keys[8], (D, EXPERTS), (4 * D) ** -0.5, 0.078125, ((0, 32),))
    w_shared_up = noise(keys[9], (D, 2 * HIDDEN_SIZE), D ** -0.5, 0.15625, ((0, 32),))
    w_shared_down = noise(keys[10], (HIDDEN_SIZE, D), HIDDEN_SIZE ** -0.5, 0.1875, ((0, 32),))
    w_expert_up = noise(keys[11], (EXPERTS, D, 2 * HIDDEN_SIZE), D ** -0.5, 0.15625, ((0, 8), (1, 4)))
    w_expert_down = noise(keys[12], (EXPERTS, HIDDEN_SIZE, D), (HIDDEN_SIZE // 4) ** -0.5, 0.375, ((0, 8), (1, 4)))
    return {"tokens": tokens, "out_grad": out_grad, "segment_ids": segment_ids, "expert_ids": expert_ids, "attn_gain": attn_gain, "ffn_gain": ffn_gain, "w_qkv": w_qkv, "w_out": w_out, "w_router": w_router, "w_shared_up": w_shared_up, "w_shared_down": w_shared_down, "w_expert_up": w_expert_up, "w_expert_down": w_expert_down}


@jax.custom_vjp
def low(v):
    return lax.optimization_barrier(v.astype(jnp.bfloat16)).astype(jnp.float32)

@jax.custom_vjp
def low_back(v):
    return v

def low_keep(v):
    return (low(v), None)

def low_pass(kept, grad):
    return (grad,)

def back_keep(v):
    return (v, None)

def back_low(kept, grad):
    return (low(grad),)
low.defvjp(low_keep, low_pass)
low_back.defvjp(back_keep, back_low)
epsilon = 1e-06
rope_base = 10000.0

def matmul_high(left, right):
    return jnp.dot(left, right, precision=lax.Precision.HIGHEST, preferred_element_type=jnp.float32)

def einsum_high(form, left, right):
    return jnp.einsum(form, left, right, precision=lax.Precision.HIGHEST)

def rms_scale(values):
    return lax.rsqrt(lax.optimization_barrier(jnp.mean(values * values, axis=-1, keepdims=True)) + epsilon)

def rotary_tables(positions):
    half_dim = HEAD_DIM // 2
    freqs = rope_base ** (-jnp.arange(half_dim, dtype=jnp.float32) * 2.0 / HEAD_DIM)
    angles = positions.astype(jnp.float32)[:, None] * freqs[None, :]
    return (jnp.cos(angles)[:, None, :], jnp.sin(angles)[:, None, :])

def rotate(values, cosine_table, sine_table):
    half_dim = values.shape[-1] // 2
    front_half = values[..., :half_dim]
    back_half = values[..., half_dim:]
    return jnp.concatenate([front_half * cosine_table - back_half * sine_table, back_half * cosine_table + front_half * sine_table], axis=-1)

def swiglu(pre_values):
    return jax.nn.silu(pre_values[..., :HIDDEN_SIZE]) * pre_values[..., HIDDEN_SIZE:]

def sequence_block(params, inputs, seg_rows, route_rows):
    gain_one, gain_two, full_qkv, full_out, full_router, full_sup, full_sdown, exp_up, exp_down = params
    length = inputs.shape[0]
    normed_one = low(inputs * rms_scale(inputs) * gain_one)
    qkv_proj = low_back(matmul_high(normed_one, full_qkv))
    positions = jnp.arange(length, dtype=jnp.int32)
    cosine_table, sine_table = rotary_tables(positions)
    queries = low(rotate(qkv_proj[:, :D].reshape(length, HEADS, HEAD_DIM), cosine_table, sine_table))
    key_rows = low(rotate(qkv_proj[:, D:2 * D].reshape(length, HEADS, HEAD_DIM), cosine_table, sine_table))
    value_rows = low(qkv_proj[:, 2 * D:].reshape(length, HEADS, HEAD_DIM))
    scores = low_back(einsum_high('qhd,khd->hqk', queries, key_rows) * HEAD_DIM ** (-0.5))
    allowed = (positions[None, :] <= positions[:, None]) & (seg_rows[None, :] == seg_rows[:, None])
    scores = jnp.where(allowed[None], scores, -1e+30)
    probs = low(jax.nn.softmax(scores, axis=-1))
    attn = einsum_high('hqk,khd->qhd', probs, value_rows).reshape(length, D)
    attn = low_back(low(attn))
    mixed_rows = inputs + low_back(matmul_high(attn, full_out))
    normed_two = low(mixed_rows * rms_scale(mixed_rows) * gain_two)
    logits = low_back(matmul_high(normed_two, full_router))
    chosen = jnp.take_along_axis(logits, route_rows, axis=1)
    gate_probs = jax.nn.softmax(chosen, axis=-1)
    shared_pre = low_back(matmul_high(normed_two, full_sup))
    shared_act = low(swiglu(shared_pre))
    shared_res = matmul_high(shared_act, full_sdown)
    blocks = length // TOK_DEV
    per_block = TOK_DEV * TOPK
    flat_ids = route_rows.reshape(blocks, per_block)
    route_marks = (flat_ids[..., None] == jnp.arange(EXPERTS, dtype=jnp.int32)[None, None, :]).astype(jnp.int32)
    slot_rank = lax.optimization_barrier(jnp.sum((jnp.cumsum(route_marks, axis=1) - 1) * route_marks, axis=-1))
    slot_index = flat_ids * (blocks * CAP) + jnp.arange(blocks, dtype=jnp.int32)[:, None] * CAP + slot_rank
    slot_index = slot_index.reshape(-1).astype(jnp.int32)
    slot_owner = jnp.zeros((EXPERTS * blocks * CAP,), jnp.int32).at[slot_index].set(jnp.arange(length * TOPK, dtype=jnp.int32) + 1)
    filled = slot_owner > 0
    source_row = jnp.maximum(slot_owner - 1, 0) // TOPK
    expert_in = low_back(jnp.where(filled[:, None], normed_two[source_row], 0.0)).reshape(EXPERTS, blocks * CAP, D)
    expert_pre = low_back(einsum_high('erd,edf->erf', expert_in, exp_up))
    expert_act = low(swiglu(expert_pre))
    expert_out = low_back(low(einsum_high('erf,efd->erd', expert_act, exp_down))).reshape(-1, D)
    routed_rows = expert_out[slot_index].reshape(length, TOPK, D)
    routed = lax.optimization_barrier(jnp.sum(gate_probs[:, :, None] * routed_rows, axis=1))
    return mixed_rows + shared_res + routed

def reference(tokens, out_grad, segment_ids, expert_ids, attn_gain, ffn_gain, w_qkv, w_out, w_router, w_shared_up, w_shared_down, w_expert_up, w_expert_down):
    params = tuple((weight.astype(jnp.float32) for weight in (attn_gain, ffn_gain, w_qkv, w_out, w_router, w_shared_up, w_shared_down, w_expert_up, w_expert_down)))
    seq_count = tokens.shape[0] // SEQ
    seq_inputs = tokens.astype(jnp.float32).reshape(seq_count, SEQ, D)
    seq_segments = segment_ids.reshape(seq_count, SEQ)
    seq_routes = expert_ids.reshape(seq_count, SEQ, TOPK)

    def forward(params, seq_inputs):
        checked = jax.checkpoint(sequence_block)
        return lax.map(lambda seq_item: checked(params, seq_item[0], seq_item[1], seq_item[2]), (seq_inputs, seq_segments, seq_routes))
    seq_outputs, pullback = jax.vjp(forward, params, seq_inputs)
    weight_grads, input_grads = pullback(out_grad.astype(jnp.float32).reshape(seq_count, SEQ, D))
    block_out = seq_outputs.reshape(tokens.shape[0], D).astype(jnp.bfloat16)
    tokens_grad = input_grads.reshape(tokens.shape[0], D).astype(jnp.bfloat16)
    return (block_out, tokens_grad, weight_grads[0], weight_grads[1], weight_grads[2], weight_grads[3], weight_grads[4], weight_grads[5], weight_grads[6], weight_grads[7], weight_grads[8])
```

```python
import functools

import jax
import jax.numpy as jnp
from jax import lax
from jax.experimental import pallas as pl
from jax.experimental.pallas import tpu as pltpu
from jax.sharding import PartitionSpec as P

HEADS = 10
HD = 128
SEQ = 1024
SLOTS = 2
EPS = 1e-06
ROPE = 10000.0
NEG = -1e30
TAIL = 64
F32 = jnp.float32
BF16 = jnp.bfloat16


MESH = pl.DeviceIdType.MESH
VMEM = pl.BlockSpec(memory_space=pltpu.VMEM)
ANY = pl.BlockSpec(memory_space=pl.ANY)


def up_to(value, step):
    return -(-value // step) * step


def rms_scale(values):
    return lax.rsqrt(jnp.mean(values * values, axis=-1, keepdims=True) + EPS)


def norm_back(grad_normed, normal_rows, scale_rows, gain_rows):
    scaled = grad_normed * gain_rows
    return scale_rows * (
        scaled - normal_rows * jnp.mean(scaled * normal_rows, axis=-1, keepdims=True)
    )


def head_table(group):
    heads, real = [], []
    for i in range(group):
        own = list(range(HEADS * i // group, HEADS * (i + 1) // group))
        assert len(own) <= SLOTS
        heads += own + [0] * (SLOTS - len(own))
        real += [1] * len(own) + [0] * (SLOTS - len(own))
    return heads, real


def dot(a, b):
    return jnp.dot(a, b, preferred_element_type=F32)


def dot_nt(a, b):
    return lax.dot_general(a, b, (((1,), (1,)), ((), ())), preferred_element_type=F32)


def dot_tn(a, b):
    return lax.dot_general(a, b, (((0,), (0,)), ((), ())), preferred_element_type=F32)


def attn_forward_kernel(
    tok_ref, gain_ref, w_ref, wo_ref, cos_ref, sin_ref, segq_ref, segk_ref,
    part_ref, normed_ref, qkv_ref, attn_ref, lse_ref,
    *, block,
):
    length, width = tok_ref.shape
    count = length // block
    step = 3 * HD

    def norm_step(i, _):
        rows = pl.ds(pl.multiple_of(i * block, block), block)
        x = tok_ref[rows, :].astype(F32)
        normed = (x * rms_scale(x) * gain_ref[...]).astype(BF16)
        normed_ref[rows, :] = normed
        cosine, sine = cos_ref[rows, :], sin_ref[rows, :]
        for s in range(SLOTS):
            proj = dot(normed, w_ref[s])
            for c in range(3):
                piece = proj[:, c * HD : (c + 1) * HD]
                if c < 2:
                    piece = piece * cosine + pltpu.roll(piece, HD // 2, 1) * sine
                qkv_ref[rows, s * step + c * HD : s * step + (c + 1) * HD] = piece.astype(BF16)
        return 0

    lax.fori_loop(0, count, norm_step, 0)
    scale = HD**-0.5
    for i in range(count):
        rows = slice(i * block, (i + 1) * block)
        keys = (i + 1) * block
        row_pos = i * block + lax.broadcasted_iota(jnp.int32, (block, keys), 0)
        key_pos = lax.broadcasted_iota(jnp.int32, (block, keys), 1)
        allowed = (key_pos <= row_pos) & (segq_ref[rows, :1] == segk_ref[:1, :keys])
        outs = []
        for s in range(SLOTS):
            at = s * step
            q = qkv_ref[rows, at : at + HD]
            k = qkv_ref[:keys, at + HD : at + 2 * HD]
            v = qkv_ref[:keys, at + 2 * HD : at + 3 * HD]
            scores = jnp.where(allowed, dot_nt(q, k) * scale, NEG)
            top = jnp.max(scores, axis=-1, keepdims=True)
            weights = jnp.exp(scores - top)
            total = jnp.sum(weights, axis=-1, keepdims=True)
            out = dot(weights.astype(BF16), v) / total
            lse_ref[rows, s * HD : (s + 1) * HD] = jnp.broadcast_to(
                top + jnp.log(total), (block, HD)
            )
            low = out.astype(BF16)
            attn_ref[rows, s * HD : (s + 1) * HD] = low
            outs.append(low)
        part_ref[rows, :] = dot(jnp.concatenate(outs, axis=-1), wo_ref[...]).astype(BF16)


def attn_forward(tok, gain, w, wo, cosine, sine, segq, segk):
    length, width = tok.shape
    return pl.pallas_call(
        functools.partial(attn_forward_kernel, block=256),
        out_shape=(
            jax.ShapeDtypeStruct((length, width), BF16),
            jax.ShapeDtypeStruct((length, width), BF16),
            jax.ShapeDtypeStruct((length, 3 * SLOTS * HD), BF16),
            jax.ShapeDtypeStruct((length, SLOTS * HD), BF16),
            jax.ShapeDtypeStruct((length, SLOTS * HD), F32),
        ),
        in_specs=[VMEM] * 8,
        out_specs=(VMEM,) * 5,
        compiler_params=pltpu.CompilerParams(vmem_limit_bytes=56 * 2**20),
        cost_estimate=pl.CostEstimate(
            flops=2 * length * width * 4 * SLOTS * HD + 4 * SLOTS * HD * length * length,
            bytes_accessed=10 * length * width,
            transcendentals=SLOTS * length * length,
        ),
        name="attn_forward",
    )(tok, gain, w, wo, cosine, sine, segq, segk)


def attn_backward_kernel(
    gm_ref, wo_ref, w_ref, normed_ref, qkv_ref, attn_ref, lse_ref, cos_ref, sin_ref,
    segq_ref, segk_ref,
    part_ref, gw_ref, gwo_ref,
    gkv_ref, gqkv_ref, wt_ref,
    *, block,
):
    length, width = gm_ref.shape
    count = length // block
    scale = HD**-0.5
    step = 3 * HD
    gkv_ref[...] = jnp.zeros_like(gkv_ref)
    for i in range(count):
        rows = slice(i * block, (i + 1) * block)
        keys = (i + 1) * block
        row_pos = i * block + lax.broadcasted_iota(jnp.int32, (block, keys), 0)
        key_pos = lax.broadcasted_iota(jnp.int32, (block, keys), 1)
        allowed = (key_pos <= row_pos) & (segq_ref[rows, :1] == segk_ref[:1, :keys])
        grad_attn = dot_nt(gm_ref[rows, :], wo_ref[...]).astype(BF16)
        for s in range(SLOTS):
            at = s * step
            cut = slice(s * HD, (s + 1) * HD)
            q = qkv_ref[rows, at : at + HD]
            k = qkv_ref[:keys, at + HD : at + 2 * HD]
            v = qkv_ref[:keys, at + 2 * HD : at + 3 * HD]
            ga = grad_attn[:, cut]
            delta = jnp.sum(ga.astype(F32) * attn_ref[rows, cut].astype(F32), axis=-1, keepdims=True)
            scores = dot_nt(q, k) * scale
            probs = jnp.where(allowed, jnp.exp(scores - lse_ref[rows, s * HD : s * HD + 1]), 0.0)
            gs = (probs * (dot_nt(ga, v) - delta)).astype(BF16)
            gq = dot(gs, k) * scale
            gq = gq * cos_ref[rows, :] - pltpu.roll(gq, HD // 2, 1) * sin_ref[rows, :]
            gqkv_ref[rows, at : at + HD] = gq.astype(BF16)
            gkv_ref[:keys, 2 * s * HD : (2 * s + 1) * HD] += dot_tn(gs, q)
            gkv_ref[:keys, (2 * s + 1) * HD : (2 * s + 2) * HD] += dot_tn(probs.astype(BF16), ga)
    for s in range(SLOTS):
        at = s * step
        gk = gkv_ref[:, 2 * s * HD : (2 * s + 1) * HD] * scale
        gk = gk * cos_ref[...] - pltpu.roll(gk, HD // 2, 1) * sin_ref[...]
        gqkv_ref[:, at + HD : at + 2 * HD] = gk.astype(BF16)
        gqkv_ref[:, at + 2 * HD : at + 3 * HD] = gkv_ref[:, (2 * s + 1) * HD : (2 * s + 2) * HD].astype(BF16)
        wt_ref[s * step : (s + 1) * step, :] = w_ref[s].T
    for i in range(count):
        rows = slice(i * block, (i + 1) * block)
        part_ref[rows, :] = dot(gqkv_ref[rows, :], wt_ref[...]).astype(BF16)
    for s in range(SLOTS):
        gw_ref[s] = dot_tn(normed_ref[...], gqkv_ref[:, s * step : (s + 1) * step]).astype(BF16)
    gwo_ref[...] = dot_tn(attn_ref[...], gm_ref[...]).astype(BF16)


def attn_backward(gm, wo, w, normed, qkv, attn, lse, cosine, sine, segq, segk):
    length, width = gm.shape
    return pl.pallas_call(
        functools.partial(attn_backward_kernel, block=256),
        out_shape=(
            jax.ShapeDtypeStruct((length, width), BF16),
            jax.ShapeDtypeStruct((SLOTS, width, 3 * HD), BF16),
            jax.ShapeDtypeStruct((SLOTS * HD, width), BF16),
        ),
        in_specs=[VMEM] * 11,
        out_specs=(VMEM,) * 3,
        scratch_shapes=[
            pltpu.VMEM((length, 2 * SLOTS * HD), F32),
            pltpu.VMEM((length, 3 * SLOTS * HD), BF16),
            pltpu.VMEM((3 * SLOTS * HD, width), BF16),
        ],
        compiler_params=pltpu.CompilerParams(vmem_limit_bytes=56 * 2**20),
        cost_estimate=pl.CostEstimate(
            flops=4 * length * width * 4 * SLOTS * HD + 10 * SLOTS * HD * length * length,
            bytes_accessed=10 * length * width,
            transcendentals=SLOTS * length * length,
        ),
        name="attn_backward",
    )(gm, wo, w, normed, qkv, attn, lse, cosine, sine, segq, segk)


def ffn_kernel(
    x_ref, g_ref, mark_ref, own_ref, eup_ref, tail_ref, edown_ref, sdown_ref,
    out_ref, gx_ref, geup_ref, gtail_ref, gedown_ref, gsdown_ref,
    up_ref, upt_ref, down_ref, downt_ref, gup_ref, gdown_ref,
    *, hidden, shared,
):
    step = pl.program_id(0)
    half = down_ref.shape[0]
    width = x_ref.shape[1]
    pair = 2 * hidden
    gap = half - pair - TAIL

    @pl.when(step == 0)
    def _():
        gup_ref[...] = jnp.zeros_like(gup_ref)
        gdown_ref[...] = jnp.zeros_like(gdown_ref)
        between = [jnp.zeros((width, gap), BF16)] if gap else []
        up_ref[...] = jnp.concatenate(
            [eup_ref[:, :pair], *between, tail_ref[:, :TAIL], eup_ref[:, pair:], *between, tail_ref[:, TAIL:]], axis=1
        )
        between = [jnp.zeros((gap, width), BF16)] if gap else []
        down_ref[...] = jnp.concatenate(
            [edown_ref[...], *between, sdown_ref[...], jnp.zeros((TAIL - shared, width), BF16)], axis=0
        )
        upt_ref[...] = up_ref[...].T
        downt_ref[...] = down_ref[...].T

    x, g = x_ref[...], g_ref[...]
    pre = dot(x, up_ref[...])
    gate, up = pre[:, :half], pre[:, half:]
    marks = mark_ref[...].astype(F32) > 0.5
    logits = jnp.where(marks, gate[:, half - HD :], NEG)
    weights = jnp.exp(logits - jnp.max(logits, axis=-1, keepdims=True))
    probs = weights / jnp.sum(weights, axis=-1, keepdims=True)
    p0 = jnp.sum(probs * own_ref[0:1, :], axis=-1, keepdims=True)
    p1 = jnp.sum(probs * own_ref[1:2, :], axis=-1, keepdims=True)
    lane = lax.broadcasted_iota(jnp.int32, (1, half), 1)
    in0 = lane < hidden
    in1 = (lane >= hidden) & (lane < pair)
    rest = jnp.where((lane >= half - TAIL) & (lane < half - TAIL + shared), 1.0, 0.0)
    weight = jnp.where(in0, p0, jnp.where(in1, p1, rest))
    sig = jax.nn.sigmoid(gate)
    silu = gate * sig
    act = silu * up
    acts = (act * weight).astype(BF16)
    out_ref[...] = dot(acts, down_ref[...]).astype(BF16)
    grad = dot(g, downt_ref[...])
    both = act * grad
    d0 = jnp.sum(jnp.where(in0, both, 0.0), axis=-1, keepdims=True)
    d1 = jnp.sum(jnp.where(in1, both, 0.0), axis=-1, keepdims=True)
    grad = grad * weight
    grad_gate = grad * up * sig * (1.0 + gate * (1.0 - sig))
    grad_up = grad * silu
    grad_pre = jnp.concatenate([grad_gate, grad_up], axis=-1).astype(BF16)
    gx_ref[:, :width] = dot(grad_pre, upt_ref[...]).astype(BF16)
    gx_ref[:, width:] = (d0 * own_ref[0:1, :] + d1 * own_ref[1:2, :]).astype(BF16)
    gup_ref[...] += dot_tn(x, grad_pre)
    gdown_ref[...] += dot_tn(acts, g)

    @pl.when(step == pl.num_programs(0) - 1)
    def _():
        geup_ref[...] = jnp.concatenate([gup_ref[:, :pair], gup_ref[:, half : half + pair]], axis=1).astype(BF16)
        gtail_ref[...] = jnp.concatenate([gup_ref[:, half - TAIL : half], gup_ref[:, 2 * half - TAIL :]], axis=1)
        gedown_ref[...] = gdown_ref[:pair, :]
        gsdown_ref[...] = gdown_ref[half - TAIL : half - TAIL + shared, :]


def ffn(x, g, marks, own, eup, tail, edown, sdown):
    total, width = x.shape
    pair, shared = edown.shape[0], sdown.shape[0]
    half = up_to(pair + TAIL, HD)
    tile = 512
    row = lambda n: pl.BlockSpec((tile, n), lambda i: (i, 0))
    return pl.pallas_call(
        functools.partial(ffn_kernel, hidden=pair // 2, shared=shared),
        out_shape=(
            jax.ShapeDtypeStruct((total, width), BF16),
            jax.ShapeDtypeStruct((total, width + HD), BF16),
            jax.ShapeDtypeStruct((width, 2 * pair), BF16),
            jax.ShapeDtypeStruct((width, HD), F32),
            jax.ShapeDtypeStruct((pair, width), F32),
            jax.ShapeDtypeStruct((shared, width), F32),
        ),
        grid=(total // tile,),
        in_specs=[row(width), row(width), row(HD)] + [VMEM] * 5,
        out_specs=(row(width), row(width + HD), VMEM, VMEM, VMEM, VMEM),
        scratch_shapes=[
            pltpu.VMEM((width, 2 * half), BF16),
            pltpu.VMEM((2 * half, width), BF16),
            pltpu.VMEM((half, width), BF16),
            pltpu.VMEM((width, half), BF16),
            pltpu.VMEM((width, 2 * half), F32),
            pltpu.VMEM((half, width), F32),
        ],
        compiler_params=pltpu.CompilerParams(vmem_limit_bytes=60 * 2**20),
        cost_estimate=pl.CostEstimate(
            flops=2 * total * width * 9 * half,
            bytes_accessed=8 * total * width,
            transcendentals=total * half,
        ),
        name="ffn",
    )(x, g, marks, own, eup, tail, edown, sdown)


def flip(f, bits):
    for b in (1, 2, 4):
        if bits & b:
            f = f + b - 2 * b * (f // b % 2)
    return f


def place():
    return lax.axis_index("dp"), lax.axis_index("fsdp")


def greet(devices):
    barrier = pltpu.get_barrier_semaphore()
    for device in devices:
        pl.semaphore_signal(barrier, inc=1, device_id=device, device_id_type=MESH)
    pl.semaphore_wait(barrier, len(devices))


def greet_all(nz, nf):
    barrier = pltpu.get_barrier_semaphore()
    z, f = place()
    me, count = z * nf + f, nz * nf

    def hail(i, _):
        d = (me + i) % count
        pl.semaphore_signal(barrier, inc=1, device_id=(d // nf, d % nf), device_id_type=MESH)
        return 0

    lax.fori_loop(1, count, hail, 0)
    pl.semaphore_wait(barrier, count - 1)


def send(src, dst, sems, index, device):
    return pltpu.make_async_remote_copy(
        src, dst, sems[0].at[index], sems[1].at[index], device_id=device, device_id_type=MESH
    )


ORDER = ((2, 4), (4, 2))


def halves(width):
    cut = (width // HD + 1) // 2 * HD
    return ((0, cut), (cut, width - cut))


class Gather:
    @staticmethod
    def copies(nz):
        return 11 * nz

    def __init__(self, own, buf, sems, nz, z, f, pieces=None):
        self.own, self.buf, self.sems, self.nz = own, buf, sems, nz
        self.z, self.f = z, f
        self.width = buf.shape[-1]
        self.sent = {}

    def piece(self, zr):
        return lax.rem(self.z - zr + self.nz, self.nz) if zr else self.z

    def source(self, zr, r, h=None):
        ref = self.own if zr == 0 and r == 0 else self.buf.at[self.piece(zr), flip(self.f, r)]
        return ref if h is None else ref.at[:, pl.ds(*halves(self.width)[h])]

    def slot(self, zr, r, h=None):
        ref = self.buf.at[self.piece(zr), flip(self.f, r)]
        return ref if h is None else ref.at[:, pl.ds(*halves(self.width)[h])]

    def go(self, src, dst, index, device):
        copy = send(src, dst, self.sems, index, device)
        copy.start()
        self.sent[index] = copy

    def along_z(self):
        for zr in range(1, self.nz):
            there = lax.rem(self.z + zr, self.nz)
            self.go(self.own, self.buf.at[self.z, self.f], zr, (there, self.f))

    def first(self, zr):
        nz = self.nz
        if zr:
            self.sent[zr].wait_recv()
        for h in range(2):
            near = (self.z, flip(self.f, ORDER[h][0]))
            self.go(self.source(zr, 0, h), self.slot(zr, 0, h), nz + 2 * zr + h, near)
        self.core(zr, 0)

    def core(self, zr, i):
        other = (self.z, flip(self.f, 1))
        self.go(self.source(zr, 2 * i), self.slot(zr, 2 * i), 7 * self.nz + 4 * zr + i, other)

    def second(self, zr):
        nz = self.nz
        for h in range(2):
            self.sent[nz + 2 * zr + h].wait_recv()
            near = (self.z, flip(self.f, ORDER[h][1]))
            for i, r in enumerate((0, ORDER[h][0])):
                self.go(self.source(zr, r, h), self.slot(zr, r, h), 3 * nz + 4 * zr + 2 * h + i, near)

    def third(self, zr):
        for k in range(4):
            self.sent[3 * self.nz + 4 * zr + k].wait_recv()
        for i in range(1, 4):
            self.core(zr, i)

    def fourth(self, zr):
        for i in range(4):
            self.sent[7 * self.nz + 4 * zr + i].wait_recv()

    def end(self):
        for copy in self.sent.values():
            copy.wait_send()


class Reduce:
    @staticmethod
    def copies(nz):
        return 11 * nz

    @staticmethod
    def scratch(nz, rows, width):
        return [
            pltpu.VMEM((nz, 4, rows, width), BF16),
            pltpu.VMEM((nz, 2, rows, width), BF16),
            pltpu.VMEM((nz, rows, width), BF16),
            pltpu.VMEM((nz, rows, width), BF16),
        ]

    def __init__(self, terms, bufs, sems, nz, z, f):
        self.terms, self.sems, self.nz, self.z, self.f = terms, sems, nz, z, f
        self.by_core, self.by_near, self.by_far, self.by_z = bufs
        self.width = terms.shape[-1]
        self.sent = {}

    def piece(self, zr):
        return lax.rem(self.z + zr, self.nz) if zr else self.z

    def go(self, src, dst, index, device):
        copy = send(src, dst, self.sems, index, device)
        copy.start()
        self.sent[index] = copy

    def core(self, zr):
        other = flip(self.f, 1)
        for i in range(4):
            self.go(
                self.terms.at[self.piece(zr), flip(self.f, 1 | 2 * i)], self.by_core.at[zr, i], 4 * zr + i, (self.z, other)
            )

    def near(self, zr):
        for i in range(4):
            self.sent[4 * zr + i].wait_recv()
            self.by_core[zr, i] = self.by_core[zr, i] + self.terms[self.piece(zr), flip(self.f, 2 * i)]
        for h in range(2):
            first, last = ORDER[1 - h]
            cols = pl.ds(*halves(self.width)[h])
            for i, r in enumerate((last, 6)):
                self.go(
                    self.by_core.at[zr, (last if i == 0 else 6) // 2, :, cols],
                    self.by_near.at[zr, i, :, cols],
                    4 * self.nz + 4 * zr + 2 * h + i,
                    (self.z, flip(self.f, last)),
                )

    def far(self, zr):
        for h in range(2):
            first, last = ORDER[1 - h]
            at, size = halves(self.width)[h]
            cols = slice(at, at + size)
            for i, r in enumerate((0, first)):
                self.sent[4 * self.nz + 4 * zr + 2 * h + i].wait_recv()
                self.by_near[zr, i, :, cols] = self.by_near[zr, i, :, cols] + self.by_core[zr, r // 2, :, cols]
            cols = pl.ds(at, size)
            self.go(
                self.by_near.at[zr, 1, :, cols], self.by_far.at[zr, :, cols], 8 * self.nz + 2 * zr + h,
                (self.z, flip(self.f, first)),
            )

    def along_z(self, zr):
        for h in range(2):
            at, size = halves(self.width)[h]
            cols = slice(at, at + size)
            self.sent[8 * self.nz + 2 * zr + h].wait_recv()
            self.by_far[zr, :, cols] = self.by_far[zr, :, cols] + self.by_near[zr, 0, :, cols]
        if zr:
            self.go(self.by_far.at[zr], self.by_z.at[zr], 10 * self.nz + zr, (self.piece(zr), self.f))

    def total(self):
        result = self.by_far[0].astype(F32)
        for zr in range(1, self.nz):
            self.sent[10 * self.nz + zr].wait_recv()
            result = result + self.by_z[zr].astype(F32)
        return result

    def end(self):
        for copy in self.sent.values():
            copy.wait_send()


def near_devices(z, f):
    return [(z, flip(f, 1)), (z, flip(f, 2)), (z, flip(f, 4))]


def z_devices(z, f, nz):
    return [(lax.rem(z + zr, nz), f) for zr in range(1, nz)]


def pair_of(count):
    return [pltpu.SemaphoreType.DMA((count,))] * 2


def first_head(member):
    return HEADS * member // 8


def out_blocks(member, dense):
    return first_head(member) * HD // dense, (first_head(member + 1) * HD - 1) // dense


def head_owner(head):
    return (8 * head + 7) // HEADS


def prologue_kernel(
    tok_ref, wqkv_ref, wout_ref, router_ref, sup_ref, gains_ref, ids_ref,
    seq_ref, wq_ref, wo_ref, tail_ref, all_ids_ref,
    qpack, tpack, tok_sems_s, tok_sems_r, all_s, all_r, wo_s, wo_r, own_sems,
    *, nz, nf, shared, heads, real,
):
    z, f = place()
    me, count = z * nf + f, nz * nf
    dense = wqkv_ref.shape[0]
    width = wqkv_ref.shape[1] // 3
    experts = router_ref.shape[1]
    hidden = shared * count
    greet_all(nz, nf)

    toks = (tok_sems_s, tok_sems_r)
    to_near = []
    for i, r in enumerate((2, 4, 6)):
        copy = send(tok_ref, seq_ref.at[f], toks, i, (z, flip(f, r)))
        copy.start()
        to_near.append(copy)
    to_core = [send(tok_ref, seq_ref.at[f], toks, 3, (z, flip(f, 1)))]
    to_core[0].start()
    own = [pltpu.make_async_copy(tok_ref, seq_ref.at[f], own_sems.at[0])]

    for m in range(8):
        for s in range(SLOTS):
            h = heads[m * SLOTS + s]
            if real[m * SLOTS + s]:
                qpack[m, s] = jnp.concatenate(
                    [wqkv_ref[:, c * width + h * HD : c * width + (h + 1) * HD] for c in range(3)], axis=1
                )
    pad = jnp.zeros((dense, TAIL - shared - experts), BF16)
    pad_two = jnp.zeros((dense, TAIL - shared - 2), BF16)
    for d in range(count):
        tpack[d] = jnp.concatenate(
            [
                sup_ref[:, d * shared : (d + 1) * shared], router_ref[...], pad,
                sup_ref[:, hidden + d * shared : hidden + (d + 1) * shared], gains_ref[...], pad_two,
            ],
            axis=1,
        )

    def two(m):
        return first_head(m + 1) - first_head(m) == 2

    def copies(d):
        device = (d // nf, d % nf)
        at = lambda k: (all_s.at[k, d], all_r.at[k, me])
        make = lambda src, dst, k: pltpu.make_async_remote_copy(
            src, dst, *at(k), device_id=device, device_id_type=MESH
        )
        return (
            make(qpack.at[d % nf, 0], wq_ref.at[0, me], 0),
            make(qpack.at[d % nf, 1], wq_ref.at[1, me], 1),
            make(tpack.at[d], tail_ref.at[me], 2),
            make(ids_ref, all_ids_ref.at[me], 3),
        )

    def out_copy(d):
        low, _ = out_blocks(d % nf, dense)
        return pltpu.make_async_remote_copy(
            wout_ref, wo_ref.at[me - low], wo_s.at[d], wo_r.at[me - low],
            device_id=(d // nf, d % nf), device_id_type=MESH,
        )

    def wanted(d, block):
        low, high = out_blocks(d % nf, dense)
        return (low <= block) & (block <= high)

    def start(i, _):
        d = (me + i) % count
        q0, q1, tail, ids = copies(d)
        q0.start()

        @pl.when(two(d % nf))
        def _():
            q1.start()

        tail.start()
        ids.start()

        @pl.when(wanted(d, me))
        def _():
            out_copy(d).start()

        return 0

    lax.fori_loop(1, count, start, 0)

    own += [
        pltpu.make_async_copy(qpack.at[f, 0], wq_ref.at[0, me], own_sems.at[1]),
        pltpu.make_async_copy(tpack.at[me], tail_ref.at[me], own_sems.at[2]),
        pltpu.make_async_copy(ids_ref, all_ids_ref.at[me], own_sems.at[3]),
    ]
    for copy in own:
        copy.start()
    own_two = pltpu.make_async_copy(qpack.at[f, 1], wq_ref.at[1, me], own_sems.at[4])
    low, high = out_blocks(f, dense)
    own_out = pltpu.make_async_copy(wout_ref, wo_ref.at[me - low], own_sems.at[5])

    @pl.when(two(f))
    def _():
        own_two.start()

    @pl.when(wanted(me, me))
    def _():
        own_out.start()

    for i, r in enumerate((2, 4, 6)):
        to_near[i].wait_recv()
        slot = seq_ref.at[flip(f, r)]
        copy = send(slot, slot, toks, 4 + i, (z, flip(f, 1)))
        copy.start()
        to_core.append(copy)
    for copy in to_core:
        copy.wait()
    for copy in to_near:
        copy.wait_send()

    def came(src, dst, k, d):
        return pltpu.make_async_remote_copy(
            src, dst, all_s.at[k, d], all_r.at[k, d], device_id=(d // nf, d % nf), device_id_type=MESH
        )

    def finish(i, _):
        d = (me + i) % count
        came(qpack.at[f, 0], wq_ref.at[0, d], 0, d).wait_recv()

        @pl.when(two(f))
        def _():
            came(qpack.at[f, 1], wq_ref.at[1, d], 1, d).wait_recv()

        came(tpack.at[d], tail_ref.at[d], 2, d).wait_recv()
        came(ids_ref, all_ids_ref.at[d], 3, d).wait_recv()
        q0, q1, tail, ids = copies(d)
        q0.wait_send()

        @pl.when(two(d % nf))
        def _():
            q1.wait_send()

        tail.wait_send()
        ids.wait_send()

        @pl.when(wanted(d, me))
        def _():
            out_copy(d).wait_send()

        return 0

    lax.fori_loop(1, count, finish, 0)
    for j in range(wo_ref.shape[0]):

        @pl.when((low + j <= high) & (low + j != me))
        def _():
            pltpu.make_async_remote_copy(
                wout_ref, wo_ref.at[j], wo_s.at[j], wo_r.at[j], device_id=(z, flip(f, 1)), device_id_type=MESH
            ).wait_recv()

    for copy in own:
        copy.wait()

    @pl.when(two(f))
    def _():
        own_two.wait()

    @pl.when(wanted(me, me))
    def _():
        own_out.wait()


def prologue(tok, wqkv, wout, router, sup, gains, ids, nz, nf, shared):
    rows, width = tok.shape
    dense, count = wqkv.shape[0], nz * nf
    heads, real = head_table(8)
    return pl.pallas_call(
        functools.partial(prologue_kernel, nz=nz, nf=nf, shared=shared, heads=heads, real=real),
        out_shape=(
            jax.ShapeDtypeStruct((8, rows, width), BF16),
            jax.ShapeDtypeStruct((SLOTS, count, dense, 3 * HD), BF16),
            jax.ShapeDtypeStruct((8, dense, width), BF16),
            jax.ShapeDtypeStruct((count, dense, 2 * TAIL), BF16),
            jax.ShapeDtypeStruct((count, *ids.shape), jnp.int32),
        ),
        in_specs=[ANY, VMEM, ANY, VMEM, VMEM, VMEM, ANY],
        out_specs=(ANY,) * 5,
        scratch_shapes=[
            pltpu.VMEM((8, SLOTS, dense, 3 * HD), BF16),
            pltpu.VMEM((count, dense, 2 * TAIL), BF16),
            *pair_of(7),
            pltpu.SemaphoreType.DMA((4, count)),
            pltpu.SemaphoreType.DMA((4, count)),
            pltpu.SemaphoreType.DMA((count,)),
            pltpu.SemaphoreType.DMA((8,)),
            pltpu.SemaphoreType.DMA((6,)),
        ],
        compiler_params=pltpu.CompilerParams(
            collective_id=1, has_side_effects=True, vmem_limit_bytes=16 * 2**20
        ),
        name="prologue",
    )(tok, wqkv, wout, router, sup, gains, ids)


def spread_kernel(
    part_ref, tok_ref, gain_ref, og_ref, eup_ref,
    all_normed_ref, all_grad_ref, pieces_ref, mixed_ref, normed_ref,
    pack, *refs, nz, hidden,
):
    bufs, (rs, rr, xs, xr, gs, gr, es, er, own_sems) = refs[:4], refs[4:]
    z, f = place()
    up_rows = eup_ref.shape[1]
    greet(near_devices(z, f) + z_devices(z, f, nz))
    reduce = Reduce(part_ref, bufs, (rs, rr), 1, 0, f)
    reduce.z = z
    reduce.piece = lambda zr: 0
    reduce.core(0)
    grads = Gather(og_ref, all_grad_ref, (gs, gr), nz, z, f)
    grads.along_z()
    own = [pltpu.make_async_copy(og_ref, all_grad_ref.at[z, f], own_sems.at[0])]
    own[0].start()
    grads.first(0)
    full = nz * hidden
    for t in range(nz):
        pack[t] = jnp.concatenate(
            [
                eup_ref[e, :, g * full + t * hidden : g * full + (t + 1) * hidden]
                for g in range(2)
                for e in range(2)
            ],
            axis=1,
        )
    ups = []
    for zr in range(1, nz):
        there = lax.rem(z + zr, nz)
        copy = send(pack.at[there], pieces_ref.at[z], (es, er), zr, (there, f))
        copy.start()
        ups.append(copy)
    own.append(pltpu.make_async_copy(pack.at[z], pieces_ref.at[z], own_sems.at[1]))
    own[1].start()

    reduce.near(0)
    grads.second(0)
    reduce.far(0)
    reduce.along_z(0)
    mixed = tok_ref[...].astype(F32) + reduce.by_far[0].astype(F32)
    mixed_ref[...] = mixed
    normed_ref[...] = (mixed * rms_scale(mixed) * gain_ref[...]).astype(BF16)
    rows = Gather(normed_ref, all_normed_ref, (xs, xr), nz, z, f)
    rows.along_z()
    own.append(pltpu.make_async_copy(normed_ref, all_normed_ref.at[z, f], own_sems.at[2]))
    own[2].start()
    rows.first(0)
    rows.second(0)
    for zr in range(1, nz):
        for part in (grads, rows):
            part.first(zr)
        for part in (grads, rows):
            part.second(zr)
    for zr in range(nz):
        for part in (grads, rows):
            part.third(zr)
    for zr in range(nz):
        for part in (grads, rows):
            part.fourth(zr)
    for part in (reduce, grads, rows):
        part.end()
    for copy in ups + own:
        copy.wait()


def spread(part, tok, gain, og, eup, nz, nf):
    rows, width = tok.shape
    hidden = eup.shape[2] // (2 * nz)
    up_rows = eup.shape[1]
    return pl.pallas_call(
        functools.partial(spread_kernel, nz=nz, hidden=hidden),
        out_shape=(
            jax.ShapeDtypeStruct((nz, 8, rows, width), BF16),
            jax.ShapeDtypeStruct((nz, 8, rows, width), BF16),
            jax.ShapeDtypeStruct((nz, up_rows, 4 * hidden), BF16),
            jax.ShapeDtypeStruct((rows, width), F32),
            jax.ShapeDtypeStruct((rows, width), BF16),
        ),
        in_specs=[VMEM, VMEM, VMEM, ANY, VMEM],
        out_specs=(ANY, ANY, ANY, VMEM, VMEM),
        scratch_shapes=[
            pltpu.VMEM((nz, up_rows, 4 * hidden), BF16),
            *Reduce.scratch(1, rows, width),
            *pair_of(Reduce.copies(1)),
            *pair_of(Gather.copies(nz)),
            *pair_of(Gather.copies(nz)),
            *pair_of(nz),
            pltpu.SemaphoreType.DMA((3,)),
        ],
        compiler_params=pltpu.CompilerParams(
            collective_id=2, has_side_effects=True, vmem_limit_bytes=40 * 2**20
        ),
        name="spread",
    )(part.reshape(1, 8, rows, width), tok, gain, og, eup)


def route_grads(gx, og, mixed, normed, router, marks, gain):
    width = mixed.shape[1]
    scale = rms_scale(mixed)
    normal = mixed * scale
    logits = jnp.where(marks > 0.5, dot(normed, router), NEG)
    weights = jnp.exp(logits - jnp.max(logits, axis=-1, keepdims=True))
    probs = weights / jnp.sum(weights, axis=-1, keepdims=True)
    grad_gates = gx[:, width:]
    grad_logits = (probs * (grad_gates - jnp.sum(probs * grad_gates, axis=-1, keepdims=True))).astype(BF16)
    grad_router = dot_tn(normed, grad_logits)
    grad_normed = gx[:, :width] + dot_nt(grad_logits, router)
    ones = jnp.where(lax.broadcasted_iota(jnp.int32, (mixed.shape[0], HD), 1) == TAIL - 1, 1.0, 0.0)
    grad_gain = lax.dot_general(
        grad_normed * normal, ones, (((0,), (0,)), ((), ())),
        precision=lax.Precision.HIGHEST, preferred_element_type=F32,
    )
    grad_mixed = og.astype(F32) + norm_back(grad_normed, normal, scale, gain)
    return grad_mixed, pltpu.roll(grad_router + grad_gain, TAIL, 1)


def turn_kernel(
    gx_ref, og_ref, mixed_ref, normed_ref, router_ref, mark_ref, gain_ref,
    seq_ref, gm_ref, small_ref,
    low, *refs, nz,
):
    bufs, (rs, rr, gs, gr, own_sem) = refs[:4], refs[4:]
    z, f = place()
    greet(near_devices(z, f) + z_devices(z, f, nz))
    reduce = Reduce(gx_ref, bufs, (rs, rr), nz, z, f)
    order = list(range(1, nz)) + [0]
    for step in (reduce.core, reduce.near, reduce.far, reduce.along_z):
        for zr in order:
            step(zr)
    grad_mixed, small = route_grads(
        reduce.total(), og_ref[...], mixed_ref[...], normed_ref[...], router_ref[...], mark_ref[...], gain_ref[...]
    )
    gm_ref[...] = grad_mixed
    low[...] = grad_mixed.astype(BF16)
    rows = Gather(low, seq_ref, (gs, gr), 1, 0, f)
    rows.z = z
    rows.piece = lambda zr: 0
    own = pltpu.make_async_copy(low, seq_ref.at[0, f], own_sem.at[0])
    own.start()
    rows.first(0)
    small_ref[...] = small
    rows.second(0)
    rows.third(0)
    rows.fourth(0)
    own.wait()
    rows.end()
    reduce.end()


def turn(gx, og, mixed, normed, router, marks, gain, nz, nf):
    rows, width = mixed.shape
    return pl.pallas_call(
        functools.partial(turn_kernel, nz=nz),
        out_shape=(
            jax.ShapeDtypeStruct((1, 8, rows, width), BF16),
            jax.ShapeDtypeStruct((rows, width), F32),
            jax.ShapeDtypeStruct((width, HD), F32),
        ),
        in_specs=[VMEM] * 7,
        out_specs=(ANY, VMEM, VMEM),
        scratch_shapes=[
            pltpu.VMEM((rows, width), BF16),
            *Reduce.scratch(nz, rows, width + HD),
            *pair_of(Reduce.copies(nz)),
            *pair_of(Gather.copies(1)),
            pltpu.SemaphoreType.DMA((1,)),
        ],
        compiler_params=pltpu.CompilerParams(
            collective_id=3, has_side_effects=True, vmem_limit_bytes=48 * 2**20
        ),
        name="turn",
    )(gx.reshape(nz, 8, rows, width + HD), og, mixed, normed, router, marks, gain)


def finish_kernel(
    part_ref, out_ref, gw_ref, gwo_ref, small_ref, eup_ref, tok_ref, mixed_ref, gm_ref, gain_ref,
    block_ref, gtok_ref, gwqkv_ref, gwout_ref, all_small_ref, pieces_ref,
    gws, gwos, smalls, *refs, nz, nf, heads, real,
):
    bufs, refs = refs[:8], refs[8:]
    rs, rr, os_, or_, all_s, all_r, wo_s, wo_r, es, er, own_sems = refs
    z, f = place()
    me, count = z * nf + f, nz * nf
    dense = gw_ref.shape[2]
    greet_all(nz, nf)
    reduce = Reduce(part_ref, bufs[:4], (rs, rr), 1, 0, f)
    reduce.z = z
    reduce.piece = lambda zr: 0
    reduce.core(0)

    def two(m):
        return first_head(m + 1) - first_head(m) == 2

    def copies(d):
        device = (d // nf, d % nf)
        make = lambda src, dst, k: pltpu.make_async_remote_copy(
            src, dst, all_s.at[k, d], all_r.at[k, me], device_id=device, device_id_type=MESH
        )
        return (
            make(gw_ref.at[0, d], gws.at[0, me], 0),
            make(gw_ref.at[1, d], gws.at[1, me], 1),
            make(small_ref.at[d], smalls.at[me], 2),
        )

    def wanted(m, block):
        low, high = out_blocks(m, dense)
        return (low <= block) & (block <= high)

    def owner_of(block):
        return head_owner(block * dense // HD)

    def out_copy(d):
        low, _ = out_blocks(f, dense)
        k = 2 * z + f - owner_of(d)
        return pltpu.make_async_remote_copy(
            gwo_ref.at[d - low], gwos.at[k], wo_s.at[d - low], wo_r.at[k],
            device_id=(d // nf, d % nf), device_id_type=MESH,
        )

    def start(i, _):
        d = (me + i) % count
        q0, q1, small = copies(d)
        q0.start()

        @pl.when(two(f))
        def _():
            q1.start()

        small.start()

        @pl.when(wanted(f, d))
        def _():
            out_copy(d).start()

        return 0

    lax.fori_loop(1, count, start, 0)
    own = [
        pltpu.make_async_copy(gw_ref.at[0, me], gws.at[0, me], own_sems.at[0]),
        pltpu.make_async_copy(small_ref.at[me], smalls.at[me], own_sems.at[1]),
        pltpu.make_async_copy(eup_ref.at[z], pieces_ref.at[z], own_sems.at[2]),
    ]
    for copy in own:
        copy.start()
    own_two = pltpu.make_async_copy(gw_ref.at[1, me], gws.at[1, me], own_sems.at[3])
    low, _ = out_blocks(f, dense)
    own_slot = 2 * z + f - owner_of(me)
    own_out = pltpu.make_async_copy(gwo_ref.at[me - low], gwos.at[own_slot], own_sems.at[4])

    @pl.when(two(f))
    def _():
        own_two.start()

    @pl.when(wanted(f, me))
    def _():
        own_out.start()

    ups = []
    for zr in range(1, nz):
        there = lax.rem(z + zr, nz)
        copy = send(eup_ref.at[there], pieces_ref.at[z], (es, er), zr, (there, f))
        copy.start()
        ups.append(copy)

    outs = Reduce(out_ref, bufs[4:], (os_, or_), nz, z, f)
    order = list(range(1, nz)) + [0]
    for zr in order:
        outs.core(zr)
    reduce.near(0)
    reduce.far(0)
    for zr in order:
        outs.near(zr)
    reduce.along_z(0)
    x = tok_ref[...].astype(F32)
    scale = rms_scale(x)
    gtok_ref[...] = (
        gm_ref[...] + norm_back(reduce.by_far[0].astype(F32), x * scale, scale, gain_ref[...])
    ).astype(BF16)
    for step in (outs.far, outs.along_z):
        for zr in order:
            step(zr)
    block_ref[...] = (mixed_ref[...] + outs.total()).astype(BF16)

    def came(src, dst, k, d):
        return pltpu.make_async_remote_copy(
            src, dst, all_s.at[k, d], all_r.at[k, d], device_id=(d // nf, d % nf), device_id_type=MESH
        )

    def finish(i, _):
        d = (me + i) % count
        came(gw_ref.at[0, d], gws.at[0, d], 0, d).wait_recv()

        @pl.when(two(d % nf))
        def _():
            came(gw_ref.at[1, d], gws.at[1, d], 1, d).wait_recv()

        came(small_ref.at[d], smalls.at[d], 2, d).wait_recv()
        q0, q1, small = copies(d)
        q0.wait_send()

        @pl.when(two(f))
        def _():
            q1.wait_send()

        small.wait_send()

        @pl.when(wanted(f, d))
        def _():
            out_copy(d).wait_send()

        return 0

    lax.fori_loop(1, count, finish, 0)
    for copy in own:
        copy.wait()

    @pl.when(two(f))
    def _():
        own_two.wait()

    @pl.when(wanted(f, me))
    def _():
        own_out.wait()

    owner = owner_of(me)
    next_owner = head_owner((me * dense + dense - 1) // HD)
    for k in range(2 * nz):
        other = k % 2 == 1
        there = ((next_owner != owner) if other else True) & ((k // 2 != z) | (f != owner + k % 2))

        @pl.when(there)
        def _():
            pltpu.make_async_remote_copy(
                gwo_ref.at[0], gwos.at[k], wo_s.at[0], wo_r.at[k], device_id=(z, flip(f, 1)), device_id_type=MESH
            ).wait_recv()

    gwout_ref[...] = sum(gwos[2 * t].astype(F32) for t in range(nz))

    @pl.when(next_owner != owner)
    def _():
        gwout_ref[...] += sum(gwos[2 * t + 1].astype(F32) for t in range(nz))

    width = part_ref.shape[-1]
    for m in range(8):
        for s in range(SLOTS):
            if real[m * SLOTS + s]:
                h = heads[m * SLOTS + s]
                both = sum(gws[s, t * nf + m].astype(F32) for t in range(nz))
                for c in range(3):
                    gwqkv_ref[:, c * width + h * HD : c * width + (h + 1) * HD] = both[:, c * HD : (c + 1) * HD]
    all_small_ref[...] = smalls[...]
    for copy in ups:
        copy.wait()
    reduce.end()
    outs.end()


def finish(part, out_part, gw, gwo, small, geup, tok, mixed, gm, gain, nz, nf):
    rows, width = tok.shape
    count = nz * nf
    dense = width // count
    pieces = geup.reshape(nz, width // nz, geup.shape[1])
    heads, real = head_table(8)
    return pl.pallas_call(
        functools.partial(finish_kernel, nz=nz, nf=nf, heads=heads, real=real),
        out_shape=(
            jax.ShapeDtypeStruct((rows, width), BF16),
            jax.ShapeDtypeStruct((rows, width), BF16),
            jax.ShapeDtypeStruct((dense, 3 * width), F32),
            jax.ShapeDtypeStruct((dense, width), F32),
            jax.ShapeDtypeStruct((count, dense, HD), F32),
            jax.ShapeDtypeStruct(pieces.shape, BF16),
        ),
        in_specs=[VMEM, VMEM, ANY, ANY, ANY, ANY, VMEM, VMEM, VMEM, VMEM],
        out_specs=(VMEM, VMEM, VMEM, VMEM, VMEM, ANY),
        scratch_shapes=[
            pltpu.VMEM((SLOTS, count, dense, 3 * HD), BF16),
            pltpu.VMEM((2 * nz, dense, width), BF16),
            pltpu.VMEM((count, dense, HD), F32),
            *Reduce.scratch(1, rows, width),
            *Reduce.scratch(nz, rows, width),
            *pair_of(Reduce.copies(1)),
            *pair_of(Reduce.copies(nz)),
            pltpu.SemaphoreType.DMA((3, count)),
            pltpu.SemaphoreType.DMA((3, count)),
            pltpu.SemaphoreType.DMA((8,)),
            pltpu.SemaphoreType.DMA((2 * nz,)),
            *pair_of(nz),
            pltpu.SemaphoreType.DMA((5,)),
        ],
        compiler_params=pltpu.CompilerParams(
            collective_id=4, has_side_effects=True, vmem_limit_bytes=56 * 2**20
        ),
        name="finish",
    )(
        part.reshape(1, 8, rows, width), out_part.reshape(nz, 8, rows, width), gw.reshape(SLOTS, count, dense, 3 * HD),
        gwo, small.reshape(count, dense, HD), pieces, tok, mixed, gm, gain,
    )


def unpack_kernel(
    pieces_ref, small_ref, wqkv_ref, gwqkv_ref, gain_ref,
    geup_ref, gsup_ref, grouter_ref, ggain_ref,
    *, shared, experts,
):
    nz = pieces_ref.shape[0]
    hidden = pieces_ref.shape[2] // 4
    for t in range(nz):
        for g in range(2):
            for e in range(2):
                at = (2 * g + e) * hidden
                to = (g * nz + t) * hidden
                geup_ref[e, :, to : to + hidden] = pieces_ref[t, :, at : at + hidden].astype(F32)
    count = small_ref.shape[0]
    total = small_ref[0]
    for d in range(count):
        if d:
            total = total + small_ref[d]
        for g in range(2):
            to = (g * count + d) * shared
            gsup_ref[:, to : to + shared] = small_ref[d, :, g * TAIL : g * TAIL + shared]
    grouter_ref[...] = total[:, shared : shared + experts]
    one = jnp.sum(wqkv_ref[...].astype(F32) * gwqkv_ref[...], axis=-1, keepdims=True) / gain_ref[:, :1].astype(F32)
    ggain_ref[...] = jnp.concatenate([one, total[:, HD - 1 :]], axis=1)


def unpack(pieces, small, wqkv, gwqkv, gains, shared, experts):
    nz, up_rows, packed = pieces.shape
    count, dense, _ = small.shape
    return pl.pallas_call(
        functools.partial(unpack_kernel, shared=shared, experts=experts),
        out_shape=(
            jax.ShapeDtypeStruct((2, up_rows, nz * packed // 2), F32),
            jax.ShapeDtypeStruct((dense, 2 * count * shared), F32),
            jax.ShapeDtypeStruct((dense, experts), F32),
            jax.ShapeDtypeStruct((dense, 2), F32),
        ),
        in_specs=[VMEM] * 5,
        out_specs=(VMEM,) * 4,
        compiler_params=pltpu.CompilerParams(vmem_limit_bytes=32 * 2**20),
        name="unpack",
    )(pieces, small, wqkv, gwqkv, gains)


def tables():
    pos = jnp.arange(SEQ, dtype=F32)
    freqs = ROPE ** (-jnp.arange(HD // 2, dtype=F32) * 2.0 / HD)
    angles = pos[:, None] * freqs[None, :]
    cosine = jnp.concatenate([jnp.cos(angles)] * 2, axis=1)
    sine = jnp.concatenate([-jnp.sin(angles), jnp.sin(angles)], axis=1)
    return cosine, sine


def local_near(
    mesh, tokens, out_grad, segment_ids, expert_ids, attn_gain, ffn_gain, w_qkv, w_out,
    w_router, w_shared_up, w_shared_down, w_expert_up, w_expert_down,
):
    nz, nf = mesh.shape["dp"], mesh.shape["fsdp"]
    rows, width = tokens.shape
    total = rows * nz * nf
    top_k, experts = expert_ids.shape[1], w_router.shape[1]
    dense = w_qkv.shape[0]
    hidden, shared = w_expert_down.shape[1], w_shared_down.shape[0]
    z, f = lax.axis_index("dp"), lax.axis_index("fsdp")
    first, last = first_head(f), first_head(f + 1)
    low, _ = out_blocks(f, dense)

    gains = jnp.stack([attn_gain, ffn_gain], axis=1)
    ids = jnp.concatenate([expert_ids.T, segment_ids[None]], axis=0)
    seq_tok, wq, wo, tail, all_ids = prologue(
        tokens, w_qkv, w_out, w_router, w_shared_up, gains, ids, nz, nf, shared
    )
    real = first + jnp.arange(SLOTS) < last
    w = jnp.where(real[:, None, None], wq.reshape(SLOTS, width, 3 * HD), 0)
    wo = lax.dynamic_slice(wo.reshape(8 * dense, width), (first * HD - low * dense, 0), (SLOTS * HD, width))
    wo = jnp.where(jnp.repeat(real, HD)[:, None], wo, 0)
    tail = tail.reshape(width, 2 * TAIL)
    all_gains = tail[:, TAIL + shared : TAIL + shared + 2].T.astype(F32)
    gain_one, gain_two = all_gains[:1], all_gains[1:]
    router = jnp.pad(tail[:, shared : shared + experts], ((0, 0), (TAIL + shared, TAIL - shared - experts)))
    lane = jnp.arange(HD, dtype=jnp.int32) - TAIL - shared
    chosen = all_ids[:, 0, :, None] == lane
    for k in range(1, top_k):
        chosen = chosen | (all_ids[:, k, :, None] == lane)
    marks = chosen.astype(BF16).reshape(total, HD)
    own_marks = lax.dynamic_slice(marks, ((z * nf + f) * rows, 0), (rows, HD)).astype(F32)
    own = (lane[None, :] == (2 * f + jnp.arange(2, dtype=jnp.int32))[:, None]).astype(F32)
    seg = lax.dynamic_slice(all_ids[:, top_k], (z * nf, 0), (nf, rows)).reshape(SEQ)
    cosine, sine = tables()
    segq = jnp.broadcast_to(seg[:, None], (SEQ, HD))
    segk = jnp.broadcast_to(seg[None, :], (8, SEQ))

    part, normed_one, qkv, attn, lse = attn_forward(
        seq_tok.reshape(SEQ, width), gain_one, w, wo, cosine, sine, segq, segk
    )
    all_normed, all_grad, pieces, mixed, normed = spread(part, tokens, gain_two, out_grad, w_expert_up, nz, nf)
    out_part, gx, geup, gtail, gedown, gsdown = ffn(
        all_normed.reshape(total, width), all_grad.reshape(total, width), marks, own, pieces.reshape(width, 4 * hidden),
        tail, w_expert_down.reshape(2 * hidden, width), w_shared_down,
    )
    seq_gm, grad_mixed, small = turn(gx, out_grad, mixed, normed, router, own_marks, gain_two, nz, nf)
    part_back, gw, gwo = attn_backward(
        seq_gm.reshape(SEQ, width), wo, w, normed_one, qkv, attn, lse, cosine, sine, segq, segk
    )
    gwo = lax.dynamic_update_slice(jnp.zeros((8 * dense, width), BF16), gwo, (first * HD - low * dense, 0))
    block_out, tokens_grad, grad_wqkv, grad_wout, smalls, gpieces = finish(
        part_back, out_part, gw, gwo.reshape(8, dense, width), small + gtail, geup, tokens, mixed, grad_mixed, gain_one,
        nz, nf,
    )
    grad_eup, grad_sup, grad_router, grad_gains = unpack(gpieces, smalls, w_qkv, grad_wqkv, gains, shared, experts)
    return (
        block_out, tokens_grad, grad_gains[:, 0], grad_gains[:, 1], grad_wqkv, grad_wout, grad_router, grad_sup,
        gsdown, grad_eup, gedown.reshape(2, hidden, width),
    )


def local_far(
    mesh, tokens, out_grad, segment_ids, expert_ids, attn_gain, ffn_gain, w_qkv, w_out,
    w_router, w_shared_up, w_shared_down, w_expert_up, w_expert_down,
):
    nz, nf = mesh.shape["dp"], mesh.shape["fsdp"]
    nd = nz * nf
    rows, width = tokens.shape
    group = SEQ // rows
    experts = w_router.shape[1]
    dense = w_qkv.shape[0]
    hidden, shared = w_expert_down.shape[1], w_shared_down.shape[0]
    up_rows = w_expert_up.shape[1]
    both = ("dp", "fsdp")
    groups = None if nf == group else [[a + i for i in range(group)] for a in range(0, nf, group)]
    f = lax.axis_index("fsdp")
    member = lax.rem(f, group)
    heads, real = head_table(group)

    by_head = w_qkv.reshape(dense, 3, HEADS, HD)
    empty = jnp.zeros((dense, 3, HD), BF16)
    cols = jnp.stack([by_head[:, :, h] if r else empty for h, r in zip(heads, real)], axis=0)
    cols = cols.reshape(group, SLOTS, dense, 3 * HD)
    cols = jnp.tile(cols, (nf // group, 1, 1, 1))
    cols = lax.all_to_all(cols, "fsdp", 0, 0, tiled=True)
    w = lax.all_gather(cols, "dp", axis=0, tiled=True).transpose(1, 0, 2, 3).reshape(SLOTS, width, 3 * HD)
    full_out = lax.all_gather(w_out, both, axis=0, tiled=True)
    first = HEADS * member // group
    own_real = (first + jnp.arange(SLOTS) < HEADS * (member + 1) // group).astype(BF16)
    padded = jnp.pad(full_out, ((0, (SLOTS - 1) * HD), (0, 0)))
    wo = lax.dynamic_slice(padded, (first * HD, 0), (SLOTS * HD, width))
    wo = wo * jnp.repeat(own_real, HD)[:, None]
    gains = lax.all_gather(jnp.stack([attn_gain, ffn_gain], axis=1).astype(F32), both, axis=0, tiled=True)
    gain_one, gain_two = gains[:, 0], gains[:, 1]
    router = lax.all_gather(w_router, both, axis=0, tiled=True)
    sup = w_shared_up.reshape(dense, 2, nd, shared).transpose(2, 0, 1, 3).reshape(nd, dense, 2 * shared)
    sup = lax.all_to_all(sup, both, 0, 0, tiled=True).reshape(width, 2, shared)
    eup = w_expert_up.reshape(2, up_rows, 2, nz, hidden).transpose(3, 1, 2, 0, 4)
    eup = lax.all_to_all(eup, "dp", 0, 0, tiled=True).reshape(width, 4 * hidden)
    rest = jnp.zeros((width, TAIL - shared), BF16)
    tail = jnp.concatenate([sup[:, 0], router, rest[:, experts:], sup[:, 1], rest], axis=1)
    chosen = jnp.any(expert_ids[:, :, None] == jnp.arange(experts, dtype=jnp.int32), axis=1)
    at = TAIL + shared
    marks = jnp.pad(chosen.astype(BF16), ((0, 0), (at, HD - experts - at)))
    marks = lax.all_gather(marks, both, axis=0, tiled=True)
    lane = jnp.arange(HD, dtype=jnp.int32)
    own = (lane[None, :] == (at + 2 * f + jnp.arange(2, dtype=jnp.int32))[:, None]).astype(F32)
    cosine, sine = tables()
    seg = lax.all_gather(segment_ids, "fsdp", axis=0, tiled=True, axis_index_groups=groups)
    segq = jnp.broadcast_to(seg[:, None], (SEQ, HD))
    segk = jnp.broadcast_to(seg[None, :], (8, SEQ))

    seq_tokens = lax.all_gather(tokens, "fsdp", axis=0, tiled=True, axis_index_groups=groups)
    part, normed_one, qkv, attn, lse = attn_forward(
        seq_tokens, gain_one[None, :], w, wo, cosine, sine, segq, segk
    )
    projected = lax.psum_scatter(part, "fsdp", scatter_dimension=0, tiled=True, axis_index_groups=groups)
    inputs = tokens.astype(F32)
    mixed = inputs + projected.astype(F32)
    scale_two = rms_scale(mixed)
    normal_two = mixed * scale_two
    normed_two = (normal_two * gain_two).astype(BF16)
    all_normed = lax.all_gather(normed_two, both, axis=0, tiled=True)
    all_grad = lax.all_gather(out_grad, both, axis=0, tiled=True)
    out_part, gx_part, geup, gtail, gedown, gsdown = ffn(
        all_normed, all_grad, marks, own, eup, tail, w_expert_down.reshape(2 * hidden, width), w_shared_down
    )
    gx = lax.psum_scatter(gx_part, both, scatter_dimension=0, tiled=True).astype(F32)
    ffn_out = lax.psum_scatter(out_part, both, scatter_dimension=0, tiled=True).astype(F32)
    block_out = (mixed + ffn_out).astype(BF16)

    logits = jnp.where(chosen, dot(normed_two, router), NEG)
    probs = jax.nn.softmax(logits, axis=-1)
    grad_gates = gx[:, width + at : width + at + experts]
    grad_logits = (
        probs * (grad_gates - jnp.sum(probs * grad_gates, axis=-1, keepdims=True))
    ).astype(BF16)
    grad_router = dot_tn(normed_two, grad_logits)
    grad_normed = gx[:, :width] + dot_nt(grad_logits, router)
    grad_gain_two = jnp.sum(grad_normed * normal_two, axis=0)
    grad_mixed = out_grad.astype(F32) + norm_back(grad_normed, normal_two, scale_two, gain_two)

    seq_gm = lax.all_gather(grad_mixed.astype(BF16), "fsdp", axis=0, tiled=True, axis_index_groups=groups)
    part_back, gw, gwo = attn_backward(
        seq_gm, wo, w, normed_one, qkv, attn, lse, cosine, sine, segq, segk
    )
    grad_normed_one = lax.psum_scatter(
        part_back, "fsdp", scatter_dimension=0, tiled=True, axis_index_groups=groups
    ).astype(F32)
    scale_one = rms_scale(inputs)
    normal_one = inputs * scale_one
    grad_gain_one = jnp.sum(grad_normed_one * normal_one, axis=0)
    tokens_grad = (grad_mixed + norm_back(grad_normed_one, normal_one, scale_one, gain_one)).astype(BF16)

    gw = lax.psum_scatter(gw, "dp", scatter_dimension=1, tiled=True)
    gw = lax.all_to_all(gw.reshape(SLOTS, nf, dense, 3 * HD), "fsdp", 1, 1, tiled=True).astype(F32)
    gw = jnp.sum(gw.reshape(SLOTS, nf // group, group, dense, 3, HD), axis=1)
    picked = [gw[i % SLOTS, i // SLOTS] for i in range(group * SLOTS) if real[i]]
    grad_wqkv = jnp.stack(picked, axis=2).reshape(dense, 3 * width)
    gwo = gwo * jnp.repeat(own_real, HD)[:, None]
    all_gwo = jnp.zeros(((HEADS + SLOTS - 1) * HD, width), BF16)
    all_gwo = lax.dynamic_update_slice(all_gwo, gwo, (first * HD, 0))[: HEADS * HD]
    grad_wout = lax.psum_scatter(all_gwo, both, scatter_dimension=0, tiled=True).astype(F32)
    small = jnp.concatenate([grad_router, grad_gain_one[:, None], grad_gain_two[:, None]], axis=1)
    small = lax.psum_scatter(small, both, scatter_dimension=0, tiled=True)
    gsup = jnp.stack([gtail[:, :shared], gtail[:, TAIL : TAIL + shared]], axis=1)
    gsup = lax.all_to_all(gsup.reshape(nd, dense, 2 * shared).astype(BF16), both, 0, 0, tiled=True)
    grad_sup = gsup.reshape(nd, dense, 2, shared).transpose(1, 2, 0, 3).reshape(dense, 2 * nd * shared).astype(F32)
    geup = lax.all_to_all(geup.reshape(nz, up_rows, 2, 2, hidden), "dp", 0, 0, tiled=True)
    grad_eup = geup.transpose(3, 1, 2, 0, 4).reshape(2, up_rows, 2 * nz * hidden).astype(F32)
    return (
        block_out, tokens_grad, small[:, experts], small[:, experts + 1], grad_wqkv, grad_wout,
        small[:, :experts], grad_sup, gsdown, grad_eup, gedown.reshape(2, hidden, width),
    )


def solution(mesh):
    one, two = P(("dp", "fsdp")), P(("dp", "fsdp"), None)
    three = P("fsdp", "dp", None)

    def local(tokens, *rest):
        near = mesh.shape["fsdp"] == 8 == SEQ // tokens.shape[0] and mesh.shape["dp"] <= 4
        return (local_near if near else local_far)(mesh, tokens, *rest)

    return jax.shard_map(
        local,
        mesh=mesh,
        in_specs=(two, two, one, two, one, one, two, two, two, two, two, three, three),
        out_specs=(two, two, one, one, two, two, two, two, two, three, three),
        check_vma=False,
    )
```

```python
import functools

import jax
import jax.numpy as jnp
import numpy as np
from jax import lax
from jax.experimental import pallas as pl
from jax.experimental.pallas import tpu as pltpu
from jax.sharding import PartitionSpec as P

HEADS = 10
HD = 128
SEQ = 1024
SLOTS = 2
EPS = 1e-06
ROPE = 10000.0
NEG = -1e30
TAIL = 64
F32 = jnp.float32
BF16 = jnp.bfloat16


MESH = pl.DeviceIdType.MESH
VMEM = pl.BlockSpec(memory_space=pltpu.VMEM)
ANY = pl.BlockSpec(memory_space=pl.ANY)


def up_to(value, step):
    return -(-value // step) * step


def rms_scale(values):
    return lax.rsqrt(jnp.mean(values * values, axis=-1, keepdims=True) + EPS)


def norm_back(grad_normed, normal_rows, scale_rows, gain_rows):
    scaled = grad_normed * gain_rows
    return scale_rows * (
        scaled - normal_rows * jnp.mean(scaled * normal_rows, axis=-1, keepdims=True)
    )


def head_table(group):
    heads, real = [], []
    for i in range(group):
        own = list(range(HEADS * i // group, HEADS * (i + 1) // group))
        assert len(own) <= SLOTS
        heads += own + [0] * (SLOTS - len(own))
        real += [1] * len(own) + [0] * (SLOTS - len(own))
    return heads, real


def dot(a, b):
    return jnp.dot(a, b, preferred_element_type=F32)


def dot_nt(a, b):
    return lax.dot_general(a, b, (((1,), (1,)), ((), ())), preferred_element_type=F32)


def dot_tn(a, b):
    return lax.dot_general(a, b, (((0,), (0,)), ((), ())), preferred_element_type=F32)


def attn_project(i, block, x, gain, w_ref, cos_ref, sin_ref, normed_ref, qkv_ref):
    rows = pl.ds(pl.multiple_of(i * block, block), block)
    x = x.astype(F32)
    normed = (x * rms_scale(x) * gain).astype(BF16)
    normed_ref[rows, :] = normed
    cosine, sine = cos_ref[rows, :], sin_ref[rows, :]
    for s in range(SLOTS):
        proj = dot(normed, w_ref[s])
        for c in range(3):
            piece = proj[:, c * HD : (c + 1) * HD]
            if c < 2:
                piece = piece * cosine + pltpu.roll(piece, HD // 2, 1) * sine
            at = (3 * s + c) * HD
            qkv_ref[rows, at : at + HD] = piece.astype(BF16)


def attn_block(i, block, segq_ref, segk_ref, qkv_ref, attn_ref, lse_ref):
    scale = HD**-0.5
    rows = slice(i * block, (i + 1) * block)
    keys = (i + 1) * block
    row_pos = i * block + lax.broadcasted_iota(jnp.int32, (block, keys), 0)
    key_pos = lax.broadcasted_iota(jnp.int32, (block, keys), 1)
    allowed = (key_pos <= row_pos) & (segq_ref[rows, :1] == segk_ref[:1, :keys])
    outs = []
    for s in range(SLOTS):
        at = 3 * s * HD
        q = qkv_ref[rows, at : at + HD]
        k = qkv_ref[:keys, at + HD : at + 2 * HD]
        v = qkv_ref[:keys, at + 2 * HD : at + 3 * HD]
        scores = jnp.where(allowed, dot_nt(q, k) * scale, NEG)
        top = jnp.max(scores, axis=-1, keepdims=True)
        weights = jnp.exp(scores - top)
        total = jnp.sum(weights, axis=-1, keepdims=True)
        out = dot(weights.astype(BF16), v) / total
        lse_ref[rows, s * HD : (s + 1) * HD] = jnp.broadcast_to(top + jnp.log(total), (block, HD))
        low = out.astype(BF16)
        attn_ref[rows, s * HD : (s + 1) * HD] = low
        outs.append(low)
    return jnp.concatenate(outs, axis=-1)


def attn_forward_kernel(
    tok_ref, gain_ref, w_ref, wo_ref, cos_ref, sin_ref, segq_ref, segk_ref,
    part_ref, normed_ref, qkv_ref, attn_ref, lse_ref,
    *, block,
):
    count = tok_ref.shape[0] // block

    def project(i, _):
        x = tok_ref[pl.ds(pl.multiple_of(i * block, block), block), :]
        attn_project(i, block, x, gain_ref[...], w_ref, cos_ref, sin_ref, normed_ref, qkv_ref)
        return 0

    lax.fori_loop(0, count, project, 0)
    for i in range(count):
        outs = attn_block(i, block, segq_ref, segk_ref, qkv_ref, attn_ref, lse_ref)
        part_ref[i * block : (i + 1) * block, :] = dot(outs, wo_ref[...]).astype(BF16)


def attn_forward(tok, gain, w, wo, cosine, sine, segq, segk):
    length, width = tok.shape
    return pl.pallas_call(
        functools.partial(attn_forward_kernel, block=256),
        out_shape=(
            jax.ShapeDtypeStruct((length, width), BF16),
            jax.ShapeDtypeStruct((length, width), BF16),
            jax.ShapeDtypeStruct((length, 3 * SLOTS * HD), BF16),
            jax.ShapeDtypeStruct((length, SLOTS * HD), BF16),
            jax.ShapeDtypeStruct((length, SLOTS * HD), F32),
        ),
        in_specs=[VMEM] * 8,
        out_specs=(VMEM,) * 5,
        compiler_params=pltpu.CompilerParams(vmem_limit_bytes=56 * 2**20),
        cost_estimate=pl.CostEstimate(
            flops=2 * length * width * 4 * SLOTS * HD + 4 * SLOTS * HD * length * length,
            bytes_accessed=10 * length * width,
            transcendentals=SLOTS * length * length,
        ),
        name="attn_forward",
    )(tok, gain, w, wo, cosine, sine, segq, segk)


def attn_back_block(
    i, block, gm_ref, wo_ref, qkv_ref, attn_ref, lse_ref, cos_ref, sin_ref, segq_ref, segk_ref, gkv_ref, gqkv_ref
):
    scale = HD**-0.5
    rows = slice(i * block, (i + 1) * block)
    keys = (i + 1) * block
    row_pos = i * block + lax.broadcasted_iota(jnp.int32, (block, keys), 0)
    key_pos = lax.broadcasted_iota(jnp.int32, (block, keys), 1)
    allowed = (key_pos <= row_pos) & (segq_ref[rows, :1] == segk_ref[:1, :keys])
    grad_attn = dot_nt(gm_ref[rows, :], wo_ref[...]).astype(BF16)
    for s in range(SLOTS):
        at = 3 * s * HD
        cut = slice(s * HD, (s + 1) * HD)
        q = qkv_ref[rows, at : at + HD]
        k = qkv_ref[:keys, at + HD : at + 2 * HD]
        v = qkv_ref[:keys, at + 2 * HD : at + 3 * HD]
        ga = grad_attn[:, cut]
        delta = jnp.sum(ga.astype(F32) * attn_ref[rows, cut].astype(F32), axis=-1, keepdims=True)
        scores = dot_nt(q, k) * scale
        probs = jnp.where(allowed, jnp.exp(scores - lse_ref[rows, s * HD : s * HD + 1]), 0.0)
        gs = (probs * (dot_nt(ga, v) - delta)).astype(BF16)
        gq = dot(gs, k) * scale
        gq = gq * cos_ref[rows, :] - pltpu.roll(gq, HD // 2, 1) * sin_ref[rows, :]
        gqkv_ref[rows, at : at + HD] = gq.astype(BF16)
        gkv_ref[:keys, 2 * s * HD : (2 * s + 1) * HD] += dot_tn(gs, q)
        gkv_ref[:keys, (2 * s + 1) * HD : (2 * s + 2) * HD] += dot_tn(probs.astype(BF16), ga)


def attn_back_keys(w_ref, cos_ref, sin_ref, gkv_ref, gqkv_ref, wt_ref):
    step = 3 * HD
    for s in range(SLOTS):
        at = s * step
        gk = gkv_ref[:, 2 * s * HD : (2 * s + 1) * HD] * HD**-0.5
        gk = gk * cos_ref[...] - pltpu.roll(gk, HD // 2, 1) * sin_ref[...]
        gqkv_ref[:, at + HD : at + 2 * HD] = gk.astype(BF16)
        gqkv_ref[:, at + 2 * HD : at + 3 * HD] = gkv_ref[:, (2 * s + 1) * HD : (2 * s + 2) * HD].astype(BF16)
        wt_ref[s * step : (s + 1) * step, :] = w_ref[s].T


def attn_backward_kernel(
    gm_ref, wo_ref, w_ref, normed_ref, qkv_ref, attn_ref, lse_ref, cos_ref, sin_ref,
    segq_ref, segk_ref,
    part_ref, gw_ref, gwo_ref,
    gkv_ref, gqkv_ref, wt_ref,
    *, block,
):
    count = gm_ref.shape[0] // block
    step = 3 * HD
    gkv_ref[...] = jnp.zeros_like(gkv_ref)
    for i in range(count):
        attn_back_block(
            i, block, gm_ref, wo_ref, qkv_ref, attn_ref, lse_ref, cos_ref, sin_ref, segq_ref, segk_ref, gkv_ref, gqkv_ref
        )
    attn_back_keys(w_ref, cos_ref, sin_ref, gkv_ref, gqkv_ref, wt_ref)
    for i in range(count):
        rows = slice(i * block, (i + 1) * block)
        part_ref[rows, :] = dot(gqkv_ref[rows, :], wt_ref[...]).astype(BF16)
    for s in range(SLOTS):
        gw_ref[s] = dot_tn(normed_ref[...], gqkv_ref[:, s * step : (s + 1) * step]).astype(BF16)
    gwo_ref[...] = dot_tn(attn_ref[...], gm_ref[...]).astype(BF16)


def attn_backward(gm, wo, w, normed, qkv, attn, lse, cosine, sine, segq, segk):
    length, width = gm.shape
    return pl.pallas_call(
        functools.partial(attn_backward_kernel, block=256),
        out_shape=(
            jax.ShapeDtypeStruct((length, width), BF16),
            jax.ShapeDtypeStruct((SLOTS, width, 3 * HD), BF16),
            jax.ShapeDtypeStruct((SLOTS * HD, width), BF16),
        ),
        in_specs=[VMEM] * 11,
        out_specs=(VMEM,) * 3,
        scratch_shapes=[
            pltpu.VMEM((length, 2 * SLOTS * HD), F32),
            pltpu.VMEM((length, 3 * SLOTS * HD), BF16),
            pltpu.VMEM((3 * SLOTS * HD, width), BF16),
        ],
        compiler_params=pltpu.CompilerParams(vmem_limit_bytes=56 * 2**20),
        cost_estimate=pl.CostEstimate(
            flops=4 * length * width * 4 * SLOTS * HD + 10 * SLOTS * HD * length * length,
            bytes_accessed=10 * length * width,
            transcendentals=SLOTS * length * length,
        ),
        name="attn_backward",
    )(gm, wo, w, normed, qkv, attn, lse, cosine, sine, segq, segk)


def ffn_weights(eup_ref, tail_ref, edown_ref, sdown_ref, up_ref, upt_ref, down_ref, downt_ref):
    width, half = downt_ref.shape
    pair, shared = edown_ref.shape[0], sdown_ref.shape[0]
    gap = half - pair - TAIL
    between = [jnp.zeros((width, gap), BF16)] if gap else []
    up_ref[...] = jnp.concatenate(
        [eup_ref[:, :pair], *between, tail_ref[:, :TAIL], eup_ref[:, pair:], *between, tail_ref[:, TAIL:]], axis=1
    )
    between = [jnp.zeros((gap, width), BF16)] if gap else []
    down_ref[...] = jnp.concatenate(
        [edown_ref[...], *between, sdown_ref[...], jnp.zeros((TAIL - shared, width), BF16)], axis=0
    )
    upt_ref[...] = up_ref[...].T
    downt_ref[...] = down_ref[...].T


def ffn_rows(x, g, marks, own, up_ref, upt_ref, down_ref, downt_ref, hidden, shared):
    half = down_ref.shape[0]
    pair = 2 * hidden
    pre = dot(x, up_ref[...])
    gate, up = pre[:, :half], pre[:, half:]
    logits = jnp.where(marks.astype(F32) > 0.5, gate[:, half - HD :], NEG)
    weights = jnp.exp(logits - jnp.max(logits, axis=-1, keepdims=True))
    probs = weights / jnp.sum(weights, axis=-1, keepdims=True)
    p0 = jnp.sum(probs * own[0:1, :], axis=-1, keepdims=True)
    p1 = jnp.sum(probs * own[1:2, :], axis=-1, keepdims=True)
    lane = lax.broadcasted_iota(jnp.int32, (1, half), 1)
    in0 = lane < hidden
    in1 = (lane >= hidden) & (lane < pair)
    rest = jnp.where((lane >= half - TAIL) & (lane < half - TAIL + shared), 1.0, 0.0)
    weight = jnp.where(in0, p0, jnp.where(in1, p1, rest))
    sig = jax.nn.sigmoid(gate)
    silu = gate * sig
    act = silu * up
    acts = (act * weight).astype(BF16)
    out = dot(acts, down_ref[...]).astype(BF16)
    grad = dot(g, downt_ref[...])
    both = act * grad
    d0 = jnp.sum(jnp.where(in0, both, 0.0), axis=-1, keepdims=True)
    d1 = jnp.sum(jnp.where(in1, both, 0.0), axis=-1, keepdims=True)
    grad = grad * weight
    grad_gate = grad * up * sig * (1.0 + gate * (1.0 - sig))
    grad_up = grad * silu
    grad_pre = jnp.concatenate([grad_gate, grad_up], axis=-1).astype(BF16)
    gates = (d0 * own[0:1, :] + d1 * own[1:2, :]).astype(BF16)
    gx = jnp.concatenate([dot(grad_pre, upt_ref[...]).astype(BF16), gates], axis=-1)
    return out, gx, grad_pre, acts


def ffn_kernel(
    x_ref, g_ref, mark_ref, own_ref, eup_ref, tail_ref, edown_ref, sdown_ref,
    out_ref, gx_ref, geup_ref, gtail_ref, gedown_ref, gsdown_ref,
    up_ref, upt_ref, down_ref, downt_ref, gup_ref, gdown_ref,
    *, hidden, shared,
):
    step = pl.program_id(0)
    half = down_ref.shape[0]
    pair = 2 * hidden

    @pl.when(step == 0)
    def _():
        gup_ref[...] = jnp.zeros_like(gup_ref)
        gdown_ref[...] = jnp.zeros_like(gdown_ref)
        ffn_weights(eup_ref, tail_ref, edown_ref, sdown_ref, up_ref, upt_ref, down_ref, downt_ref)

    out, gx, grad_pre, acts = ffn_rows(
        x_ref[...], g_ref[...], mark_ref[...], own_ref[...], up_ref, upt_ref, down_ref, downt_ref, hidden, shared
    )
    out_ref[...] = out
    gx_ref[...] = gx
    gup_ref[...] += dot_tn(x_ref[...], grad_pre)
    gdown_ref[...] += dot_tn(acts, g_ref[...])

    @pl.when(step == pl.num_programs(0) - 1)
    def _():
        geup_ref[...] = jnp.concatenate([gup_ref[:, :pair], gup_ref[:, half : half + pair]], axis=1).astype(BF16)
        gtail_ref[...] = jnp.concatenate([gup_ref[:, half - TAIL : half], gup_ref[:, 2 * half - TAIL :]], axis=1)
        gedown_ref[...] = gdown_ref[:pair, :]
        gsdown_ref[...] = gdown_ref[half - TAIL : half - TAIL + shared, :]


def ffn(x, g, marks, own, eup, tail, edown, sdown):
    total, width = x.shape
    pair, shared = edown.shape[0], sdown.shape[0]
    half = up_to(pair + TAIL, HD)
    tile = 512
    row = lambda n: pl.BlockSpec((tile, n), lambda i: (i, 0))
    return pl.pallas_call(
        functools.partial(ffn_kernel, hidden=pair // 2, shared=shared),
        out_shape=(
            jax.ShapeDtypeStruct((total, width), BF16),
            jax.ShapeDtypeStruct((total, width + HD), BF16),
            jax.ShapeDtypeStruct((width, 2 * pair), BF16),
            jax.ShapeDtypeStruct((width, HD), F32),
            jax.ShapeDtypeStruct((pair, width), F32),
            jax.ShapeDtypeStruct((shared, width), F32),
        ),
        grid=(total // tile,),
        in_specs=[row(width), row(width), row(HD)] + [VMEM] * 5,
        out_specs=(row(width), row(width + HD), VMEM, VMEM, VMEM, VMEM),
        scratch_shapes=[
            pltpu.VMEM((width, 2 * half), BF16),
            pltpu.VMEM((2 * half, width), BF16),
            pltpu.VMEM((half, width), BF16),
            pltpu.VMEM((width, half), BF16),
            pltpu.VMEM((width, 2 * half), F32),
            pltpu.VMEM((half, width), F32),
        ],
        compiler_params=pltpu.CompilerParams(vmem_limit_bytes=60 * 2**20),
        cost_estimate=pl.CostEstimate(
            flops=2 * total * width * 9 * half,
            bytes_accessed=8 * total * width,
            transcendentals=total * half,
        ),
        name="ffn",
    )(x, g, marks, own, eup, tail, edown, sdown)


def flip(f, bits):
    for b in (1, 2, 4):
        if bits & b:
            f = f + b - 2 * b * (f // b % 2)
    return f


def place():
    return lax.axis_index("dp"), lax.axis_index("fsdp")


def greet(devices):
    barrier = pltpu.get_barrier_semaphore()
    for device in devices:
        pl.semaphore_signal(barrier, inc=1, device_id=device, device_id_type=MESH)
    pl.semaphore_wait(barrier, len(devices))


def greet_all(nz, nf):
    barrier = pltpu.get_barrier_semaphore()
    z, f = place()
    me, count = z * nf + f, nz * nf

    def hail(i, _):
        d = (me + i) % count
        pl.semaphore_signal(barrier, inc=1, device_id=(d // nf, d % nf), device_id_type=MESH)
        return 0

    lax.fori_loop(1, count, hail, 0)
    pl.semaphore_wait(barrier, count - 1)


def send(src, dst, sems, index, device):
    return pltpu.make_async_remote_copy(
        src, dst, sems[0].at[index], sems[1].at[index], device_id=device, device_id_type=MESH
    )


ORDER = ((2, 4), (4, 2))


def halves(rows):
    return ((0, rows // 2), (rows // 2, rows - rows // 2))


def away(j, nz):
    if nz < 3:
        return j
    if isinstance(j, int):
        return j if j < 2 else nz - 1 if j == 2 else j - 1
    return jnp.where(j < 2, j, jnp.where(j == 2, nz - 1, j - 1))


class Gather:
    @staticmethod
    def copies(nz):
        return 11 * nz

    def __init__(self, buf, sems, nz, z, f):
        self.buf, self.sems, self.nz, self.z, self.f = buf, sems, nz, z, f

    def slot(self, j, r, h=None):
        piece = lax.rem(self.z - away(j, self.nz) + self.nz, self.nz) if self.nz > 1 else 0
        ref = self.buf.at[piece, flip(self.f, r)]
        return ref if h is None else ref.at[pl.ds(*halves(self.buf.shape[-2])[h])]

    def here(self, j, r, h, index, device):
        ref = self.slot(j, r, h)
        return send(ref, ref, self.sems, index, device)

    def by_z(self, j):
        own = self.slot(0, 0)
        return send(own, own, self.sems, j, (lax.rem(self.z + away(j, self.nz), self.nz), self.f))

    def near(self, j, h):
        return self.here(j, 0, h, self.nz + 2 * j + h, (self.z, flip(self.f, ORDER[h][0])))

    def far(self, j, h, i):
        r = ORDER[h][0] if i else 0
        return self.here(j, r, h, 3 * self.nz + 4 * j + 2 * h + i, (self.z, flip(self.f, ORDER[h][1])))

    def core(self, j, i):
        return self.here(j, 2 * i, None, 7 * self.nz + 4 * j + i, (self.z, flip(self.f, 1)))

    def along_z(self, j):
        if 1 < j <= self.nz:
            self.by_z(j - 1).wait_send()
        if j < self.nz:
            self.by_z(j).start()

    def first(self, j, own=False):
        if not own:
            self.by_z(j).wait_recv()
        for h in range(2):
            self.near(j, h).start()
        self.core(j, 0).start()

    def second(self, j):
        for h in range(2):
            self.near(j, h).wait_recv()
            for i in range(2):
                self.far(j, h, i).start()

    def third(self, j):
        for h in range(2):
            for i in range(2):
                self.far(j, h, i).wait_recv()
        for i in range(1, 4):
            self.core(j, i).start()

    def fourth(self, j):
        for i in range(4):
            self.core(j, i).wait_recv()

    def end(self, first=0):
        for j in range(first, self.nz):
            for h in range(2):
                self.near(j, h).wait_send()
                for i in range(2):
                    self.far(j, h, i).wait_send()
            for i in range(4):
                self.core(j, i).wait_send()


class Reduce:
    @staticmethod
    def copies(nz):
        return 11 * nz

    @staticmethod
    def scratch(nz, rows, width):
        return [
            pltpu.VMEM((nz, 4, rows, width), BF16),
            pltpu.VMEM((nz, 2, rows, width), BF16),
            pltpu.VMEM((nz, rows, width), BF16),
            pltpu.VMEM((nz, rows, width), BF16),
        ]

    def __init__(self, bufs, sems, nz, z, f):
        self.by_core, self.by_near, self.by_far, self.by_z = bufs
        self.sems, self.nz, self.z, self.f = sems, nz, z, f
        self.parts = halves(self.by_core.shape[-2])

    def core(self, j, i, src):
        to = self.by_core.at[j, i]
        return send(to if src is None else src, to, self.sems, 4 * j + i, (self.z, flip(self.f, 1)))

    def near(self, j, h, i):
        last = ORDER[1 - h][1]
        rows = pl.ds(*self.parts[h])
        return send(
            self.by_core.at[j, 3 if i else last // 2, rows], self.by_near.at[j, i, rows], self.sems,
            4 * self.nz + 4 * j + 2 * h + i, (self.z, flip(self.f, last)),
        )

    def far_copy(self, j, h):
        rows = pl.ds(*self.parts[h])
        return send(
            self.by_near.at[j, 1, rows], self.by_far.at[j, rows], self.sems,
            8 * self.nz + 2 * j + h, (self.z, flip(self.f, ORDER[1 - h][0])),
        )

    def z_copy(self, j):
        there = lax.rem(self.z - away(j, self.nz) + self.nz, self.nz)
        return send(self.by_far.at[j], self.by_z.at[j], self.sems, 10 * self.nz + j, (there, self.f))

    def send_near(self, j):
        for h in range(2):
            for i in range(2):
                self.near(j, h, i).start()

    def far(self, j):
        for h in range(2):
            at, size = self.parts[h]
            rows = slice(at, at + size)
            for i, r in enumerate((0, ORDER[1 - h][0])):
                self.near(j, h, i).wait_recv()
                self.by_near[j, i, rows] = self.by_near[j, i, rows] + self.by_core[j, r // 2, rows]
            self.far_copy(j, h).start()

    def along_z(self, j):
        for h in range(2):
            at, size = self.parts[h]
            rows = slice(at, at + size)
            self.far_copy(j, h).wait_recv()
            self.by_far[j, rows] = self.by_far[j, rows] + self.by_near[j, 0, rows]
        if isinstance(j, int):
            if j:
                self.z_copy(j).start()
        else:

            @pl.when(j > 0)
            def _():
                self.z_copy(j).start()

    def total(self):
        result = self.by_far[0].astype(F32)
        for j in range(1, self.nz):
            self.z_copy(j).wait_recv()
            result = result + self.by_z[j].astype(F32)
        return result

    def end(self):
        for j in range(self.nz):
            for h in range(2):
                for i in range(2):
                    self.near(j, h, i).wait_send()
                self.far_copy(j, h).wait_send()
            if j:
                self.z_copy(j).wait_send()


def near_devices(z, f):
    return [(z, flip(f, 1)), (z, flip(f, 2)), (z, flip(f, 4))]


def z_devices(z, f, nz):
    return [(lax.rem(z + zr, nz), f) for zr in range(1, nz)]


def pair_of(count):
    return [pltpu.SemaphoreType.DMA((count,))] * 2


def first_head(member):
    return HEADS * member // 8


def out_blocks(member, dense):
    return first_head(member) * HD // dense, (first_head(member + 1) * HD - 1) // dense


def head_owner(head):
    return (8 * head + 7) // HEADS


def front_kernel(
    tok_ref, wqkv_ref, wout_ref, router_ref, sup_ref, gains_ref, ids_ref, cos_ref, sin_ref, og_ref, eup_ref,
    w_ref, wo_ref, tail_ref, gain_ref, mark_ref, own_mark_ref, segq_ref, segk_ref,
    normed_ref, qkv_ref, attn_ref, lse_ref, mixed_ref, low_ref, plane_ref, all_grad_ref, pieces_ref,
    seq, wq, wo_in, all_ids, qpack, tpack, part, wide, pack, *refs, nz, nf, hidden, shared, heads, real,
):
    bufs, refs = refs[:4], refs[4:]
    tok_s, tok_r, all_s, all_r, wo_s, wo_r, rs, rr, gs, gr, xs, xr, es, er, own_sems = refs
    z, f = place()
    me, count = z * nf + f, nz * nf
    rows, width = tok_ref.shape
    dense = wqkv_ref.shape[0]
    experts = router_ref.shape[1]
    full = shared * count
    greet_all(nz, nf)

    toks = (tok_s, tok_r)
    to_near = [send(tok_ref, seq.at[f], toks, i, (z, flip(f, r))) for i, r in enumerate((2, 4, 6))]
    to_core = [send(tok_ref, seq.at[f], toks, 3, (z, flip(f, 1)))]
    own = [
        pltpu.make_async_copy(tok_ref, seq.at[f], own_sems.at[0]),
        pltpu.make_async_copy(ids_ref, all_ids.at[me], own_sems.at[1]),
        pltpu.make_async_copy(og_ref, all_grad_ref.at[z, f], own_sems.at[2]),
    ]
    for copy in to_near + to_core + own:
        copy.start()

    for m in range(8):
        for s in range(SLOTS):
            h = heads[m * SLOTS + s]
            if real[m * SLOTS + s]:
                qpack[m, s] = jnp.concatenate(
                    [wqkv_ref[:, c * width + h * HD : c * width + (h + 1) * HD] for c in range(3)], axis=1
                )
    pad = jnp.zeros((dense, TAIL - shared - experts), BF16)
    pad_two = jnp.zeros((dense, TAIL - shared - 2), BF16)
    for d in range(count):
        tpack[d] = jnp.concatenate(
            [
                sup_ref[:, d * shared : (d + 1) * shared], router_ref[...], pad,
                sup_ref[:, full + d * shared : full + (d + 1) * shared], gains_ref[...], pad_two,
            ],
            axis=1,
        )

    def two(m):
        return first_head(m + 1) - first_head(m) == 2

    def copies(d, k):
        src, dst = (
            (qpack.at[d % nf, 0], wq.at[0, me]),
            (qpack.at[d % nf, 1], wq.at[1, me]),
            (tpack.at[d], tail_ref.at[me]),
            (ids_ref, all_ids.at[me]),
        )[k]
        return pltpu.make_async_remote_copy(
            src, dst, all_s.at[k, d], all_r.at[k, me], device_id=(d // nf, d % nf), device_id_type=MESH
        )

    def came(d, k):
        dst = (wq.at[0, d], wq.at[1, d], tail_ref.at[d], all_ids.at[d])[k]
        return pltpu.make_async_remote_copy(
            dst, dst, all_s.at[k, d], all_r.at[k, d], device_id=(d // nf, d % nf), device_id_type=MESH
        )

    def out_copy(d):
        first, _ = out_blocks(d % nf, dense)
        return pltpu.make_async_remote_copy(
            wout_ref, wo_in.at[me - first], wo_s.at[d], wo_r.at[me - first],
            device_id=(d // nf, d % nf), device_id_type=MESH,
        )

    def wanted(d, block):
        low, high = out_blocks(d % nf, dense)
        return (low <= block) & (block <= high)

    def start(i, _):
        d = (me + i) % count
        copies(d, 0).start()

        @pl.when(two(d % nf))
        def _():
            copies(d, 1).start()

        copies(d, 2).start()
        copies(d, 3).start()
        return 0

    lax.fori_loop(1, count, start, 0)

    def start_out(i, _):
        d = (me + i) % count

        @pl.when(wanted(d, me))
        def _():
            out_copy(d).start()

        return 0

    lax.fori_loop(1, count, start_out, 0)
    own_packs = [
        pltpu.make_async_copy(qpack.at[f, 0], wq.at[0, me], own_sems.at[3]),
        pltpu.make_async_copy(tpack.at[me], tail_ref.at[me], own_sems.at[4]),
    ]
    for copy in own_packs:
        copy.start()
    own_two = pltpu.make_async_copy(qpack.at[f, 1], wq.at[1, me], own_sems.at[5])
    low, high = out_blocks(f, dense)
    own_out = pltpu.make_async_copy(wout_ref, wo_in.at[me - low], own_sems.at[6])

    @pl.when(two(f))
    def _():
        own_two.start()

    @pl.when(wanted(me, me))
    def _():
        own_out.start()

    whole = nz * hidden
    for t in range(nz):
        pack[t] = jnp.concatenate(
            [
                eup_ref[e, :, g * whole + t * hidden : g * whole + (t + 1) * hidden]
                for g in range(2)
                for e in range(2)
            ],
            axis=1,
        )
    for i, r in enumerate((2, 4, 6)):
        to_near[i].wait_recv()
        slot = seq.at[flip(f, r)]
        copy = send(slot, slot, toks, 4 + i, (z, flip(f, 1)))
        copy.start()
        to_core.append(copy)

    def arrive(i, _):
        d = (me + i) % count
        came(d, 0).wait_recv()

        @pl.when(two(f))
        def _():
            came(d, 1).wait_recv()

        came(d, 2).wait_recv()
        came(d, 3).wait_recv()
        return 0

    lax.fori_loop(1, count, arrive, 0)
    for copy in own + own_packs:
        copy.wait()

    @pl.when(two(f))
    def _():
        own_two.wait()

    for copy in to_core:
        copy.wait_recv()

    grads = Gather(all_grad_ref, (gs, gr), nz, z, f)
    grads.along_z(1)
    grads.first(0, own=True)

    w_ref[0] = wq[0].reshape(width, 3 * HD)
    w_ref[1] = jnp.where(two(f), wq[1].astype(F32), 0.0).reshape(width, 3 * HD).astype(BF16)
    gain_ref[...] = tail_ref[...].reshape(width, 2 * TAIL)[:, TAIL + shared : TAIL + shared + 2].astype(F32).T
    for m in range(8):
        ids = all_ids[z * nf + m]
        segk_ref[:, m * rows : (m + 1) * rows] = jnp.broadcast_to(ids[-1:], (8, rows))
        segq_ref[m * rows : (m + 1) * rows, :] = jnp.broadcast_to(ids.T[:, -1:], (rows, HD))
    block = 256
    gain_one = gain_ref[0:1, :]

    def project(i, _):
        x = seq[pl.ds(i * (block // rows), block // rows)].reshape(block, width)
        attn_project(i, block, x, gain_one, w_ref, cos_ref, sin_ref, normed_ref, qkv_ref)
        return 0

    lax.fori_loop(0, 8 * rows // block, project, 0)
    grads.second(0)
    grads.along_z(2)

    def arrive_out(j, _):
        @pl.when((low + j <= high) & (low + j != me))
        def _():
            pltpu.make_async_remote_copy(
                wo_in.at[j], wo_in.at[j], wo_s.at[j], wo_r.at[j], device_id=(z, flip(f, 1)), device_id_type=MESH
            ).wait_recv()

        return 0

    lax.fori_loop(0, wo_in.shape[0], arrive_out, 0)

    @pl.when(wanted(me, me))
    def _():
        own_out.wait()

    wide[...] = wo_in[...].astype(F32).reshape(wide.shape)
    offset = pl.multiple_of(first_head(f) * HD - low * dense, 8)
    wo_ref[:HD, :] = wide[pl.ds(offset, HD), :].astype(BF16)
    wo_ref[HD:, :] = jnp.where(two(f), wide[pl.ds(offset + HD, HD), :], 0.0).astype(BF16)
    reduce = Reduce(bufs, (rs, rr), 1, z, f)
    for i in range(8 * rows // block):
        outs = attn_block(i, block, segq_ref, segk_ref, qkv_ref, attn_ref, lse_ref)
        at = i * (block // rows)
        part[at : at + block // rows] = dot(outs, wo_ref[...]).astype(BF16).reshape(block // rows, rows, width)
        if i == 1:
            grads.third(0)
    for i in range(4):
        reduce.core(0, i, part.at[flip(f, 1 | 2 * i)]).start()
    for i in range(4):
        reduce.core(0, i, None).wait_recv()
        reduce.by_core[0, i] = reduce.by_core[0, i] + part[flip(f, 2 * i)]
    reduce.send_near(0)
    grads.along_z(3)
    reduce.far(0)
    reduce.along_z(0)
    mixed = tok_ref[...].astype(F32) + reduce.by_far[0].astype(F32)
    mixed_ref[...] = mixed
    low_ref[...] = (mixed * rms_scale(mixed) * gain_ref[1:2, :]).astype(BF16)
    near_own = pltpu.make_async_copy(low_ref, plane_ref.at[0, f], own_sems.at[7])
    near_own.start()
    near = Gather(plane_ref, (xs, xr), 1, z, f)
    near_own.wait()
    near.first(0, own=True)

    ups = []
    for j in range(1, nz):
        there = lax.rem(z + j, nz)
        copy = send(pack.at[there], pieces_ref.at[z], (es, er), j, (there, f))
        copy.start()
        ups.append(copy)
    ups.append(pltpu.make_async_copy(pack.at[z], pieces_ref.at[z], own_sems.at[8]))
    ups[-1].start()

    near.second(0)
    lane = lax.broadcasted_iota(jnp.int32, (rows, HD), 1) - TAIL - shared

    def mark(d, _):
        ids = all_ids[d].T
        found = ids[:, 0:1] == lane
        for k in range(1, ids.shape[1] - 1):
            found = found | (ids[:, k : k + 1] == lane)
        value = jnp.where(found, 1.0, 0.0)
        mark_ref[d] = value.astype(BF16)

        @pl.when(d == me)
        def _():
            own_mark_ref[...] = value

        return 0

    lax.fori_loop(0, count, mark, 0)
    near.third(0)
    for j in range(1, nz):
        grads.first(j)
        grads.second(j)
        if j + 3 <= nz:
            grads.along_z(j + 3)
        grads.third(j)
    for j in range(nz):
        grads.fourth(j)
    near.fourth(0)

    def left(i, _):
        d = (me + i) % count
        copies(d, 0).wait_send()

        @pl.when(two(d % nf))
        def _():
            copies(d, 1).wait_send()

        copies(d, 2).wait_send()
        copies(d, 3).wait_send()

        @pl.when(wanted(d, me))
        def _():
            out_copy(d).wait_send()

        return 0

    lax.fori_loop(1, count, left, 0)
    for copy in to_near + to_core:
        copy.wait_send()
    for i in range(4):
        reduce.core(0, i, part.at[0]).wait_send()
    reduce.end()
    grads.end()
    near.end()
    for copy in ups:
        copy.wait()


def front(tok, wqkv, wout, router, sup, gains, ids, cosine, sine, og, eup, nz, nf, shared):
    rows, width = tok.shape
    dense, count = wqkv.shape[0], nz * nf
    length = 8 * rows
    hidden, up_rows = eup.shape[2] // (2 * nz), eup.shape[1]
    heads, real = head_table(8)
    shape = jax.ShapeDtypeStruct
    return pl.pallas_call(
        functools.partial(front_kernel, nz=nz, nf=nf, hidden=hidden, shared=shared, heads=heads, real=real),
        out_shape=(
            shape((SLOTS, width, 3 * HD), BF16),
            shape((SLOTS * HD, width), BF16),
            shape((count, dense, 2 * TAIL), BF16),
            shape((2, width), F32),
            shape((count, rows, HD), BF16),
            shape((rows, HD), F32),
            shape((length, HD), jnp.int32),
            shape((8, length), jnp.int32),
            shape((length, width), BF16),
            shape((length, 3 * SLOTS * HD), BF16),
            shape((length, SLOTS * HD), BF16),
            shape((length, SLOTS * HD), F32),
            shape((rows, width), F32),
            shape((rows, width), BF16),
            shape((1, 8, rows, width), BF16),
            shape((nz, 8, rows, width), BF16),
            shape((nz, up_rows, 4 * hidden), BF16),
        ),
        in_specs=[VMEM] * 9 + [ANY, VMEM],
        out_specs=(VMEM,) * 14 + (ANY,) * 3,
        scratch_shapes=[
            pltpu.VMEM((8, rows, width), BF16),
            pltpu.VMEM((SLOTS, count, dense, 3 * HD), BF16),
            pltpu.VMEM((8, dense, width), BF16),
            pltpu.VMEM((count, *ids.shape), jnp.int32),
            pltpu.VMEM((8, SLOTS, dense, 3 * HD), BF16),
            pltpu.VMEM((count, dense, 2 * TAIL), BF16),
            pltpu.VMEM((8, rows, width), BF16),
            pltpu.VMEM((8 * dense, width), F32),
            pltpu.VMEM((nz, up_rows, 4 * hidden), BF16),
            *Reduce.scratch(1, rows, width),
            *pair_of(7),
            pltpu.SemaphoreType.DMA((4, count)),
            pltpu.SemaphoreType.DMA((4, count)),
            pltpu.SemaphoreType.DMA((count,)),
            pltpu.SemaphoreType.DMA((8,)),
            *pair_of(Reduce.copies(1)),
            *pair_of(Gather.copies(nz)),
            *pair_of(Gather.copies(1)),
            *pair_of(nz),
            pltpu.SemaphoreType.DMA((9,)),
        ],
        compiler_params=pltpu.CompilerParams(
            collective_id=1, has_side_effects=True, vmem_limit_bytes=58 * 2**20
        ),
        name="front",
    )(tok, wqkv, wout, router, sup, gains, ids, cosine, sine, og, eup)


def route_grads(gx, og, mixed, normed, router, marks, gain):
    width = mixed.shape[1]
    scale = rms_scale(mixed)
    normal = mixed * scale
    logits = jnp.where(marks > 0.5, dot(normed, router), NEG)
    weights = jnp.exp(logits - jnp.max(logits, axis=-1, keepdims=True))
    probs = weights / jnp.sum(weights, axis=-1, keepdims=True)
    grad_gates = gx[:, width:]
    grad_logits = (probs * (grad_gates - jnp.sum(probs * grad_gates, axis=-1, keepdims=True))).astype(BF16)
    grad_router = dot_tn(normed, grad_logits)
    grad_normed = gx[:, :width] + dot_nt(grad_logits, router)
    ones = jnp.where(lax.broadcasted_iota(jnp.int32, (mixed.shape[0], HD), 1) == TAIL - 1, 1.0, 0.0)
    grad_gain = lax.dot_general(
        grad_normed * normal, ones, (((0,), (0,)), ((), ())),
        precision=lax.Precision.HIGHEST, preferred_element_type=F32,
    )
    grad_mixed = og.astype(F32) + norm_back(grad_normed, normal, scale, gain)
    return grad_mixed, pltpu.roll(grad_router + grad_gain, TAIL, 1)


def experts_kernel(
    normed_ref, plane_ref, all_grad_ref, mark_ref, own_ref, eup_ref, tail_ref, edown_ref, sdown_ref,
    og_ref, mixed_ref, router_ref, own_mark_ref, gain_ref,
    out_ref, seq_ref, gm_ref, small_ref, pieces_ref, gedown_ref, gsdown_ref, all_normed_ref,
    up_ref, upt_ref, down_ref, downt_ref, gup_ref, gdown_ref,
    xt, gt, mt, px, po, low, *refs, nz, hidden, shared,
):
    bufs, (tile_sems, rs, rr, os_, or_, xs, xr, gs, gr, es, er, own_sems) = refs[:4], refs[4:]
    z, f = place()
    rows, width = mixed_ref.shape
    half = down_ref.shape[0]
    pair = 2 * hidden
    greet(near_devices(z, f) + z_devices(z, f, nz))
    own = pltpu.make_async_copy(normed_ref, all_normed_ref.at[z, f], own_sems.at[0])
    own.start()
    gather = Gather(all_normed_ref, (xs, xr), nz, z, f)
    reduce = Reduce(bufs, (rs, rr), nz, z, f)
    outs = Reduce([out_ref, out_ref, out_ref, out_ref], (os_, or_), nz, z, f)
    own.wait()
    gather.along_z(1)
    ffn_weights(eup_ref, tail_ref, edown_ref, sdown_ref, up_ref, upt_ref, down_ref, downt_ref)
    gup_ref[...] = jnp.zeros_like(gup_ref)
    gdown_ref[...] = jnp.zeros_like(gdown_ref)
    gather.along_z(2)
    if nz > 1:
        gather.first(1)

    def loads(i, rows_ref=all_normed_ref):
        j, t, slot = i // 4, i % 4, i % 2
        piece = lax.rem(z - away(j, nz) + nz, nz)
        base = f + (1 - 2 * (f % 2)) * (1 - t // 2) + (4 - 8 * (f // 4 % 2)) * (t % 2)
        copies = []
        for b in range(2):
            block = flip(base, 2 * b)
            there = piece if rows_ref is all_normed_ref else 0
            copies += [
                pltpu.make_async_copy(rows_ref.at[there, block], xt.at[slot, b], tile_sems.at[slot, b]),
                pltpu.make_async_copy(all_grad_ref.at[piece, block], gt.at[slot, b], tile_sems.at[slot, 2 + b]),
                pltpu.make_async_copy(mark_ref.at[piece, block], mt.at[slot, b], tile_sems.at[slot, 4 + b]),
            ]
        return copies

    for copy in loads(0, plane_ref):
        copy.start()
    last = 4 * nz - 1

    def tile(i, _):
        j, t, slot = i // 4, i % 4, i % 2
        more = j < nz - 1

        @pl.when((t == 0) & more)
        def _():
            gather.second(j + 1)

        @pl.when(i == 1)
        def _():
            gather.along_z(3)

        @pl.when((t == 2) & more)
        def _():
            gather.third(j + 1)

        @pl.when((t == 2) & (j < nz - 2))
        def _():
            gather.first(j + 2)

        @pl.when((t == 3) & more)
        def _():
            gather.fourth(j + 1)

        @pl.when((t == 0) & (j > 0))
        def _():
            for k in range(4):
                reduce.core(j - 1, k, px.at[k]).wait_send()
                outs.core(j - 1, k, po.at[k]).wait_send()

        for copy in loads(i):
            copy.wait()

        @pl.when(i < 3)
        def _():
            for copy in loads(i + 1, plane_ref):
                copy.start()

        @pl.when((i >= 3) & (i < last))
        def _():
            for copy in loads(i + 1):
                copy.start()

        x = xt[slot].reshape(2 * rows, width)
        g = gt[slot].reshape(2 * rows, width)
        out, gx, grad_pre, acts = ffn_rows(
            x, g, mt[slot].reshape(2 * rows, HD), own_ref[...], up_ref, upt_ref, down_ref, downt_ref, hidden, shared
        )
        at = pl.ds(2 * t, 2)
        po[at] = out.reshape(2, rows, width)
        px[at] = gx.reshape(2, rows, width + HD)
        gup_ref[...] += dot_tn(x, grad_pre)
        gdown_ref[...] += dot_tn(acts, g)

        @pl.when(t == 1)
        def _():
            for k in range(4):
                reduce.core(j, k, px.at[k]).start()
            for k in range(4):
                outs.core(j, k, po.at[k]).start()

        @pl.when((t == 1) & (j > 0))
        def _():
            reduce.far(j - 1)

        @pl.when((t == 2) & (j > 0))
        def _():
            reduce.along_z(j - 1)

        @pl.when(t == 3)
        def _():
            for k in range(4):
                reduce.core(j, k, None).wait_recv()
                reduce.by_core[j, k] = reduce.by_core[j, k] + px[4 + k]
            reduce.send_near(j)
            for k in range(4):
                outs.core(j, k, None).wait_recv()
                out_ref[j, k] = out_ref[j, k] + po[4 + k]

        return 0

    lax.fori_loop(0, 4 * nz, tile, 0)
    up_ref[:, : 2 * pair] = jnp.concatenate([gup_ref[:, :pair], gup_ref[:, half : half + pair]], axis=1).astype(BF16)
    up_rows = width // nz

    def ups(j):
        there = lax.rem(z + j, nz)
        src = up_ref.at[pl.ds(pl.multiple_of(there * up_rows, up_rows), up_rows), pl.ds(0, 2 * pair)]
        if j == 0:
            return pltpu.make_async_copy(src, pieces_ref.at[z], own_sems.at[1])
        return send(src, pieces_ref.at[z], (es, er), j, (there, f))

    for j in (1, nz - 1):
        ups(j).start()
    own_down = pltpu.make_async_copy(gdown_ref.at[pl.ds(0, pair)], gedown_ref, own_sems.at[2])
    own_down.start()
    ups(0).start()
    reduce.far(nz - 1)
    gtail = jnp.concatenate([gup_ref[:, half - TAIL : half], gup_ref[:, 2 * half - TAIL :]], axis=1)
    gsdown_ref[...] = gdown_ref[half - TAIL : half - TAIL + shared, :]
    reduce.along_z(nz - 1)
    for j in range(2, nz - 1):
        ups(j).start()
    grad_mixed, small = route_grads(
        reduce.total(), og_ref[...], mixed_ref[...], normed_ref[...], router_ref[...], own_mark_ref[...], gain_ref[...]
    )
    gm_ref[...] = grad_mixed
    low[...] = grad_mixed.astype(BF16)
    own = pltpu.make_async_copy(low, seq_ref.at[0, f], own_sems.at[3])
    own.start()
    turned = Gather(seq_ref, (gs, gr), 1, z, f)
    own.wait()
    turned.first(0, own=True)
    small_ref[...] = small + gtail
    turned.second(0)
    turned.third(0)
    turned.fourth(0)
    for k in range(4):
        reduce.core(nz - 1, k, px.at[k]).wait_send()
        outs.core(nz - 1, k, po.at[k]).wait_send()
    own_down.wait()
    for j in range(nz):
        ups(j).wait()
    for j in range(4, nz + 1):
        gather.along_z(j)
    gather.end(1)
    reduce.end()
    turned.end()


def experts_turn(
    normed, plane, all_grad, marks, own, eup, tail, edown, sdown, og, mixed, router, own_marks, gain, nz, nf
):
    rows, width = mixed.shape
    pair, shared = edown.shape[0], sdown.shape[0]
    half = up_to(pair + TAIL, HD)
    wide = width + HD
    return pl.pallas_call(
        functools.partial(experts_kernel, nz=nz, hidden=pair // 2, shared=shared),
        out_shape=(
            jax.ShapeDtypeStruct((nz, 4, rows, width), BF16),
            jax.ShapeDtypeStruct((1, 8, rows, width), BF16),
            jax.ShapeDtypeStruct((rows, width), F32),
            jax.ShapeDtypeStruct((width, HD), F32),
            jax.ShapeDtypeStruct((nz, width // nz, 2 * pair), BF16),
            jax.ShapeDtypeStruct((pair, width), F32),
            jax.ShapeDtypeStruct((shared, width), F32),
            jax.ShapeDtypeStruct((nz, 8, rows, width), BF16),
        ),
        in_specs=[VMEM, ANY, ANY, ANY] + [VMEM] * 10,
        out_specs=(VMEM, ANY, VMEM, VMEM, ANY, ANY, VMEM, ANY),
        scratch_shapes=[
            pltpu.VMEM((width, 2 * half), BF16),
            pltpu.VMEM((2 * half, width), BF16),
            pltpu.VMEM((half, width), BF16),
            pltpu.VMEM((width, half), BF16),
            pltpu.VMEM((width, 2 * half), F32),
            pltpu.VMEM((half, width), F32),
            pltpu.VMEM((2, 2, rows, width), BF16),
            pltpu.VMEM((2, 2, rows, width), BF16),
            pltpu.VMEM((2, 2, rows, HD), BF16),
            pltpu.VMEM((8, rows, wide), BF16),
            pltpu.VMEM((8, rows, width), BF16),
            pltpu.VMEM((rows, width), BF16),
            *Reduce.scratch(nz, rows, wide),
            pltpu.SemaphoreType.DMA((2, 6)),
            *pair_of(Reduce.copies(nz)),
            *pair_of(Reduce.copies(nz)),
            *pair_of(Gather.copies(nz)),
            *pair_of(Gather.copies(1)),
            *pair_of(nz),
            pltpu.SemaphoreType.DMA((4,)),
        ],
        compiler_params=pltpu.CompilerParams(
            collective_id=3, has_side_effects=True, vmem_limit_bytes=60 * 2**20
        ),
        name="experts_turn",
    )(
        normed, plane, all_grad, marks.reshape(nz, 8, rows, HD), own, eup, tail, edown, sdown, og, mixed, router, own_marks, gain
    )[:7]


def back_kernel(
    gm_ref, wo_ref, w_ref, normed_ref, qkv_ref, attn_ref, lse_ref, cos_ref, sin_ref, segq_ref, segk_ref,
    out_ref, small_ref, tok_ref, mixed_ref, own_gm_ref, gain_ref,
    block_ref, gtok_ref, gwqkv_ref, gwout_ref, all_small_ref,
    gkv_ref, gqkv_ref, wt_ref, part_ref, gw_ref, gwo_ref, gws, gwos, smalls, *refs, nz, nf, heads, real,
):
    bufs, refs = refs[:7], refs[7:]
    rs, rr, os_, or_, all_s, all_r, wo_s, wo_r, own_sems = refs
    z, f = place()
    me, count = z * nf + f, nz * nf
    dense = gw_ref.shape[2]
    rows, width = tok_ref.shape
    length = gm_ref.shape[0]
    greet_all(nz, nf)
    outs = Reduce([out_ref, *bufs[4:]], (os_, or_), nz, z, f)
    order = list(range(1, nz)) + [0]
    outs.send_near(order[0])

    def two(m):
        return first_head(m + 1) - first_head(m) == 2

    def copies(d, k):
        device = (d // nf, d % nf)
        src, dst = ((gw_ref.at[0, d], gws.at[0, me]), (gw_ref.at[1, d], gws.at[1, me]), (small_ref.at[d], smalls.at[me]))[k]
        return pltpu.make_async_remote_copy(
            src, dst, all_s.at[k, d], all_r.at[k, me], device_id=device, device_id_type=MESH
        )

    def wanted(m, block):
        low, high = out_blocks(m, dense)
        return (low <= block) & (block <= high)

    def owner_of(block):
        return head_owner(block * dense // HD)

    low, _ = out_blocks(f, dense)

    def out_copy(d):
        k = 2 * z + f - owner_of(d)
        return pltpu.make_async_remote_copy(
            gwo_ref.at[d - low], gwos.at[k], wo_s.at[d - low], wo_r.at[k],
            device_id=(d // nf, d % nf), device_id_type=MESH,
        )

    spare = gwo_ref.shape[0] * dense
    wide = up_to(spare, HD)
    shift = first_head(f) * HD - low * dense
    moved = jnp.concatenate([attn_ref[...].astype(F32), jnp.zeros((length, wide - SLOTS * HD), F32)], axis=1)
    moved = pltpu.roll(moved, shift, 1).astype(BF16)
    gwo_ref[...] = dot_tn(moved, gm_ref[...])[:spare].reshape(gwo_ref.shape).astype(BF16)

    def start_small(i, _):
        d = (me + i) % count
        copies(d, 2).start()

        @pl.when(wanted(f, d))
        def _():
            out_copy(d).start()

        return 0

    lax.fori_loop(1, count, start_small, 0)
    own_slot = 2 * z + f - owner_of(me)
    own_out = pltpu.make_async_copy(gwo_ref.at[me - low], gwos.at[own_slot], own_sems.at[0])
    own_small = pltpu.make_async_copy(small_ref.at[me], smalls.at[me], own_sems.at[1])
    own_small.start()

    @pl.when(wanted(f, me))
    def _():
        own_out.start()

    gkv_ref[...] = jnp.zeros_like(gkv_ref)
    block = 256
    for i in range(length // block):
        attn_back_block(
            i, block, gm_ref, wo_ref, qkv_ref, attn_ref, lse_ref, cos_ref, sin_ref, segq_ref, segk_ref, gkv_ref, gqkv_ref
        )
        if i + 1 < nz:
            outs.send_near(order[i + 1])
        if i < nz:
            outs.far(order[i])
        if 0 < i <= nz:
            outs.along_z(order[i - 1])
    attn_back_keys(w_ref, cos_ref, sin_ref, gkv_ref, gqkv_ref, wt_ref)
    step = 3 * HD
    reduce = Reduce(bufs[:4], (rs, rr), 1, z, f)
    for i in range(length // block):
        mine = slice(i * block, (i + 1) * block)
        at = i * block // rows
        part_ref[at : at + block // rows] = (
            dot(gqkv_ref[mine, :], wt_ref[...]).astype(BF16).reshape(block // rows, rows, width)
        )
    for i in range(4):
        reduce.core(0, i, part_ref.at[flip(f, 1 | 2 * i)]).start()

    own_gw = [pltpu.make_async_copy(gw_ref.at[s, me], gws.at[s, me], own_sems.at[2 + s]) for s in range(SLOTS)]

    def weights(s):
        value = dot_tn(normed_ref[...], gqkv_ref[:, s * step : (s + 1) * step])
        gw_ref[s] = value.reshape(count, dense, step).astype(BF16)

        def start(i, _):
            copies((me + i) % count, s).start()
            return 0

        lax.fori_loop(1, count, start, 0)
        own_gw[s].start()

    weights(0)
    for i in range(4):
        reduce.core(0, i, None).wait_recv()
        reduce.by_core[0, i] = reduce.by_core[0, i] + part_ref[flip(f, 2 * i)]
    reduce.send_near(0)

    @pl.when(two(f))
    def _():
        weights(1)

    for k in range(length // block, nz):
        outs.far(order[k])
    for k in range(length // block - 1, nz):
        outs.along_z(order[k])
    reduce.far(0)
    reduce.along_z(0)
    x = tok_ref[...].astype(F32)
    scale = rms_scale(x)
    gtok_ref[...] = (
        own_gm_ref[...] + norm_back(reduce.by_far[0].astype(F32), x * scale, scale, gain_ref[...])
    ).astype(BF16)
    block_ref[...] = (mixed_ref[...] + outs.total()).astype(BF16)

    owner = owner_of(me)
    next_owner = head_owner((me * dense + dense - 1) // HD)
    for k in range(2 * nz):
        there = (k // 2 != z) | (f != owner + k % 2)
        if k % 2:
            there = there & (next_owner != owner)

        @pl.when(there)
        def _():
            pltpu.make_async_remote_copy(
                gwo_ref.at[0], gwos.at[k], wo_s.at[0], wo_r.at[k], device_id=(z, flip(f, 1)), device_id_type=MESH
            ).wait_recv()

    @pl.when(wanted(f, me))
    def _():
        own_out.wait()

    gwout_ref[...] = sum(gwos[2 * t].astype(F32) for t in range(nz))

    @pl.when(next_owner != owner)
    def _():
        gwout_ref[...] += sum(gwos[2 * t + 1].astype(F32) for t in range(nz))

    def came(d, k):
        dst = (gws.at[0, d], gws.at[1, d], smalls.at[d])[k]
        return pltpu.make_async_remote_copy(
            dst, dst, all_s.at[k, d], all_r.at[k, d], device_id=(d // nf, d % nf), device_id_type=MESH
        )

    def finish(i, _):
        d = (me + i) % count
        came(d, 0).wait_recv()

        @pl.when(two(d % nf))
        def _():
            came(d, 1).wait_recv()

        came(d, 2).wait_recv()
        copies(d, 0).wait_send()

        @pl.when(two(f))
        def _():
            copies(d, 1).wait_send()

        copies(d, 2).wait_send()

        @pl.when(wanted(f, d))
        def _():
            out_copy(d).wait_send()

        return 0

    lax.fori_loop(1, count, finish, 0)
    own_small.wait()
    own_gw[0].wait()

    @pl.when(two(f))
    def _():
        own_gw[1].wait()

    for m in range(8):
        for s in range(SLOTS):
            if real[m * SLOTS + s]:
                h = heads[m * SLOTS + s]
                both = sum(gws[s, t * nf + m].astype(F32) for t in range(nz))
                for c in range(3):
                    gwqkv_ref[:, c * width + h * HD : c * width + (h + 1) * HD] = both[:, c * HD : (c + 1) * HD]
    all_small_ref[...] = smalls[...]
    for i in range(4):
        reduce.core(0, i, part_ref.at[0]).wait_send()
    reduce.end()
    outs.end()


def back(
    gm, wo, w, normed, qkv, attn, lse, cosine, sine, segq, segk, out_part, small, tok, mixed, own_gm, gain, nz, nf
):
    rows, width = tok.shape
    length, count = gm.shape[0], nz * nf
    dense = width // count
    heads, real = head_table(8)
    return pl.pallas_call(
        functools.partial(back_kernel, nz=nz, nf=nf, heads=heads, real=real),
        out_shape=(
            jax.ShapeDtypeStruct((rows, width), BF16),
            jax.ShapeDtypeStruct((rows, width), BF16),
            jax.ShapeDtypeStruct((dense, 3 * width), F32),
            jax.ShapeDtypeStruct((dense, width), F32),
            jax.ShapeDtypeStruct((count, dense, HD), BF16),
        ),
        in_specs=[VMEM] * 17,
        out_specs=(VMEM,) * 5,
        scratch_shapes=[
            pltpu.VMEM((length, 2 * SLOTS * HD), F32),
            pltpu.VMEM((length, 3 * SLOTS * HD), BF16),
            pltpu.VMEM((3 * SLOTS * HD, width), BF16),
            pltpu.VMEM((8, rows, width), BF16),
            pltpu.VMEM((SLOTS, count, dense, 3 * HD), BF16),
            pltpu.VMEM((8, dense, width), BF16),
            pltpu.VMEM((SLOTS, count, dense, 3 * HD), BF16),
            pltpu.VMEM((2 * nz, dense, width), BF16),
            pltpu.VMEM((count, dense, HD), BF16),
            *Reduce.scratch(1, rows, width),
            *Reduce.scratch(nz, rows, width)[1:],
            *pair_of(Reduce.copies(1)),
            *pair_of(Reduce.copies(nz)),
            pltpu.SemaphoreType.DMA((3, count)),
            pltpu.SemaphoreType.DMA((3, count)),
            pltpu.SemaphoreType.DMA((8,)),
            pltpu.SemaphoreType.DMA((2 * nz,)),
            pltpu.SemaphoreType.DMA((4,)),
        ],
        compiler_params=pltpu.CompilerParams(
            collective_id=4, has_side_effects=True, vmem_limit_bytes=60 * 2**20
        ),
        name="back",
    )(
        gm, wo, w, normed, qkv, attn, lse, cosine, sine, segq, segk, out_part,
        small.astype(BF16).reshape(count, dense, HD), tok, mixed, own_gm, gain,
    )


def unpack_kernel(
    pieces_ref, small_ref, wqkv_ref, gwqkv_ref, gain_ref,
    geup_ref, gsup_ref, grouter_ref, ggain_ref,
    *, shared, experts,
):
    nz = pieces_ref.shape[0]
    hidden = pieces_ref.shape[2] // 4
    for t in range(nz):
        for g in range(2):
            for e in range(2):
                at = (2 * g + e) * hidden
                to = (g * nz + t) * hidden
                geup_ref[e, :, to : to + hidden] = pieces_ref[t, :, at : at + hidden].astype(F32)
    count = small_ref.shape[0]
    total = small_ref[0].astype(F32)
    for d in range(count):
        if d:
            total = total + small_ref[d].astype(F32)
        for g in range(2):
            to = (g * count + d) * shared
            gsup_ref[:, to : to + shared] = small_ref[d, :, g * TAIL : g * TAIL + shared].astype(F32)
    grouter_ref[...] = total[:, shared : shared + experts]
    one = jnp.sum(wqkv_ref[...].astype(F32) * gwqkv_ref[...], axis=-1, keepdims=True) / gain_ref[:, :1].astype(F32)
    ggain_ref[...] = jnp.concatenate([one, total[:, HD - 1 :]], axis=1)


def unpack(pieces, small, wqkv, gwqkv, gains, shared, experts):
    nz, up_rows, packed = pieces.shape
    count, dense, _ = small.shape
    return pl.pallas_call(
        functools.partial(unpack_kernel, shared=shared, experts=experts),
        out_shape=(
            jax.ShapeDtypeStruct((2, up_rows, nz * packed // 2), F32),
            jax.ShapeDtypeStruct((dense, 2 * count * shared), F32),
            jax.ShapeDtypeStruct((dense, experts), F32),
            jax.ShapeDtypeStruct((dense, 2), F32),
        ),
        in_specs=[VMEM] * 5,
        out_specs=(VMEM,) * 4,
        compiler_params=pltpu.CompilerParams(vmem_limit_bytes=32 * 2**20),
        name="unpack",
    )(pieces, small, wqkv, gwqkv, gains)


def tables():
    pos = np.arange(SEQ, dtype=np.float32)
    freqs = np.float32(ROPE) ** (-np.arange(HD // 2, dtype=np.float32) * np.float32(2.0 / HD))
    angles = (pos[:, None] * freqs[None, :]).astype(np.float32)
    cosine = np.concatenate([np.cos(angles)] * 2, axis=1).astype(np.float32)
    sine = np.concatenate([-np.sin(angles), np.sin(angles)], axis=1).astype(np.float32)
    return jnp.asarray(cosine), jnp.asarray(sine)


def local_near(
    mesh, tokens, out_grad, segment_ids, expert_ids, attn_gain, ffn_gain, w_qkv, w_out,
    w_router, w_shared_up, w_shared_down, w_expert_up, w_expert_down,
):
    nz, nf = mesh.shape["dp"], mesh.shape["fsdp"]
    rows, width = tokens.shape
    experts = w_router.shape[1]
    hidden, shared = w_expert_down.shape[1], w_shared_down.shape[0]
    f = lax.axis_index("fsdp")
    gains = jnp.stack([attn_gain, ffn_gain], axis=1)
    ids = jnp.concatenate([expert_ids.T, segment_ids[None]], axis=0)
    cosine, sine = tables()
    (
        w, wo, tail, all_gains, marks, own_marks, segq, segk, normed_one, qkv, attn, lse, mixed, normed, plane, all_grad,
        pieces,
    ) = front(
        tokens, w_qkv, w_out, w_router, w_shared_up, gains, ids, cosine, sine, out_grad, w_expert_up, nz, nf, shared
    )
    tail = tail.reshape(width, 2 * TAIL)
    gain_one, gain_two = all_gains[:1], all_gains[1:]
    router = jnp.pad(tail[:, shared : shared + experts], ((0, 0), (TAIL + shared, TAIL - shared - experts)))
    lane = jnp.arange(HD, dtype=jnp.int32) - TAIL - shared
    own = (lane[None, :] == (2 * f + jnp.arange(2, dtype=jnp.int32))[:, None]).astype(F32)
    out_part, seq_gm, grad_mixed, small, gpieces, gedown, gsdown = experts_turn(
        normed, plane, all_grad, marks, own, pieces.reshape(width, 4 * hidden), tail,
        w_expert_down.reshape(2 * hidden, width), w_shared_down, out_grad, mixed, router, own_marks, gain_two, nz, nf,
    )
    block_out, tokens_grad, grad_wqkv, grad_wout, smalls = back(
        seq_gm.reshape(SEQ, width), wo, w, normed_one, qkv, attn, lse, cosine, sine, segq, segk, out_part, small,
        tokens, mixed, grad_mixed, gain_one, nz, nf,
    )
    grad_eup, grad_sup, grad_router, grad_gains = unpack(gpieces, smalls, w_qkv, grad_wqkv, gains, shared, experts)
    return (
        block_out, tokens_grad, grad_gains[:, 0], grad_gains[:, 1], grad_wqkv, grad_wout, grad_router, grad_sup,
        gsdown, grad_eup, gedown.reshape(2, hidden, width),
    )


def local_far(
    mesh, tokens, out_grad, segment_ids, expert_ids, attn_gain, ffn_gain, w_qkv, w_out,
    w_router, w_shared_up, w_shared_down, w_expert_up, w_expert_down,
):
    nz, nf = mesh.shape["dp"], mesh.shape["fsdp"]
    nd = nz * nf
    rows, width = tokens.shape
    group = SEQ // rows
    experts = w_router.shape[1]
    dense = w_qkv.shape[0]
    hidden, shared = w_expert_down.shape[1], w_shared_down.shape[0]
    up_rows = w_expert_up.shape[1]
    both = ("dp", "fsdp")
    groups = None if nf == group else [[a + i for i in range(group)] for a in range(0, nf, group)]
    f = lax.axis_index("fsdp")
    member = lax.rem(f, group)
    heads, real = head_table(group)

    by_head = w_qkv.reshape(dense, 3, HEADS, HD)
    empty = jnp.zeros((dense, 3, HD), BF16)
    cols = jnp.stack([by_head[:, :, h] if r else empty for h, r in zip(heads, real)], axis=0)
    cols = cols.reshape(group, SLOTS, dense, 3 * HD)
    cols = jnp.tile(cols, (nf // group, 1, 1, 1))
    cols = lax.all_to_all(cols, "fsdp", 0, 0, tiled=True)
    w = lax.all_gather(cols, "dp", axis=0, tiled=True).transpose(1, 0, 2, 3).reshape(SLOTS, width, 3 * HD)
    full_out = lax.all_gather(w_out, both, axis=0, tiled=True)
    first = HEADS * member // group
    own_real = (first + jnp.arange(SLOTS) < HEADS * (member + 1) // group).astype(BF16)
    padded = jnp.pad(full_out, ((0, (SLOTS - 1) * HD), (0, 0)))
    wo = lax.dynamic_slice(padded, (first * HD, 0), (SLOTS * HD, width))
    wo = wo * jnp.repeat(own_real, HD)[:, None]
    gains = lax.all_gather(jnp.stack([attn_gain, ffn_gain], axis=1).astype(F32), both, axis=0, tiled=True)
    gain_one, gain_two = gains[:, 0], gains[:, 1]
    router = lax.all_gather(w_router, both, axis=0, tiled=True)
    sup = w_shared_up.reshape(dense, 2, nd, shared).transpose(2, 0, 1, 3).reshape(nd, dense, 2 * shared)
    sup = lax.all_to_all(sup, both, 0, 0, tiled=True).reshape(width, 2, shared)
    eup = w_expert_up.reshape(2, up_rows, 2, nz, hidden).transpose(3, 1, 2, 0, 4)
    eup = lax.all_to_all(eup, "dp", 0, 0, tiled=True).reshape(width, 4 * hidden)
    rest = jnp.zeros((width, TAIL - shared), BF16)
    tail = jnp.concatenate([sup[:, 0], router, rest[:, experts:], sup[:, 1], rest], axis=1)
    chosen = jnp.any(expert_ids[:, :, None] == jnp.arange(experts, dtype=jnp.int32), axis=1)
    at = TAIL + shared
    marks = jnp.pad(chosen.astype(BF16), ((0, 0), (at, HD - experts - at)))
    marks = lax.all_gather(marks, both, axis=0, tiled=True)
    lane = jnp.arange(HD, dtype=jnp.int32)
    own = (lane[None, :] == (at + 2 * f + jnp.arange(2, dtype=jnp.int32))[:, None]).astype(F32)
    cosine, sine = tables()
    seg = lax.all_gather(segment_ids, "fsdp", axis=0, tiled=True, axis_index_groups=groups)
    segq = jnp.broadcast_to(seg[:, None], (SEQ, HD))
    segk = jnp.broadcast_to(seg[None, :], (8, SEQ))

    seq_tokens = lax.all_gather(tokens, "fsdp", axis=0, tiled=True, axis_index_groups=groups)
    part, normed_one, qkv, attn, lse = attn_forward(
        seq_tokens, gain_one[None, :], w, wo, cosine, sine, segq, segk
    )
    projected = lax.psum_scatter(part, "fsdp", scatter_dimension=0, tiled=True, axis_index_groups=groups)
    inputs = tokens.astype(F32)
    mixed = inputs + projected.astype(F32)
    scale_two = rms_scale(mixed)
    normal_two = mixed * scale_two
    normed_two = (normal_two * gain_two).astype(BF16)
    all_normed = lax.all_gather(normed_two, both, axis=0, tiled=True)
    all_grad = lax.all_gather(out_grad, both, axis=0, tiled=True)
    out_part, gx_part, geup, gtail, gedown, gsdown = ffn(
        all_normed, all_grad, marks, own, eup, tail, w_expert_down.reshape(2 * hidden, width), w_shared_down
    )
    gx = lax.psum_scatter(gx_part, both, scatter_dimension=0, tiled=True).astype(F32)
    ffn_out = lax.psum_scatter(out_part, both, scatter_dimension=0, tiled=True).astype(F32)
    block_out = (mixed + ffn_out).astype(BF16)

    logits = jnp.where(chosen, dot(normed_two, router), NEG)
    probs = jax.nn.softmax(logits, axis=-1)
    grad_gates = gx[:, width + at : width + at + experts]
    grad_logits = (
        probs * (grad_gates - jnp.sum(probs * grad_gates, axis=-1, keepdims=True))
    ).astype(BF16)
    grad_router = dot_tn(normed_two, grad_logits)
    grad_normed = gx[:, :width] + dot_nt(grad_logits, router)
    grad_gain_two = jnp.sum(grad_normed * normal_two, axis=0)
    grad_mixed = out_grad.astype(F32) + norm_back(grad_normed, normal_two, scale_two, gain_two)

    seq_gm = lax.all_gather(grad_mixed.astype(BF16), "fsdp", axis=0, tiled=True, axis_index_groups=groups)
    part_back, gw, gwo = attn_backward(
        seq_gm, wo, w, normed_one, qkv, attn, lse, cosine, sine, segq, segk
    )
    grad_normed_one = lax.psum_scatter(
        part_back, "fsdp", scatter_dimension=0, tiled=True, axis_index_groups=groups
    ).astype(F32)
    scale_one = rms_scale(inputs)
    normal_one = inputs * scale_one
    grad_gain_one = jnp.sum(grad_normed_one * normal_one, axis=0)
    tokens_grad = (grad_mixed + norm_back(grad_normed_one, normal_one, scale_one, gain_one)).astype(BF16)

    gw = lax.psum_scatter(gw, "dp", scatter_dimension=1, tiled=True)
    gw = lax.all_to_all(gw.reshape(SLOTS, nf, dense, 3 * HD), "fsdp", 1, 1, tiled=True).astype(F32)
    gw = jnp.sum(gw.reshape(SLOTS, nf // group, group, dense, 3, HD), axis=1)
    picked = [gw[i % SLOTS, i // SLOTS] for i in range(group * SLOTS) if real[i]]
    grad_wqkv = jnp.stack(picked, axis=2).reshape(dense, 3 * width)
    gwo = gwo * jnp.repeat(own_real, HD)[:, None]
    all_gwo = jnp.zeros(((HEADS + SLOTS - 1) * HD, width), BF16)
    all_gwo = lax.dynamic_update_slice(all_gwo, gwo, (first * HD, 0))[: HEADS * HD]
    grad_wout = lax.psum_scatter(all_gwo, both, scatter_dimension=0, tiled=True).astype(F32)
    small = jnp.concatenate([grad_router, grad_gain_one[:, None], grad_gain_two[:, None]], axis=1)
    small = lax.psum_scatter(small, both, scatter_dimension=0, tiled=True)
    gsup = jnp.stack([gtail[:, :shared], gtail[:, TAIL : TAIL + shared]], axis=1)
    gsup = lax.all_to_all(gsup.reshape(nd, dense, 2 * shared).astype(BF16), both, 0, 0, tiled=True)
    grad_sup = gsup.reshape(nd, dense, 2, shared).transpose(1, 2, 0, 3).reshape(dense, 2 * nd * shared).astype(F32)
    geup = lax.all_to_all(geup.reshape(nz, up_rows, 2, 2, hidden), "dp", 0, 0, tiled=True)
    grad_eup = geup.transpose(3, 1, 2, 0, 4).reshape(2, up_rows, 2 * nz * hidden).astype(F32)
    return (
        block_out, tokens_grad, small[:, experts], small[:, experts + 1], grad_wqkv, grad_wout,
        small[:, :experts], grad_sup, gsdown, grad_eup, gedown.reshape(2, hidden, width),
    )


def solution(mesh):
    one, two = P(("dp", "fsdp")), P(("dp", "fsdp"), None)
    three = P("fsdp", "dp", None)

    def local(tokens, *rest):
        near = mesh.shape["fsdp"] == 8 == SEQ // tokens.shape[0] and mesh.shape["dp"] <= 4
        return (local_near if near else local_far)(mesh, tokens, *rest)

    return jax.shard_map(
        local,
        mesh=mesh,
        in_specs=(two, two, one, two, one, one, two, two, two, two, two, three, three),
        out_specs=(two, two, one, one, two, two, two, two, two, three, three),
        check_vma=False,
    )
```

```python
import functools

import jax
import jax.numpy as jnp
import numpy as np
from jax import lax
from jax.experimental import pallas as pl
from jax.experimental.pallas import tpu as pltpu
from jax.sharding import PartitionSpec as P

HEADS = 10
HD = 128
SEQ = 1024
SLOTS = 2
EPS = 1e-06
ROPE = 10000.0
NEG = -1e30
TAIL = 64
F32 = jnp.float32
BF16 = jnp.bfloat16


MESH = pl.DeviceIdType.MESH
VMEM = pl.BlockSpec(memory_space=pltpu.VMEM)
ANY = pl.BlockSpec(memory_space=pl.ANY)


def up_to(value, step):
    return -(-value // step) * step


def rms_scale(values):
    return lax.rsqrt(jnp.mean(values * values, axis=-1, keepdims=True) + EPS)


def norm_back(grad_normed, normal_rows, scale_rows, gain_rows):
    scaled = grad_normed * gain_rows
    return scale_rows * (
        scaled - normal_rows * jnp.mean(scaled * normal_rows, axis=-1, keepdims=True)
    )


def head_table(group):
    heads, real = [], []
    for i in range(group):
        own = list(range(HEADS * i // group, HEADS * (i + 1) // group))
        assert len(own) <= SLOTS
        heads += own + [0] * (SLOTS - len(own))
        real += [1] * len(own) + [0] * (SLOTS - len(own))
    return heads, real


def dot(a, b):
    return jnp.dot(a, b, preferred_element_type=F32)


def dot_nt(a, b):
    return lax.dot_general(a, b, (((1,), (1,)), ((), ())), preferred_element_type=F32)


def dot_tn(a, b):
    return lax.dot_general(a, b, (((0,), (0,)), ((), ())), preferred_element_type=F32)


def attn_project(i, block, x, gain, w_ref, cos_ref, sin_ref, normed_ref, qkv_ref):
    rows = pl.ds(pl.multiple_of(i * block, block), block)
    x = x.astype(F32)
    normed = (x * rms_scale(x) * gain).astype(BF16)
    normed_ref[rows, :] = normed
    cosine, sine = cos_ref[rows, :], sin_ref[rows, :]
    for s in range(SLOTS):
        proj = dot(normed, w_ref[s])
        for c in range(3):
            piece = proj[:, c * HD : (c + 1) * HD]
            if c < 2:
                piece = piece * cosine + pltpu.roll(piece, HD // 2, 1) * sine
            at = (3 * s + c) * HD
            qkv_ref[rows, at : at + HD] = piece.astype(BF16)


def attn_block(i, block, segq_ref, segk_ref, qkv_ref, attn_ref, lse_ref):
    scale = HD**-0.5
    rows = slice(i * block, (i + 1) * block)
    keys = (i + 1) * block
    row_pos = i * block + lax.broadcasted_iota(jnp.int32, (block, keys), 0)
    key_pos = lax.broadcasted_iota(jnp.int32, (block, keys), 1)
    allowed = (key_pos <= row_pos) & (segq_ref[rows, :1] == segk_ref[:1, :keys])
    outs = []
    for s in range(SLOTS):
        at = 3 * s * HD
        q = qkv_ref[rows, at : at + HD]
        k = qkv_ref[:keys, at + HD : at + 2 * HD]
        v = qkv_ref[:keys, at + 2 * HD : at + 3 * HD]
        scores = jnp.where(allowed, dot_nt(q, k) * scale, NEG)
        top = jnp.max(scores, axis=-1, keepdims=True)
        weights = jnp.exp(scores - top)
        total = jnp.sum(weights, axis=-1, keepdims=True)
        out = dot(weights.astype(BF16), v) / total
        lse_ref[rows, s * HD : (s + 1) * HD] = jnp.broadcast_to(top + jnp.log(total), (block, HD))
        low = out.astype(BF16)
        attn_ref[rows, s * HD : (s + 1) * HD] = low
        outs.append(low)
    return jnp.concatenate(outs, axis=-1)


def attn_forward_kernel(
    tok_ref, gain_ref, w_ref, wo_ref, cos_ref, sin_ref, segq_ref, segk_ref,
    part_ref, normed_ref, qkv_ref, attn_ref, lse_ref,
    *, block,
):
    count = tok_ref.shape[0] // block

    def project(i, _):
        x = tok_ref[pl.ds(pl.multiple_of(i * block, block), block), :]
        attn_project(i, block, x, gain_ref[...], w_ref, cos_ref, sin_ref, normed_ref, qkv_ref)
        return 0

    lax.fori_loop(0, count, project, 0)
    for i in range(count):
        outs = attn_block(i, block, segq_ref, segk_ref, qkv_ref, attn_ref, lse_ref)
        part_ref[i * block : (i + 1) * block, :] = dot(outs, wo_ref[...]).astype(BF16)


def attn_forward(tok, gain, w, wo, cosine, sine, segq, segk):
    length, width = tok.shape
    return pl.pallas_call(
        functools.partial(attn_forward_kernel, block=256),
        out_shape=(
            jax.ShapeDtypeStruct((length, width), BF16),
            jax.ShapeDtypeStruct((length, width), BF16),
            jax.ShapeDtypeStruct((length, 3 * SLOTS * HD), BF16),
            jax.ShapeDtypeStruct((length, SLOTS * HD), BF16),
            jax.ShapeDtypeStruct((length, SLOTS * HD), F32),
        ),
        in_specs=[VMEM] * 8,
        out_specs=(VMEM,) * 5,
        compiler_params=pltpu.CompilerParams(vmem_limit_bytes=56 * 2**20),
        cost_estimate=pl.CostEstimate(
            flops=2 * length * width * 4 * SLOTS * HD + 4 * SLOTS * HD * length * length,
            bytes_accessed=10 * length * width,
            transcendentals=SLOTS * length * length,
        ),
        name="attn_forward",
    )(tok, gain, w, wo, cosine, sine, segq, segk)


def attn_back_block(
    i, block, gm, wo_ref, qkv_ref, attn_ref, lse_ref, cos_ref, sin_ref, segq_ref, segk_ref, gkv_ref, gqkv_ref
):
    scale = HD**-0.5
    rows = slice(i * block, (i + 1) * block)
    keys = (i + 1) * block
    row_pos = i * block + lax.broadcasted_iota(jnp.int32, (block, keys), 0)
    key_pos = lax.broadcasted_iota(jnp.int32, (block, keys), 1)
    allowed = (key_pos <= row_pos) & (segq_ref[rows, :1] == segk_ref[:1, :keys])
    grad_attn = dot_nt(gm, wo_ref[...]).astype(BF16)
    for s in range(SLOTS):
        at = 3 * s * HD
        cut = slice(s * HD, (s + 1) * HD)
        q = qkv_ref[rows, at : at + HD]
        k = qkv_ref[:keys, at + HD : at + 2 * HD]
        v = qkv_ref[:keys, at + 2 * HD : at + 3 * HD]
        ga = grad_attn[:, cut]
        delta = jnp.sum(ga.astype(F32) * attn_ref[rows, cut].astype(F32), axis=-1, keepdims=True)
        scores = dot_nt(q, k) * scale
        probs = jnp.where(allowed, jnp.exp(scores - lse_ref[rows, s * HD : s * HD + 1]), 0.0)
        gs = (probs * (dot_nt(ga, v) - delta)).astype(BF16)
        gq = dot(gs, k) * scale
        gq = gq * cos_ref[rows, :] - pltpu.roll(gq, HD // 2, 1) * sin_ref[rows, :]
        gqkv_ref[rows, at : at + HD] = gq.astype(BF16)
        gkv_ref[:keys, 2 * s * HD : (2 * s + 1) * HD] += dot_tn(gs, q)
        gkv_ref[:keys, (2 * s + 1) * HD : (2 * s + 2) * HD] += dot_tn(probs.astype(BF16), ga)


def attn_back_keys(w_ref, cos_ref, sin_ref, gkv_ref, gqkv_ref, wt_ref):
    step = 3 * HD
    for s in range(SLOTS):
        at = s * step
        gk = gkv_ref[:, 2 * s * HD : (2 * s + 1) * HD] * HD**-0.5
        gk = gk * cos_ref[...] - pltpu.roll(gk, HD // 2, 1) * sin_ref[...]
        gqkv_ref[:, at + HD : at + 2 * HD] = gk.astype(BF16)
        gqkv_ref[:, at + 2 * HD : at + 3 * HD] = gkv_ref[:, (2 * s + 1) * HD : (2 * s + 2) * HD].astype(BF16)
        wt_ref[s * step : (s + 1) * step, :] = w_ref[s].T


def attn_backward_kernel(
    gm_ref, wo_ref, w_ref, normed_ref, qkv_ref, attn_ref, lse_ref, cos_ref, sin_ref,
    segq_ref, segk_ref,
    part_ref, gw_ref, gwo_ref,
    gkv_ref, gqkv_ref, wt_ref,
    *, block,
):
    count = gm_ref.shape[0] // block
    step = 3 * HD
    gkv_ref[...] = jnp.zeros_like(gkv_ref)
    for i in range(count):
        attn_back_block(
            i, block, gm_ref[i * block : (i + 1) * block, :], wo_ref, qkv_ref, attn_ref, lse_ref, cos_ref, sin_ref, segq_ref, segk_ref, gkv_ref, gqkv_ref
        )
    attn_back_keys(w_ref, cos_ref, sin_ref, gkv_ref, gqkv_ref, wt_ref)
    for i in range(count):
        rows = slice(i * block, (i + 1) * block)
        part_ref[rows, :] = dot(gqkv_ref[rows, :], wt_ref[...]).astype(BF16)
    for s in range(SLOTS):
        gw_ref[s] = dot_tn(normed_ref[...], gqkv_ref[:, s * step : (s + 1) * step]).astype(BF16)
    gwo_ref[...] = dot_tn(attn_ref[...], gm_ref[...]).astype(BF16)


def attn_backward(gm, wo, w, normed, qkv, attn, lse, cosine, sine, segq, segk):
    length, width = gm.shape
    return pl.pallas_call(
        functools.partial(attn_backward_kernel, block=256),
        out_shape=(
            jax.ShapeDtypeStruct((length, width), BF16),
            jax.ShapeDtypeStruct((SLOTS, width, 3 * HD), BF16),
            jax.ShapeDtypeStruct((SLOTS * HD, width), BF16),
        ),
        in_specs=[VMEM] * 11,
        out_specs=(VMEM,) * 3,
        scratch_shapes=[
            pltpu.VMEM((length, 2 * SLOTS * HD), F32),
            pltpu.VMEM((length, 3 * SLOTS * HD), BF16),
            pltpu.VMEM((3 * SLOTS * HD, width), BF16),
        ],
        compiler_params=pltpu.CompilerParams(vmem_limit_bytes=56 * 2**20),
        cost_estimate=pl.CostEstimate(
            flops=4 * length * width * 4 * SLOTS * HD + 10 * SLOTS * HD * length * length,
            bytes_accessed=10 * length * width,
            transcendentals=SLOTS * length * length,
        ),
        name="attn_backward",
    )(gm, wo, w, normed, qkv, attn, lse, cosine, sine, segq, segk)


def ffn_weights(eup_ref, tail_ref, edown_ref, sdown_ref, up_ref, upt_ref, down_ref, downt_ref):
    width, half = downt_ref.shape
    pair, shared = edown_ref.shape[0], sdown_ref.shape[0]
    gap = half - pair - TAIL
    between = [jnp.zeros((width, gap), BF16)] if gap else []
    up_ref[...] = jnp.concatenate(
        [eup_ref[:, :pair], *between, tail_ref[:, :TAIL], eup_ref[:, pair:], *between, tail_ref[:, TAIL:]], axis=1
    )
    between = [jnp.zeros((gap, width), BF16)] if gap else []
    down_ref[...] = jnp.concatenate(
        [edown_ref[...], *between, sdown_ref[...], jnp.zeros((TAIL - shared, width), BF16)], axis=0
    )
    upt_ref[...] = up_ref[...].T
    downt_ref[...] = down_ref[...].T


def ffn_rows(x, g, marks, own, up_ref, upt_ref, down_ref, downt_ref, hidden, shared):
    half = down_ref.shape[0]
    pair = 2 * hidden
    pre = dot(x, up_ref[...])
    gate, up = pre[:, :half], pre[:, half:]
    logits = jnp.where(marks.astype(F32) > 0.5, gate[:, half - HD :], NEG)
    weights = jnp.exp(logits - jnp.max(logits, axis=-1, keepdims=True))
    probs = weights / jnp.sum(weights, axis=-1, keepdims=True)
    p0 = jnp.sum(probs * own[0:1, :], axis=-1, keepdims=True)
    p1 = jnp.sum(probs * own[1:2, :], axis=-1, keepdims=True)
    lane = lax.broadcasted_iota(jnp.int32, (1, half), 1)
    in0 = lane < hidden
    in1 = (lane >= hidden) & (lane < pair)
    rest = jnp.where((lane >= half - TAIL) & (lane < half - TAIL + shared), 1.0, 0.0)
    weight = jnp.where(in0, p0, jnp.where(in1, p1, rest))
    sig = jax.nn.sigmoid(gate)
    silu = gate * sig
    act = silu * up
    acts = (act * weight).astype(BF16)
    out = dot(acts, down_ref[...]).astype(BF16)
    grad = dot(g, downt_ref[...])
    both = act * grad
    d0 = jnp.sum(jnp.where(in0, both, 0.0), axis=-1, keepdims=True)
    d1 = jnp.sum(jnp.where(in1, both, 0.0), axis=-1, keepdims=True)
    grad = grad * weight
    grad_gate = grad * up * sig * (1.0 + gate * (1.0 - sig))
    grad_up = grad * silu
    grad_pre = jnp.concatenate([grad_gate, grad_up], axis=-1).astype(BF16)
    gates = (d0 * own[0:1, :] + d1 * own[1:2, :]).astype(BF16)
    gx = jnp.concatenate([dot(grad_pre, upt_ref[...]).astype(BF16), gates], axis=-1)
    return out, gx, grad_pre, acts


def ffn_kernel(
    x_ref, g_ref, mark_ref, own_ref, eup_ref, tail_ref, edown_ref, sdown_ref,
    out_ref, gx_ref, geup_ref, gtail_ref, gedown_ref, gsdown_ref,
    up_ref, upt_ref, down_ref, downt_ref, gup_ref, gdown_ref,
    *, hidden, shared,
):
    step = pl.program_id(0)
    half = down_ref.shape[0]
    pair = 2 * hidden

    @pl.when(step == 0)
    def _():
        gup_ref[...] = jnp.zeros_like(gup_ref)
        gdown_ref[...] = jnp.zeros_like(gdown_ref)
        ffn_weights(eup_ref, tail_ref, edown_ref, sdown_ref, up_ref, upt_ref, down_ref, downt_ref)

    out, gx, grad_pre, acts = ffn_rows(
        x_ref[...], g_ref[...], mark_ref[...], own_ref[...], up_ref, upt_ref, down_ref, downt_ref, hidden, shared
    )
    out_ref[...] = out
    gx_ref[...] = gx
    gup_ref[...] += dot_tn(x_ref[...], grad_pre)
    gdown_ref[...] += dot_tn(acts, g_ref[...])

    @pl.when(step == pl.num_programs(0) - 1)
    def _():
        geup_ref[...] = jnp.concatenate([gup_ref[:, :pair], gup_ref[:, half : half + pair]], axis=1).astype(BF16)
        gtail_ref[...] = jnp.concatenate([gup_ref[:, half - TAIL : half], gup_ref[:, 2 * half - TAIL :]], axis=1)
        gedown_ref[...] = gdown_ref[:pair, :]
        gsdown_ref[...] = gdown_ref[half - TAIL : half - TAIL + shared, :]


def ffn(x, g, marks, own, eup, tail, edown, sdown):
    total, width = x.shape
    pair, shared = edown.shape[0], sdown.shape[0]
    half = up_to(pair + TAIL, HD)
    tile = 512
    row = lambda n: pl.BlockSpec((tile, n), lambda i: (i, 0))
    return pl.pallas_call(
        functools.partial(ffn_kernel, hidden=pair // 2, shared=shared),
        out_shape=(
            jax.ShapeDtypeStruct((total, width), BF16),
            jax.ShapeDtypeStruct((total, width + HD), BF16),
            jax.ShapeDtypeStruct((width, 2 * pair), BF16),
            jax.ShapeDtypeStruct((width, HD), F32),
            jax.ShapeDtypeStruct((pair, width), F32),
            jax.ShapeDtypeStruct((shared, width), F32),
        ),
        grid=(total // tile,),
        in_specs=[row(width), row(width), row(HD)] + [VMEM] * 5,
        out_specs=(row(width), row(width + HD), VMEM, VMEM, VMEM, VMEM),
        scratch_shapes=[
            pltpu.VMEM((width, 2 * half), BF16),
            pltpu.VMEM((2 * half, width), BF16),
            pltpu.VMEM((half, width), BF16),
            pltpu.VMEM((width, half), BF16),
            pltpu.VMEM((width, 2 * half), F32),
            pltpu.VMEM((half, width), F32),
        ],
        compiler_params=pltpu.CompilerParams(vmem_limit_bytes=60 * 2**20),
        cost_estimate=pl.CostEstimate(
            flops=2 * total * width * 9 * half,
            bytes_accessed=8 * total * width,
            transcendentals=total * half,
        ),
        name="ffn",
    )(x, g, marks, own, eup, tail, edown, sdown)


def flip(f, bits):
    for b in (1, 2, 4):
        if bits & b:
            f = f + b - 2 * b * (f // b % 2)
    return f


def place():
    return lax.axis_index("dp"), lax.axis_index("fsdp")


def greet(devices):
    barrier = pltpu.get_barrier_semaphore()
    for device in devices:
        pl.semaphore_signal(barrier, inc=1, device_id=device, device_id_type=MESH)
    pl.semaphore_wait(barrier, len(devices))


def greet_all(nz, nf):
    barrier = pltpu.get_barrier_semaphore()
    z, f = place()
    me, count = z * nf + f, nz * nf

    def hail(i, _):
        d = (me + i) % count
        pl.semaphore_signal(barrier, inc=1, device_id=(d // nf, d % nf), device_id_type=MESH)
        return 0

    lax.fori_loop(1, count, hail, 0)
    pl.semaphore_wait(barrier, count - 1)


def send(src, dst, sems, index, device):
    return pltpu.make_async_remote_copy(
        src, dst, sems[0].at[index], sems[1].at[index], device_id=device, device_id_type=MESH
    )


ORDER = ((2, 4), (4, 2))


def halves(rows):
    return ((0, rows // 2), (rows // 2, rows - rows // 2))


def away(j, nz):
    if nz < 3:
        return j
    if isinstance(j, int):
        return j if j < 2 else nz - 1 if j == 2 else j - 1
    return jnp.where(j < 2, j, jnp.where(j == 2, nz - 1, j - 1))


class Gather:
    @staticmethod
    def copies(nz):
        return 11 * nz

    def __init__(self, buf, sems, nz, z, f):
        self.buf, self.sems, self.nz, self.z, self.f = buf, sems, nz, z, f

    def slot(self, j, r, h=None):
        piece = lax.rem(self.z - away(j, self.nz) + self.nz, self.nz) if self.nz > 1 else 0
        ref = self.buf.at[piece, flip(self.f, r)]
        return ref if h is None else ref.at[pl.ds(*halves(self.buf.shape[-2])[h])]

    def here(self, j, r, h, index, device):
        ref = self.slot(j, r, h)
        return send(ref, ref, self.sems, index, device)

    def by_z(self, j):
        own = self.slot(0, 0)
        return send(own, own, self.sems, j, (lax.rem(self.z + away(j, self.nz), self.nz), self.f))

    def near(self, j, h):
        return self.here(j, 0, h, self.nz + 2 * j + h, (self.z, flip(self.f, ORDER[h][0])))

    def far(self, j, h, i):
        r = ORDER[h][0] if i else 0
        return self.here(j, r, h, 3 * self.nz + 4 * j + 2 * h + i, (self.z, flip(self.f, ORDER[h][1])))

    def core(self, j, i):
        return self.here(j, 2 * i, None, 7 * self.nz + 4 * j + i, (self.z, flip(self.f, 1)))

    def along_z(self, j):
        if 1 < j <= self.nz:
            self.by_z(j - 1).wait_send()
        if j < self.nz:
            self.by_z(j).start()

    def first(self, j, own=False):
        if not own:
            self.by_z(j).wait_recv()
        for h in range(2):
            self.near(j, h).start()
        self.core(j, 0).start()

    def second(self, j):
        for h in range(2):
            self.near(j, h).wait_recv()
            for i in range(2):
                self.far(j, h, i).start()

    def third(self, j):
        for h in range(2):
            for i in range(2):
                self.far(j, h, i).wait_recv()
        for i in range(1, 4):
            self.core(j, i).start()

    def fourth(self, j):
        for i in range(4):
            self.core(j, i).wait_recv()

    def end(self, first=0):
        for j in range(first, self.nz):
            for h in range(2):
                self.near(j, h).wait_send()
                for i in range(2):
                    self.far(j, h, i).wait_send()
            for i in range(4):
                self.core(j, i).wait_send()


class Reduce:
    @staticmethod
    def copies(nz):
        return 11 * nz

    @staticmethod
    def scratch(nz, rows, width):
        return [
            pltpu.VMEM((nz, 4, rows, width), BF16),
            pltpu.VMEM((nz, 2, rows, width), BF16),
            pltpu.VMEM((nz, rows, width), BF16),
            pltpu.VMEM((nz, rows, width), BF16),
        ]

    def __init__(self, bufs, sems, nz, z, f):
        self.by_core, self.by_near, self.by_far, self.by_z = bufs
        self.sems, self.nz, self.z, self.f = sems, nz, z, f
        self.parts = halves(self.by_core.shape[-2])

    def core(self, j, i, src):
        to = self.by_core.at[j, i]
        return send(to if src is None else src, to, self.sems, 4 * j + i, (self.z, flip(self.f, 1)))

    def near(self, j, h, i):
        last = ORDER[1 - h][1]
        rows = pl.ds(*self.parts[h])
        return send(
            self.by_core.at[j, 3 if i else last // 2, rows], self.by_near.at[j, i, rows], self.sems,
            4 * self.nz + 4 * j + 2 * h + i, (self.z, flip(self.f, last)),
        )

    def far_copy(self, j, h):
        rows = pl.ds(*self.parts[h])
        return send(
            self.by_near.at[j, 1, rows], self.by_far.at[j, rows], self.sems,
            8 * self.nz + 2 * j + h, (self.z, flip(self.f, ORDER[1 - h][0])),
        )

    def z_copy(self, j):
        there = lax.rem(self.z - away(j, self.nz) + self.nz, self.nz)
        return send(self.by_far.at[j], self.by_z.at[j], self.sems, 10 * self.nz + j, (there, self.f))

    def send_near(self, j):
        for h in range(2):
            for i in range(2):
                self.near(j, h, i).start()

    def far(self, j):
        for h in range(2):
            at, size = self.parts[h]
            rows = slice(at, at + size)
            for i, r in enumerate((0, ORDER[1 - h][0])):
                self.near(j, h, i).wait_recv()
                self.by_near[j, i, rows] = self.by_near[j, i, rows] + self.by_core[j, r // 2, rows]
            self.far_copy(j, h).start()

    def along_z(self, j):
        for h in range(2):
            at, size = self.parts[h]
            rows = slice(at, at + size)
            self.far_copy(j, h).wait_recv()
            self.by_far[j, rows] = self.by_far[j, rows] + self.by_near[j, 0, rows]
        if isinstance(j, int):
            if j:
                self.z_copy(j).start()
        else:

            @pl.when(j > 0)
            def _():
                self.z_copy(j).start()

    def total(self):
        result = self.by_far[0].astype(F32)
        for j in range(1, self.nz):
            self.z_copy(j).wait_recv()
            result = result + self.by_z[j].astype(F32)
        return result

    def end(self):
        for j in range(self.nz):
            for h in range(2):
                for i in range(2):
                    self.near(j, h, i).wait_send()
                self.far_copy(j, h).wait_send()
            if j:
                self.z_copy(j).wait_send()


def near_devices(z, f):
    return [(z, flip(f, 1)), (z, flip(f, 2)), (z, flip(f, 4))]


def z_devices(z, f, nz):
    return [(lax.rem(z + zr, nz), f) for zr in range(1, nz)]


def pair_of(count):
    return [pltpu.SemaphoreType.DMA((count,))] * 2


def first_head(member):
    return HEADS * member // 8


def out_blocks(member, dense):
    return first_head(member) * HD // dense, (first_head(member + 1) * HD - 1) // dense


def head_owner(head):
    return (8 * head + 7) // HEADS


def front_kernel(
    tok_ref, wqkv_ref, wout_ref, router_ref, sup_ref, again_ref, fgain_ref, eids_ref, seg_ref, cos_ref, sin_ref, og_ref,
    eup_ref,
    w_out, wo_ref, tail_out, router_out, gain_one_ref, gain_two_ref, mark_out, own_mark_ref, segq_ref, segk_ref,
    normed_out, qkv_out, attn_out, lse_out, mixed_ref, low_ref, plane_ref, all_grad_ref, pieces_ref,
    w_ref, tail_ref, mark_ref, normed_ref, qkv_ref, attn_ref, lse_ref, ids_ref, out_sems,
    seq, wq, wo_in, wz, wzo, all_ids, qpack, tpack, part, wide, pack, *refs, nz, nf, hidden, shared, heads, real,
):
    bufs, refs = refs[:4], refs[4:]
    (
        tok_s, tok_r, all_s, all_r, q_s, q_r, wo_s, wo_r, zq_s, zq_r, zo_s, zo_r, rs, rr, gs, gr, xs, xr, es, er,
        own_sems,
    ) = refs
    z, f = place()
    me, count = z * nf + f, nz * nf
    rows, width = tok_ref.shape
    dense = wqkv_ref.shape[0]
    experts = router_ref.shape[0]
    full = shared * count
    greet_all(nz, nf)

    toks = (tok_s, tok_r)
    to_near = [send(tok_ref, seq.at[f], toks, i, (z, flip(f, r))) for i, r in enumerate((2, 4, 6))]
    to_core = [send(tok_ref, seq.at[f], toks, 3, (z, flip(f, 1)))]
    own = pltpu.make_async_copy(og_ref, all_grad_ref.at[z, f], own_sems.at[0])
    own.start()
    for copy in to_near + to_core:
        copy.start()
    seq[f] = tok_ref[...]
    ids_ref[...] = jnp.concatenate([eids_ref[...], seg_ref[...]], axis=0)
    all_ids[me] = ids_ref[...]
    router = router_ref[...].astype(F32).T.astype(BF16)
    both_gains = jnp.concatenate([again_ref[...], fgain_ref[...]], axis=1)

    def leave(k, src, dst):
        return pltpu.make_async_copy(src, dst, out_sems.at[k])

    outgoing = [
        leave(k, src, dst)
        for k, (src, dst) in enumerate(
            (
                (w_ref, w_out), (tail_ref, tail_out), (mark_ref, mark_out), (normed_ref, normed_out),
                (qkv_ref, qkv_out), (attn_ref, attn_out), (lse_ref, lse_out),
            )
        )
    ]
    own.wait()
    grads = Gather(all_grad_ref, (gs, gr), nz, z, f)
    grads.first(0, own=True)

    def two(m):
        return first_head(m + 1) - first_head(m) == 2

    def wanted(m, block):
        low, high = out_blocks(m, dense)
        return (low <= block) & (block <= high)

    low, high = out_blocks(f, dense)

    def piece(j):
        return lax.rem(z - away(j, nz) + nz, nz) if j else z

    def along(src, dst, sems, j):
        return send(src, dst.at[z], sems, j, (lax.rem(z + away(j, nz), nz), f))

    zq = [None] + [along(wqkv_ref, wz, (zq_s, zq_r), j) for j in range(1, nz)]
    zo = [None] + [along(wout_ref, wzo, (zo_s, zo_r), j) for j in range(1, nz)]
    for copy in zq[1:] + zo[1:]:
        copy.start()

    pad = jnp.zeros((dense, TAIL - shared - experts), BF16)
    pad_two = jnp.zeros((dense, TAIL - shared - 2), BF16)
    for d in range(count):
        tpack[d] = jnp.concatenate(
            [
                sup_ref[:, d * shared : (d + 1) * shared], router, pad,
                sup_ref[:, full + d * shared : full + (d + 1) * shared], both_gains, pad_two,
            ],
            axis=1,
        )

    def copies(d, k):
        src, dst = ((tpack.at[d], tail_ref.at[me]), (ids_ref, all_ids.at[me]))[k]
        return pltpu.make_async_remote_copy(
            src, dst, all_s.at[k, d], all_r.at[k, me], device_id=(d // nf, d % nf), device_id_type=MESH
        )

    def came(d, k):
        dst = (tail_ref.at[d], all_ids.at[d])[k]
        return pltpu.make_async_remote_copy(
            dst, dst, all_s.at[k, d], all_r.at[k, d], device_id=(d // nf, d % nf), device_id_type=MESH
        )

    def start(i, _):
        d = (me + i) % count
        copies(d, 0).start()
        copies(d, 1).start()
        return 0

    whole = nz * hidden
    for t in range(nz):
        pack[t] = jnp.concatenate(
            [
                eup_ref[e, :, g * whole + t * hidden : g * whole + (t + 1) * hidden]
                for g in range(2)
                for e in range(2)
            ],
            axis=1,
        )
    tail_ref[me] = tpack[me]
    lax.fori_loop(1, count, start, 0)

    def q_copy(j, m, s):
        return pltpu.make_async_remote_copy(
            qpack.at[j, m, s], wq.at[s, piece(j) * nf + f], q_s.at[j, m, s], q_r.at[j, f, s],
            device_id=(z, m), device_id_type=MESH,
        )

    def q_came(j, m, s):
        dst = wq.at[s, piece(j) * nf + m]
        return pltpu.make_async_remote_copy(
            dst, dst, q_s.at[j, m, s], q_r.at[j, m, s], device_id=(z, m), device_id_type=MESH
        )

    def q_own(j, s):
        wq[s, piece(j) * nf + f] = qpack[j, f, s]

    def q_each(act, m):
        act(0)

        @pl.when(two(m))
        def _():
            act(1)

    def q_send(j):
        ref = wz.at[piece(j)] if j else wqkv_ref
        for m in range(8):
            for s in range(SLOTS):
                h = heads[m * SLOTS + s]
                if real[m * SLOTS + s]:
                    qpack[j, m, s] = jnp.concatenate(
                        [ref[:, c * width + h * HD : c * width + (h + 1) * HD] for c in range(3)], axis=1
                    )

        def go(i, _):
            m = (f + i) % nf
            q_each(lambda s: q_copy(j, m, s).start(), m)
            return 0

        lax.fori_loop(1, nf, go, 0)
        q_each(lambda s: q_own(j, s), f)

    grads.second(0)
    for i, r in enumerate((2, 4, 6)):
        to_near[i].wait_recv()
        slot = seq.at[flip(f, r)]
        copy = send(slot, slot, toks, 4 + i, (z, flip(f, 1)))
        copy.start()
        to_core.append(copy)
    q_send(0)
    grads.third(0)
    for copy in zq[1:]:
        copy.wait_send()
    for j in range(1, nz):
        grads.by_z(j).start()
    for j in range(1, nz):
        zq[j].wait_recv()
        q_send(j)

    def arrive(i, _):
        d = (me + i) % count
        came(d, 0).wait_recv()
        came(d, 1).wait_recv()
        return 0

    lax.fori_loop(1, count, arrive, 0)

    def q_arrive(i, _):
        m = (f + i) % nf
        for j in range(nz):
            q_each(lambda s: q_came(j, m, s).wait_recv(), f)
        return 0

    lax.fori_loop(1, nf, q_arrive, 0)
    for copy in to_core:
        copy.wait_recv()

    w_ref[0] = wq[0].reshape(width, 3 * HD)
    w_ref[1] = jnp.where(two(f), wq[1].astype(F32), 0.0).reshape(width, 3 * HD).astype(BF16)
    outgoing[0].start()
    outgoing[1].start()
    tails = tail_ref[...].reshape(width, 2 * TAIL)
    gains = tails[:, TAIL + shared : TAIL + shared + 2].astype(F32).T
    gain_one_ref[...] = gains[0:1]
    gain_two_ref[...] = gains[1:2]
    router_out[...] = jnp.concatenate(
        [
            jnp.zeros((width, TAIL + shared), BF16), tails[:, shared : shared + experts],
            jnp.zeros((width, TAIL - shared - experts), BF16),
        ],
        axis=1,
    )
    for m in range(8):
        ids = all_ids[z * nf + m]
        segk_ref[:, m * rows : (m + 1) * rows] = jnp.broadcast_to(ids[-1:], (8, rows))
        segq_ref[m * rows : (m + 1) * rows, :] = jnp.broadcast_to(ids.T[:, -1:], (rows, HD))
    block = 256
    gain_one = gain_one_ref[...]

    def project(i, _):
        x = seq[pl.ds(i * (block // rows), block // rows)].reshape(block, width)
        attn_project(i, block, x, gain_one, w_ref, cos_ref, sin_ref, normed_ref, qkv_ref)
        return 0

    lax.fori_loop(0, 8 * rows // block, project, 0)
    outgoing[3].start()
    outgoing[4].start()
    def out_block(j):
        return piece(j) * nf + f

    def out_src(j):
        return wzo.at[piece(j)] if j else wout_ref

    def out_copy(j, m):
        first, _ = out_blocks(m, dense)
        slot = out_block(j) - first
        return pltpu.make_async_remote_copy(
            out_src(j), wo_in.at[slot], wo_s.at[j, m], wo_r.at[slot], device_id=(z, m), device_id_type=MESH
        )

    def out_own(j):
        wo_in[out_block(j) - low] = wzo[piece(j)] if j else wout_ref[...]

    def out_each(act, act_own):
        for j in range(nz):

            def one(i, _):
                m = (f + i) % nf

                @pl.when(wanted(m, out_block(j)))
                def _():
                    act(j, m)

                return 0

            lax.fori_loop(1, nf, one, 0)

            @pl.when(wanted(f, out_block(j)))
            def _():
                act_own(j)

    for j in range(1, nz):
        zo[j].wait()
    out_each(lambda j, m: out_copy(j, m).start(), out_own)

    reduce = Reduce(bufs, (rs, rr), 1, z, f)
    for i in range(8 * rows // block):
        attn_block(i, block, segq_ref, segk_ref, qkv_ref, attn_ref, lse_ref)

    outgoing[5].start()
    outgoing[6].start()

    def arrive_out(j, _):
        @pl.when((low + j <= high) & (lax.rem(low + j, nf) != f))
        def _():
            pltpu.make_async_remote_copy(
                wo_in.at[j], wo_in.at[j], wo_s.at[0, j], wo_r.at[j], device_id=(z, flip(f, 1)), device_id_type=MESH
            ).wait_recv()

        return 0

    lax.fori_loop(0, wo_in.shape[0], arrive_out, 0)
    wide[...] = wo_in[...].astype(F32).reshape(wide.shape)
    offset = pl.multiple_of(first_head(f) * HD - low * dense, 8)
    wo_ref[:HD, :] = wide[pl.ds(offset, HD), :].astype(BF16)
    wo_ref[HD:, :] = jnp.where(two(f), wide[pl.ds(offset + HD, HD), :], 0.0).astype(BF16)
    for i in range(8 * rows // block):
        at = i * (block // rows)
        part[at : at + block // rows] = (
            dot(attn_ref[i * block : (i + 1) * block, :], wo_ref[...]).astype(BF16).reshape(block // rows, rows, width)
        )
    for i in range(4):
        reduce.core(0, i, part.at[flip(f, 1 | 2 * i)]).start()
    ups = []
    for j in range(1, nz):
        there = lax.rem(z + j, nz)
        copy = send(pack.at[there], pieces_ref.at[z], (es, er), j, (there, f))
        copy.start()
        ups.append(copy)
    ups.append(pltpu.make_async_copy(pack.at[z], pieces_ref.at[z], own_sems.at[2]))
    ups[-1].start()
    for i in range(4):
        reduce.core(0, i, None).wait_recv()
        reduce.by_core[0, i] = reduce.by_core[0, i] + part[flip(f, 2 * i)]
    reduce.send_near(0)
    reduce.far(0)
    reduce.along_z(0)
    mixed = tok_ref[...].astype(F32) + reduce.by_far[0].astype(F32)
    mixed_ref[...] = mixed
    low_ref[...] = (mixed * rms_scale(mixed) * gain_two_ref[...]).astype(BF16)
    near_own = pltpu.make_async_copy(low_ref, plane_ref.at[0, f], own_sems.at[1])
    near_own.start()
    near = Gather(plane_ref, (xs, xr), 1, z, f)
    near_own.wait()
    near.first(0, own=True)
    for j in range(1, nz):
        grads.first(j)
    near.second(0)
    for j in range(1, nz):
        grads.second(j)
    lane = lax.broadcasted_iota(jnp.int32, (rows, HD), 1) - TAIL - shared

    def mark(d, _):
        ids = all_ids[d].T
        found = ids[:, 0:1] == lane
        for k in range(1, ids.shape[1] - 1):
            found = found | (ids[:, k : k + 1] == lane)
        value = jnp.where(found, 1.0, 0.0)
        mark_ref[d] = value.astype(BF16)

        @pl.when(d == me)
        def _():
            own_mark_ref[...] = value

        return 0

    lax.fori_loop(0, count, mark, 0)
    outgoing[2].start()
    near.third(0)
    for j in range(1, nz):
        grads.third(j)
    for j in range(nz):
        grads.fourth(j)
    near.fourth(0)

    def left(i, _):
        d = (me + i) % count
        copies(d, 0).wait_send()
        copies(d, 1).wait_send()
        return 0

    lax.fori_loop(1, count, left, 0)

    def q_left(i, _):
        m = (f + i) % nf
        for j in range(nz):
            q_each(lambda s: q_copy(j, m, s).wait_send(), m)
        return 0

    lax.fori_loop(1, nf, q_left, 0)
    out_each(lambda j, m: out_copy(j, m).wait_send(), lambda j: None)
    for copy in to_near + to_core:
        copy.wait_send()
    for i in range(4):
        reduce.core(0, i, part.at[0]).wait_send()
    reduce.end()
    for j in range(1, nz):
        grads.by_z(j).wait_send()
    grads.end()
    near.end()
    for copy in ups + outgoing:
        copy.wait()


def front(tok, wqkv, wout, router, sup, again, fgain, eids, seg, cosine, sine, og, eup, nz, nf, shared):
    rows, width = tok.shape
    dense, count = wqkv.shape[0], nz * nf
    length = 8 * rows
    hidden, up_rows = eup.shape[2] // (2 * nz), eup.shape[1]
    heads, real = head_table(8)
    shape = jax.ShapeDtypeStruct
    return pl.pallas_call(
        functools.partial(front_kernel, nz=nz, nf=nf, hidden=hidden, shared=shared, heads=heads, real=real),
        out_shape=(
            shape((SLOTS, width, 3 * HD), BF16),
            shape((SLOTS * HD, width), BF16),
            shape((count, dense, 2 * TAIL), BF16),
            shape((width, HD), BF16),
            shape((1, width), F32),
            shape((1, width), F32),
            shape((count, rows, HD), BF16),
            shape((rows, HD), F32),
            shape((length, HD), jnp.int32),
            shape((8, length), jnp.int32),
            shape((length, width), BF16),
            shape((length, 3 * SLOTS * HD), BF16),
            shape((length, SLOTS * HD), BF16),
            shape((length, SLOTS * HD), F32),
            shape((rows, width), F32),
            shape((rows, width), BF16),
            shape((1, 8, rows, width), BF16),
            shape((nz, 8, rows, width), BF16),
            shape((nz, up_rows, 4 * hidden), BF16),
        ),
        in_specs=[VMEM] * 13,
        out_specs=(ANY, VMEM, ANY, VMEM, VMEM, VMEM, ANY, VMEM, VMEM, VMEM) + (ANY,) * 4 + (VMEM,) * 2 + (ANY,) * 3,
        scratch_shapes=[
            pltpu.VMEM((SLOTS, width, 3 * HD), BF16),
            pltpu.VMEM((count, dense, 2 * TAIL), BF16),
            pltpu.VMEM((count, rows, HD), BF16),
            pltpu.VMEM((length, width), BF16),
            pltpu.VMEM((length, 3 * SLOTS * HD), BF16),
            pltpu.VMEM((length, SLOTS * HD), BF16),
            pltpu.VMEM((length, SLOTS * HD), F32),
            pltpu.VMEM((eids.shape[0] + 1, rows), jnp.int32),
            pltpu.SemaphoreType.DMA((7,)),
            pltpu.VMEM((8, rows, width), BF16),
            pltpu.VMEM((SLOTS, count, dense, 3 * HD), BF16),
            pltpu.VMEM((8, dense, width), BF16),
            pltpu.VMEM((nz, dense, 3 * width), BF16),
            pltpu.VMEM((nz, dense, width), BF16),
            pltpu.VMEM((count, eids.shape[0] + 1, rows), jnp.int32),
            pltpu.VMEM((nz, 8, SLOTS, dense, 3 * HD), BF16),
            pltpu.VMEM((count, dense, 2 * TAIL), BF16),
            pltpu.VMEM((8, rows, width), BF16),
            pltpu.VMEM((8 * dense, width), F32),
            pltpu.VMEM((nz, up_rows, 4 * hidden), BF16),
            *Reduce.scratch(1, rows, width),
            *pair_of(7),
            pltpu.SemaphoreType.DMA((2, count)),
            pltpu.SemaphoreType.DMA((2, count)),
            pltpu.SemaphoreType.DMA((nz, 8, SLOTS)),
            pltpu.SemaphoreType.DMA((nz, 8, SLOTS)),
            pltpu.SemaphoreType.DMA((nz, 8)),
            pltpu.SemaphoreType.DMA((8,)),
            *pair_of(nz),
            *pair_of(nz),
            *pair_of(Reduce.copies(1)),
            *pair_of(Gather.copies(nz)),
            *pair_of(Gather.copies(1)),
            *pair_of(nz),
            pltpu.SemaphoreType.DMA((3,)),
        ],
        compiler_params=pltpu.CompilerParams(
            collective_id=1, has_side_effects=True, vmem_limit_bytes=58 * 2**20
        ),
        name="front",
    )(tok, wqkv, wout, router, sup, again, fgain, eids, seg, cosine, sine, og, eup)


def route_grads(gx, og, mixed, normed, router, marks, gain):
    width = mixed.shape[1]
    scale = rms_scale(mixed)
    normal = mixed * scale
    logits = jnp.where(marks > 0.5, dot(normed, router), NEG)
    weights = jnp.exp(logits - jnp.max(logits, axis=-1, keepdims=True))
    probs = weights / jnp.sum(weights, axis=-1, keepdims=True)
    grad_gates = gx[:, width:]
    grad_logits = (probs * (grad_gates - jnp.sum(probs * grad_gates, axis=-1, keepdims=True))).astype(BF16)
    grad_router = dot_tn(normed, grad_logits)
    grad_normed = gx[:, :width] + dot_nt(grad_logits, router)
    ones = jnp.where(lax.broadcasted_iota(jnp.int32, (mixed.shape[0], HD), 1) == TAIL - 1, 1.0, 0.0)
    grad_gain = lax.dot_general(
        grad_normed * normal, ones, (((0,), (0,)), ((), ())),
        precision=lax.Precision.HIGHEST, preferred_element_type=F32,
    )
    grad_mixed = og.astype(F32) + norm_back(grad_normed, normal, scale, gain)
    return grad_mixed, pltpu.roll(grad_router + grad_gain, TAIL, 1)


def experts_kernel(
    normed_ref, plane_ref, all_grad_ref, mark_ref, own_ref, eup_ref, tail_ref, edown_ref, sdown_ref,
    og_ref, mixed_ref, router_ref, own_mark_ref, gain_ref,
    out_any, low_ref, gm_ref, small_ref, geup_ref, gedown_ref, gsdown_ref, all_normed_ref,
    out_ref,
    up_ref, upt_ref, down_ref, downt_ref, gup_ref, gdown_ref,
    xt, gt, mt, px, po, *refs, nz, hidden, shared,
):
    bufs, (tile_sems, rs, rr, os_, or_, xs, xr, own_sems) = refs[:4], refs[4:]
    z, f = place()
    rows, width = mixed_ref.shape
    half = down_ref.shape[0]
    pair = 2 * hidden
    greet(near_devices(z, f) + z_devices(z, f, nz))
    own = pltpu.make_async_copy(normed_ref, all_normed_ref.at[z, f], own_sems.at[0])
    own.start()
    gather = Gather(all_normed_ref, (xs, xr), nz, z, f)
    reduce = Reduce(bufs, (rs, rr), nz, z, f)
    outs = Reduce([out_ref, out_ref, out_ref, out_ref], (os_, or_), nz, z, f)
    own.wait()
    gather.along_z(1)
    ffn_weights(eup_ref, tail_ref, edown_ref, sdown_ref, up_ref, upt_ref, down_ref, downt_ref)
    gup_ref[...] = jnp.zeros_like(gup_ref)
    gdown_ref[...] = jnp.zeros_like(gdown_ref)
    gather.along_z(2)
    if nz > 1:
        gather.first(1)

    def loads(i, rows_ref=all_normed_ref):
        j, t, slot = i // 4, i % 4, i % 2
        piece = lax.rem(z - away(j, nz) + nz, nz)
        base = f + (1 - 2 * (f % 2)) * (1 - t // 2) + (4 - 8 * (f // 4 % 2)) * (t % 2)
        copies = []
        for b in range(2):
            block = flip(base, 2 * b)
            there = piece if rows_ref is all_normed_ref else 0
            copies += [
                pltpu.make_async_copy(rows_ref.at[there, block], xt.at[slot, b], tile_sems.at[slot, b]),
                pltpu.make_async_copy(all_grad_ref.at[piece, block], gt.at[slot, b], tile_sems.at[slot, 2 + b]),
                pltpu.make_async_copy(mark_ref.at[piece, block], mt.at[slot, b], tile_sems.at[slot, 4 + b]),
            ]
        return copies

    for copy in loads(0, plane_ref):
        copy.start()
    last = 4 * nz - 1

    def tile(i, _):
        j, t, slot = i // 4, i % 4, i % 2
        more = j < nz - 1

        @pl.when((t == 0) & more)
        def _():
            gather.second(j + 1)

        @pl.when(i == 1)
        def _():
            gather.along_z(3)

        @pl.when((t == 2) & more)
        def _():
            gather.third(j + 1)

        @pl.when((t == 2) & (j < nz - 2))
        def _():
            gather.first(j + 2)

        @pl.when((t == 3) & more)
        def _():
            gather.fourth(j + 1)

        @pl.when((t == 0) & (j > 0))
        def _():
            for k in range(4):
                reduce.core(j - 1, k, px.at[k]).wait_send()
                outs.core(j - 1, k, po.at[k]).wait_send()

        for copy in loads(i):
            copy.wait()

        @pl.when(i < 3)
        def _():
            for copy in loads(i + 1, plane_ref):
                copy.start()

        @pl.when((i >= 3) & (i < last))
        def _():
            for copy in loads(i + 1):
                copy.start()

        x = xt[slot].reshape(2 * rows, width)
        g = gt[slot].reshape(2 * rows, width)
        out, gx, grad_pre, acts = ffn_rows(
            x, g, mt[slot].reshape(2 * rows, HD), own_ref[...], up_ref, upt_ref, down_ref, downt_ref, hidden, shared
        )
        at = pl.ds(2 * t, 2)
        po[at] = out.reshape(2, rows, width)
        px[at] = gx.reshape(2, rows, width + HD)
        gup_ref[...] += dot_tn(x, grad_pre)
        gdown_ref[...] += dot_tn(acts, g)

        @pl.when(t == 1)
        def _():
            for k in range(4):
                reduce.core(j, k, px.at[k]).start()
            for k in range(4):
                outs.core(j, k, po.at[k]).start()

        @pl.when((t == 1) & (j > 0))
        def _():
            reduce.far(j - 1)

        @pl.when((t == 2) & (j > 0))
        def _():
            reduce.along_z(j - 1)

        @pl.when(t == 3)
        def _():
            for k in range(4):
                reduce.core(j, k, None).wait_recv()
                reduce.by_core[j, k] = reduce.by_core[j, k] + px[4 + k]
            reduce.send_near(j)
            for k in range(4):
                outs.core(j, k, None).wait_recv()
                out_ref[j, k] = out_ref[j, k] + po[4 + k]

        return 0

    lax.fori_loop(0, 4 * nz, tile, 0)
    up_ref[:, : 2 * pair] = jnp.concatenate([gup_ref[:, :pair], gup_ref[:, half : half + pair]], axis=1).astype(BF16)
    up_rows = width // nz
    ends = [
        pltpu.make_async_copy(up_ref.at[pl.ds(p * up_rows, up_rows), pl.ds(0, 2 * pair)], geup_ref.at[p], own_sems.at[p])
        for p in range(nz)
    ]
    ends.append(pltpu.make_async_copy(gdown_ref.at[pl.ds(0, pair)], gedown_ref, own_sems.at[nz]))
    ends.append(pltpu.make_async_copy(out_ref, out_any, own_sems.at[nz + 1]))
    for copy in ends:
        copy.start()
    reduce.far(nz - 1)
    gtail = jnp.concatenate([gup_ref[:, half - TAIL : half], gup_ref[:, 2 * half - TAIL :]], axis=1)
    gsdown_ref[...] = gdown_ref[half - TAIL : half - TAIL + shared, :]
    reduce.along_z(nz - 1)
    grad_mixed, small = route_grads(
        reduce.total(), og_ref[...], mixed_ref[...], normed_ref[...], router_ref[...], own_mark_ref[...], gain_ref[...]
    )
    gm_ref[...] = grad_mixed
    low_ref[...] = grad_mixed.astype(BF16)
    small_ref[...] = (small + gtail).astype(BF16)
    for k in range(4):
        reduce.core(nz - 1, k, px.at[k]).wait_send()
        outs.core(nz - 1, k, po.at[k]).wait_send()
    for copy in ends:
        copy.wait()
    for j in range(4, nz + 1):
        gather.along_z(j)
    gather.end(1)
    reduce.end()


def experts_turn(
    normed, plane, all_grad, marks, own, eup, tail, edown, sdown, og, mixed, router, own_marks, gain, nz, nf
):
    rows, width = mixed.shape
    pair, shared = edown.shape[0], sdown.shape[0]
    half = up_to(pair + TAIL, HD)
    wide = width + HD
    return pl.pallas_call(
        functools.partial(experts_kernel, nz=nz, hidden=pair // 2, shared=shared),
        out_shape=(
            jax.ShapeDtypeStruct((nz, 4, rows, width), BF16),
            jax.ShapeDtypeStruct((rows, width), BF16),
            jax.ShapeDtypeStruct((rows, width), F32),
            jax.ShapeDtypeStruct((width, HD), BF16),
            jax.ShapeDtypeStruct((nz, width // nz, 2 * pair), BF16),
            jax.ShapeDtypeStruct((pair, width), F32),
            jax.ShapeDtypeStruct((shared, width), F32),
            jax.ShapeDtypeStruct((nz, 8, rows, width), BF16),
        ),
        in_specs=[VMEM, ANY, ANY, ANY] + [VMEM] * 10,
        out_specs=(ANY, VMEM, VMEM, VMEM, ANY, ANY, VMEM, ANY),
        scratch_shapes=[
            pltpu.VMEM((nz, 4, rows, width), BF16),
            pltpu.VMEM((width, 2 * half), BF16),
            pltpu.VMEM((2 * half, width), BF16),
            pltpu.VMEM((half, width), BF16),
            pltpu.VMEM((width, half), BF16),
            pltpu.VMEM((width, 2 * half), F32),
            pltpu.VMEM((half, width), F32),
            pltpu.VMEM((2, 2, rows, width), BF16),
            pltpu.VMEM((2, 2, rows, width), BF16),
            pltpu.VMEM((2, 2, rows, HD), BF16),
            pltpu.VMEM((8, rows, wide), BF16),
            pltpu.VMEM((8, rows, width), BF16),
            *Reduce.scratch(nz, rows, wide),
            pltpu.SemaphoreType.DMA((2, 6)),
            *pair_of(Reduce.copies(nz)),
            *pair_of(Reduce.copies(nz)),
            *pair_of(Gather.copies(nz)),
            pltpu.SemaphoreType.DMA((nz + 2,)),
        ],
        compiler_params=pltpu.CompilerParams(
            collective_id=3, has_side_effects=True, vmem_limit_bytes=60 * 2**20
        ),
        name="experts_turn",
    )(
        normed, plane, all_grad, marks.reshape(nz, 8, rows, HD), own, eup, tail, edown, sdown, og, mixed, router, own_marks, gain
    )[:7]


def back_kernel(
    low_ref, geup_ref, *refs, nz, nf, heads, real,
):
    sources, refs = refs[:11], refs[11:]
    (wo_ref, w_ref, normed_ref, qkv_ref, attn_ref, lse_ref, cos_ref, sin_ref, segq_ref, segk_ref, out_ref), refs = (
        refs[-12:-1],
        refs[:-12] + refs[-1:],
    )
    back_body(sources, low_ref, geup_ref, wo_ref, w_ref, normed_ref, qkv_ref, attn_ref, lse_ref, cos_ref, sin_ref,
              segq_ref, segk_ref, out_ref, *refs, nz=nz, nf=nf, heads=heads, real=real)


def back_body(
    sources, low_ref, geup_ref, wo_ref, w_ref, normed_ref, qkv_ref, attn_ref, lse_ref, cos_ref, sin_ref, segq_ref, segk_ref,
    out_ref, small_ref, tok_ref, mixed_ref, own_gm_ref, gain_ref,
    block_ref, gtok_ref, gwqkv_ref, gwout_ref, all_small_ref, pieces_ref,
    seq, gkv_ref, gqkv_ref, wt_ref, part_ref, gw_ref, gwo_ref, gws, gwos, smalls, *refs, nz, nf, heads, real,
):
    bufs, refs = refs[:7], refs[7:]
    rs, rr, os_, or_, all_s, all_r, wo_s, wo_r, gs, gr, es, er, own_sems, in_sems = refs
    local = (wo_ref, w_ref, normed_ref, qkv_ref, attn_ref, lse_ref, cos_ref, sin_ref, segq_ref, segk_ref, out_ref)
    loads = [pltpu.make_async_copy(src, dst, in_sems.at[k]) for k, (src, dst) in enumerate(zip(sources, local))]
    for copy in loads:
        copy.start()
    z, f = place()
    me, count = z * nf + f, nz * nf
    dense = gw_ref.shape[2]
    rows, width = tok_ref.shape
    length = 8 * rows
    greet_all(nz, nf)
    seq[0, f] = low_ref[...]
    turned = Gather(seq, (gs, gr), 1, z, f)
    turned.first(0, own=True)
    ups = []
    for j in range(1, nz):
        there = lax.rem(z + j, nz)
        ups.append(send(geup_ref.at[there], pieces_ref.at[z], (es, er), j, (there, f)))
    ups.append(pltpu.make_async_copy(geup_ref.at[z], pieces_ref.at[z], own_sems.at[0]))
    for copy in ups:
        copy.start()
    turned.second(0)
    outs = Reduce([out_ref, *bufs[4:]], (os_, or_), nz, z, f)
    order = list(range(1, nz)) + [0]
    loads[10].wait()
    outs.send_near(order[0])
    turned.third(0)

    def two(m):
        return first_head(m + 1) - first_head(m) == 2

    def copies(d, k):
        device = (d // nf, d % nf)
        src, dst = ((gw_ref.at[0, d], gws.at[0, me]), (gw_ref.at[1, d], gws.at[1, me]), (small_ref.at[d], smalls.at[me]))[k]
        return pltpu.make_async_remote_copy(
            src, dst, all_s.at[k, d], all_r.at[k, me], device_id=device, device_id_type=MESH
        )

    def wanted(m, block):
        low, high = out_blocks(m, dense)
        return (low <= block) & (block <= high)

    def owner_of(block):
        return head_owner(block * dense // HD)

    low, _ = out_blocks(f, dense)

    def out_copy(d):
        k = 2 * z + f - owner_of(d)
        return pltpu.make_async_remote_copy(
            gwo_ref.at[d - low], gwos.at[k], wo_s.at[d - low], wo_r.at[k],
            device_id=(d // nf, d % nf), device_id_type=MESH,
        )

    for copy in loads[:10]:
        copy.wait()
    turned.fourth(0)
    spare = gwo_ref.shape[0] * dense
    wide = up_to(spare, HD)
    shift = first_head(f) * HD - low * dense
    moved = jnp.concatenate([attn_ref[...].astype(F32), jnp.zeros((length, wide - SLOTS * HD), F32)], axis=1)
    moved = pltpu.roll(moved, shift, 1).astype(BF16)
    gwo_ref[...] = dot_tn(moved, seq[0].reshape(length, width))[:spare].reshape(gwo_ref.shape).astype(BF16)

    def start_small(i, _):
        d = (me + i) % count
        copies(d, 2).start()

        @pl.when(wanted(f, d))
        def _():
            out_copy(d).start()

        return 0

    lax.fori_loop(1, count, start_small, 0)
    own_slot = 2 * z + f - owner_of(me)
    smalls[me] = small_ref[me]

    @pl.when(wanted(f, me))
    def _():
        gwos[own_slot] = gwo_ref[me - low]

    gkv_ref[...] = jnp.zeros_like(gkv_ref)
    block = 256
    for i in range(length // block):
        attn_back_block(
            i, block, seq[0, i * block // rows : (i + 1) * block // rows].reshape(block, width), wo_ref, qkv_ref, attn_ref, lse_ref, cos_ref, sin_ref, segq_ref, segk_ref, gkv_ref, gqkv_ref
        )
        if i + 1 < nz:
            outs.send_near(order[i + 1])
        if i < nz:
            outs.far(order[i])
        if 0 < i <= nz:
            outs.along_z(order[i - 1])
    attn_back_keys(w_ref, cos_ref, sin_ref, gkv_ref, gqkv_ref, wt_ref)
    step = 3 * HD
    reduce = Reduce(bufs[:4], (rs, rr), 1, z, f)
    for i in range(length // block):
        mine = slice(i * block, (i + 1) * block)
        at = i * block // rows
        part_ref[at : at + block // rows] = (
            dot(gqkv_ref[mine, :], wt_ref[...]).astype(BF16).reshape(block // rows, rows, width)
        )
    for i in range(4):
        reduce.core(0, i, part_ref.at[flip(f, 1 | 2 * i)]).start()

    def weights(s):
        value = dot_tn(normed_ref[...], gqkv_ref[:, s * step : (s + 1) * step])
        gw_ref[s] = value.reshape(count, dense, step).astype(BF16)

        def start(i, _):
            copies((me + i) % count, s).start()
            return 0

        lax.fori_loop(1, count, start, 0)
        gws[s, me] = gw_ref[s, me]

    weights(0)
    for i in range(4):
        reduce.core(0, i, None).wait_recv()
        reduce.by_core[0, i] = reduce.by_core[0, i] + part_ref[flip(f, 2 * i)]
    reduce.send_near(0)

    @pl.when(two(f))
    def _():
        weights(1)

    for k in range(length // block, nz):
        outs.far(order[k])
    for k in range(length // block - 1, nz):
        outs.along_z(order[k])
    reduce.far(0)
    reduce.along_z(0)
    x = tok_ref[...].astype(F32)
    scale = rms_scale(x)
    gtok_ref[...] = (
        own_gm_ref[...] + norm_back(reduce.by_far[0].astype(F32), x * scale, scale, gain_ref[...])
    ).astype(BF16)
    block_ref[...] = (mixed_ref[...] + outs.total()).astype(BF16)

    owner = owner_of(me)
    next_owner = head_owner((me * dense + dense - 1) // HD)
    for k in range(2 * nz):
        there = (k // 2 != z) | (f != owner + k % 2)
        if k % 2:
            there = there & (next_owner != owner)

        @pl.when(there)
        def _():
            pltpu.make_async_remote_copy(
                gwo_ref.at[0], gwos.at[k], wo_s.at[0], wo_r.at[k], device_id=(z, flip(f, 1)), device_id_type=MESH
            ).wait_recv()

    gwout_ref[...] = sum(gwos[2 * t].astype(F32) for t in range(nz))

    @pl.when(next_owner != owner)
    def _():
        gwout_ref[...] += sum(gwos[2 * t + 1].astype(F32) for t in range(nz))

    def came(d, k):
        dst = (gws.at[0, d], gws.at[1, d], smalls.at[d])[k]
        return pltpu.make_async_remote_copy(
            dst, dst, all_s.at[k, d], all_r.at[k, d], device_id=(d // nf, d % nf), device_id_type=MESH
        )

    def finish(i, _):
        d = (me + i) % count
        came(d, 0).wait_recv()

        @pl.when(two(d % nf))
        def _():
            came(d, 1).wait_recv()

        came(d, 2).wait_recv()
        copies(d, 0).wait_send()

        @pl.when(two(f))
        def _():
            copies(d, 1).wait_send()

        copies(d, 2).wait_send()

        @pl.when(wanted(f, d))
        def _():
            out_copy(d).wait_send()

        return 0

    lax.fori_loop(1, count, finish, 0)
    for m in range(8):
        for s in range(SLOTS):
            if real[m * SLOTS + s]:
                h = heads[m * SLOTS + s]
                both = sum(gws[s, t * nf + m].astype(F32) for t in range(nz))
                for c in range(3):
                    gwqkv_ref[:, c * width + h * HD : c * width + (h + 1) * HD] = both[:, c * HD : (c + 1) * HD]
    all_small_ref[...] = smalls[...]
    for i in range(4):
        reduce.core(0, i, part_ref.at[0]).wait_send()
    reduce.end()
    outs.end()
    turned.end()
    for copy in ups:
        copy.wait()


def back(
    low, geup, wo, w, normed, qkv, attn, lse, cosine, sine, segq, segk, out_part, small, tok, mixed, own_gm, gain, nz, nf
):
    rows, width = tok.shape
    length, count = 8 * rows, nz * nf
    dense = width // count
    heads, real = head_table(8)
    return pl.pallas_call(
        functools.partial(back_kernel, nz=nz, nf=nf, heads=heads, real=real),
        out_shape=(
            jax.ShapeDtypeStruct((rows, width), BF16),
            jax.ShapeDtypeStruct((rows, width), BF16),
            jax.ShapeDtypeStruct((dense, 3 * width), F32),
            jax.ShapeDtypeStruct((dense, width), F32),
            jax.ShapeDtypeStruct((count, dense, HD), BF16),
            jax.ShapeDtypeStruct(geup.shape, BF16),
        ),
        in_specs=[VMEM] + [ANY] * 12 + [VMEM] * 5,
        out_specs=(VMEM,) * 5 + (ANY,),
        scratch_shapes=[
            pltpu.VMEM((1, 8, rows, width), BF16),
            pltpu.VMEM((length, 2 * SLOTS * HD), F32),
            pltpu.VMEM((length, 3 * SLOTS * HD), BF16),
            pltpu.VMEM((3 * SLOTS * HD, width), BF16),
            pltpu.VMEM((8, rows, width), BF16),
            pltpu.VMEM((SLOTS, count, dense, 3 * HD), BF16),
            pltpu.VMEM((8, dense, width), BF16),
            pltpu.VMEM((SLOTS, count, dense, 3 * HD), BF16),
            pltpu.VMEM((2 * nz, dense, width), BF16),
            pltpu.VMEM((count, dense, HD), BF16),
            *Reduce.scratch(1, rows, width),
            *Reduce.scratch(nz, rows, width)[1:],
            *pair_of(Reduce.copies(1)),
            *pair_of(Reduce.copies(nz)),
            pltpu.SemaphoreType.DMA((3, count)),
            pltpu.SemaphoreType.DMA((3, count)),
            pltpu.SemaphoreType.DMA((8,)),
            pltpu.SemaphoreType.DMA((2 * nz,)),
            *pair_of(Gather.copies(1)),
            *pair_of(nz),
            pltpu.SemaphoreType.DMA((1,)),
            *[pltpu.VMEM(a.shape, a.dtype) for a in (wo, w, normed, qkv, attn, lse, cosine, sine, segq, segk, out_part)],
            pltpu.SemaphoreType.DMA((11,)),
        ],
        compiler_params=pltpu.CompilerParams(
            collective_id=4, has_side_effects=True, vmem_limit_bytes=60 * 2**20
        ),
        name="back",
    )(
        low, geup, wo, w, normed, qkv, attn, lse, cosine, sine, segq, segk, out_part,
        small.reshape(count, dense, HD), tok, mixed, own_gm, gain,
    )


def unpack_kernel(
    pieces_ref, small_ref, wqkv_ref, gwqkv_ref, gain_ref, block_in, tok_in, wout_in, edown_in, sdown_in,
    geup_ref, gsup_ref, grouter_ref, gone_ref, gtwo_ref, block_ref, tok_ref, gqkv_ref, wout_ref, edown_ref, sdown_ref,
    *, shared, experts,
):
    for src, dst in (
        (block_in, block_ref), (tok_in, tok_ref), (gwqkv_ref, gqkv_ref), (wout_in, wout_ref), (edown_in, edown_ref),
        (sdown_in, sdown_ref),
    ):
        dst[...] = src[...]
    nz = pieces_ref.shape[0]
    hidden = pieces_ref.shape[2] // 4
    for t in range(nz):
        for g in range(2):
            for e in range(2):
                at = (2 * g + e) * hidden
                to = (g * nz + t) * hidden
                geup_ref[e, :, to : to + hidden] = pieces_ref[t, :, at : at + hidden].astype(F32)
    count = small_ref.shape[0]
    total = small_ref[0].astype(F32)
    for d in range(count):
        if d:
            total = total + small_ref[d].astype(F32)
        for g in range(2):
            to = (g * count + d) * shared
            gsup_ref[:, to : to + shared] = small_ref[d, :, g * TAIL : g * TAIL + shared].astype(F32)
    grouter_ref[...] = total[:, shared : shared + experts].T
    one = jnp.sum(wqkv_ref[...].astype(F32) * gwqkv_ref[...], axis=-1, keepdims=True) / gain_ref[...].astype(F32)
    gone_ref[...] = one.T
    gtwo_ref[...] = total[:, HD - 1 :].T


def unpack(pieces, small, wqkv, gwqkv, gain, rest, shared, experts):
    nz, up_rows, packed = pieces.shape
    count, dense, _ = small.shape
    return pl.pallas_call(
        functools.partial(unpack_kernel, shared=shared, experts=experts),
        out_shape=(
            jax.ShapeDtypeStruct((2, up_rows, nz * packed // 2), F32),
            jax.ShapeDtypeStruct((dense, 2 * count * shared), F32),
            jax.ShapeDtypeStruct((experts, dense), F32),
            jax.ShapeDtypeStruct((1, dense), F32),
            jax.ShapeDtypeStruct((1, dense), F32),
            *[jax.ShapeDtypeStruct(a.shape, a.dtype) for a in (*rest[:2], gwqkv, *rest[2:])],
        ),
        in_specs=[VMEM] * 10,
        out_specs=(VMEM,) * 11,
        compiler_params=pltpu.CompilerParams(vmem_limit_bytes=40 * 2**20),
        name="unpack",
    )(pieces, small, wqkv, gwqkv, gain, *rest)


def tables():
    pos = np.arange(SEQ, dtype=np.float32)
    freqs = np.float32(ROPE) ** (-np.arange(HD // 2, dtype=np.float32) * np.float32(2.0 / HD))
    angles = (pos[:, None] * freqs[None, :]).astype(np.float32)
    cosine = np.concatenate([np.cos(angles)] * 2, axis=1).astype(np.float32)
    sine = np.concatenate([-np.sin(angles), np.sin(angles)], axis=1).astype(np.float32)
    return jnp.asarray(cosine), jnp.asarray(sine)


def local_near(
    mesh, tokens, out_grad, segment_ids, expert_ids, attn_gain, ffn_gain, w_qkv, w_out,
    w_router, w_shared_up, w_shared_down, w_expert_up, w_expert_down,
):
    nz, nf = mesh.shape["dp"], mesh.shape["fsdp"]
    rows, width = tokens.shape
    experts = w_router.shape[1]
    hidden, shared = w_expert_down.shape[1], w_shared_down.shape[0]
    f = lax.axis_index("fsdp")
    cosine, sine = tables()
    (
        w, wo, tail, router, gain_one, gain_two, marks, own_marks, segq, segk, normed_one, qkv, attn, lse, mixed, normed,
        plane, all_grad, pieces,
    ) = front(
        tokens, w_qkv, w_out, w_router.T, w_shared_up, attn_gain[:, None], ffn_gain[:, None], expert_ids.T,
        segment_ids[None], cosine, sine, out_grad, w_expert_up, nz, nf, shared,
    )
    tail = tail.reshape(width, 2 * TAIL)
    lane = jnp.arange(HD, dtype=jnp.int32) - TAIL - shared
    own = (lane[None, :] == (2 * f + jnp.arange(2, dtype=jnp.int32))[:, None]).astype(F32)
    out_part, low, grad_mixed, small, geup, gedown, gsdown = experts_turn(
        normed, plane, all_grad, marks, own, pieces.reshape(width, 4 * hidden), tail,
        w_expert_down.reshape(2 * hidden, width), w_shared_down, out_grad, mixed, router, own_marks, gain_two, nz, nf,
    )
    block_out, tokens_grad, grad_wqkv, grad_wout, smalls, gpieces = back(
        low, geup, wo, w, normed_one, qkv, attn, lse, cosine, sine, segq, segk, out_part, small,
        tokens, mixed, grad_mixed, gain_one, nz, nf,
    )
    (
        grad_eup, grad_sup, grad_router, grad_one, grad_two, block_out, tokens_grad, grad_wqkv, grad_wout, gedown, gsdown,
    ) = unpack(
        gpieces, smalls, w_qkv, grad_wqkv, attn_gain[:, None], (block_out, tokens_grad, grad_wout, gedown, gsdown),
        shared, experts,
    )
    return (
        block_out, tokens_grad, grad_one[0], grad_two[0], grad_wqkv, grad_wout, grad_router.T, grad_sup,
        gsdown, grad_eup, gedown.reshape(2, hidden, width),
    )


def local_far(
    mesh, tokens, out_grad, segment_ids, expert_ids, attn_gain, ffn_gain, w_qkv, w_out,
    w_router, w_shared_up, w_shared_down, w_expert_up, w_expert_down,
):
    nz, nf = mesh.shape["dp"], mesh.shape["fsdp"]
    nd = nz * nf
    rows, width = tokens.shape
    group = SEQ // rows
    experts = w_router.shape[1]
    dense = w_qkv.shape[0]
    hidden, shared = w_expert_down.shape[1], w_shared_down.shape[0]
    up_rows = w_expert_up.shape[1]
    both = ("dp", "fsdp")
    groups = None if nf == group else [[a + i for i in range(group)] for a in range(0, nf, group)]
    f = lax.axis_index("fsdp")
    member = lax.rem(f, group)
    heads, real = head_table(group)

    by_head = w_qkv.reshape(dense, 3, HEADS, HD)
    empty = jnp.zeros((dense, 3, HD), BF16)
    cols = jnp.stack([by_head[:, :, h] if r else empty for h, r in zip(heads, real)], axis=0)
    cols = cols.reshape(group, SLOTS, dense, 3 * HD)
    cols = jnp.tile(cols, (nf // group, 1, 1, 1))
    cols = lax.all_to_all(cols, "fsdp", 0, 0, tiled=True)
    w = lax.all_gather(cols, "dp", axis=0, tiled=True).transpose(1, 0, 2, 3).reshape(SLOTS, width, 3 * HD)
    full_out = lax.all_gather(w_out, both, axis=0, tiled=True)
    first = HEADS * member // group
    own_real = (first + jnp.arange(SLOTS) < HEADS * (member + 1) // group).astype(BF16)
    padded = jnp.pad(full_out, ((0, (SLOTS - 1) * HD), (0, 0)))
    wo = lax.dynamic_slice(padded, (first * HD, 0), (SLOTS * HD, width))
    wo = wo * jnp.repeat(own_real, HD)[:, None]
    gains = lax.all_gather(jnp.stack([attn_gain, ffn_gain], axis=1).astype(F32), both, axis=0, tiled=True)
    gain_one, gain_two = gains[:, 0], gains[:, 1]
    router = lax.all_gather(w_router, both, axis=0, tiled=True)
    sup = w_shared_up.reshape(dense, 2, nd, shared).transpose(2, 0, 1, 3).reshape(nd, dense, 2 * shared)
    sup = lax.all_to_all(sup, both, 0, 0, tiled=True).reshape(width, 2, shared)
    eup = w_expert_up.reshape(2, up_rows, 2, nz, hidden).transpose(3, 1, 2, 0, 4)
    eup = lax.all_to_all(eup, "dp", 0, 0, tiled=True).reshape(width, 4 * hidden)
    rest = jnp.zeros((width, TAIL - shared), BF16)
    tail = jnp.concatenate([sup[:, 0], router, rest[:, experts:], sup[:, 1], rest], axis=1)
    chosen = jnp.any(expert_ids[:, :, None] == jnp.arange(experts, dtype=jnp.int32), axis=1)
    at = TAIL + shared
    marks = jnp.pad(chosen.astype(BF16), ((0, 0), (at, HD - experts - at)))
    marks = lax.all_gather(marks, both, axis=0, tiled=True)
    lane = jnp.arange(HD, dtype=jnp.int32)
    own = (lane[None, :] == (at + 2 * f + jnp.arange(2, dtype=jnp.int32))[:, None]).astype(F32)
    cosine, sine = tables()
    seg = lax.all_gather(segment_ids, "fsdp", axis=0, tiled=True, axis_index_groups=groups)
    segq = jnp.broadcast_to(seg[:, None], (SEQ, HD))
    segk = jnp.broadcast_to(seg[None, :], (8, SEQ))

    seq_tokens = lax.all_gather(tokens, "fsdp", axis=0, tiled=True, axis_index_groups=groups)
    part, normed_one, qkv, attn, lse = attn_forward(
        seq_tokens, gain_one[None, :], w, wo, cosine, sine, segq, segk
    )
    projected = lax.psum_scatter(part, "fsdp", scatter_dimension=0, tiled=True, axis_index_groups=groups)
    inputs = tokens.astype(F32)
    mixed = inputs + projected.astype(F32)
    scale_two = rms_scale(mixed)
    normal_two = mixed * scale_two
    normed_two = (normal_two * gain_two).astype(BF16)
    all_normed = lax.all_gather(normed_two, both, axis=0, tiled=True)
    all_grad = lax.all_gather(out_grad, both, axis=0, tiled=True)
    out_part, gx_part, geup, gtail, gedown, gsdown = ffn(
        all_normed, all_grad, marks, own, eup, tail, w_expert_down.reshape(2 * hidden, width), w_shared_down
    )
    gx = lax.psum_scatter(gx_part, both, scatter_dimension=0, tiled=True).astype(F32)
    ffn_out = lax.psum_scatter(out_part, both, scatter_dimension=0, tiled=True).astype(F32)
    block_out = (mixed + ffn_out).astype(BF16)

    logits = jnp.where(chosen, dot(normed_two, router), NEG)
    probs = jax.nn.softmax(logits, axis=-1)
    grad_gates = gx[:, width + at : width + at + experts]
    grad_logits = (
        probs * (grad_gates - jnp.sum(probs * grad_gates, axis=-1, keepdims=True))
    ).astype(BF16)
    grad_router = dot_tn(normed_two, grad_logits)
    grad_normed = gx[:, :width] + dot_nt(grad_logits, router)
    grad_gain_two = jnp.sum(grad_normed * normal_two, axis=0)
    grad_mixed = out_grad.astype(F32) + norm_back(grad_normed, normal_two, scale_two, gain_two)

    seq_gm = lax.all_gather(grad_mixed.astype(BF16), "fsdp", axis=0, tiled=True, axis_index_groups=groups)
    part_back, gw, gwo = attn_backward(
        seq_gm, wo, w, normed_one, qkv, attn, lse, cosine, sine, segq, segk
    )
    grad_normed_one = lax.psum_scatter(
        part_back, "fsdp", scatter_dimension=0, tiled=True, axis_index_groups=groups
    ).astype(F32)
    scale_one = rms_scale(inputs)
    normal_one = inputs * scale_one
    grad_gain_one = jnp.sum(grad_normed_one * normal_one, axis=0)
    tokens_grad = (grad_mixed + norm_back(grad_normed_one, normal_one, scale_one, gain_one)).astype(BF16)

    gw = lax.psum_scatter(gw, "dp", scatter_dimension=1, tiled=True)
    gw = lax.all_to_all(gw.reshape(SLOTS, nf, dense, 3 * HD), "fsdp", 1, 1, tiled=True).astype(F32)
    gw = jnp.sum(gw.reshape(SLOTS, nf // group, group, dense, 3, HD), axis=1)
    picked = [gw[i % SLOTS, i // SLOTS] for i in range(group * SLOTS) if real[i]]
    grad_wqkv = jnp.stack(picked, axis=2).reshape(dense, 3 * width)
    gwo = gwo * jnp.repeat(own_real, HD)[:, None]
    all_gwo = jnp.zeros(((HEADS + SLOTS - 1) * HD, width), BF16)
    all_gwo = lax.dynamic_update_slice(all_gwo, gwo, (first * HD, 0))[: HEADS * HD]
    grad_wout = lax.psum_scatter(all_gwo, both, scatter_dimension=0, tiled=True).astype(F32)
    small = jnp.concatenate([grad_router, grad_gain_one[:, None], grad_gain_two[:, None]], axis=1)
    small = lax.psum_scatter(small, both, scatter_dimension=0, tiled=True)
    gsup = jnp.stack([gtail[:, :shared], gtail[:, TAIL : TAIL + shared]], axis=1)
    gsup = lax.all_to_all(gsup.reshape(nd, dense, 2 * shared).astype(BF16), both, 0, 0, tiled=True)
    grad_sup = gsup.reshape(nd, dense, 2, shared).transpose(1, 2, 0, 3).reshape(dense, 2 * nd * shared).astype(F32)
    geup = lax.all_to_all(geup.reshape(nz, up_rows, 2, 2, hidden), "dp", 0, 0, tiled=True)
    grad_eup = geup.transpose(3, 1, 2, 0, 4).reshape(2, up_rows, 2 * nz * hidden).astype(F32)
    return (
        block_out, tokens_grad, small[:, experts], small[:, experts + 1], grad_wqkv, grad_wout,
        small[:, :experts], grad_sup, gsdown, grad_eup, gedown.reshape(2, hidden, width),
    )


def solution(mesh):
    one, two = P(("dp", "fsdp")), P(("dp", "fsdp"), None)
    three = P("fsdp", "dp", None)

    def local(tokens, *rest):
        near = mesh.shape["fsdp"] == 8 == SEQ // tokens.shape[0] and mesh.shape["dp"] <= 4
        return (local_near if near else local_far)(mesh, tokens, *rest)

    return jax.shard_map(
        local,
        mesh=mesh,
        in_specs=(two, two, one, two, one, one, two, two, two, two, two, three, three),
        out_specs=(two, two, one, one, two, two, two, two, two, three, three),
        check_vma=False,
    )
```

```python
import functools

import jax
import jax.numpy as jnp
import numpy as np
from jax import lax
from jax.experimental import pallas as pl
from jax.experimental.pallas import tpu as pltpu
from jax.sharding import PartitionSpec as P

HEADS = 10
HD = 128
SEQ = 1024
SLOTS = 2
EPS = 1e-06
ROPE = 10000.0
NEG = -1e30
TAIL = 64
F32 = jnp.float32
BF16 = jnp.bfloat16


MESH = pl.DeviceIdType.MESH
VMEM = pl.BlockSpec(memory_space=pltpu.VMEM)
ANY = pl.BlockSpec(memory_space=pl.ANY)


def up_to(value, step):
    return -(-value // step) * step


def rms_scale(values):
    return lax.rsqrt(jnp.mean(values * values, axis=-1, keepdims=True) + EPS)


def norm_back(grad_normed, normal_rows, scale_rows, gain_rows):
    scaled = grad_normed * gain_rows
    return scale_rows * (
        scaled - normal_rows * jnp.mean(scaled * normal_rows, axis=-1, keepdims=True)
    )


def head_table(group):
    heads, real = [], []
    for i in range(group):
        own = list(range(HEADS * i // group, HEADS * (i + 1) // group))
        assert len(own) <= SLOTS
        heads += own + [0] * (SLOTS - len(own))
        real += [1] * len(own) + [0] * (SLOTS - len(own))
    return heads, real


def dot(a, b):
    return jnp.dot(a, b, preferred_element_type=F32)


def dot_nt(a, b):
    return lax.dot_general(a, b, (((1,), (1,)), ((), ())), preferred_element_type=F32)


def dot_tn(a, b):
    return lax.dot_general(a, b, (((0,), (0,)), ((), ())), preferred_element_type=F32)


def attn_project(i, block, x, gain, w_ref, cos_ref, sin_ref, normed_ref, qkv_ref):
    rows = pl.ds(pl.multiple_of(i * block, block), block)
    x = x.astype(F32)
    normed = (x * rms_scale(x) * gain).astype(BF16)
    normed_ref[rows, :] = normed
    cosine, sine = cos_ref[rows, :], sin_ref[rows, :]
    for s in range(SLOTS):
        proj = dot(normed, w_ref[s])
        for c in range(3):
            piece = proj[:, c * HD : (c + 1) * HD]
            if c < 2:
                piece = piece * cosine + pltpu.roll(piece, HD // 2, 1) * sine
            at = (3 * s + c) * HD
            qkv_ref[rows, at : at + HD] = piece.astype(BF16)


def attn_block(i, block, segq_ref, segk_ref, qkv_ref, attn_ref, lse_ref):
    scale = HD**-0.5
    rows = slice(i * block, (i + 1) * block)
    keys = (i + 1) * block
    row_pos = i * block + lax.broadcasted_iota(jnp.int32, (block, keys), 0)
    key_pos = lax.broadcasted_iota(jnp.int32, (block, keys), 1)
    allowed = (key_pos <= row_pos) & (segq_ref[rows, :1] == segk_ref[:1, :keys])
    outs = []
    for s in range(SLOTS):
        at = 3 * s * HD
        q = qkv_ref[rows, at : at + HD]
        k = qkv_ref[:keys, at + HD : at + 2 * HD]
        v = qkv_ref[:keys, at + 2 * HD : at + 3 * HD]
        scores = jnp.where(allowed, dot_nt(q, k) * scale, NEG)
        top = jnp.max(scores, axis=-1, keepdims=True)
        weights = jnp.exp(scores - top)
        total = jnp.sum(weights, axis=-1, keepdims=True)
        out = dot(weights.astype(BF16), v) / total
        lse_ref[rows, s * HD : (s + 1) * HD] = jnp.broadcast_to(top + jnp.log(total), (block, HD))
        low = out.astype(BF16)
        attn_ref[rows, s * HD : (s + 1) * HD] = low
        outs.append(low)
    return jnp.concatenate(outs, axis=-1)


def attn_forward_kernel(
    tok_ref, gain_ref, w_ref, wo_ref, cos_ref, sin_ref, segq_ref, segk_ref,
    part_ref, normed_ref, qkv_ref, attn_ref, lse_ref,
    *, block,
):
    count = tok_ref.shape[0] // block

    def project(i, _):
        x = tok_ref[pl.ds(pl.multiple_of(i * block, block), block), :]
        attn_project(i, block, x, gain_ref[...], w_ref, cos_ref, sin_ref, normed_ref, qkv_ref)
        return 0

    lax.fori_loop(0, count, project, 0)
    for i in range(count):
        outs = attn_block(i, block, segq_ref, segk_ref, qkv_ref, attn_ref, lse_ref)
        part_ref[i * block : (i + 1) * block, :] = dot(outs, wo_ref[...]).astype(BF16)


def attn_forward(tok, gain, w, wo, cosine, sine, segq, segk):
    length, width = tok.shape
    return pl.pallas_call(
        functools.partial(attn_forward_kernel, block=256),
        out_shape=(
            jax.ShapeDtypeStruct((length, width), BF16),
            jax.ShapeDtypeStruct((length, width), BF16),
            jax.ShapeDtypeStruct((length, 3 * SLOTS * HD), BF16),
            jax.ShapeDtypeStruct((length, SLOTS * HD), BF16),
            jax.ShapeDtypeStruct((length, SLOTS * HD), F32),
        ),
        in_specs=[VMEM] * 8,
        out_specs=(VMEM,) * 5,
        compiler_params=pltpu.CompilerParams(vmem_limit_bytes=56 * 2**20),
        cost_estimate=pl.CostEstimate(
            flops=2 * length * width * 4 * SLOTS * HD + 4 * SLOTS * HD * length * length,
            bytes_accessed=10 * length * width,
            transcendentals=SLOTS * length * length,
        ),
        name="attn_forward",
    )(tok, gain, w, wo, cosine, sine, segq, segk)


def attn_back_block(
    i, block, gm, wo_ref, qkv_ref, attn_ref, lse_ref, cos_ref, sin_ref, segq_ref, segk_ref, gkv_ref, gqkv_ref
):
    scale = HD**-0.5
    rows = slice(i * block, (i + 1) * block)
    keys = (i + 1) * block
    row_pos = i * block + lax.broadcasted_iota(jnp.int32, (block, keys), 0)
    key_pos = lax.broadcasted_iota(jnp.int32, (block, keys), 1)
    allowed = (key_pos <= row_pos) & (segq_ref[rows, :1] == segk_ref[:1, :keys])
    grad_attn = dot_nt(gm, wo_ref[...]).astype(BF16)
    for s in range(SLOTS):
        at = 3 * s * HD
        cut = slice(s * HD, (s + 1) * HD)
        q = qkv_ref[rows, at : at + HD]
        k = qkv_ref[:keys, at + HD : at + 2 * HD]
        v = qkv_ref[:keys, at + 2 * HD : at + 3 * HD]
        ga = grad_attn[:, cut]
        delta = jnp.sum(ga.astype(F32) * attn_ref[rows, cut].astype(F32), axis=-1, keepdims=True)
        scores = dot_nt(q, k) * scale
        probs = jnp.where(allowed, jnp.exp(scores - lse_ref[rows, s * HD : s * HD + 1]), 0.0)
        gs = (probs * (dot_nt(ga, v) - delta)).astype(BF16)
        gq = dot(gs, k) * scale
        gq = gq * cos_ref[rows, :] - pltpu.roll(gq, HD // 2, 1) * sin_ref[rows, :]
        gqkv_ref[rows, at : at + HD] = gq.astype(BF16)
        gkv_ref[:keys, 2 * s * HD : (2 * s + 1) * HD] += dot_tn(gs, q)
        gkv_ref[:keys, (2 * s + 1) * HD : (2 * s + 2) * HD] += dot_tn(probs.astype(BF16), ga)


def attn_back_keys(w_ref, cos_ref, sin_ref, gkv_ref, gqkv_ref, wt_ref):
    step = 3 * HD
    for s in range(SLOTS):
        at = s * step
        gk = gkv_ref[:, 2 * s * HD : (2 * s + 1) * HD] * HD**-0.5
        gk = gk * cos_ref[...] - pltpu.roll(gk, HD // 2, 1) * sin_ref[...]
        gqkv_ref[:, at + HD : at + 2 * HD] = gk.astype(BF16)
        gqkv_ref[:, at + 2 * HD : at + 3 * HD] = gkv_ref[:, (2 * s + 1) * HD : (2 * s + 2) * HD].astype(BF16)
        wt_ref[s * step : (s + 1) * step, :] = w_ref[s].T


def attn_backward_kernel(
    gm_ref, wo_ref, w_ref, normed_ref, qkv_ref, attn_ref, lse_ref, cos_ref, sin_ref,
    segq_ref, segk_ref,
    part_ref, gw_ref, gwo_ref,
    gkv_ref, gqkv_ref, wt_ref,
    *, block,
):
    count = gm_ref.shape[0] // block
    step = 3 * HD
    gkv_ref[...] = jnp.zeros_like(gkv_ref)
    for i in range(count):
        attn_back_block(
            i, block, gm_ref[i * block : (i + 1) * block, :], wo_ref, qkv_ref, attn_ref, lse_ref, cos_ref, sin_ref, segq_ref, segk_ref, gkv_ref, gqkv_ref
        )
    attn_back_keys(w_ref, cos_ref, sin_ref, gkv_ref, gqkv_ref, wt_ref)
    for i in range(count):
        rows = slice(i * block, (i + 1) * block)
        part_ref[rows, :] = dot(gqkv_ref[rows, :], wt_ref[...]).astype(BF16)
    for s in range(SLOTS):
        gw_ref[s] = dot_tn(normed_ref[...], gqkv_ref[:, s * step : (s + 1) * step]).astype(BF16)
    gwo_ref[...] = dot_tn(attn_ref[...], gm_ref[...]).astype(BF16)


def attn_backward(gm, wo, w, normed, qkv, attn, lse, cosine, sine, segq, segk):
    length, width = gm.shape
    return pl.pallas_call(
        functools.partial(attn_backward_kernel, block=256),
        out_shape=(
            jax.ShapeDtypeStruct((length, width), BF16),
            jax.ShapeDtypeStruct((SLOTS, width, 3 * HD), BF16),
            jax.ShapeDtypeStruct((SLOTS * HD, width), BF16),
        ),
        in_specs=[VMEM] * 11,
        out_specs=(VMEM,) * 3,
        scratch_shapes=[
            pltpu.VMEM((length, 2 * SLOTS * HD), F32),
            pltpu.VMEM((length, 3 * SLOTS * HD), BF16),
            pltpu.VMEM((3 * SLOTS * HD, width), BF16),
        ],
        compiler_params=pltpu.CompilerParams(vmem_limit_bytes=56 * 2**20),
        cost_estimate=pl.CostEstimate(
            flops=4 * length * width * 4 * SLOTS * HD + 10 * SLOTS * HD * length * length,
            bytes_accessed=10 * length * width,
            transcendentals=SLOTS * length * length,
        ),
        name="attn_backward",
    )(gm, wo, w, normed, qkv, attn, lse, cosine, sine, segq, segk)


def ffn_weights(eup_ref, tail_ref, edown_ref, sdown_ref, up_ref, upt_ref, down_ref, downt_ref):
    width, half = downt_ref.shape
    pair, shared = edown_ref.shape[0], sdown_ref.shape[0]
    gap = half - pair - TAIL
    between = [jnp.zeros((width, gap), BF16)] if gap else []
    up_ref[...] = jnp.concatenate(
        [eup_ref[:, :pair], *between, tail_ref[:, :TAIL], eup_ref[:, pair:], *between, tail_ref[:, TAIL:]], axis=1
    )
    between = [jnp.zeros((gap, width), BF16)] if gap else []
    down_ref[...] = jnp.concatenate(
        [edown_ref[...], *between, sdown_ref[...], jnp.zeros((TAIL - shared, width), BF16)], axis=0
    )
    upt_ref[...] = up_ref[...].T
    downt_ref[...] = down_ref[...].T


def ffn_rows(x, g, marks, own, up_ref, upt_ref, down_ref, downt_ref, hidden, shared):
    half = down_ref.shape[0]
    pair = 2 * hidden
    pre = dot(x, up_ref[...])
    gate, up = pre[:, :half], pre[:, half:]
    logits = jnp.where(marks.astype(F32) > 0.5, gate[:, half - HD :], NEG)
    weights = jnp.exp(logits - jnp.max(logits, axis=-1, keepdims=True))
    probs = weights / jnp.sum(weights, axis=-1, keepdims=True)
    p0 = jnp.sum(probs * own[0:1, :], axis=-1, keepdims=True)
    p1 = jnp.sum(probs * own[1:2, :], axis=-1, keepdims=True)
    lane = lax.broadcasted_iota(jnp.int32, (1, half), 1)
    in0 = lane < hidden
    in1 = (lane >= hidden) & (lane < pair)
    rest = jnp.where((lane >= half - TAIL) & (lane < half - TAIL + shared), 1.0, 0.0)
    weight = jnp.where(in0, p0, jnp.where(in1, p1, rest))
    sig = jax.nn.sigmoid(gate)
    silu = gate * sig
    act = silu * up
    acts = (act * weight).astype(BF16)
    out = dot(acts, down_ref[...]).astype(BF16)
    grad = dot(g, downt_ref[...])
    both = act * grad
    d0 = jnp.sum(jnp.where(in0, both, 0.0), axis=-1, keepdims=True)
    d1 = jnp.sum(jnp.where(in1, both, 0.0), axis=-1, keepdims=True)
    grad = grad * weight
    grad_gate = grad * up * sig * (1.0 + gate * (1.0 - sig))
    grad_up = grad * silu
    grad_pre = jnp.concatenate([grad_gate, grad_up], axis=-1).astype(BF16)
    gates = (d0 * own[0:1, :] + d1 * own[1:2, :]).astype(BF16)
    gx = jnp.concatenate([dot(grad_pre, upt_ref[...]).astype(BF16), gates], axis=-1)
    return out, gx, grad_pre, acts


def ffn_kernel(
    x_ref, g_ref, mark_ref, own_ref, eup_ref, tail_ref, edown_ref, sdown_ref,
    out_ref, gx_ref, geup_ref, gtail_ref, gedown_ref, gsdown_ref,
    up_ref, upt_ref, down_ref, downt_ref, gup_ref, gdown_ref,
    *, hidden, shared,
):
    step = pl.program_id(0)
    half = down_ref.shape[0]
    pair = 2 * hidden

    @pl.when(step == 0)
    def _():
        gup_ref[...] = jnp.zeros_like(gup_ref)
        gdown_ref[...] = jnp.zeros_like(gdown_ref)
        ffn_weights(eup_ref, tail_ref, edown_ref, sdown_ref, up_ref, upt_ref, down_ref, downt_ref)

    out, gx, grad_pre, acts = ffn_rows(
        x_ref[...], g_ref[...], mark_ref[...], own_ref[...], up_ref, upt_ref, down_ref, downt_ref, hidden, shared
    )
    out_ref[...] = out
    gx_ref[...] = gx
    gup_ref[...] += dot_tn(x_ref[...], grad_pre)
    gdown_ref[...] += dot_tn(acts, g_ref[...])

    @pl.when(step == pl.num_programs(0) - 1)
    def _():
        geup_ref[...] = jnp.concatenate([gup_ref[:, :pair], gup_ref[:, half : half + pair]], axis=1).astype(BF16)
        gtail_ref[...] = jnp.concatenate([gup_ref[:, half - TAIL : half], gup_ref[:, 2 * half - TAIL :]], axis=1)
        gedown_ref[...] = gdown_ref[:pair, :]
        gsdown_ref[...] = gdown_ref[half - TAIL : half - TAIL + shared, :]


def ffn(x, g, marks, own, eup, tail, edown, sdown):
    total, width = x.shape
    pair, shared = edown.shape[0], sdown.shape[0]
    half = up_to(pair + TAIL, HD)
    tile = 512
    row = lambda n: pl.BlockSpec((tile, n), lambda i: (i, 0))
    return pl.pallas_call(
        functools.partial(ffn_kernel, hidden=pair // 2, shared=shared),
        out_shape=(
            jax.ShapeDtypeStruct((total, width), BF16),
            jax.ShapeDtypeStruct((total, width + HD), BF16),
            jax.ShapeDtypeStruct((width, 2 * pair), BF16),
            jax.ShapeDtypeStruct((width, HD), F32),
            jax.ShapeDtypeStruct((pair, width), F32),
            jax.ShapeDtypeStruct((shared, width), F32),
        ),
        grid=(total // tile,),
        in_specs=[row(width), row(width), row(HD)] + [VMEM] * 5,
        out_specs=(row(width), row(width + HD), VMEM, VMEM, VMEM, VMEM),
        scratch_shapes=[
            pltpu.VMEM((width, 2 * half), BF16),
            pltpu.VMEM((2 * half, width), BF16),
            pltpu.VMEM((half, width), BF16),
            pltpu.VMEM((width, half), BF16),
            pltpu.VMEM((width, 2 * half), F32),
            pltpu.VMEM((half, width), F32),
        ],
        compiler_params=pltpu.CompilerParams(vmem_limit_bytes=60 * 2**20),
        cost_estimate=pl.CostEstimate(
            flops=2 * total * width * 9 * half,
            bytes_accessed=8 * total * width,
            transcendentals=total * half,
        ),
        name="ffn",
    )(x, g, marks, own, eup, tail, edown, sdown)


def flip(f, bits):
    for b in (1, 2, 4):
        if bits & b:
            f = f + b - 2 * b * (f // b % 2)
    return f


def place():
    return lax.axis_index("dp"), lax.axis_index("fsdp")


def greet(devices):
    barrier = pltpu.get_barrier_semaphore()
    for device in devices:
        pl.semaphore_signal(barrier, inc=1, device_id=device, device_id_type=MESH)
    pl.semaphore_wait(barrier, len(devices))


def greet_all(nz, nf):
    barrier = pltpu.get_barrier_semaphore()
    z, f = place()
    me, count = z * nf + f, nz * nf

    def hail(i, _):
        d = (me + i) % count
        pl.semaphore_signal(barrier, inc=1, device_id=(d // nf, d % nf), device_id_type=MESH)
        return 0

    lax.fori_loop(1, count, hail, 0)
    pl.semaphore_wait(barrier, count - 1)


def send(src, dst, sems, index, device):
    return pltpu.make_async_remote_copy(
        src, dst, sems[0].at[index], sems[1].at[index], device_id=device, device_id_type=MESH
    )


ORDER = ((2, 4), (4, 2))


def halves(rows):
    return ((0, rows // 2), (rows // 2, rows - rows // 2))


def away(j, nz):
    if nz < 3:
        return j
    if isinstance(j, int):
        return j if j < 2 else nz - 1 if j == 2 else j - 1
    return jnp.where(j < 2, j, jnp.where(j == 2, nz - 1, j - 1))


def spot(ref, piece, f):
    return ref.at[piece, f // 4, f // 2 % 2, f % 2] if len(ref.shape) == 6 else ref.at[piece, f]


class Gather:
    @staticmethod
    def copies(nz):
        return 11 * nz

    def __init__(self, buf, sems, nz, z, f):
        self.buf, self.sems, self.nz, self.z, self.f = buf, sems, nz, z, f

    def slot(self, j, r, h=None):
        piece = lax.rem(self.z - away(j, self.nz) + self.nz, self.nz) if self.nz > 1 else 0
        ref = spot(self.buf, piece, flip(self.f, r))
        return ref if h is None else ref.at[pl.ds(*halves(self.buf.shape[-2])[h])]

    def here(self, j, r, h, index, device):
        ref = self.slot(j, r, h)
        return send(ref, ref, self.sems, index, device)

    def by_z(self, j):
        own = self.slot(0, 0)
        return send(own, own, self.sems, j, (lax.rem(self.z + away(j, self.nz), self.nz), self.f))

    def near(self, j, h):
        return self.here(j, 0, h, self.nz + 2 * j + h, (self.z, flip(self.f, ORDER[h][0])))

    def far(self, j, h, i):
        r = ORDER[h][0] if i else 0
        return self.here(j, r, h, 3 * self.nz + 4 * j + 2 * h + i, (self.z, flip(self.f, ORDER[h][1])))

    def core(self, j, i):
        return self.here(j, 2 * i, None, 7 * self.nz + 4 * j + i, (self.z, flip(self.f, 1)))

    def along_z(self, j):
        if 1 < j <= self.nz:
            self.by_z(j - 1).wait_send()
        if j < self.nz:
            self.by_z(j).start()

    def first(self, j, own=False):
        if not own:
            self.by_z(j).wait_recv()
        for h in range(2):
            self.near(j, h).start()
        self.core(j, 0).start()

    def second(self, j):
        for h in range(2):
            self.near(j, h).wait_recv()
            for i in range(2):
                self.far(j, h, i).start()

    def third(self, j):
        for h in range(2):
            for i in range(2):
                self.far(j, h, i).wait_recv()
        for i in range(1, 4):
            self.core(j, i).start()

    def fourth(self, j):
        for i in range(4):
            self.core(j, i).wait_recv()

    def end(self, first=0):
        for j in range(first, self.nz):
            for h in range(2):
                self.near(j, h).wait_send()
                for i in range(2):
                    self.far(j, h, i).wait_send()
            for i in range(4):
                self.core(j, i).wait_send()


class Reduce:
    @staticmethod
    def copies(nz):
        return 11 * nz

    @staticmethod
    def scratch(nz, rows, width):
        return [
            pltpu.VMEM((nz, 4, rows, width), BF16),
            pltpu.VMEM((nz, 2, rows, width), BF16),
            pltpu.VMEM((nz, rows, width), BF16),
            pltpu.VMEM((nz, rows, width), BF16),
        ]

    def __init__(self, bufs, sems, nz, z, f):
        self.by_core, self.by_near, self.by_far, self.by_z = bufs
        self.sems, self.nz, self.z, self.f = sems, nz, z, f
        self.parts = halves(self.by_core.shape[-2])

    def core(self, j, i, src):
        to = self.by_core.at[j, i]
        return send(to if src is None else src, to, self.sems, 4 * j + i, (self.z, flip(self.f, 1)))

    def near(self, j, h, i):
        last = ORDER[1 - h][1]
        rows = pl.ds(*self.parts[h])
        return send(
            self.by_core.at[j, 3 if i else last // 2, rows], self.by_near.at[j, i, rows], self.sems,
            4 * self.nz + 4 * j + 2 * h + i, (self.z, flip(self.f, last)),
        )

    def far_copy(self, j, h):
        rows = pl.ds(*self.parts[h])
        return send(
            self.by_near.at[j, 1, rows], self.by_far.at[j, rows], self.sems,
            8 * self.nz + 2 * j + h, (self.z, flip(self.f, ORDER[1 - h][0])),
        )

    def z_copy(self, j):
        there = lax.rem(self.z - away(j, self.nz) + self.nz, self.nz)
        return send(self.by_far.at[j], self.by_z.at[j], self.sems, 10 * self.nz + j, (there, self.f))

    def send_near(self, j):
        for h in range(2):
            for i in range(2):
                self.near(j, h, i).start()

    def far(self, j):
        for h in range(2):
            at, size = self.parts[h]
            rows = slice(at, at + size)
            for i, r in enumerate((0, ORDER[1 - h][0])):
                self.near(j, h, i).wait_recv()
                self.by_near[j, i, rows] = self.by_near[j, i, rows] + self.by_core[j, r // 2, rows]
            self.far_copy(j, h).start()

    def along_z(self, j):
        for h in range(2):
            at, size = self.parts[h]
            rows = slice(at, at + size)
            self.far_copy(j, h).wait_recv()
            self.by_far[j, rows] = self.by_far[j, rows] + self.by_near[j, 0, rows]
        if isinstance(j, int):
            if j:
                self.z_copy(j).start()
        else:

            @pl.when(j > 0)
            def _():
                self.z_copy(j).start()

    def total(self):
        result = self.by_far[0].astype(F32)
        for j in range(1, self.nz):
            self.z_copy(j).wait_recv()
            result = result + self.by_z[j].astype(F32)
        return result

    def end(self):
        for j in range(self.nz):
            for h in range(2):
                for i in range(2):
                    self.near(j, h, i).wait_send()
                self.far_copy(j, h).wait_send()
            if j:
                self.z_copy(j).wait_send()


def near_devices(z, f):
    return [(z, flip(f, 1)), (z, flip(f, 2)), (z, flip(f, 4))]


def z_devices(z, f, nz):
    return [(lax.rem(z + zr, nz), f) for zr in range(1, nz)]


def pair_of(count):
    return [pltpu.SemaphoreType.DMA((count,))] * 2


def first_head(member):
    return HEADS * member // 8


def out_blocks(member, dense):
    return first_head(member) * HD // dense, (first_head(member + 1) * HD - 1) // dense


def head_owner(head):
    return (8 * head + 7) // HEADS


def front_kernel(
    tok_ref, wqkv_ref, wout_ref, router_ref, sup_ref, again_ref, fgain_ref, eids_ref, seg_ref, cos_ref, sin_ref, og_ref,
    eup_ref,
    w_out, wo_ref, tail_out, router_out, gain_one_ref, gain_two_ref, mark_out, own_mark_ref, segq_ref, segk_ref,
    normed_out, qkv_out, attn_out, lse_out, mixed_ref, low_ref, plane_ref, all_grad_ref, pieces_ref,
    w_ref, tail_ref, mark_ref, normed_ref, qkv_ref, attn_ref, lse_ref, ids_ref, out_sems,
    seq, wq, wo_in, wz, wzo, all_ids, qpack, tpack, part, wide, pack, *refs, nz, nf, hidden, shared, heads, real,
):
    bufs, refs = refs[:4], refs[4:]
    (
        tok_s, tok_r, all_s, all_r, q_s, q_r, wo_s, wo_r, zq_s, zq_r, zo_s, zo_r, rs, rr, gs, gr, xs, xr, es, er,
        own_sems,
    ) = refs
    z, f = place()
    me, count = z * nf + f, nz * nf
    rows, width = tok_ref.shape
    dense = wqkv_ref.shape[0]
    experts = router_ref.shape[0]
    full = shared * count
    greet_all(nz, nf)

    toks = (tok_s, tok_r)
    to_near = [send(tok_ref, seq.at[f], toks, i, (z, flip(f, r))) for i, r in enumerate((2, 4, 6))]
    to_core = [send(tok_ref, seq.at[f], toks, 3, (z, flip(f, 1)))]
    own = pltpu.make_async_copy(og_ref, all_grad_ref.at[z, f], own_sems.at[0])
    own.start()
    for copy in to_near + to_core:
        copy.start()
    seq[f] = tok_ref[...]
    ids_ref[...] = jnp.concatenate([eids_ref[...], seg_ref[...]], axis=0)
    all_ids[me] = ids_ref[...]
    router = router_ref[...].astype(F32).T.astype(BF16)
    both_gains = jnp.concatenate([again_ref[...].astype(F32).T, fgain_ref[...].astype(F32).T], axis=1).astype(BF16)

    def leave(k, src, dst):
        return pltpu.make_async_copy(src, dst, out_sems.at[k])

    outgoing = [
        leave(k, src, dst)
        for k, (src, dst) in enumerate(
            (
                (w_ref, w_out), (tail_ref, tail_out), (mark_ref, mark_out), (normed_ref, normed_out),
                (qkv_ref, qkv_out), (attn_ref, attn_out), (lse_ref, lse_out),
            )
        )
    ]
    own.wait()
    grads = Gather(all_grad_ref, (gs, gr), nz, z, f)
    grads.first(0, own=True)

    def two(m):
        return first_head(m + 1) - first_head(m) == 2

    def wanted(m, block):
        low, high = out_blocks(m, dense)
        return (low <= block) & (block <= high)

    low, high = out_blocks(f, dense)

    def piece(j):
        return lax.rem(z - away(j, nz) + nz, nz) if j else z

    def along(src, dst, sems, j):
        return send(src, dst.at[z], sems, j, (lax.rem(z + away(j, nz), nz), f))

    zq = [None] + [along(wqkv_ref, wz, (zq_s, zq_r), j) for j in range(1, nz)]
    zo = [None] + [along(wout_ref, wzo, (zo_s, zo_r), j) for j in range(1, nz)]
    for copy in zq[1:] + zo[1:]:
        copy.start()

    pad = jnp.zeros((dense, TAIL - shared - experts), BF16)
    pad_two = jnp.zeros((dense, TAIL - shared - 2), BF16)
    for d in range(count):
        tpack[d] = jnp.concatenate(
            [
                sup_ref[:, d * shared : (d + 1) * shared], router, pad,
                sup_ref[:, full + d * shared : full + (d + 1) * shared], both_gains, pad_two,
            ],
            axis=1,
        )

    def copies(d, k):
        src, dst = ((tpack.at[d], tail_ref.at[me]), (ids_ref, all_ids.at[me]))[k]
        return pltpu.make_async_remote_copy(
            src, dst, all_s.at[k, d], all_r.at[k, me], device_id=(d // nf, d % nf), device_id_type=MESH
        )

    def came(d, k):
        dst = (tail_ref.at[d], all_ids.at[d])[k]
        return pltpu.make_async_remote_copy(
            dst, dst, all_s.at[k, d], all_r.at[k, d], device_id=(d // nf, d % nf), device_id_type=MESH
        )

    def start(i, _):
        d = (me + i) % count
        copies(d, 0).start()
        copies(d, 1).start()
        return 0

    whole = nz * hidden
    for t in range(nz):
        pack[t] = jnp.concatenate(
            [
                eup_ref[e, :, g * whole + t * hidden : g * whole + (t + 1) * hidden]
                for g in range(2)
                for e in range(2)
            ],
            axis=1,
        )
    tail_ref[me] = tpack[me]
    lax.fori_loop(1, count, start, 0)

    def q_copy(j, m, s):
        return pltpu.make_async_remote_copy(
            qpack.at[j, m, s], wq.at[s, piece(j) * nf + f], q_s.at[j, m, s], q_r.at[j, f, s],
            device_id=(z, m), device_id_type=MESH,
        )

    def q_came(j, m, s):
        dst = wq.at[s, piece(j) * nf + m]
        return pltpu.make_async_remote_copy(
            dst, dst, q_s.at[j, m, s], q_r.at[j, m, s], device_id=(z, m), device_id_type=MESH
        )

    def q_own(j, s):
        wq[s, piece(j) * nf + f] = qpack[j, f, s]

    def q_each(act, m):
        act(0)

        @pl.when(two(m))
        def _():
            act(1)

    def q_send(j):
        ref = wz.at[piece(j)] if j else wqkv_ref
        for m in range(8):
            for s in range(SLOTS):
                h = heads[m * SLOTS + s]
                if real[m * SLOTS + s]:
                    qpack[j, m, s] = jnp.concatenate(
                        [ref[:, c * width + h * HD : c * width + (h + 1) * HD] for c in range(3)], axis=1
                    )

        def go(i, _):
            m = (f + i) % nf
            q_each(lambda s: q_copy(j, m, s).start(), m)
            return 0

        lax.fori_loop(1, nf, go, 0)
        q_each(lambda s: q_own(j, s), f)

    grads.second(0)
    for i, r in enumerate((2, 4, 6)):
        to_near[i].wait_recv()
        slot = seq.at[flip(f, r)]
        copy = send(slot, slot, toks, 4 + i, (z, flip(f, 1)))
        copy.start()
        to_core.append(copy)
    q_send(0)
    grads.third(0)
    for copy in zq[1:]:
        copy.wait_send()
    for j in range(1, nz):
        grads.by_z(j).start()
    for j in range(1, nz):
        zq[j].wait_recv()
        q_send(j)

    def arrive(i, _):
        d = (me + i) % count
        came(d, 0).wait_recv()
        came(d, 1).wait_recv()
        return 0

    lax.fori_loop(1, count, arrive, 0)

    def q_arrive(i, _):
        m = (f + i) % nf
        for j in range(nz):
            q_each(lambda s: q_came(j, m, s).wait_recv(), f)
        return 0

    lax.fori_loop(1, nf, q_arrive, 0)
    for copy in to_core:
        copy.wait_recv()

    w_ref[0] = wq[0].reshape(width, 3 * HD)
    w_ref[1] = jnp.where(two(f), wq[1].astype(F32), 0.0).reshape(width, 3 * HD).astype(BF16)
    outgoing[0].start()
    outgoing[1].start()
    tails = tail_ref[...].reshape(width, 2 * TAIL)
    gains = tails[:, TAIL + shared : TAIL + shared + 2].astype(F32).T
    gain_one_ref[...] = gains[0:1]
    gain_two_ref[...] = gains[1:2]
    router_out[...] = jnp.concatenate(
        [
            jnp.zeros((width, TAIL + shared), BF16), tails[:, shared : shared + experts],
            jnp.zeros((width, TAIL - shared - experts), BF16),
        ],
        axis=1,
    )
    for m in range(8):
        ids = all_ids[z * nf + m]
        segk_ref[:, m * rows : (m + 1) * rows] = jnp.broadcast_to(ids[-1:], (8, rows))
        segq_ref[m * rows : (m + 1) * rows, :] = jnp.broadcast_to(ids.T[:, -1:], (rows, HD))
    block = 256
    gain_one = gain_one_ref[...]

    def project(i, _):
        x = seq[pl.ds(i * (block // rows), block // rows)].reshape(block, width)
        attn_project(i, block, x, gain_one, w_ref, cos_ref, sin_ref, normed_ref, qkv_ref)
        return 0

    lax.fori_loop(0, 8 * rows // block, project, 0)
    outgoing[3].start()
    outgoing[4].start()
    def out_block(j):
        return piece(j) * nf + f

    def out_src(j):
        return wzo.at[piece(j)] if j else wout_ref

    def out_copy(j, m):
        first, _ = out_blocks(m, dense)
        slot = out_block(j) - first
        return pltpu.make_async_remote_copy(
            out_src(j), wo_in.at[slot], wo_s.at[j, m], wo_r.at[slot], device_id=(z, m), device_id_type=MESH
        )

    def out_own(j):
        wo_in[out_block(j) - low] = wzo[piece(j)] if j else wout_ref[...]

    def out_each(act, act_own):
        for j in range(nz):

            def one(i, _):
                m = (f + i) % nf

                @pl.when(wanted(m, out_block(j)))
                def _():
                    act(j, m)

                return 0

            lax.fori_loop(1, nf, one, 0)

            @pl.when(wanted(f, out_block(j)))
            def _():
                act_own(j)

    for j in range(1, nz):
        zo[j].wait()
    out_each(lambda j, m: out_copy(j, m).start(), out_own)

    reduce = Reduce(bufs, (rs, rr), 1, z, f)
    for i in range(8 * rows // block):
        attn_block(i, block, segq_ref, segk_ref, qkv_ref, attn_ref, lse_ref)

    outgoing[5].start()
    outgoing[6].start()

    def arrive_out(j, _):
        @pl.when((low + j <= high) & (lax.rem(low + j, nf) != f))
        def _():
            pltpu.make_async_remote_copy(
                wo_in.at[j], wo_in.at[j], wo_s.at[0, j], wo_r.at[j], device_id=(z, flip(f, 1)), device_id_type=MESH
            ).wait_recv()

        return 0

    lax.fori_loop(0, wo_in.shape[0], arrive_out, 0)
    wide[...] = wo_in[...].astype(F32).reshape(wide.shape)
    offset = pl.multiple_of(first_head(f) * HD - low * dense, 8)
    wo_ref[:HD, :] = wide[pl.ds(offset, HD), :].astype(BF16)
    wo_ref[HD:, :] = jnp.where(two(f), wide[pl.ds(offset + HD, HD), :], 0.0).astype(BF16)
    for i in range(8 * rows // block):
        at = i * (block // rows)
        part[at : at + block // rows] = (
            dot(attn_ref[i * block : (i + 1) * block, :], wo_ref[...]).astype(BF16).reshape(block // rows, rows, width)
        )
    for i in range(4):
        reduce.core(0, i, part.at[flip(f, 1 | 2 * i)]).start()
    ups = []
    for j in range(1, nz):
        there = lax.rem(z + j, nz)
        copy = send(pack.at[there], pieces_ref.at[z], (es, er), j, (there, f))
        copy.start()
        ups.append(copy)
    ups.append(pltpu.make_async_copy(pack.at[z], pieces_ref.at[z], own_sems.at[2]))
    ups[-1].start()
    for i in range(4):
        reduce.core(0, i, None).wait_recv()
        reduce.by_core[0, i] = reduce.by_core[0, i] + part[flip(f, 2 * i)]
    reduce.send_near(0)
    reduce.far(0)
    reduce.along_z(0)
    mixed = tok_ref[...].astype(F32) + reduce.by_far[0].astype(F32)
    mixed_ref[...] = mixed
    low_ref[...] = (mixed * rms_scale(mixed) * gain_two_ref[...]).astype(BF16)
    near_own = pltpu.make_async_copy(low_ref, plane_ref.at[0, f], own_sems.at[1])
    near_own.start()
    near = Gather(plane_ref, (xs, xr), 1, z, f)
    near_own.wait()
    near.first(0, own=True)
    for j in range(1, nz):
        grads.first(j)
    near.second(0)
    for j in range(1, nz):
        grads.second(j)
    lane = lax.broadcasted_iota(jnp.int32, (rows, HD), 1) - TAIL - shared

    def mark(d, _):
        ids = all_ids[d].T
        found = ids[:, 0:1] == lane
        for k in range(1, ids.shape[1] - 1):
            found = found | (ids[:, k : k + 1] == lane)
        value = jnp.where(found, 1.0, 0.0)
        mark_ref[d] = value.astype(BF16)

        @pl.when(d == me)
        def _():
            own_mark_ref[...] = value

        return 0

    lax.fori_loop(0, count, mark, 0)
    outgoing[2].start()
    near.third(0)
    for j in range(1, nz):
        grads.third(j)
    for j in range(nz):
        grads.fourth(j)
    near.fourth(0)

    def left(i, _):
        d = (me + i) % count
        copies(d, 0).wait_send()
        copies(d, 1).wait_send()
        return 0

    lax.fori_loop(1, count, left, 0)

    def q_left(i, _):
        m = (f + i) % nf
        for j in range(nz):
            q_each(lambda s: q_copy(j, m, s).wait_send(), m)
        return 0

    lax.fori_loop(1, nf, q_left, 0)
    out_each(lambda j, m: out_copy(j, m).wait_send(), lambda j: None)
    for copy in to_near + to_core:
        copy.wait_send()
    for i in range(4):
        reduce.core(0, i, part.at[0]).wait_send()
    reduce.end()
    for j in range(1, nz):
        grads.by_z(j).wait_send()
    grads.end()
    near.end()
    for copy in ups + outgoing:
        copy.wait()


def front(tok, wqkv, wout, router, sup, again, fgain, eids, seg, cosine, sine, og, eup, nz, nf, shared):
    rows, width = tok.shape
    dense, count = wqkv.shape[0], nz * nf
    length = 8 * rows
    hidden, up_rows = eup.shape[2] // (2 * nz), eup.shape[1]
    heads, real = head_table(8)
    shape = jax.ShapeDtypeStruct
    return pl.pallas_call(
        functools.partial(front_kernel, nz=nz, nf=nf, hidden=hidden, shared=shared, heads=heads, real=real),
        out_shape=(
            shape((SLOTS, width, 3 * HD), BF16),
            shape((SLOTS * HD, width), BF16),
            shape((count, dense, 2 * TAIL), BF16),
            shape((width, HD), BF16),
            shape((1, width), F32),
            shape((1, width), F32),
            shape((count, rows, HD), BF16),
            shape((rows, HD), F32),
            shape((length, HD), jnp.int32),
            shape((8, length), jnp.int32),
            shape((length, width), BF16),
            shape((length, 3 * SLOTS * HD), BF16),
            shape((length, SLOTS * HD), BF16),
            shape((length, SLOTS * HD), F32),
            shape((rows, width), F32),
            shape((rows, width), BF16),
            shape((1, 8, rows, width), BF16),
            shape((nz, 8, rows, width), BF16),
            shape((nz, up_rows, 4 * hidden), BF16),
        ),
        in_specs=[VMEM] * 13,
        out_specs=(ANY, VMEM, ANY, VMEM, VMEM, VMEM, ANY, VMEM, VMEM, VMEM) + (ANY,) * 4 + (VMEM,) * 2 + (ANY,) * 3,
        scratch_shapes=[
            pltpu.VMEM((SLOTS, width, 3 * HD), BF16),
            pltpu.VMEM((count, dense, 2 * TAIL), BF16),
            pltpu.VMEM((count, rows, HD), BF16),
            pltpu.VMEM((length, width), BF16),
            pltpu.VMEM((length, 3 * SLOTS * HD), BF16),
            pltpu.VMEM((length, SLOTS * HD), BF16),
            pltpu.VMEM((length, SLOTS * HD), F32),
            pltpu.VMEM((eids.shape[0] + 1, rows), jnp.int32),
            pltpu.SemaphoreType.DMA((7,)),
            pltpu.VMEM((8, rows, width), BF16),
            pltpu.VMEM((SLOTS, count, dense, 3 * HD), BF16),
            pltpu.VMEM((8, dense, width), BF16),
            pltpu.VMEM((nz, dense, 3 * width), BF16),
            pltpu.VMEM((nz, dense, width), BF16),
            pltpu.VMEM((count, eids.shape[0] + 1, rows), jnp.int32),
            pltpu.VMEM((nz, 8, SLOTS, dense, 3 * HD), BF16),
            pltpu.VMEM((count, dense, 2 * TAIL), BF16),
            pltpu.VMEM((8, rows, width), BF16),
            pltpu.VMEM((8 * dense, width), F32),
            pltpu.VMEM((nz, up_rows, 4 * hidden), BF16),
            *Reduce.scratch(1, rows, width),
            *pair_of(7),
            pltpu.SemaphoreType.DMA((2, count)),
            pltpu.SemaphoreType.DMA((2, count)),
            pltpu.SemaphoreType.DMA((nz, 8, SLOTS)),
            pltpu.SemaphoreType.DMA((nz, 8, SLOTS)),
            pltpu.SemaphoreType.DMA((nz, 8)),
            pltpu.SemaphoreType.DMA((8,)),
            *pair_of(nz),
            *pair_of(nz),
            *pair_of(Reduce.copies(1)),
            *pair_of(Gather.copies(nz)),
            *pair_of(Gather.copies(1)),
            *pair_of(nz),
            pltpu.SemaphoreType.DMA((3,)),
        ],
        compiler_params=pltpu.CompilerParams(
            collective_id=1, has_side_effects=True, vmem_limit_bytes=58 * 2**20
        ),
        name="front",
    )(tok, wqkv, wout, router, sup, again, fgain, eids, seg, cosine, sine, og, eup)


def route_grads(gx, og, mixed, normed, router, marks, gain):
    width = mixed.shape[1]
    scale = rms_scale(mixed)
    normal = mixed * scale
    logits = jnp.where(marks > 0.5, dot(normed, router), NEG)
    weights = jnp.exp(logits - jnp.max(logits, axis=-1, keepdims=True))
    probs = weights / jnp.sum(weights, axis=-1, keepdims=True)
    grad_gates = gx[:, width:]
    grad_logits = (probs * (grad_gates - jnp.sum(probs * grad_gates, axis=-1, keepdims=True))).astype(BF16)
    grad_router = dot_tn(normed, grad_logits)
    grad_normed = gx[:, :width] + dot_nt(grad_logits, router)
    ones = jnp.where(lax.broadcasted_iota(jnp.int32, (mixed.shape[0], HD), 1) == TAIL - 1, 1.0, 0.0)
    grad_gain = lax.dot_general(
        grad_normed * normal, ones, (((0,), (0,)), ((), ())),
        precision=lax.Precision.HIGHEST, preferred_element_type=F32,
    )
    grad_mixed = og.astype(F32) + norm_back(grad_normed, normal, scale, gain)
    return grad_mixed, pltpu.roll(grad_router + grad_gain, TAIL, 1)


def experts_kernel(
    normed_ref, plane_ref, all_grad_ref, mark_ref, own_ref, eup_ref, tail_ref, edown_ref, sdown_ref,
    og_ref, mixed_ref, router_ref, own_mark_ref, gain_ref,
    out_any, low_ref, gm_ref, small_ref, geup_ref, gedown_ref, gsdown_ref, all_normed_ref,
    out_ref,
    up_ref, upt_ref, down_ref, downt_ref, gup_ref, gdown_ref,
    xt, gt, px, po, *refs, nz, hidden, shared,
):
    bufs, (tile_sems, rs, rr, os_, or_, xs, xr, own_sems) = refs[:4], refs[4:]
    z, f = place()
    rows, width = mixed_ref.shape
    half = down_ref.shape[0]
    pair = 2 * hidden
    greet(near_devices(z, f) + z_devices(z, f, nz))
    own = pltpu.make_async_copy(normed_ref, spot(all_normed_ref, z, f), own_sems.at[0])
    own.start()
    gather = Gather(all_normed_ref, (xs, xr), nz, z, f)
    reduce = Reduce(bufs, (rs, rr), nz, z, f)
    outs = Reduce([out_ref, out_ref, out_ref, out_ref], (os_, or_), nz, z, f)
    own.wait()
    gather.along_z(1)
    ffn_weights(eup_ref, tail_ref, edown_ref, sdown_ref, up_ref, upt_ref, down_ref, downt_ref)
    gup_ref[...] = jnp.zeros_like(gup_ref)
    gdown_ref[...] = jnp.zeros_like(gdown_ref)
    gather.along_z(2)
    if nz > 1:
        gather.first(1)

    def where(i):
        j, t = i // 4, i % 4
        base = f + (1 - 2 * (f % 2)) * (1 - t // 2) + (4 - 8 * (f // 4 % 2)) * (t % 2)
        return lax.rem(z - away(j, nz) + nz, nz), base // 4, base % 2

    def loads(i, rows_ref=all_normed_ref):
        piece, y, core = where(i)
        there = piece if rows_ref is all_normed_ref else 0
        slot = i % 2
        return [
            pltpu.make_async_copy(rows_ref.at[there, y, :, core], xt.at[slot], tile_sems.at[slot, 0]),
            pltpu.make_async_copy(all_grad_ref.at[piece, y, :, core], gt.at[slot], tile_sems.at[slot, 1]),
        ]

    for copy in loads(0, plane_ref):
        copy.start()
    last = 4 * nz - 1

    def tile(i, _):
        j, t = i // 4, i % 4
        more = j < nz - 1

        @pl.when((t == 0) & more)
        def _():
            gather.second(j + 1)

        @pl.when(i == 1)
        def _():
            gather.along_z(3)

        @pl.when((t == 2) & more)
        def _():
            gather.third(j + 1)

        @pl.when((t == 2) & (j < nz - 2))
        def _():
            gather.first(j + 2)

        @pl.when((t == 3) & more)
        def _():
            gather.fourth(j + 1)

        @pl.when((t == 0) & (j > 0))
        def _():
            for k in range(4):
                reduce.core(j - 1, k, px.at[k]).wait_send()
                outs.core(j - 1, k, po.at[k]).wait_send()

        for copy in loads(i):
            copy.wait()

        @pl.when(i < 3)
        def _():
            for copy in loads(i + 1, plane_ref):
                copy.start()

        @pl.when((i >= 3) & (i < last))
        def _():
            for copy in loads(i + 1):
                copy.start()

        piece, y, core = where(i)
        marks = jnp.concatenate([mark_ref[piece, 4 * y + core], mark_ref[piece, 4 * y + 2 + core]], axis=0)
        x, g = xt[i % 2].reshape(2 * rows, width), gt[i % 2].reshape(2 * rows, width)
        out, gx, grad_pre, acts = ffn_rows(
            x, g, marks, own_ref[...], up_ref, upt_ref, down_ref, downt_ref, hidden, shared
        )
        x_at = f // 2 % 2
        for b in range(2):
            at = 2 * t + (1 - x_at if b else x_at)
            po[at] = out[b * rows : (b + 1) * rows]
            px[at] = gx[b * rows : (b + 1) * rows]
        gup_ref[...] += dot_tn(x, grad_pre)
        gdown_ref[...] += dot_tn(acts, g)

        @pl.when(t == 1)
        def _():
            for k in range(4):
                reduce.core(j, k, px.at[k]).start()
            for k in range(4):
                outs.core(j, k, po.at[k]).start()

        @pl.when((t == 1) & (j > 0))
        def _():
            reduce.far(j - 1)

        @pl.when((t == 2) & (j > 0))
        def _():
            reduce.along_z(j - 1)

        @pl.when(t == 3)
        def _():
            for k in range(4):
                reduce.core(j, k, None).wait_recv()
                reduce.by_core[j, k] = reduce.by_core[j, k] + px[4 + k]
            reduce.send_near(j)
            for k in range(4):
                outs.core(j, k, None).wait_recv()
                out_ref[j, k] = out_ref[j, k] + po[4 + k]

        return 0

    lax.fori_loop(0, 4 * nz, tile, 0)
    up_ref[:, : 2 * pair] = jnp.concatenate([gup_ref[:, :pair], gup_ref[:, half : half + pair]], axis=1).astype(BF16)
    up_rows = width // nz
    ends = [
        pltpu.make_async_copy(up_ref.at[pl.ds(p * up_rows, up_rows), pl.ds(0, 2 * pair)], geup_ref.at[p], own_sems.at[p])
        for p in range(nz)
    ]
    ends.append(pltpu.make_async_copy(gdown_ref.at[pl.ds(0, pair)], gedown_ref, own_sems.at[nz]))
    ends.append(pltpu.make_async_copy(out_ref, out_any, own_sems.at[nz + 1]))
    for copy in ends:
        copy.start()
    reduce.far(nz - 1)
    gtail = jnp.concatenate([gup_ref[:, half - TAIL : half], gup_ref[:, 2 * half - TAIL :]], axis=1)
    gsdown_ref[...] = gdown_ref[half - TAIL : half - TAIL + shared, :]
    reduce.along_z(nz - 1)
    grad_mixed, small = route_grads(
        reduce.total(), og_ref[...], mixed_ref[...], normed_ref[...], router_ref[...], own_mark_ref[...], gain_ref[...]
    )
    gm_ref[...] = grad_mixed
    low_ref[...] = grad_mixed.astype(BF16)
    small_ref[...] = (small + gtail).astype(BF16)
    for k in range(4):
        reduce.core(nz - 1, k, px.at[k]).wait_send()
        outs.core(nz - 1, k, po.at[k]).wait_send()
    for copy in ends:
        copy.wait()
    for j in range(4, nz + 1):
        gather.along_z(j)
    gather.end(1)
    reduce.end()


def experts_turn(
    normed, plane, all_grad, marks, own, eup, tail, edown, sdown, og, mixed, router, own_marks, gain, nz, nf
):
    rows, width = mixed.shape
    pair, shared = edown.shape[0], sdown.shape[0]
    half = up_to(pair + TAIL, HD)
    wide = width + HD
    return pl.pallas_call(
        functools.partial(experts_kernel, nz=nz, hidden=pair // 2, shared=shared),
        out_shape=(
            jax.ShapeDtypeStruct((nz, 4, rows, width), BF16),
            jax.ShapeDtypeStruct((rows, width), BF16),
            jax.ShapeDtypeStruct((rows, width), F32),
            jax.ShapeDtypeStruct((width, HD), BF16),
            jax.ShapeDtypeStruct((nz, width // nz, 2 * pair), BF16),
            jax.ShapeDtypeStruct((pair, width), F32),
            jax.ShapeDtypeStruct((shared, width), F32),
            jax.ShapeDtypeStruct((nz, 2, 2, 2, rows, width), BF16),
        ),
        in_specs=[VMEM, ANY, ANY, VMEM] + [VMEM] * 10,
        out_specs=(ANY, VMEM, VMEM, VMEM, ANY, ANY, VMEM, ANY),
        scratch_shapes=[
            pltpu.VMEM((nz, 4, rows, width), BF16),
            pltpu.VMEM((width, 2 * half), BF16),
            pltpu.VMEM((2 * half, width), BF16),
            pltpu.VMEM((half, width), BF16),
            pltpu.VMEM((width, half), BF16),
            pltpu.VMEM((width, 2 * half), F32),
            pltpu.VMEM((half, width), F32),
            pltpu.VMEM((2, 2, rows, width), BF16),
            pltpu.VMEM((2, 2, rows, width), BF16),
            pltpu.VMEM((8, rows, wide), BF16),
            pltpu.VMEM((8, rows, width), BF16),
            *Reduce.scratch(nz, rows, wide),
            pltpu.SemaphoreType.DMA((2, 2)),
            *pair_of(Reduce.copies(nz)),
            *pair_of(Reduce.copies(nz)),
            *pair_of(Gather.copies(nz)),
            pltpu.SemaphoreType.DMA((nz + 2,)),
        ],
        compiler_params=pltpu.CompilerParams(
            collective_id=3, has_side_effects=True, vmem_limit_bytes=60 * 2**20
        ),
        name="experts_turn",
    )(
        normed, plane.reshape(1, 2, 2, 2, rows, width), all_grad.reshape(nz, 2, 2, 2, rows, width),
        marks.reshape(nz, 8, rows, HD), own, eup, tail, edown, sdown, og, mixed, router, own_marks, gain
    )[:7]


def back_kernel(
    low_ref, geup_ref, *refs, nz, nf, heads, real,
):
    sources, refs = refs[:11], refs[11:]
    (wo_ref, w_ref, normed_ref, qkv_ref, attn_ref, lse_ref, cos_ref, sin_ref, segq_ref, segk_ref, out_ref), refs = (
        refs[-12:-1],
        refs[:-12] + refs[-1:],
    )
    back_body(sources, low_ref, geup_ref, wo_ref, w_ref, normed_ref, qkv_ref, attn_ref, lse_ref, cos_ref, sin_ref,
              segq_ref, segk_ref, out_ref, *refs, nz=nz, nf=nf, heads=heads, real=real)


def back_body(
    sources, low_ref, geup_ref, wo_ref, w_ref, normed_ref, qkv_ref, attn_ref, lse_ref, cos_ref, sin_ref, segq_ref, segk_ref,
    out_ref, small_ref, tok_ref, mixed_ref, own_gm_ref, gain_ref,
    block_ref, gtok_ref, gwqkv_ref, gwout_ref, all_small_ref, pieces_ref,
    seq, gkv_ref, gqkv_ref, wt_ref, part_ref, gw_ref, gwo_ref, gq, gob, gpk, gz, smalls, *refs, nz, nf, heads, real,
):
    bufs, refs = refs[:7], refs[7:]
    rs, rr, os_, or_, all_s, all_r, q_s, q_r, wo_s, wo_r, zs, zr, gs, gr, es, er, own_sems, in_sems = refs
    local = (wo_ref, w_ref, normed_ref, qkv_ref, attn_ref, lse_ref, cos_ref, sin_ref, segq_ref, segk_ref, out_ref)
    loads = [pltpu.make_async_copy(src, dst, in_sems.at[k]) for k, (src, dst) in enumerate(zip(sources, local))]
    for copy in loads:
        copy.start()
    z, f = place()
    me, count = z * nf + f, nz * nf
    dense = gw_ref.shape[2]
    rows, width = tok_ref.shape
    length = 8 * rows
    greet_all(nz, nf)
    seq[0, f] = low_ref[...]
    turned = Gather(seq, (gs, gr), 1, z, f)
    turned.first(0, own=True)
    ups = []
    for j in range(1, nz):
        there = lax.rem(z + j, nz)
        ups.append(send(geup_ref.at[there], pieces_ref.at[z], (es, er), j, (there, f)))
    ups.append(pltpu.make_async_copy(geup_ref.at[z], pieces_ref.at[z], own_sems.at[0]))
    for copy in ups:
        copy.start()
    turned.second(0)
    outs = Reduce([out_ref, *bufs[4:]], (os_, or_), nz, z, f)
    order = list(range(1, nz)) + [0]
    loads[10].wait()
    outs.send_near(order[0])
    turned.third(0)

    def two(m):
        return first_head(m + 1) - first_head(m) == 2

    def small_copy(d):
        return pltpu.make_async_remote_copy(
            small_ref.at[d], smalls.at[me], all_s.at[d], all_r.at[me], device_id=(d // nf, d % nf), device_id_type=MESH
        )

    def small_came(d):
        return pltpu.make_async_remote_copy(
            smalls.at[d], smalls.at[d], all_s.at[d], all_r.at[d], device_id=(d // nf, d % nf), device_id_type=MESH
        )

    def q_copy(p, m, s):
        return pltpu.make_async_remote_copy(
            gw_ref.at[s, p * nf + m], gq.at[p, f, s], q_s.at[p, m, s], q_r.at[p, f, s],
            device_id=(z, m), device_id_type=MESH,
        )

    def q_came(p, m, s):
        dst = gq.at[p, m, s]
        return pltpu.make_async_remote_copy(
            dst, dst, q_s.at[p, m, s], q_r.at[p, m, s], device_id=(z, m), device_id_type=MESH
        )

    def owner_of(block):
        return head_owner(block * dense // HD)

    low, high = out_blocks(f, dense)

    def out_copy(i):
        d = low + i
        k = 2 * (d // nf) + f - owner_of(d)
        return pltpu.make_async_remote_copy(
            gwo_ref.at[i], gob.at[k], wo_s.at[i], wo_r.at[k], device_id=(z, d % nf), device_id_type=MESH
        )

    for copy in loads[:10]:
        copy.wait()
    turned.fourth(0)
    spare = gwo_ref.shape[0] * dense
    wide = up_to(spare, HD)
    shift = first_head(f) * HD - low * dense
    moved = jnp.concatenate([attn_ref[...].astype(F32), jnp.zeros((length, wide - SLOTS * HD), F32)], axis=1)
    moved = pltpu.roll(moved, shift, 1).astype(BF16)
    gwo_ref[...] = dot_tn(moved, seq[0].reshape(length, width))[:spare].reshape(gwo_ref.shape).astype(BF16)

    def start_small(i, _):
        small_copy((me + i) % count).start()
        return 0

    lax.fori_loop(1, count, start_small, 0)
    smalls[me] = small_ref[me]

    def start_out(i, _):
        d = low + i

        @pl.when((d <= high) & (d % nf != f))
        def _():
            out_copy(i).start()

        @pl.when((d <= high) & (d % nf == f))
        def _():
            gob[2 * (d // nf) + f - owner_of(d)] = gwo_ref[i]

        return 0

    lax.fori_loop(0, gwo_ref.shape[0], start_out, 0)
    gkv_ref[...] = jnp.zeros_like(gkv_ref)
    block = 256
    for i in range(length // block):
        attn_back_block(
            i, block, seq[0, i * block // rows : (i + 1) * block // rows].reshape(block, width), wo_ref, qkv_ref, attn_ref, lse_ref, cos_ref, sin_ref, segq_ref, segk_ref, gkv_ref, gqkv_ref
        )
        if i + 1 < nz:
            outs.send_near(order[i + 1])
        if i < nz:
            outs.far(order[i])
        if 0 < i <= nz:
            outs.along_z(order[i - 1])
    attn_back_keys(w_ref, cos_ref, sin_ref, gkv_ref, gqkv_ref, wt_ref)
    step = 3 * HD
    reduce = Reduce(bufs[:4], (rs, rr), 1, z, f)
    for i in range(length // block):
        mine = slice(i * block, (i + 1) * block)
        at = i * block // rows
        part_ref[at : at + block // rows] = (
            dot(gqkv_ref[mine, :], wt_ref[...]).astype(BF16).reshape(block // rows, rows, width)
        )
    for i in range(4):
        reduce.core(0, i, part_ref.at[flip(f, 1 | 2 * i)]).start()

    def weights(s):
        value = dot_tn(normed_ref[...], gqkv_ref[:, s * step : (s + 1) * step])
        gw_ref[s] = value.reshape(count, dense, step).astype(BF16)

        def start(i, _):
            for p in range(nz):
                q_copy(p, (f + i) % nf, s).start()
            return 0

        lax.fori_loop(1, nf, start, 0)
        for p in range(nz):
            gq[p, f, s] = gw_ref[s, p * nf + f]

    weights(0)
    for i in range(4):
        reduce.core(0, i, None).wait_recv()
        reduce.by_core[0, i] = reduce.by_core[0, i] + part_ref[flip(f, 2 * i)]
    reduce.send_near(0)

    @pl.when(two(f))
    def _():
        weights(1)

    reduce.far(0)

    def q_arrive(i, _):
        m = (f + i) % nf
        for p in range(nz):
            q_came(p, m, 0).wait_recv()

        @pl.when(two(m))
        def _():
            for p in range(nz):
                q_came(p, m, 1).wait_recv()

        return 0

    lax.fori_loop(1, nf, q_arrive, 0)

    def arrive_out(k, _):
        d = (k // 2) * nf + f
        source = owner_of(d) + k % 2
        last = head_owner((d * dense + dense - 1) // HD)

        @pl.when((source <= last) & (source != f))
        def _():
            pltpu.make_async_remote_copy(
                gob.at[k], gob.at[k], wo_s.at[0], wo_r.at[k], device_id=(z, flip(f, 1)), device_id_type=MESH
            ).wait_recv()

        return 0

    lax.fori_loop(0, 2 * nz, arrive_out, 0)
    for p in range(nz):
        for m in range(8):
            for s in range(SLOTS):
                if real[m * SLOTS + s]:
                    at = heads[m * SLOTS + s] * HD
                    for c in range(3):
                        gpk[p, :, c * width + at : c * width + at + HD] = gq[p, m, s, :, c * HD : (c + 1) * HD]
        d = p * nf + f
        gpk[p, :, 3 * width :] = gob[2 * p]

        @pl.when(head_owner((d * dense + dense - 1) // HD) != owner_of(d))
        def _():
            gpk[p, :, 3 * width :] = gob[2 * p] + gob[2 * p + 1]

    alongs = []
    for j in range(1, nz):
        there = lax.rem(z + j, nz)
        copy = send(gpk.at[there], gz.at[z], (zs, zr), j, (there, f))
        copy.start()
        alongs.append(copy)
    gz[z] = gpk[z]
    for k in range(length // block, nz):
        outs.far(order[k])
    for k in range(length // block - 1, nz):
        outs.along_z(order[k])
    reduce.along_z(0)
    x = tok_ref[...].astype(F32)
    scale = rms_scale(x)
    gtok_ref[...] = (
        own_gm_ref[...] + norm_back(reduce.by_far[0].astype(F32), x * scale, scale, gain_ref[...])
    ).astype(BF16)
    block_ref[...] = (mixed_ref[...] + outs.total()).astype(BF16)

    def finish(i, _):
        d = (me + i) % count
        small_came(d).wait_recv()
        small_copy(d).wait_send()
        return 0

    lax.fori_loop(1, count, finish, 0)

    def q_left(i, _):
        m = (f + i) % nf
        for p in range(nz):
            q_copy(p, m, 0).wait_send()

        @pl.when(two(f))
        def _():
            for p in range(nz):
                q_copy(p, m, 1).wait_send()

        return 0

    lax.fori_loop(1, nf, q_left, 0)

    def out_left(i, _):
        @pl.when((low + i <= high) & ((low + i) % nf != f))
        def _():
            out_copy(i).wait_send()

        return 0

    lax.fori_loop(0, gwo_ref.shape[0], out_left, 0)
    for copy in alongs:
        copy.wait()
    gwqkv_ref[...] = sum(gz[p, :, : 3 * width].astype(F32) for p in range(nz))
    gwout_ref[...] = sum(gz[p, :, 3 * width :].astype(F32) for p in range(nz))
    all_small_ref[...] = smalls[...]
    for i in range(4):
        reduce.core(0, i, part_ref.at[0]).wait_send()
    reduce.end()
    outs.end()
    turned.end()
    for copy in ups:
        copy.wait()


def back(
    low, geup, wo, w, normed, qkv, attn, lse, cosine, sine, segq, segk, out_part, small, tok, mixed, own_gm, gain, nz, nf
):
    rows, width = tok.shape
    length, count = 8 * rows, nz * nf
    dense = width // count
    heads, real = head_table(8)
    return pl.pallas_call(
        functools.partial(back_kernel, nz=nz, nf=nf, heads=heads, real=real),
        out_shape=(
            jax.ShapeDtypeStruct((rows, width), BF16),
            jax.ShapeDtypeStruct((rows, width), BF16),
            jax.ShapeDtypeStruct((dense, 3 * width), F32),
            jax.ShapeDtypeStruct((dense, width), F32),
            jax.ShapeDtypeStruct((count, dense, HD), BF16),
            jax.ShapeDtypeStruct(geup.shape, BF16),
        ),
        in_specs=[VMEM] + [ANY] * 12 + [VMEM] * 5,
        out_specs=(VMEM,) * 5 + (ANY,),
        scratch_shapes=[
            pltpu.VMEM((1, 8, rows, width), BF16),
            pltpu.VMEM((length, 2 * SLOTS * HD), F32),
            pltpu.VMEM((length, 3 * SLOTS * HD), BF16),
            pltpu.VMEM((3 * SLOTS * HD, width), BF16),
            pltpu.VMEM((8, rows, width), BF16),
            pltpu.VMEM((SLOTS, count, dense, 3 * HD), BF16),
            pltpu.VMEM((8, dense, width), BF16),
            pltpu.VMEM((nz, 8, SLOTS, dense, 3 * HD), BF16),
            pltpu.VMEM((2 * nz, dense, width), BF16),
            pltpu.VMEM((nz, dense, 4 * width), BF16),
            pltpu.VMEM((nz, dense, 4 * width), BF16),
            pltpu.VMEM((count, dense, HD), BF16),
            *Reduce.scratch(1, rows, width),
            *Reduce.scratch(nz, rows, width)[1:],
            *pair_of(Reduce.copies(1)),
            *pair_of(Reduce.copies(nz)),
            *pair_of(count),
            pltpu.SemaphoreType.DMA((nz, 8, SLOTS)),
            pltpu.SemaphoreType.DMA((nz, 8, SLOTS)),
            pltpu.SemaphoreType.DMA((8,)),
            pltpu.SemaphoreType.DMA((2 * nz,)),
            *pair_of(nz),
            *pair_of(Gather.copies(1)),
            *pair_of(nz),
            pltpu.SemaphoreType.DMA((1,)),
            *[pltpu.VMEM(a.shape, a.dtype) for a in (wo, w, normed, qkv, attn, lse, cosine, sine, segq, segk, out_part)],
            pltpu.SemaphoreType.DMA((11,)),
        ],
        compiler_params=pltpu.CompilerParams(
            collective_id=4, has_side_effects=True, vmem_limit_bytes=60 * 2**20
        ),
        name="back",
    )(
        low, geup, wo, w, normed, qkv, attn, lse, cosine, sine, segq, segk, out_part,
        small.reshape(count, dense, HD), tok, mixed, own_gm, gain,
    )


def unpack_kernel(
    pieces_ref, small_ref, wqkv_ref, gwqkv_ref, gain_ref, block_in, tok_in, wout_in, edown_in, sdown_in,
    geup_ref, gsup_ref, grouter_ref, gone_ref, gtwo_ref, block_ref, tok_ref, gqkv_ref, wout_ref, edown_ref, sdown_ref,
    *, shared, experts,
):
    for src, dst in (
        (block_in, block_ref), (tok_in, tok_ref), (gwqkv_ref, gqkv_ref), (wout_in, wout_ref), (edown_in, edown_ref),
        (sdown_in, sdown_ref),
    ):
        dst[...] = src[...]
    nz = pieces_ref.shape[0]
    hidden = pieces_ref.shape[2] // 4
    for t in range(nz):
        for g in range(2):
            for e in range(2):
                at = (2 * g + e) * hidden
                to = (g * nz + t) * hidden
                geup_ref[e, :, to : to + hidden] = pieces_ref[t, :, at : at + hidden].astype(F32)
    count = small_ref.shape[0]
    total = small_ref[0].astype(F32)
    for d in range(count):
        if d:
            total = total + small_ref[d].astype(F32)
        for g in range(2):
            to = (g * count + d) * shared
            gsup_ref[:, to : to + shared] = small_ref[d, :, g * TAIL : g * TAIL + shared].astype(F32)
    grouter_ref[...] = total[:, shared : shared + experts].T
    one = jnp.sum(wqkv_ref[...].astype(F32) * gwqkv_ref[...], axis=-1, keepdims=True) / gain_ref[...].astype(F32).T
    gone_ref[...] = one.T
    gtwo_ref[...] = total[:, HD - 1 :].T


def unpack(pieces, small, wqkv, gwqkv, gain, rest, shared, experts):
    nz, up_rows, packed = pieces.shape
    count, dense, _ = small.shape
    return pl.pallas_call(
        functools.partial(unpack_kernel, shared=shared, experts=experts),
        out_shape=(
            jax.ShapeDtypeStruct((2, up_rows, nz * packed // 2), F32),
            jax.ShapeDtypeStruct((dense, 2 * count * shared), F32),
            jax.ShapeDtypeStruct((experts, dense), F32),
            jax.ShapeDtypeStruct((1, dense), F32),
            jax.ShapeDtypeStruct((1, dense), F32),
            *[jax.ShapeDtypeStruct(a.shape, a.dtype) for a in (*rest[:2], gwqkv, *rest[2:])],
        ),
        in_specs=[VMEM] * 10,
        out_specs=(VMEM,) * 11,
        compiler_params=pltpu.CompilerParams(vmem_limit_bytes=40 * 2**20),
        name="unpack",
    )(pieces, small, wqkv, gwqkv, gain, *rest)


def tables():
    pos = np.arange(SEQ, dtype=np.float32)
    freqs = np.float32(ROPE) ** (-np.arange(HD // 2, dtype=np.float32) * np.float32(2.0 / HD))
    angles = (pos[:, None] * freqs[None, :]).astype(np.float32)
    cosine = np.concatenate([np.cos(angles)] * 2, axis=1).astype(np.float32)
    sine = np.concatenate([-np.sin(angles), np.sin(angles)], axis=1).astype(np.float32)
    return jnp.asarray(cosine), jnp.asarray(sine)


def local_near(
    mesh, tokens, out_grad, segment_ids, expert_ids, attn_gain, ffn_gain, w_qkv, w_out,
    w_router, w_shared_up, w_shared_down, w_expert_up, w_expert_down,
):
    nz, nf = mesh.shape["dp"], mesh.shape["fsdp"]
    rows, width = tokens.shape
    experts = w_router.shape[1]
    hidden, shared = w_expert_down.shape[1], w_shared_down.shape[0]
    f = lax.axis_index("fsdp")
    cosine, sine = tables()
    (
        w, wo, tail, router, gain_one, gain_two, marks, own_marks, segq, segk, normed_one, qkv, attn, lse, mixed, normed,
        plane, all_grad, pieces,
    ) = front(
        tokens, w_qkv, w_out, w_router.T, w_shared_up, attn_gain[None], ffn_gain[None], expert_ids.T,
        segment_ids[None], cosine, sine, out_grad, w_expert_up, nz, nf, shared,
    )
    tail = tail.reshape(width, 2 * TAIL)
    lane = jnp.arange(HD, dtype=jnp.int32) - TAIL - shared
    own = (lane[None, :] == (2 * f + jnp.arange(2, dtype=jnp.int32))[:, None]).astype(F32)
    out_part, low, grad_mixed, small, geup, gedown, gsdown = experts_turn(
        normed, plane, all_grad, marks, own, pieces.reshape(width, 4 * hidden), tail,
        w_expert_down.reshape(2 * hidden, width), w_shared_down, out_grad, mixed, router, own_marks, gain_two, nz, nf,
    )
    block_out, tokens_grad, grad_wqkv, grad_wout, smalls, gpieces = back(
        low, geup, wo, w, normed_one, qkv, attn, lse, cosine, sine, segq, segk, out_part, small,
        tokens, mixed, grad_mixed, gain_one, nz, nf,
    )
    (
        grad_eup, grad_sup, grad_router, grad_one, grad_two, block_out, tokens_grad, grad_wqkv, grad_wout, gedown, gsdown,
    ) = unpack(
        gpieces, smalls, w_qkv, grad_wqkv, attn_gain[None], (block_out, tokens_grad, grad_wout, gedown, gsdown),
        shared, experts,
    )
    return (
        block_out, tokens_grad, grad_one[0], grad_two[0], grad_wqkv, grad_wout, grad_router.T, grad_sup,
        gsdown, grad_eup, gedown.reshape(2, hidden, width),
    )


def local_far(
    mesh, tokens, out_grad, segment_ids, expert_ids, attn_gain, ffn_gain, w_qkv, w_out,
    w_router, w_shared_up, w_shared_down, w_expert_up, w_expert_down,
):
    nz, nf = mesh.shape["dp"], mesh.shape["fsdp"]
    nd = nz * nf
    rows, width = tokens.shape
    group = SEQ // rows
    experts = w_router.shape[1]
    dense = w_qkv.shape[0]
    hidden, shared = w_expert_down.shape[1], w_shared_down.shape[0]
    up_rows = w_expert_up.shape[1]
    both = ("dp", "fsdp")
    groups = None if nf == group else [[a + i for i in range(group)] for a in range(0, nf, group)]
    f = lax.axis_index("fsdp")
    member = lax.rem(f, group)
    heads, real = head_table(group)

    by_head = w_qkv.reshape(dense, 3, HEADS, HD)
    empty = jnp.zeros((dense, 3, HD), BF16)
    cols = jnp.stack([by_head[:, :, h] if r else empty for h, r in zip(heads, real)], axis=0)
    cols = cols.reshape(group, SLOTS, dense, 3 * HD)
    cols = jnp.tile(cols, (nf // group, 1, 1, 1))
    cols = lax.all_to_all(cols, "fsdp", 0, 0, tiled=True)
    w = lax.all_gather(cols, "dp", axis=0, tiled=True).transpose(1, 0, 2, 3).reshape(SLOTS, width, 3 * HD)
    full_out = lax.all_gather(w_out, both, axis=0, tiled=True)
    first = HEADS * member // group
    own_real = (first + jnp.arange(SLOTS) < HEADS * (member + 1) // group).astype(BF16)
    padded = jnp.pad(full_out, ((0, (SLOTS - 1) * HD), (0, 0)))
    wo = lax.dynamic_slice(padded, (first * HD, 0), (SLOTS * HD, width))
    wo = wo * jnp.repeat(own_real, HD)[:, None]
    gains = lax.all_gather(jnp.stack([attn_gain, ffn_gain], axis=1).astype(F32), both, axis=0, tiled=True)
    gain_one, gain_two = gains[:, 0], gains[:, 1]
    router = lax.all_gather(w_router, both, axis=0, tiled=True)
    sup = w_shared_up.reshape(dense, 2, nd, shared).transpose(2, 0, 1, 3).reshape(nd, dense, 2 * shared)
    sup = lax.all_to_all(sup, both, 0, 0, tiled=True).reshape(width, 2, shared)
    eup = w_expert_up.reshape(2, up_rows, 2, nz, hidden).transpose(3, 1, 2, 0, 4)
    eup = lax.all_to_all(eup, "dp", 0, 0, tiled=True).reshape(width, 4 * hidden)
    rest = jnp.zeros((width, TAIL - shared), BF16)
    tail = jnp.concatenate([sup[:, 0], router, rest[:, experts:], sup[:, 1], rest], axis=1)
    chosen = jnp.any(expert_ids[:, :, None] == jnp.arange(experts, dtype=jnp.int32), axis=1)
    at = TAIL + shared
    marks = jnp.pad(chosen.astype(BF16), ((0, 0), (at, HD - experts - at)))
    marks = lax.all_gather(marks, both, axis=0, tiled=True)
    lane = jnp.arange(HD, dtype=jnp.int32)
    own = (lane[None, :] == (at + 2 * f + jnp.arange(2, dtype=jnp.int32))[:, None]).astype(F32)
    cosine, sine = tables()
    seg = lax.all_gather(segment_ids, "fsdp", axis=0, tiled=True, axis_index_groups=groups)
    segq = jnp.broadcast_to(seg[:, None], (SEQ, HD))
    segk = jnp.broadcast_to(seg[None, :], (8, SEQ))

    seq_tokens = lax.all_gather(tokens, "fsdp", axis=0, tiled=True, axis_index_groups=groups)
    part, normed_one, qkv, attn, lse = attn_forward(
        seq_tokens, gain_one[None, :], w, wo, cosine, sine, segq, segk
    )
    projected = lax.psum_scatter(part, "fsdp", scatter_dimension=0, tiled=True, axis_index_groups=groups)
    inputs = tokens.astype(F32)
    mixed = inputs + projected.astype(F32)
    scale_two = rms_scale(mixed)
    normal_two = mixed * scale_two
    normed_two = (normal_two * gain_two).astype(BF16)
    all_normed = lax.all_gather(normed_two, both, axis=0, tiled=True)
    all_grad = lax.all_gather(out_grad, both, axis=0, tiled=True)
    out_part, gx_part, geup, gtail, gedown, gsdown = ffn(
        all_normed, all_grad, marks, own, eup, tail, w_expert_down.reshape(2 * hidden, width), w_shared_down
    )
    gx = lax.psum_scatter(gx_part, both, scatter_dimension=0, tiled=True).astype(F32)
    ffn_out = lax.psum_scatter(out_part, both, scatter_dimension=0, tiled=True).astype(F32)
    block_out = (mixed + ffn_out).astype(BF16)

    logits = jnp.where(chosen, dot(normed_two, router), NEG)
    probs = jax.nn.softmax(logits, axis=-1)
    grad_gates = gx[:, width + at : width + at + experts]
    grad_logits = (
        probs * (grad_gates - jnp.sum(probs * grad_gates, axis=-1, keepdims=True))
    ).astype(BF16)
    grad_router = dot_tn(normed_two, grad_logits)
    grad_normed = gx[:, :width] + dot_nt(grad_logits, router)
    grad_gain_two = jnp.sum(grad_normed * normal_two, axis=0)
    grad_mixed = out_grad.astype(F32) + norm_back(grad_normed, normal_two, scale_two, gain_two)

    seq_gm = lax.all_gather(grad_mixed.astype(BF16), "fsdp", axis=0, tiled=True, axis_index_groups=groups)
    part_back, gw, gwo = attn_backward(
        seq_gm, wo, w, normed_one, qkv, attn, lse, cosine, sine, segq, segk
    )
    grad_normed_one = lax.psum_scatter(
        part_back, "fsdp", scatter_dimension=0, tiled=True, axis_index_groups=groups
    ).astype(F32)
    scale_one = rms_scale(inputs)
    normal_one = inputs * scale_one
    grad_gain_one = jnp.sum(grad_normed_one * normal_one, axis=0)
    tokens_grad = (grad_mixed + norm_back(grad_normed_one, normal_one, scale_one, gain_one)).astype(BF16)

    gw = lax.psum_scatter(gw, "dp", scatter_dimension=1, tiled=True)
    gw = lax.all_to_all(gw.reshape(SLOTS, nf, dense, 3 * HD), "fsdp", 1, 1, tiled=True).astype(F32)
    gw = jnp.sum(gw.reshape(SLOTS, nf // group, group, dense, 3, HD), axis=1)
    picked = [gw[i % SLOTS, i // SLOTS] for i in range(group * SLOTS) if real[i]]
    grad_wqkv = jnp.stack(picked, axis=2).reshape(dense, 3 * width)
    gwo = gwo * jnp.repeat(own_real, HD)[:, None]
    all_gwo = jnp.zeros(((HEADS + SLOTS - 1) * HD, width), BF16)
    all_gwo = lax.dynamic_update_slice(all_gwo, gwo, (first * HD, 0))[: HEADS * HD]
    grad_wout = lax.psum_scatter(all_gwo, both, scatter_dimension=0, tiled=True).astype(F32)
    small = jnp.concatenate([grad_router, grad_gain_one[:, None], grad_gain_two[:, None]], axis=1)
    small = lax.psum_scatter(small, both, scatter_dimension=0, tiled=True)
    gsup = jnp.stack([gtail[:, :shared], gtail[:, TAIL : TAIL + shared]], axis=1)
    gsup = lax.all_to_all(gsup.reshape(nd, dense, 2 * shared).astype(BF16), both, 0, 0, tiled=True)
    grad_sup = gsup.reshape(nd, dense, 2, shared).transpose(1, 2, 0, 3).reshape(dense, 2 * nd * shared).astype(F32)
    geup = lax.all_to_all(geup.reshape(nz, up_rows, 2, 2, hidden), "dp", 0, 0, tiled=True)
    grad_eup = geup.transpose(3, 1, 2, 0, 4).reshape(2, up_rows, 2 * nz * hidden).astype(F32)
    return (
        block_out, tokens_grad, small[:, experts], small[:, experts + 1], grad_wqkv, grad_wout,
        small[:, :experts], grad_sup, gsdown, grad_eup, gedown.reshape(2, hidden, width),
    )


def solution(mesh):
    one, two = P(("dp", "fsdp")), P(("dp", "fsdp"), None)
    three = P("fsdp", "dp", None)

    def local(tokens, *rest):
        near = mesh.shape["fsdp"] == 8 == SEQ // tokens.shape[0] and mesh.shape["dp"] <= 4
        return (local_near if near else local_far)(mesh, tokens, *rest)

    return jax.shard_map(
        local,
        mesh=mesh,
        in_specs=(two, two, one, two, one, one, two, two, two, two, two, three, three),
        out_specs=(two, two, one, one, two, two, two, two, two, three, three),
        check_vma=False,
    )
```

```python
import functools

import jax
import jax.numpy as jnp
import numpy as np
from jax import lax
from jax.experimental import pallas as pl
from jax.experimental.pallas import tpu as pltpu
from jax.sharding import PartitionSpec as P

HEADS = 10
HD = 128
SEQ = 1024
SLOTS = 2
EPS = 1e-06
ROPE = 10000.0
NEG = -1e30
TAIL = 64
F32 = jnp.float32
BF16 = jnp.bfloat16


MESH = pl.DeviceIdType.MESH
VMEM = pl.BlockSpec(memory_space=pltpu.VMEM)
ANY = pl.BlockSpec(memory_space=pl.ANY)


def up_to(value, step):
    return -(-value // step) * step


def rms_scale(values):
    return lax.rsqrt(jnp.mean(values * values, axis=-1, keepdims=True) + EPS)


def norm_back(grad_normed, normal_rows, scale_rows, gain_rows):
    scaled = grad_normed * gain_rows
    return scale_rows * (
        scaled - normal_rows * jnp.mean(scaled * normal_rows, axis=-1, keepdims=True)
    )


def head_table(group):
    heads, real = [], []
    for i in range(group):
        own = list(range(HEADS * i // group, HEADS * (i + 1) // group))
        assert len(own) <= SLOTS
        heads += own + [0] * (SLOTS - len(own))
        real += [1] * len(own) + [0] * (SLOTS - len(own))
    return heads, real


def dot(a, b):
    return jnp.dot(a, b, preferred_element_type=F32)


def dot_nt(a, b):
    return lax.dot_general(a, b, (((1,), (1,)), ((), ())), preferred_element_type=F32)


def dot_tn(a, b):
    return lax.dot_general(a, b, (((0,), (0,)), ((), ())), preferred_element_type=F32)


def attn_project(i, block, x, gain, w_ref, cos_ref, sin_ref, normed_ref, qkv_ref):
    rows = pl.ds(pl.multiple_of(i * block, block), block)
    x = x.astype(F32)
    normed = (x * rms_scale(x) * gain).astype(BF16)
    normed_ref[rows, :] = normed
    cosine, sine = cos_ref[rows, :], sin_ref[rows, :]
    for s in range(SLOTS):
        proj = dot(normed, w_ref[s])
        for c in range(3):
            piece = proj[:, c * HD : (c + 1) * HD]
            if c < 2:
                piece = piece * cosine + pltpu.roll(piece, HD // 2, 1) * sine
            at = (3 * s + c) * HD
            qkv_ref[rows, at : at + HD] = piece.astype(BF16)


def attn_block(i, block, segq_ref, segk_ref, qkv_ref, attn_ref, lse_ref):
    scale = HD**-0.5
    rows = slice(i * block, (i + 1) * block)
    keys = (i + 1) * block
    row_pos = i * block + lax.broadcasted_iota(jnp.int32, (block, keys), 0)
    key_pos = lax.broadcasted_iota(jnp.int32, (block, keys), 1)
    allowed = (key_pos <= row_pos) & (segq_ref[rows, :1] == segk_ref[:1, :keys])
    outs = []
    for s in range(SLOTS):
        at = 3 * s * HD
        q = qkv_ref[rows, at : at + HD]
        k = qkv_ref[:keys, at + HD : at + 2 * HD]
        v = qkv_ref[:keys, at + 2 * HD : at + 3 * HD]
        scores = jnp.where(allowed, dot_nt(q, k) * scale, NEG)
        top = jnp.max(scores, axis=-1, keepdims=True)
        weights = jnp.exp(scores - top)
        total = jnp.sum(weights, axis=-1, keepdims=True)
        out = dot(weights.astype(BF16), v) / total
        lse_ref[rows, s * HD : (s + 1) * HD] = jnp.broadcast_to(top + jnp.log(total), (block, HD))
        low = out.astype(BF16)
        attn_ref[rows, s * HD : (s + 1) * HD] = low
        outs.append(low)
    return jnp.concatenate(outs, axis=-1)


def attn_forward_kernel(
    tok_ref, gain_ref, w_ref, wo_ref, cos_ref, sin_ref, segq_ref, segk_ref,
    part_ref, normed_ref, qkv_ref, attn_ref, lse_ref,
    *, block,
):
    count = tok_ref.shape[0] // block

    def project(i, _):
        x = tok_ref[pl.ds(pl.multiple_of(i * block, block), block), :]
        attn_project(i, block, x, gain_ref[...], w_ref, cos_ref, sin_ref, normed_ref, qkv_ref)
        return 0

    lax.fori_loop(0, count, project, 0)
    for i in range(count):
        outs = attn_block(i, block, segq_ref, segk_ref, qkv_ref, attn_ref, lse_ref)
        part_ref[i * block : (i + 1) * block, :] = dot(outs, wo_ref[...]).astype(BF16)


def attn_forward(tok, gain, w, wo, cosine, sine, segq, segk):
    length, width = tok.shape
    return pl.pallas_call(
        functools.partial(attn_forward_kernel, block=256),
        out_shape=(
            jax.ShapeDtypeStruct((length, width), BF16),
            jax.ShapeDtypeStruct((length, width), BF16),
            jax.ShapeDtypeStruct((length, 3 * SLOTS * HD), BF16),
            jax.ShapeDtypeStruct((length, SLOTS * HD), BF16),
            jax.ShapeDtypeStruct((length, SLOTS * HD), F32),
        ),
        in_specs=[VMEM] * 8,
        out_specs=(VMEM,) * 5,
        compiler_params=pltpu.CompilerParams(vmem_limit_bytes=56 * 2**20),
        cost_estimate=pl.CostEstimate(
            flops=2 * length * width * 4 * SLOTS * HD + 4 * SLOTS * HD * length * length,
            bytes_accessed=10 * length * width,
            transcendentals=SLOTS * length * length,
        ),
        name="attn_forward",
    )(tok, gain, w, wo, cosine, sine, segq, segk)


def attn_back_block(
    i, block, gm, wo_ref, qkv_ref, attn_ref, lse_ref, cos_ref, sin_ref, segq_ref, segk_ref, gkv_ref, gqkv_ref
):
    scale = HD**-0.5
    rows = slice(i * block, (i + 1) * block)
    keys = (i + 1) * block
    row_pos = i * block + lax.broadcasted_iota(jnp.int32, (block, keys), 0)
    key_pos = lax.broadcasted_iota(jnp.int32, (block, keys), 1)
    allowed = (key_pos <= row_pos) & (segq_ref[rows, :1] == segk_ref[:1, :keys])
    grad_attn = dot_nt(gm, wo_ref[...]).astype(BF16)
    for s in range(SLOTS):
        at = 3 * s * HD
        cut = slice(s * HD, (s + 1) * HD)
        q = qkv_ref[rows, at : at + HD]
        k = qkv_ref[:keys, at + HD : at + 2 * HD]
        v = qkv_ref[:keys, at + 2 * HD : at + 3 * HD]
        ga = grad_attn[:, cut]
        delta = jnp.sum(ga.astype(F32) * attn_ref[rows, cut].astype(F32), axis=-1, keepdims=True)
        scores = dot_nt(q, k) * scale
        probs = jnp.where(allowed, jnp.exp(scores - lse_ref[rows, s * HD : s * HD + 1]), 0.0)
        gs = (probs * (dot_nt(ga, v) - delta)).astype(BF16)
        gq = dot(gs, k) * scale
        gq = gq * cos_ref[rows, :] - pltpu.roll(gq, HD // 2, 1) * sin_ref[rows, :]
        gqkv_ref[rows, at : at + HD] = gq.astype(BF16)
        gkv_ref[:keys, 2 * s * HD : (2 * s + 1) * HD] += dot_tn(gs, q)
        gkv_ref[:keys, (2 * s + 1) * HD : (2 * s + 2) * HD] += dot_tn(probs.astype(BF16), ga)


def attn_back_keys(w_ref, cos_ref, sin_ref, gkv_ref, gqkv_ref, wt_ref):
    step = 3 * HD
    for s in range(SLOTS):
        at = s * step
        gk = gkv_ref[:, 2 * s * HD : (2 * s + 1) * HD] * HD**-0.5
        gk = gk * cos_ref[...] - pltpu.roll(gk, HD // 2, 1) * sin_ref[...]
        gqkv_ref[:, at + HD : at + 2 * HD] = gk.astype(BF16)
        gqkv_ref[:, at + 2 * HD : at + 3 * HD] = gkv_ref[:, (2 * s + 1) * HD : (2 * s + 2) * HD].astype(BF16)
        wt_ref[s * step : (s + 1) * step, :] = w_ref[s].T


def attn_backward_kernel(
    gm_ref, wo_ref, w_ref, normed_ref, qkv_ref, attn_ref, lse_ref, cos_ref, sin_ref,
    segq_ref, segk_ref,
    part_ref, gw_ref, gwo_ref,
    gkv_ref, gqkv_ref, wt_ref,
    *, block,
):
    count = gm_ref.shape[0] // block
    step = 3 * HD
    gkv_ref[...] = jnp.zeros_like(gkv_ref)
    for i in range(count):
        attn_back_block(
            i, block, gm_ref[i * block : (i + 1) * block, :], wo_ref, qkv_ref, attn_ref, lse_ref, cos_ref, sin_ref, segq_ref, segk_ref, gkv_ref, gqkv_ref
        )
    attn_back_keys(w_ref, cos_ref, sin_ref, gkv_ref, gqkv_ref, wt_ref)
    for i in range(count):
        rows = slice(i * block, (i + 1) * block)
        part_ref[rows, :] = dot(gqkv_ref[rows, :], wt_ref[...]).astype(BF16)
    for s in range(SLOTS):
        gw_ref[s] = dot_tn(normed_ref[...], gqkv_ref[:, s * step : (s + 1) * step]).astype(BF16)
    gwo_ref[...] = dot_tn(attn_ref[...], gm_ref[...]).astype(BF16)


def attn_backward(gm, wo, w, normed, qkv, attn, lse, cosine, sine, segq, segk):
    length, width = gm.shape
    return pl.pallas_call(
        functools.partial(attn_backward_kernel, block=256),
        out_shape=(
            jax.ShapeDtypeStruct((length, width), BF16),
            jax.ShapeDtypeStruct((SLOTS, width, 3 * HD), BF16),
            jax.ShapeDtypeStruct((SLOTS * HD, width), BF16),
        ),
        in_specs=[VMEM] * 11,
        out_specs=(VMEM,) * 3,
        scratch_shapes=[
            pltpu.VMEM((length, 2 * SLOTS * HD), F32),
            pltpu.VMEM((length, 3 * SLOTS * HD), BF16),
            pltpu.VMEM((3 * SLOTS * HD, width), BF16),
        ],
        compiler_params=pltpu.CompilerParams(vmem_limit_bytes=56 * 2**20),
        cost_estimate=pl.CostEstimate(
            flops=4 * length * width * 4 * SLOTS * HD + 10 * SLOTS * HD * length * length,
            bytes_accessed=10 * length * width,
            transcendentals=SLOTS * length * length,
        ),
        name="attn_backward",
    )(gm, wo, w, normed, qkv, attn, lse, cosine, sine, segq, segk)


def ffn_weights(eup_ref, tail_ref, edown_ref, sdown_ref, up_ref, upt_ref, down_ref, downt_ref):
    width, half = downt_ref.shape
    pair, shared = edown_ref.shape[0], sdown_ref.shape[0]
    gap = half - pair - TAIL
    between = [jnp.zeros((width, gap), BF16)] if gap else []
    up_ref[...] = jnp.concatenate(
        [eup_ref[:, :pair], *between, tail_ref[:, :TAIL], eup_ref[:, pair:], *between, tail_ref[:, TAIL:]], axis=1
    )
    between = [jnp.zeros((gap, width), BF16)] if gap else []
    down_ref[...] = jnp.concatenate(
        [edown_ref[...], *between, sdown_ref[...], jnp.zeros((TAIL - shared, width), BF16)], axis=0
    )
    upt_ref[...] = up_ref[...].T
    downt_ref[...] = down_ref[...].T


def ffn_rows(x, g, marks, own, up_ref, upt_ref, down_ref, downt_ref, hidden, shared):
    half = down_ref.shape[0]
    pair = 2 * hidden
    pre = dot(x, up_ref[...])
    gate, up = pre[:, :half], pre[:, half:]
    logits = jnp.where(marks.astype(F32) > 0.5, gate[:, half - HD :], NEG)
    weights = jnp.exp(logits - jnp.max(logits, axis=-1, keepdims=True))
    probs = weights / jnp.sum(weights, axis=-1, keepdims=True)
    p0 = jnp.sum(probs * own[0:1, :], axis=-1, keepdims=True)
    p1 = jnp.sum(probs * own[1:2, :], axis=-1, keepdims=True)
    lane = lax.broadcasted_iota(jnp.int32, (1, half), 1)
    in0 = lane < hidden
    in1 = (lane >= hidden) & (lane < pair)
    rest = jnp.where((lane >= half - TAIL) & (lane < half - TAIL + shared), 1.0, 0.0)
    weight = jnp.where(in0, p0, jnp.where(in1, p1, rest))
    sig = jax.nn.sigmoid(gate)
    silu = gate * sig
    act = silu * up
    acts = (act * weight).astype(BF16)
    out = dot(acts, down_ref[...]).astype(BF16)
    grad = dot(g, downt_ref[...])
    both = act * grad
    d0 = jnp.sum(jnp.where(in0, both, 0.0), axis=-1, keepdims=True)
    d1 = jnp.sum(jnp.where(in1, both, 0.0), axis=-1, keepdims=True)
    grad = grad * weight
    grad_gate = grad * up * sig * (1.0 + gate * (1.0 - sig))
    grad_up = grad * silu
    grad_pre = jnp.concatenate([grad_gate, grad_up], axis=-1).astype(BF16)
    gates = (d0 * own[0:1, :] + d1 * own[1:2, :]).astype(BF16)
    gx = jnp.concatenate([dot(grad_pre, upt_ref[...]).astype(BF16), gates], axis=-1)
    return out, gx, grad_pre, acts


def ffn_kernel(
    x_ref, g_ref, mark_ref, own_ref, eup_ref, tail_ref, edown_ref, sdown_ref,
    out_ref, gx_ref, geup_ref, gtail_ref, gedown_ref, gsdown_ref,
    up_ref, upt_ref, down_ref, downt_ref, gup_ref, gdown_ref,
    *, hidden, shared,
):
    step = pl.program_id(0)
    half = down_ref.shape[0]
    pair = 2 * hidden

    @pl.when(step == 0)
    def _():
        gup_ref[...] = jnp.zeros_like(gup_ref)
        gdown_ref[...] = jnp.zeros_like(gdown_ref)
        ffn_weights(eup_ref, tail_ref, edown_ref, sdown_ref, up_ref, upt_ref, down_ref, downt_ref)

    out, gx, grad_pre, acts = ffn_rows(
        x_ref[...], g_ref[...], mark_ref[...], own_ref[...], up_ref, upt_ref, down_ref, downt_ref, hidden, shared
    )
    out_ref[...] = out
    gx_ref[...] = gx
    gup_ref[...] += dot_tn(x_ref[...], grad_pre)
    gdown_ref[...] += dot_tn(acts, g_ref[...])

    @pl.when(step == pl.num_programs(0) - 1)
    def _():
        geup_ref[...] = jnp.concatenate([gup_ref[:, :pair], gup_ref[:, half : half + pair]], axis=1).astype(BF16)
        gtail_ref[...] = jnp.concatenate([gup_ref[:, half - TAIL : half], gup_ref[:, 2 * half - TAIL :]], axis=1)
        gedown_ref[...] = gdown_ref[:pair, :]
        gsdown_ref[...] = gdown_ref[half - TAIL : half - TAIL + shared, :]


def ffn(x, g, marks, own, eup, tail, edown, sdown):
    total, width = x.shape
    pair, shared = edown.shape[0], sdown.shape[0]
    half = up_to(pair + TAIL, HD)
    tile = 512
    row = lambda n: pl.BlockSpec((tile, n), lambda i: (i, 0))
    return pl.pallas_call(
        functools.partial(ffn_kernel, hidden=pair // 2, shared=shared),
        out_shape=(
            jax.ShapeDtypeStruct((total, width), BF16),
            jax.ShapeDtypeStruct((total, width + HD), BF16),
            jax.ShapeDtypeStruct((width, 2 * pair), BF16),
            jax.ShapeDtypeStruct((width, HD), F32),
            jax.ShapeDtypeStruct((pair, width), F32),
            jax.ShapeDtypeStruct((shared, width), F32),
        ),
        grid=(total // tile,),
        in_specs=[row(width), row(width), row(HD)] + [VMEM] * 5,
        out_specs=(row(width), row(width + HD), VMEM, VMEM, VMEM, VMEM),
        scratch_shapes=[
            pltpu.VMEM((width, 2 * half), BF16),
            pltpu.VMEM((2 * half, width), BF16),
            pltpu.VMEM((half, width), BF16),
            pltpu.VMEM((width, half), BF16),
            pltpu.VMEM((width, 2 * half), F32),
            pltpu.VMEM((half, width), F32),
        ],
        compiler_params=pltpu.CompilerParams(vmem_limit_bytes=60 * 2**20),
        cost_estimate=pl.CostEstimate(
            flops=2 * total * width * 9 * half,
            bytes_accessed=8 * total * width,
            transcendentals=total * half,
        ),
        name="ffn",
    )(x, g, marks, own, eup, tail, edown, sdown)


def flip(f, bits):
    for b in (1, 2, 4):
        if bits & b:
            f = f + b - 2 * b * (f // b % 2)
    return f


def place():
    return lax.axis_index("dp"), lax.axis_index("fsdp")


def greet(devices):
    barrier = pltpu.get_barrier_semaphore()
    for device in devices:
        pl.semaphore_signal(barrier, inc=1, device_id=device, device_id_type=MESH)
    pl.semaphore_wait(barrier, len(devices))


def greet_all(nz, nf):
    barrier = pltpu.get_barrier_semaphore()
    z, f = place()
    me, count = z * nf + f, nz * nf

    def hail(i, _):
        d = (me + i) % count
        pl.semaphore_signal(barrier, inc=1, device_id=(d // nf, d % nf), device_id_type=MESH)
        return 0

    lax.fori_loop(1, count, hail, 0)
    pl.semaphore_wait(barrier, count - 1)


def send(src, dst, sems, index, device):
    return pltpu.make_async_remote_copy(
        src, dst, sems[0].at[index], sems[1].at[index], device_id=device, device_id_type=MESH
    )


ORDER = ((2, 4), (4, 2))


def halves(rows):
    return ((0, rows // 2), (rows // 2, rows - rows // 2))


def away(j, nz):
    if nz < 3:
        return j
    if isinstance(j, int):
        return j if j < 2 else nz - 1 if j == 2 else j - 1
    return jnp.where(j < 2, j, jnp.where(j == 2, nz - 1, j - 1))


def spot(ref, piece, f):
    return ref.at[piece, f // 4, f // 2 % 2, f % 2] if len(ref.shape) == 6 else ref.at[piece, f]


class Gather:
    @staticmethod
    def copies(nz):
        return 11 * nz

    def __init__(self, buf, sems, nz, z, f):
        self.buf, self.sems, self.nz, self.z, self.f = buf, sems, nz, z, f

    def slot(self, j, r, h=None):
        piece = lax.rem(self.z - away(j, self.nz) + self.nz, self.nz) if self.nz > 1 else 0
        ref = spot(self.buf, piece, flip(self.f, r))
        return ref if h is None else ref.at[pl.ds(*halves(self.buf.shape[-2])[h])]

    def here(self, j, r, h, index, device):
        ref = self.slot(j, r, h)
        return send(ref, ref, self.sems, index, device)

    def by_z(self, j):
        own = self.slot(0, 0)
        return send(own, own, self.sems, j, (lax.rem(self.z + away(j, self.nz), self.nz), self.f))

    def near(self, j, h):
        return self.here(j, 0, h, self.nz + 2 * j + h, (self.z, flip(self.f, ORDER[h][0])))

    def far(self, j, h, i):
        r = ORDER[h][0] if i else 0
        return self.here(j, r, h, 3 * self.nz + 4 * j + 2 * h + i, (self.z, flip(self.f, ORDER[h][1])))

    def core(self, j, i):
        return self.here(j, 2 * i, None, 7 * self.nz + 4 * j + i, (self.z, flip(self.f, 1)))

    def along_z(self, j):
        if 1 < j <= self.nz:
            self.by_z(j - 1).wait_send()
        if j < self.nz:
            self.by_z(j).start()

    def first(self, j, own=False):
        if not own:
            self.by_z(j).wait_recv()
        for h in range(2):
            self.near(j, h).start()
        self.core(j, 0).start()

    def second(self, j):
        for h in range(2):
            self.near(j, h).wait_recv()
            for i in range(2):
                self.far(j, h, i).start()

    def third(self, j):
        for h in range(2):
            for i in range(2):
                self.far(j, h, i).wait_recv()
        for i in range(1, 4):
            self.core(j, i).start()

    def fourth(self, j):
        for i in range(4):
            self.core(j, i).wait_recv()

    def end(self, first=0):
        for j in range(first, self.nz):
            for h in range(2):
                self.near(j, h).wait_send()
                for i in range(2):
                    self.far(j, h, i).wait_send()
            for i in range(4):
                self.core(j, i).wait_send()


class Reduce:
    @staticmethod
    def copies(nz):
        return 11 * nz

    @staticmethod
    def scratch(nz, rows, width):
        return [
            pltpu.VMEM((nz, 4, rows, width), BF16),
            pltpu.VMEM((nz, 2, rows, width), BF16),
            pltpu.VMEM((nz, rows, width), BF16),
            pltpu.VMEM((nz, rows, width), BF16),
        ]

    def __init__(self, bufs, sems, nz, z, f):
        self.by_core, self.by_near, self.by_far, self.by_z = bufs
        self.sems, self.nz, self.z, self.f = sems, nz, z, f
        self.parts = halves(self.by_core.shape[-2])

    def core(self, j, i, src):
        to = self.by_core.at[j, i]
        return send(to if src is None else src, to, self.sems, 4 * j + i, (self.z, flip(self.f, 1)))

    def near(self, j, h, i):
        last = ORDER[1 - h][1]
        rows = pl.ds(*self.parts[h])
        return send(
            self.by_core.at[j, 3 if i else last // 2, rows], self.by_near.at[j, i, rows], self.sems,
            4 * self.nz + 4 * j + 2 * h + i, (self.z, flip(self.f, last)),
        )

    def far_copy(self, j, h):
        rows = pl.ds(*self.parts[h])
        return send(
            self.by_near.at[j, 1, rows], self.by_far.at[j, rows], self.sems,
            8 * self.nz + 2 * j + h, (self.z, flip(self.f, ORDER[1 - h][0])),
        )

    def z_copy(self, j):
        there = lax.rem(self.z - away(j, self.nz) + self.nz, self.nz)
        return send(self.by_far.at[j], self.by_z.at[j], self.sems, 10 * self.nz + j, (there, self.f))

    def send_near(self, j):
        for h in range(2):
            for i in range(2):
                self.near(j, h, i).start()

    def far(self, j):
        for h in range(2):
            at, size = self.parts[h]
            rows = slice(at, at + size)
            for i, r in enumerate((0, ORDER[1 - h][0])):
                self.near(j, h, i).wait_recv()
                self.by_near[j, i, rows] = self.by_near[j, i, rows] + self.by_core[j, r // 2, rows]
            self.far_copy(j, h).start()

    def along_z(self, j):
        for h in range(2):
            at, size = self.parts[h]
            rows = slice(at, at + size)
            self.far_copy(j, h).wait_recv()
            self.by_far[j, rows] = self.by_far[j, rows] + self.by_near[j, 0, rows]
        if isinstance(j, int):
            if j:
                self.z_copy(j).start()
        else:

            @pl.when(j > 0)
            def _():
                self.z_copy(j).start()

    def total(self):
        result = self.by_far[0].astype(F32)
        for j in range(1, self.nz):
            self.z_copy(j).wait_recv()
            result = result + self.by_z[j].astype(F32)
        return result

    def end(self):
        for j in range(self.nz):
            for h in range(2):
                for i in range(2):
                    self.near(j, h, i).wait_send()
                self.far_copy(j, h).wait_send()
            if j:
                self.z_copy(j).wait_send()


def near_devices(z, f):
    return [(z, flip(f, 1)), (z, flip(f, 2)), (z, flip(f, 4))]


def z_devices(z, f, nz):
    return [(lax.rem(z + zr, nz), f) for zr in range(1, nz)]


def pair_of(count):
    return [pltpu.SemaphoreType.DMA((count,))] * 2


def first_head(member):
    return HEADS * member // 8


def out_blocks(member, dense):
    return first_head(member) * HD // dense, (first_head(member + 1) * HD - 1) // dense


def head_owner(head):
    return (8 * head + 7) // HEADS


def front_kernel(
    tok_ref, wqkv_ref, wout_ref, router_ref, sup_ref, again_ref, fgain_ref, eids_ref, seg_ref, cos_ref, sin_ref, og_ref,
    eup_ref,
    w_out, wo_ref, tail_out, router_out, gain_one_ref, gain_two_ref, mark_out, own_mark_ref, segq_ref, segk_ref,
    normed_out, qkv_out, attn_out, lse_out, mixed_ref, low_ref, plane_ref, all_grad_ref, pieces_ref,
    w_ref, tail_ref, mark_ref, normed_ref, qkv_ref, attn_ref, lse_ref, ids_ref, out_sems,
    seq, wq, wo_in, wz, wzo, all_ids, qpack, tpack, part, wide, pack, *refs, nz, nf, hidden, shared, heads, real,
):
    bufs, refs = refs[:4], refs[4:]
    (
        tok_s, tok_r, all_s, all_r, q_s, q_r, wo_s, wo_r, zq_s, zq_r, zo_s, zo_r, rs, rr, gs, gr, xs, xr, es, er,
        own_sems,
    ) = refs
    z, f = place()
    me, count = z * nf + f, nz * nf
    rows, width = tok_ref.shape
    dense = wqkv_ref.shape[0]
    experts = router_ref.shape[0]
    full = shared * count
    greet_all(nz, nf)

    toks = (tok_s, tok_r)
    to_near = [send(tok_ref, seq.at[f], toks, i, (z, flip(f, r))) for i, r in enumerate((2, 4, 6))]
    to_core = [send(tok_ref, seq.at[f], toks, 3, (z, flip(f, 1)))]
    own = pltpu.make_async_copy(og_ref, all_grad_ref.at[z, f], own_sems.at[0])
    own.start()
    for copy in to_near + to_core:
        copy.start()
    seq[f] = tok_ref[...]
    ids_ref[...] = jnp.concatenate([eids_ref[...], seg_ref[...]], axis=0)
    all_ids[me] = ids_ref[...]
    router = router_ref[...].astype(F32).T.astype(BF16)
    both_gains = jnp.concatenate([again_ref[...].astype(F32).T, fgain_ref[...].astype(F32).T], axis=1).astype(BF16)

    def leave(k, src, dst):
        return pltpu.make_async_copy(src, dst, out_sems.at[k])

    outgoing = [
        leave(k, src, dst)
        for k, (src, dst) in enumerate(
            (
                (w_ref, w_out), (tail_ref, tail_out), (mark_ref, mark_out), (normed_ref, normed_out),
                (qkv_ref, qkv_out), (attn_ref, attn_out), (lse_ref, lse_out),
            )
        )
    ]
    own.wait()
    grads = Gather(all_grad_ref, (gs, gr), nz, z, f)
    grads.first(0, own=True)

    def two(m):
        return first_head(m + 1) - first_head(m) == 2

    def wanted(m, block):
        low, high = out_blocks(m, dense)
        return (low <= block) & (block <= high)

    low, high = out_blocks(f, dense)

    def piece(j):
        return lax.rem(z - away(j, nz) + nz, nz) if j else z

    def along(src, dst, sems, j):
        return send(src, dst.at[z], sems, j, (lax.rem(z + away(j, nz), nz), f))

    zq = [None] + [along(wqkv_ref, wz, (zq_s, zq_r), j) for j in range(1, nz)]
    zo = [None] + [along(wout_ref, wzo, (zo_s, zo_r), j) for j in range(1, nz)]
    for copy in zq[1:] + zo[1:]:
        copy.start()

    pad = jnp.zeros((dense, TAIL - shared - experts), BF16)
    pad_two = jnp.zeros((dense, TAIL - shared - 2), BF16)
    for d in range(count):
        tpack[d] = jnp.concatenate(
            [
                sup_ref[:, d * shared : (d + 1) * shared], router, pad,
                sup_ref[:, full + d * shared : full + (d + 1) * shared], both_gains, pad_two,
            ],
            axis=1,
        )

    def copies(d, k):
        src, dst = ((tpack.at[d], tail_ref.at[me]), (ids_ref, all_ids.at[me]))[k]
        return pltpu.make_async_remote_copy(
            src, dst, all_s.at[k, d], all_r.at[k, me], device_id=(d // nf, d % nf), device_id_type=MESH
        )

    def came(d, k):
        dst = (tail_ref.at[d], all_ids.at[d])[k]
        return pltpu.make_async_remote_copy(
            dst, dst, all_s.at[k, d], all_r.at[k, d], device_id=(d // nf, d % nf), device_id_type=MESH
        )

    def start(i, _):
        d = (me + i) % count
        copies(d, 0).start()
        copies(d, 1).start()
        return 0

    whole = nz * hidden
    for t in range(nz):
        pack[t] = jnp.concatenate(
            [
                eup_ref[e, :, g * whole + t * hidden : g * whole + (t + 1) * hidden]
                for g in range(2)
                for e in range(2)
            ],
            axis=1,
        )
    tail_ref[me] = tpack[me]
    lax.fori_loop(1, count, start, 0)

    def q_copy(j, m, s):
        return pltpu.make_async_remote_copy(
            qpack.at[j, m, s], wq.at[s, piece(j) * nf + f], q_s.at[j, m, s], q_r.at[j, f, s],
            device_id=(z, m), device_id_type=MESH,
        )

    def q_came(j, m, s):
        dst = wq.at[s, piece(j) * nf + m]
        return pltpu.make_async_remote_copy(
            dst, dst, q_s.at[j, m, s], q_r.at[j, m, s], device_id=(z, m), device_id_type=MESH
        )

    def q_own(j, s):
        wq[s, piece(j) * nf + f] = qpack[j, f, s]

    def q_each(act, m):
        act(0)

        @pl.when(two(m))
        def _():
            act(1)

    def q_send(j):
        ref = wz.at[piece(j)] if j else wqkv_ref
        for m in range(8):
            for s in range(SLOTS):
                h = heads[m * SLOTS + s]
                if real[m * SLOTS + s]:
                    qpack[j, m, s] = jnp.concatenate(
                        [ref[:, c * width + h * HD : c * width + (h + 1) * HD] for c in range(3)], axis=1
                    )

        def go(i, _):
            m = (f + i) % nf
            q_each(lambda s: q_copy(j, m, s).start(), m)
            return 0

        lax.fori_loop(1, nf, go, 0)
        q_each(lambda s: q_own(j, s), f)

    grads.second(0)
    for i, r in enumerate((2, 4, 6)):
        to_near[i].wait_recv()
        slot = seq.at[flip(f, r)]
        copy = send(slot, slot, toks, 4 + i, (z, flip(f, 1)))
        copy.start()
        to_core.append(copy)
    q_send(0)
    grads.third(0)
    for copy in zq[1:]:
        copy.wait_send()
    for j in range(1, nz):
        grads.by_z(j).start()
    for j in range(1, nz):
        zq[j].wait_recv()
        q_send(j)

    def arrive(i, _):
        d = (me + i) % count
        came(d, 0).wait_recv()
        came(d, 1).wait_recv()
        return 0

    lax.fori_loop(1, count, arrive, 0)

    def q_arrive(i, _):
        m = (f + i) % nf
        for j in range(nz):
            q_each(lambda s: q_came(j, m, s).wait_recv(), f)
        return 0

    lax.fori_loop(1, nf, q_arrive, 0)
    for copy in to_core:
        copy.wait_recv()

    w_ref[0] = wq[0].reshape(width, 3 * HD)
    w_ref[1] = jnp.where(two(f), wq[1].astype(F32), 0.0).reshape(width, 3 * HD).astype(BF16)
    outgoing[0].start()
    outgoing[1].start()
    tails = tail_ref[...].reshape(width, 2 * TAIL)
    gains = tails[:, TAIL + shared : TAIL + shared + 2].astype(F32).T
    gain_one_ref[...] = gains[0:1]
    gain_two_ref[...] = gains[1:2]
    router_out[...] = jnp.concatenate(
        [
            jnp.zeros((width, TAIL + shared), BF16), tails[:, shared : shared + experts],
            jnp.zeros((width, TAIL - shared - experts), BF16),
        ],
        axis=1,
    )
    for m in range(8):
        ids = all_ids[z * nf + m]
        segk_ref[:, m * rows : (m + 1) * rows] = jnp.broadcast_to(ids[-1:], (8, rows))
        segq_ref[m * rows : (m + 1) * rows, :] = jnp.broadcast_to(ids.T[:, -1:], (rows, HD))
    block = 256
    gain_one = gain_one_ref[...]

    def project(i, _):
        x = seq[pl.ds(i * (block // rows), block // rows)].reshape(block, width)
        attn_project(i, block, x, gain_one, w_ref, cos_ref, sin_ref, normed_ref, qkv_ref)
        return 0

    lax.fori_loop(0, 8 * rows // block, project, 0)
    outgoing[3].start()
    outgoing[4].start()
    def out_block(j):
        return piece(j) * nf + f

    def out_src(j):
        return wzo.at[piece(j)] if j else wout_ref

    def out_copy(j, m):
        first, _ = out_blocks(m, dense)
        slot = out_block(j) - first
        return pltpu.make_async_remote_copy(
            out_src(j), wo_in.at[slot], wo_s.at[j, m], wo_r.at[slot], device_id=(z, m), device_id_type=MESH
        )

    def out_own(j):
        wo_in[out_block(j) - low] = wzo[piece(j)] if j else wout_ref[...]

    def out_each(act, act_own):
        for j in range(nz):

            def one(i, _):
                m = (f + i) % nf

                @pl.when(wanted(m, out_block(j)))
                def _():
                    act(j, m)

                return 0

            lax.fori_loop(1, nf, one, 0)

            @pl.when(wanted(f, out_block(j)))
            def _():
                act_own(j)

    for j in range(1, nz):
        zo[j].wait()
    out_each(lambda j, m: out_copy(j, m).start(), out_own)

    reduce = Reduce(bufs, (rs, rr), 1, z, f)
    for i in range(8 * rows // block):
        attn_block(i, block, segq_ref, segk_ref, qkv_ref, attn_ref, lse_ref)

    outgoing[5].start()
    outgoing[6].start()

    def arrive_out(j, _):
        @pl.when((low + j <= high) & (lax.rem(low + j, nf) != f))
        def _():
            pltpu.make_async_remote_copy(
                wo_in.at[j], wo_in.at[j], wo_s.at[0, j], wo_r.at[j], device_id=(z, flip(f, 1)), device_id_type=MESH
            ).wait_recv()

        return 0

    lax.fori_loop(0, wo_in.shape[0], arrive_out, 0)
    wide[...] = wo_in[...].astype(F32).reshape(wide.shape)
    offset = pl.multiple_of(first_head(f) * HD - low * dense, 8)
    wo_ref[:HD, :] = wide[pl.ds(offset, HD), :].astype(BF16)
    wo_ref[HD:, :] = jnp.where(two(f), wide[pl.ds(offset + HD, HD), :], 0.0).astype(BF16)
    for i in range(8 * rows // block):
        at = i * (block // rows)
        part[at : at + block // rows] = (
            dot(attn_ref[i * block : (i + 1) * block, :], wo_ref[...]).astype(BF16).reshape(block // rows, rows, width)
        )
    for i in range(4):
        reduce.core(0, i, part.at[flip(f, 1 | 2 * i)]).start()
    ups = []
    for j in range(1, nz):
        there = lax.rem(z + j, nz)
        copy = send(pack.at[there], pieces_ref.at[z], (es, er), j, (there, f))
        copy.start()
        ups.append(copy)
    ups.append(pltpu.make_async_copy(pack.at[z], pieces_ref.at[z], own_sems.at[2]))
    ups[-1].start()
    for i in range(4):
        reduce.core(0, i, None).wait_recv()
        reduce.by_core[0, i] = reduce.by_core[0, i] + part[flip(f, 2 * i)]
    reduce.send_near(0)
    reduce.far(0)
    reduce.along_z(0)
    mixed = tok_ref[...].astype(F32) + reduce.by_far[0].astype(F32)
    mixed_ref[...] = mixed
    low_ref[...] = (mixed * rms_scale(mixed) * gain_two_ref[...]).astype(BF16)
    near_own = pltpu.make_async_copy(low_ref, plane_ref.at[0, f], own_sems.at[1])
    near_own.start()
    near = Gather(plane_ref, (xs, xr), 1, z, f)
    near_own.wait()
    near.first(0, own=True)
    for j in range(1, nz):
        grads.first(j)
    near.second(0)
    for j in range(1, nz):
        grads.second(j)
    lane = lax.broadcasted_iota(jnp.int32, (rows, HD), 1) - TAIL - shared

    def mark(d, _):
        ids = all_ids[d].T
        found = ids[:, 0:1] == lane
        for k in range(1, ids.shape[1] - 1):
            found = found | (ids[:, k : k + 1] == lane)
        value = jnp.where(found, 1.0, 0.0)
        mark_ref[d] = value.astype(BF16)

        @pl.when(d == me)
        def _():
            own_mark_ref[...] = value

        return 0

    lax.fori_loop(0, count, mark, 0)
    outgoing[2].start()
    near.third(0)
    for j in range(1, nz):
        grads.third(j)
    for j in range(nz):
        grads.fourth(j)
    near.fourth(0)

    def left(i, _):
        d = (me + i) % count
        copies(d, 0).wait_send()
        copies(d, 1).wait_send()
        return 0

    lax.fori_loop(1, count, left, 0)

    def q_left(i, _):
        m = (f + i) % nf
        for j in range(nz):
            q_each(lambda s: q_copy(j, m, s).wait_send(), m)
        return 0

    lax.fori_loop(1, nf, q_left, 0)
    out_each(lambda j, m: out_copy(j, m).wait_send(), lambda j: None)
    for copy in to_near + to_core:
        copy.wait_send()
    for i in range(4):
        reduce.core(0, i, part.at[0]).wait_send()
    reduce.end()
    for j in range(1, nz):
        grads.by_z(j).wait_send()
    grads.end()
    near.end()
    for copy in ups + outgoing:
        copy.wait()


def front(tok, wqkv, wout, router, sup, again, fgain, eids, seg, cosine, sine, og, eup, nz, nf, shared):
    rows, width = tok.shape
    dense, count = wqkv.shape[0], nz * nf
    length = 8 * rows
    hidden, up_rows = eup.shape[2] // (2 * nz), eup.shape[1]
    heads, real = head_table(8)
    shape = jax.ShapeDtypeStruct
    return pl.pallas_call(
        functools.partial(front_kernel, nz=nz, nf=nf, hidden=hidden, shared=shared, heads=heads, real=real),
        out_shape=(
            shape((SLOTS, width, 3 * HD), BF16),
            shape((SLOTS * HD, width), BF16),
            shape((count, dense, 2 * TAIL), BF16),
            shape((width, HD), BF16),
            shape((1, width), F32),
            shape((1, width), F32),
            shape((count, rows, HD), BF16),
            shape((rows, HD), F32),
            shape((length, HD), jnp.int32),
            shape((8, length), jnp.int32),
            shape((length, width), BF16),
            shape((length, 3 * SLOTS * HD), BF16),
            shape((length, SLOTS * HD), BF16),
            shape((length, SLOTS * HD), F32),
            shape((rows, width), F32),
            shape((rows, width), BF16),
            shape((1, 8, rows, width), BF16),
            shape((nz, 8, rows, width), BF16),
            shape((nz, up_rows, 4 * hidden), BF16),
        ),
        in_specs=[VMEM] * 13,
        out_specs=(ANY, VMEM, ANY, VMEM, VMEM, VMEM, ANY, VMEM, VMEM, VMEM) + (ANY,) * 4 + (VMEM,) * 2 + (ANY,) * 3,
        scratch_shapes=[
            pltpu.VMEM((SLOTS, width, 3 * HD), BF16),
            pltpu.VMEM((count, dense, 2 * TAIL), BF16),
            pltpu.VMEM((count, rows, HD), BF16),
            pltpu.VMEM((length, width), BF16),
            pltpu.VMEM((length, 3 * SLOTS * HD), BF16),
            pltpu.VMEM((length, SLOTS * HD), BF16),
            pltpu.VMEM((length, SLOTS * HD), F32),
            pltpu.VMEM((eids.shape[0] + 1, rows), jnp.int32),
            pltpu.SemaphoreType.DMA((7,)),
            pltpu.VMEM((8, rows, width), BF16),
            pltpu.VMEM((SLOTS, count, dense, 3 * HD), BF16),
            pltpu.VMEM((8, dense, width), BF16),
            pltpu.VMEM((nz, dense, 3 * width), BF16),
            pltpu.VMEM((nz, dense, width), BF16),
            pltpu.VMEM((count, eids.shape[0] + 1, rows), jnp.int32),
            pltpu.VMEM((nz, 8, SLOTS, dense, 3 * HD), BF16),
            pltpu.VMEM((count, dense, 2 * TAIL), BF16),
            pltpu.VMEM((8, rows, width), BF16),
            pltpu.VMEM((8 * dense, width), F32),
            pltpu.VMEM((nz, up_rows, 4 * hidden), BF16),
            *Reduce.scratch(1, rows, width),
            *pair_of(7),
            pltpu.SemaphoreType.DMA((2, count)),
            pltpu.SemaphoreType.DMA((2, count)),
            pltpu.SemaphoreType.DMA((nz, 8, SLOTS)),
            pltpu.SemaphoreType.DMA((nz, 8, SLOTS)),
            pltpu.SemaphoreType.DMA((nz, 8)),
            pltpu.SemaphoreType.DMA((8,)),
            *pair_of(nz),
            *pair_of(nz),
            *pair_of(Reduce.copies(1)),
            *pair_of(Gather.copies(nz)),
            *pair_of(Gather.copies(1)),
            *pair_of(nz),
            pltpu.SemaphoreType.DMA((3,)),
        ],
        compiler_params=pltpu.CompilerParams(
            collective_id=1, has_side_effects=True, vmem_limit_bytes=58 * 2**20
        ),
        name="front",
    )(tok, wqkv, wout, router, sup, again, fgain, eids, seg, cosine, sine, og, eup)


def route_grads(gx, og, mixed, normed, router, marks, gain):
    width = mixed.shape[1]
    scale = rms_scale(mixed)
    normal = mixed * scale
    logits = jnp.where(marks > 0.5, dot(normed, router), NEG)
    weights = jnp.exp(logits - jnp.max(logits, axis=-1, keepdims=True))
    probs = weights / jnp.sum(weights, axis=-1, keepdims=True)
    grad_gates = gx[:, width:]
    grad_logits = (probs * (grad_gates - jnp.sum(probs * grad_gates, axis=-1, keepdims=True))).astype(BF16)
    grad_router = dot_tn(normed, grad_logits)
    grad_normed = gx[:, :width] + dot_nt(grad_logits, router)
    ones = jnp.where(lax.broadcasted_iota(jnp.int32, (mixed.shape[0], HD), 1) == TAIL - 1, 1.0, 0.0)
    grad_gain = lax.dot_general(
        grad_normed * normal, ones, (((0,), (0,)), ((), ())),
        precision=lax.Precision.HIGHEST, preferred_element_type=F32,
    )
    grad_mixed = og.astype(F32) + norm_back(grad_normed, normal, scale, gain)
    return grad_mixed, pltpu.roll(grad_router + grad_gain, TAIL, 1)


def experts_kernel(
    normed_ref, plane_ref, all_grad_ref, mark_ref, own_ref, eup_ref, tail_ref, edown_ref, sdown_ref,
    og_ref, mixed_ref, router_ref, own_mark_ref, gain_ref,
    out_any, low_ref, gm_ref, small_ref, geup_ref, gedown_ref, gsdown_ref, all_normed_ref,
    out_ref,
    up_ref, upt_ref, down_ref, downt_ref, gup_ref, gdown_ref,
    xt, gt, px, po, *refs, nz, hidden, shared,
):
    bufs, (tile_sems, rs, rr, os_, or_, xs, xr, own_sems) = refs[:4], refs[4:]
    z, f = place()
    rows, width = mixed_ref.shape
    half = down_ref.shape[0]
    pair = 2 * hidden
    greet(near_devices(z, f) + z_devices(z, f, nz))
    own = pltpu.make_async_copy(normed_ref, spot(all_normed_ref, z, f), own_sems.at[0])
    own.start()
    gather = Gather(all_normed_ref, (xs, xr), nz, z, f)
    reduce = Reduce(bufs, (rs, rr), nz, z, f)
    outs = Reduce([out_ref, out_ref, out_ref, out_ref], (os_, or_), nz, z, f)
    own.wait()
    gather.along_z(1)
    ffn_weights(eup_ref, tail_ref, edown_ref, sdown_ref, up_ref, upt_ref, down_ref, downt_ref)
    gup_ref[...] = jnp.zeros_like(gup_ref)
    gdown_ref[...] = jnp.zeros_like(gdown_ref)
    gather.along_z(2)
    if nz > 1:
        gather.first(1)

    def where(i):
        j, t = i // 4, i % 4
        base = f + (1 - 2 * (f % 2)) * (1 - t // 2) + (4 - 8 * (f // 4 % 2)) * (t % 2)
        return lax.rem(z - away(j, nz) + nz, nz), base // 4, base % 2

    def loads(i, rows_ref=all_normed_ref):
        piece, y, core = where(i)
        there = piece if rows_ref is all_normed_ref else 0
        slot = i % 2
        return [
            pltpu.make_async_copy(rows_ref.at[there, y, :, core], xt.at[slot], tile_sems.at[slot, 0]),
            pltpu.make_async_copy(all_grad_ref.at[piece, y, :, core], gt.at[slot], tile_sems.at[slot, 1]),
        ]

    for copy in loads(0, plane_ref):
        copy.start()
    last = 4 * nz - 1

    def tile(i, _):
        j, t = i // 4, i % 4
        more = j < nz - 1

        @pl.when((t == 0) & more)
        def _():
            gather.second(j + 1)

        @pl.when(i == 1)
        def _():
            gather.along_z(3)

        @pl.when((t == 2) & more)
        def _():
            gather.third(j + 1)

        @pl.when((t == 2) & (j < nz - 2))
        def _():
            gather.first(j + 2)

        @pl.when((t == 3) & more)
        def _():
            gather.fourth(j + 1)

        @pl.when((t == 0) & (j > 0))
        def _():
            for k in range(4):
                reduce.core(j - 1, k, px.at[k]).wait_send()
                outs.core(j - 1, k, po.at[k]).wait_send()

        for copy in loads(i):
            copy.wait()

        @pl.when(i < 3)
        def _():
            for copy in loads(i + 1, plane_ref):
                copy.start()

        @pl.when((i >= 3) & (i < last))
        def _():
            for copy in loads(i + 1):
                copy.start()

        piece, y, core = where(i)
        marks = jnp.concatenate([mark_ref[piece, 4 * y + core], mark_ref[piece, 4 * y + 2 + core]], axis=0)
        x, g = xt[i % 2].reshape(2 * rows, width), gt[i % 2].reshape(2 * rows, width)
        out, gx, grad_pre, acts = ffn_rows(
            x, g, marks, own_ref[...], up_ref, upt_ref, down_ref, downt_ref, hidden, shared
        )
        x_at = f // 2 % 2
        for b in range(2):
            at = 2 * t + (1 - x_at if b else x_at)
            po[at] = out[b * rows : (b + 1) * rows]
            px[at] = gx[b * rows : (b + 1) * rows]
        gup_ref[...] += dot_tn(x, grad_pre)
        gdown_ref[...] += dot_tn(acts, g)

        @pl.when(t == 1)
        def _():
            for k in range(4):
                reduce.core(j, k, px.at[k]).start()
            for k in range(4):
                outs.core(j, k, po.at[k]).start()

        @pl.when((t == 1) & (j > 0))
        def _():
            reduce.far(j - 1)

        @pl.when((t == 2) & (j > 0))
        def _():
            reduce.along_z(j - 1)

        @pl.when(t == 3)
        def _():
            for k in range(4):
                reduce.core(j, k, None).wait_recv()
                reduce.by_core[j, k] = reduce.by_core[j, k] + px[4 + k]
            reduce.send_near(j)
            for k in range(4):
                outs.core(j, k, None).wait_recv()
                out_ref[j, k] = out_ref[j, k] + po[4 + k]

        return 0

    lax.fori_loop(0, 4 * nz, tile, 0)
    up_ref[:, : 2 * pair] = jnp.concatenate([gup_ref[:, :pair], gup_ref[:, half : half + pair]], axis=1).astype(BF16)
    up_rows = width // nz
    ends = [
        pltpu.make_async_copy(up_ref.at[pl.ds(p * up_rows, up_rows), pl.ds(0, 2 * pair)], geup_ref.at[p], own_sems.at[p])
        for p in range(nz)
    ]
    ends.append(pltpu.make_async_copy(gdown_ref.at[pl.ds(0, pair)], gedown_ref, own_sems.at[nz]))
    ends.append(pltpu.make_async_copy(out_ref, out_any, own_sems.at[nz + 1]))
    for copy in ends:
        copy.start()
    reduce.far(nz - 1)
    gtail = jnp.concatenate([gup_ref[:, half - TAIL : half], gup_ref[:, 2 * half - TAIL :]], axis=1)
    gsdown_ref[...] = gdown_ref[half - TAIL : half - TAIL + shared, :]
    reduce.along_z(nz - 1)
    grad_mixed, small = route_grads(
        reduce.total(), og_ref[...], mixed_ref[...], normed_ref[...], router_ref[...], own_mark_ref[...], gain_ref[...]
    )
    gm_ref[...] = grad_mixed
    low_ref[...] = grad_mixed.astype(BF16)
    small_ref[...] = (small + gtail).astype(BF16)
    for k in range(4):
        reduce.core(nz - 1, k, px.at[k]).wait_send()
        outs.core(nz - 1, k, po.at[k]).wait_send()
    for copy in ends:
        copy.wait()
    for j in range(4, nz + 1):
        gather.along_z(j)
    gather.end(1)
    reduce.end()


def experts_turn(
    normed, plane, all_grad, marks, own, eup, tail, edown, sdown, og, mixed, router, own_marks, gain, nz, nf
):
    rows, width = mixed.shape
    pair, shared = edown.shape[0], sdown.shape[0]
    half = up_to(pair + TAIL, HD)
    wide = width + HD
    return pl.pallas_call(
        functools.partial(experts_kernel, nz=nz, hidden=pair // 2, shared=shared),
        out_shape=(
            jax.ShapeDtypeStruct((nz, 4, rows, width), BF16),
            jax.ShapeDtypeStruct((rows, width), BF16),
            jax.ShapeDtypeStruct((rows, width), F32),
            jax.ShapeDtypeStruct((width, HD), BF16),
            jax.ShapeDtypeStruct((nz, width // nz, 2 * pair), BF16),
            jax.ShapeDtypeStruct((pair, width), F32),
            jax.ShapeDtypeStruct((shared, width), F32),
            jax.ShapeDtypeStruct((nz, 2, 2, 2, rows, width), BF16),
        ),
        in_specs=[VMEM, ANY, ANY, VMEM] + [VMEM] * 10,
        out_specs=(ANY, VMEM, VMEM, VMEM, ANY, ANY, VMEM, ANY),
        scratch_shapes=[
            pltpu.VMEM((nz, 4, rows, width), BF16),
            pltpu.VMEM((width, 2 * half), BF16),
            pltpu.VMEM((2 * half, width), BF16),
            pltpu.VMEM((half, width), BF16),
            pltpu.VMEM((width, half), BF16),
            pltpu.VMEM((width, 2 * half), F32),
            pltpu.VMEM((half, width), F32),
            pltpu.VMEM((2, 2, rows, width), BF16),
            pltpu.VMEM((2, 2, rows, width), BF16),
            pltpu.VMEM((8, rows, wide), BF16),
            pltpu.VMEM((8, rows, width), BF16),
            *Reduce.scratch(nz, rows, wide),
            pltpu.SemaphoreType.DMA((2, 2)),
            *pair_of(Reduce.copies(nz)),
            *pair_of(Reduce.copies(nz)),
            *pair_of(Gather.copies(nz)),
            pltpu.SemaphoreType.DMA((nz + 2,)),
        ],
        compiler_params=pltpu.CompilerParams(
            collective_id=3, has_side_effects=True, vmem_limit_bytes=60 * 2**20
        ),
        name="experts_turn",
    )(
        normed, plane.reshape(1, 2, 2, 2, rows, width), all_grad.reshape(nz, 2, 2, 2, rows, width),
        marks.reshape(nz, 8, rows, HD), own, eup, tail, edown, sdown, og, mixed, router, own_marks, gain
    )[:7]


def back_kernel(
    low_ref, geup_ref, *refs, nz, nf, heads, real,
):
    sources, refs = refs[:11], refs[11:]
    (wo_ref, w_ref, normed_ref, qkv_ref, attn_ref, lse_ref, cos_ref, sin_ref, segq_ref, segk_ref, out_ref), refs = (
        refs[-12:-1],
        refs[:-12] + refs[-1:],
    )
    back_body(sources, low_ref, geup_ref, wo_ref, w_ref, normed_ref, qkv_ref, attn_ref, lse_ref, cos_ref, sin_ref,
              segq_ref, segk_ref, out_ref, *refs, nz=nz, nf=nf, heads=heads, real=real)


def back_body(
    sources, low_ref, geup_ref, wo_ref, w_ref, normed_ref, qkv_ref, attn_ref, lse_ref, cos_ref, sin_ref, segq_ref, segk_ref,
    out_ref, small_ref, tok_ref, mixed_ref, own_gm_ref, gain_ref,
    block_ref, gtok_ref, gwqkv_ref, gwout_ref, all_small_ref, pieces_ref,
    seq, gkv_ref, gqkv_ref, wt_ref, part_ref, gw_ref, gwo_ref, gq, gob, gpk, gz, smalls, *refs, nz, nf, heads, real,
):
    bufs, refs = refs[:7], refs[7:]
    rs, rr, os_, or_, all_s, all_r, q_s, q_r, wo_s, wo_r, zs, zr, gs, gr, es, er, own_sems, in_sems = refs
    local = (wo_ref, w_ref, normed_ref, qkv_ref, attn_ref, lse_ref, cos_ref, sin_ref, segq_ref, segk_ref, out_ref)
    loads = [pltpu.make_async_copy(src, dst, in_sems.at[k]) for k, (src, dst) in enumerate(zip(sources, local))]
    for copy in loads:
        copy.start()
    z, f = place()
    me, count = z * nf + f, nz * nf
    dense = gw_ref.shape[2]
    rows, width = tok_ref.shape
    length = 8 * rows
    greet_all(nz, nf)
    seq[0, f] = low_ref[...]
    turned = Gather(seq, (gs, gr), 1, z, f)
    turned.first(0, own=True)
    ups = []
    for j in range(1, nz):
        there = lax.rem(z + j, nz)
        ups.append(send(geup_ref.at[there], pieces_ref.at[z], (es, er), j, (there, f)))
    ups.append(pltpu.make_async_copy(geup_ref.at[z], pieces_ref.at[z], own_sems.at[0]))
    for copy in ups:
        copy.start()
    turned.second(0)
    outs = Reduce([out_ref, *bufs[4:]], (os_, or_), nz, z, f)
    order = list(range(1, nz)) + [0]
    loads[10].wait()
    outs.send_near(order[0])
    turned.third(0)

    def two(m):
        return first_head(m + 1) - first_head(m) == 2

    def small_copy(d):
        return pltpu.make_async_remote_copy(
            small_ref.at[d], smalls.at[me], all_s.at[d], all_r.at[me], device_id=(d // nf, d % nf), device_id_type=MESH
        )

    def small_came(d):
        return pltpu.make_async_remote_copy(
            smalls.at[d], smalls.at[d], all_s.at[d], all_r.at[d], device_id=(d // nf, d % nf), device_id_type=MESH
        )

    def q_copy(p, m, s):
        return pltpu.make_async_remote_copy(
            gw_ref.at[s, p * nf + m], gq.at[p, f, s], q_s.at[p, m, s], q_r.at[p, f, s],
            device_id=(z, m), device_id_type=MESH,
        )

    def q_came(p, m, s):
        dst = gq.at[p, m, s]
        return pltpu.make_async_remote_copy(
            dst, dst, q_s.at[p, m, s], q_r.at[p, m, s], device_id=(z, m), device_id_type=MESH
        )

    def owner_of(block):
        return head_owner(block * dense // HD)

    low, high = out_blocks(f, dense)

    def out_copy(i):
        d = low + i
        k = 2 * (d // nf) + f - owner_of(d)
        return pltpu.make_async_remote_copy(
            gwo_ref.at[i], gob.at[k], wo_s.at[i], wo_r.at[k], device_id=(z, d % nf), device_id_type=MESH
        )

    for copy in loads[:10]:
        copy.wait()
    turned.fourth(0)
    spare = gwo_ref.shape[0] * dense
    wide = up_to(spare, HD)
    shift = first_head(f) * HD - low * dense
    moved = jnp.concatenate([attn_ref[...].astype(F32), jnp.zeros((length, wide - SLOTS * HD), F32)], axis=1)
    moved = pltpu.roll(moved, shift, 1).astype(BF16)
    gwo_ref[...] = dot_tn(moved, seq[0].reshape(length, width))[:spare].reshape(gwo_ref.shape).astype(BF16)

    def start_small(i, _):
        small_copy((me + i) % count).start()
        return 0

    lax.fori_loop(1, count, start_small, 0)
    smalls[me] = small_ref[me]

    def start_out(i, _):
        d = low + i

        @pl.when((d <= high) & (d % nf != f))
        def _():
            out_copy(i).start()

        @pl.when((d <= high) & (d % nf == f))
        def _():
            gob[2 * (d // nf) + f - owner_of(d)] = gwo_ref[i]

        return 0

    lax.fori_loop(0, gwo_ref.shape[0], start_out, 0)
    gkv_ref[...] = jnp.zeros_like(gkv_ref)
    block = 256
    for i in range(length // block):
        attn_back_block(
            i, block, seq[0, i * block // rows : (i + 1) * block // rows].reshape(block, width), wo_ref, qkv_ref, attn_ref, lse_ref, cos_ref, sin_ref, segq_ref, segk_ref, gkv_ref, gqkv_ref
        )
        if i + 1 < nz:
            outs.send_near(order[i + 1])
    attn_back_keys(w_ref, cos_ref, sin_ref, gkv_ref, gqkv_ref, wt_ref)
    if nz > 0:
        outs.far(order[0])
    if nz > 1:
        outs.far(order[1])
    step = 3 * HD
    reduce = Reduce(bufs[:4], (rs, rr), 1, z, f)
    for i in range(length // block):
        mine = slice(i * block, (i + 1) * block)
        at = i * block // rows
        part_ref[at : at + block // rows] = (
            dot(gqkv_ref[mine, :], wt_ref[...]).astype(BF16).reshape(block // rows, rows, width)
        )
    for i in range(4):
        reduce.core(0, i, part_ref.at[flip(f, 1 | 2 * i)]).start()
    if nz > 2:
        outs.far(order[2])
    if nz > 3:
        outs.far(order[3])

    def weights(s):
        value = dot_tn(normed_ref[...], gqkv_ref[:, s * step : (s + 1) * step])
        gw_ref[s] = value.reshape(count, dense, step).astype(BF16)

        def start(i, _):
            for p in range(nz):
                q_copy(p, (f + i) % nf, s).start()
            return 0

        lax.fori_loop(1, nf, start, 0)
        for p in range(nz):
            gq[p, f, s] = gw_ref[s, p * nf + f]

    weights(0)
    for i in range(4):
        reduce.core(0, i, None).wait_recv()
        reduce.by_core[0, i] = reduce.by_core[0, i] + part_ref[flip(f, 2 * i)]
    reduce.send_near(0)
    if nz > 0:
        outs.along_z(order[0])
    if nz > 1:
        outs.along_z(order[1])

    @pl.when(two(f))
    def _():
        weights(1)

    if nz > 2:
        outs.along_z(order[2])
    reduce.far(0)
    if nz > 3:
        outs.along_z(order[3])

    def q_arrive(i, _):
        m = (f + i) % nf
        for p in range(nz):
            q_came(p, m, 0).wait_recv()

        @pl.when(two(m))
        def _():
            for p in range(nz):
                q_came(p, m, 1).wait_recv()

        return 0

    lax.fori_loop(1, nf, q_arrive, 0)

    def arrive_out(k, _):
        d = (k // 2) * nf + f
        source = owner_of(d) + k % 2
        last = head_owner((d * dense + dense - 1) // HD)

        @pl.when((source <= last) & (source != f))
        def _():
            pltpu.make_async_remote_copy(
                gob.at[k], gob.at[k], wo_s.at[0], wo_r.at[k], device_id=(z, flip(f, 1)), device_id_type=MESH
            ).wait_recv()

        return 0

    lax.fori_loop(0, 2 * nz, arrive_out, 0)
    for p in range(nz):
        for m in range(8):
            for s in range(SLOTS):
                if real[m * SLOTS + s]:
                    at = heads[m * SLOTS + s] * HD
                    for c in range(3):
                        gpk[p, :, c * width + at : c * width + at + HD] = gq[p, m, s, :, c * HD : (c + 1) * HD]
        d = p * nf + f
        gpk[p, :, 3 * width :] = gob[2 * p]

        @pl.when(head_owner((d * dense + dense - 1) // HD) != owner_of(d))
        def _():
            gpk[p, :, 3 * width :] = gob[2 * p] + gob[2 * p + 1]

    alongs = []
    for j in range(1, nz):
        there = lax.rem(z + j, nz)
        copy = send(gpk.at[there], gz.at[z], (zs, zr), j, (there, f))
        copy.start()
        alongs.append(copy)
    gz[z] = gpk[z]
    reduce.along_z(0)
    x = tok_ref[...].astype(F32)
    scale = rms_scale(x)
    gtok_ref[...] = (
        own_gm_ref[...] + norm_back(reduce.by_far[0].astype(F32), x * scale, scale, gain_ref[...])
    ).astype(BF16)
    block_ref[...] = (mixed_ref[...] + outs.total()).astype(BF16)

    def finish(i, _):
        d = (me + i) % count
        small_came(d).wait_recv()
        small_copy(d).wait_send()
        return 0

    lax.fori_loop(1, count, finish, 0)

    def q_left(i, _):
        m = (f + i) % nf
        for p in range(nz):
            q_copy(p, m, 0).wait_send()

        @pl.when(two(f))
        def _():
            for p in range(nz):
                q_copy(p, m, 1).wait_send()

        return 0

    lax.fori_loop(1, nf, q_left, 0)

    def out_left(i, _):
        @pl.when((low + i <= high) & ((low + i) % nf != f))
        def _():
            out_copy(i).wait_send()

        return 0

    lax.fori_loop(0, gwo_ref.shape[0], out_left, 0)
    for copy in alongs:
        copy.wait()
    gwqkv_ref[...] = sum(gz[p, :, : 3 * width].astype(F32) for p in range(nz))
    gwout_ref[...] = sum(gz[p, :, 3 * width :].astype(F32) for p in range(nz))
    all_small_ref[...] = smalls[...]
    for i in range(4):
        reduce.core(0, i, part_ref.at[0]).wait_send()
    reduce.end()
    outs.end()
    turned.end()
    for copy in ups:
        copy.wait()


def back(
    low, geup, wo, w, normed, qkv, attn, lse, cosine, sine, segq, segk, out_part, small, tok, mixed, own_gm, gain, nz, nf
):
    rows, width = tok.shape
    length, count = 8 * rows, nz * nf
    dense = width // count
    heads, real = head_table(8)
    return pl.pallas_call(
        functools.partial(back_kernel, nz=nz, nf=nf, heads=heads, real=real),
        out_shape=(
            jax.ShapeDtypeStruct((rows, width), BF16),
            jax.ShapeDtypeStruct((rows, width), BF16),
            jax.ShapeDtypeStruct((dense, 3 * width), F32),
            jax.ShapeDtypeStruct((dense, width), F32),
            jax.ShapeDtypeStruct((count, dense, HD), BF16),
            jax.ShapeDtypeStruct(geup.shape, BF16),
        ),
        in_specs=[VMEM] + [ANY] * 12 + [VMEM] * 5,
        out_specs=(VMEM,) * 5 + (ANY,),
        scratch_shapes=[
            pltpu.VMEM((1, 8, rows, width), BF16),
            pltpu.VMEM((length, 2 * SLOTS * HD), F32),
            pltpu.VMEM((length, 3 * SLOTS * HD), BF16),
            pltpu.VMEM((3 * SLOTS * HD, width), BF16),
            pltpu.VMEM((8, rows, width), BF16),
            pltpu.VMEM((SLOTS, count, dense, 3 * HD), BF16),
            pltpu.VMEM((8, dense, width), BF16),
            pltpu.VMEM((nz, 8, SLOTS, dense, 3 * HD), BF16),
            pltpu.VMEM((2 * nz, dense, width), BF16),
            pltpu.VMEM((nz, dense, 4 * width), BF16),
            pltpu.VMEM((nz, dense, 4 * width), BF16),
            pltpu.VMEM((count, dense, HD), BF16),
            *Reduce.scratch(1, rows, width),
            *Reduce.scratch(nz, rows, width)[1:],
            *pair_of(Reduce.copies(1)),
            *pair_of(Reduce.copies(nz)),
            *pair_of(count),
            pltpu.SemaphoreType.DMA((nz, 8, SLOTS)),
            pltpu.SemaphoreType.DMA((nz, 8, SLOTS)),
            pltpu.SemaphoreType.DMA((8,)),
            pltpu.SemaphoreType.DMA((2 * nz,)),
            *pair_of(nz),
            *pair_of(Gather.copies(1)),
            *pair_of(nz),
            pltpu.SemaphoreType.DMA((1,)),
            *[pltpu.VMEM(a.shape, a.dtype) for a in (wo, w, normed, qkv, attn, lse, cosine, sine, segq, segk, out_part)],
            pltpu.SemaphoreType.DMA((11,)),
        ],
        compiler_params=pltpu.CompilerParams(
            collective_id=4, has_side_effects=True, vmem_limit_bytes=60 * 2**20
        ),
        name="back",
    )(
        low, geup, wo, w, normed, qkv, attn, lse, cosine, sine, segq, segk, out_part,
        small.reshape(count, dense, HD), tok, mixed, own_gm, gain,
    )


def unpack_kernel(
    pieces_ref, small_ref, wqkv_ref, gwqkv_ref, gain_ref, block_in, tok_in, wout_in, edown_in, sdown_in,
    geup_ref, gsup_ref, grouter_ref, gone_ref, gtwo_ref, block_ref, tok_ref, gqkv_ref, wout_ref, edown_ref, sdown_ref,
    *, shared, experts,
):
    for src, dst in (
        (block_in, block_ref), (tok_in, tok_ref), (gwqkv_ref, gqkv_ref), (wout_in, wout_ref), (edown_in, edown_ref),
        (sdown_in, sdown_ref),
    ):
        dst[...] = src[...]
    nz = pieces_ref.shape[0]
    hidden = pieces_ref.shape[2] // 4
    for t in range(nz):
        for g in range(2):
            for e in range(2):
                at = (2 * g + e) * hidden
                to = (g * nz + t) * hidden
                geup_ref[e, :, to : to + hidden] = pieces_ref[t, :, at : at + hidden].astype(F32)
    count = small_ref.shape[0]
    total = small_ref[0].astype(F32)
    for d in range(count):
        if d:
            total = total + small_ref[d].astype(F32)
        for g in range(2):
            to = (g * count + d) * shared
            gsup_ref[:, to : to + shared] = small_ref[d, :, g * TAIL : g * TAIL + shared].astype(F32)
    grouter_ref[...] = total[:, shared : shared + experts].T
    one = jnp.sum(wqkv_ref[...].astype(F32) * gwqkv_ref[...], axis=-1, keepdims=True) / gain_ref[...].astype(F32).T
    gone_ref[...] = one.T
    gtwo_ref[...] = total[:, HD - 1 :].T


def unpack(pieces, small, wqkv, gwqkv, gain, rest, shared, experts):
    nz, up_rows, packed = pieces.shape
    count, dense, _ = small.shape
    return pl.pallas_call(
        functools.partial(unpack_kernel, shared=shared, experts=experts),
        out_shape=(
            jax.ShapeDtypeStruct((2, up_rows, nz * packed // 2), F32),
            jax.ShapeDtypeStruct((dense, 2 * count * shared), F32),
            jax.ShapeDtypeStruct((experts, dense), F32),
            jax.ShapeDtypeStruct((1, dense), F32),
            jax.ShapeDtypeStruct((1, dense), F32),
            *[jax.ShapeDtypeStruct(a.shape, a.dtype) for a in (*rest[:2], gwqkv, *rest[2:])],
        ),
        in_specs=[VMEM] * 10,
        out_specs=(VMEM,) * 11,
        compiler_params=pltpu.CompilerParams(vmem_limit_bytes=60 * 2**20),
        name="unpack",
    )(pieces, small, wqkv, gwqkv, gain, *rest)


def tables():
    pos = np.arange(SEQ, dtype=np.float32)
    freqs = np.float32(ROPE) ** (-np.arange(HD // 2, dtype=np.float32) * np.float32(2.0 / HD))
    angles = (pos[:, None] * freqs[None, :]).astype(np.float32)
    cosine = np.concatenate([np.cos(angles)] * 2, axis=1).astype(np.float32)
    sine = np.concatenate([-np.sin(angles), np.sin(angles)], axis=1).astype(np.float32)
    return jnp.asarray(cosine), jnp.asarray(sine)


def local_near(
    mesh, tokens, out_grad, segment_ids, expert_ids, attn_gain, ffn_gain, w_qkv, w_out,
    w_router, w_shared_up, w_shared_down, w_expert_up, w_expert_down,
):
    nz, nf = mesh.shape["dp"], mesh.shape["fsdp"]
    rows, width = tokens.shape
    experts = w_router.shape[1]
    hidden, shared = w_expert_down.shape[1], w_shared_down.shape[0]
    f = lax.axis_index("fsdp")
    cosine, sine = tables()
    (
        w, wo, tail, router, gain_one, gain_two, marks, own_marks, segq, segk, normed_one, qkv, attn, lse, mixed, normed,
        plane, all_grad, pieces,
    ) = front(
        tokens, w_qkv, w_out, w_router.T, w_shared_up, attn_gain[None], ffn_gain[None], expert_ids.T,
        segment_ids[None], cosine, sine, out_grad, w_expert_up, nz, nf, shared,
    )
    tail = tail.reshape(width, 2 * TAIL)
    lane = jnp.arange(HD, dtype=jnp.int32) - TAIL - shared
    own = (lane[None, :] == (2 * f + jnp.arange(2, dtype=jnp.int32))[:, None]).astype(F32)
    out_part, low, grad_mixed, small, geup, gedown, gsdown = experts_turn(
        normed, plane, all_grad, marks, own, pieces.reshape(width, 4 * hidden), tail,
        w_expert_down.reshape(2 * hidden, width), w_shared_down, out_grad, mixed, router, own_marks, gain_two, nz, nf,
    )
    block_out, tokens_grad, grad_wqkv, grad_wout, smalls, gpieces = back(
        low, geup, wo, w, normed_one, qkv, attn, lse, cosine, sine, segq, segk, out_part, small,
        tokens, mixed, grad_mixed, gain_one, nz, nf,
    )
    (
        grad_eup, grad_sup, grad_router, grad_one, grad_two, block_out, tokens_grad, grad_wqkv, grad_wout, gedown, gsdown,
    ) = unpack(
        gpieces, smalls, w_qkv, grad_wqkv, attn_gain[None], (block_out, tokens_grad, grad_wout, gedown, gsdown),
        shared, experts,
    )
    return (
        block_out, tokens_grad, grad_one[0], grad_two[0], grad_wqkv, grad_wout, grad_router.T, grad_sup,
        gsdown, grad_eup, gedown.reshape(2, hidden, width),
    )


def local_far(
    mesh, tokens, out_grad, segment_ids, expert_ids, attn_gain, ffn_gain, w_qkv, w_out,
    w_router, w_shared_up, w_shared_down, w_expert_up, w_expert_down,
):
    nz, nf = mesh.shape["dp"], mesh.shape["fsdp"]
    nd = nz * nf
    rows, width = tokens.shape
    group = SEQ // rows
    experts = w_router.shape[1]
    dense = w_qkv.shape[0]
    hidden, shared = w_expert_down.shape[1], w_shared_down.shape[0]
    up_rows = w_expert_up.shape[1]
    both = ("dp", "fsdp")
    groups = None if nf == group else [[a + i for i in range(group)] for a in range(0, nf, group)]
    f = lax.axis_index("fsdp")
    member = lax.rem(f, group)
    heads, real = head_table(group)

    by_head = w_qkv.reshape(dense, 3, HEADS, HD)
    empty = jnp.zeros((dense, 3, HD), BF16)
    cols = jnp.stack([by_head[:, :, h] if r else empty for h, r in zip(heads, real)], axis=0)
    cols = cols.reshape(group, SLOTS, dense, 3 * HD)
    cols = jnp.tile(cols, (nf // group, 1, 1, 1))
    cols = lax.all_to_all(cols, "fsdp", 0, 0, tiled=True)
    w = lax.all_gather(cols, "dp", axis=0, tiled=True).transpose(1, 0, 2, 3).reshape(SLOTS, width, 3 * HD)
    full_out = lax.all_gather(w_out, both, axis=0, tiled=True)
    first = HEADS * member // group
    own_real = (first + jnp.arange(SLOTS) < HEADS * (member + 1) // group).astype(BF16)
    padded = jnp.pad(full_out, ((0, (SLOTS - 1) * HD), (0, 0)))
    wo = lax.dynamic_slice(padded, (first * HD, 0), (SLOTS * HD, width))
    wo = wo * jnp.repeat(own_real, HD)[:, None]
    gains = lax.all_gather(jnp.stack([attn_gain, ffn_gain], axis=1).astype(F32), both, axis=0, tiled=True)
    gain_one, gain_two = gains[:, 0], gains[:, 1]
    router = lax.all_gather(w_router, both, axis=0, tiled=True)
    sup = w_shared_up.reshape(dense, 2, nd, shared).transpose(2, 0, 1, 3).reshape(nd, dense, 2 * shared)
    sup = lax.all_to_all(sup, both, 0, 0, tiled=True).reshape(width, 2, shared)
    eup = w_expert_up.reshape(2, up_rows, 2, nz, hidden).transpose(3, 1, 2, 0, 4)
    eup = lax.all_to_all(eup, "dp", 0, 0, tiled=True).reshape(width, 4 * hidden)
    rest = jnp.zeros((width, TAIL - shared), BF16)
    tail = jnp.concatenate([sup[:, 0], router, rest[:, experts:], sup[:, 1], rest], axis=1)
    chosen = jnp.any(expert_ids[:, :, None] == jnp.arange(experts, dtype=jnp.int32), axis=1)
    at = TAIL + shared
    marks = jnp.pad(chosen.astype(BF16), ((0, 0), (at, HD - experts - at)))
    marks = lax.all_gather(marks, both, axis=0, tiled=True)
    lane = jnp.arange(HD, dtype=jnp.int32)
    own = (lane[None, :] == (at + 2 * f + jnp.arange(2, dtype=jnp.int32))[:, None]).astype(F32)
    cosine, sine = tables()
    seg = lax.all_gather(segment_ids, "fsdp", axis=0, tiled=True, axis_index_groups=groups)
    segq = jnp.broadcast_to(seg[:, None], (SEQ, HD))
    segk = jnp.broadcast_to(seg[None, :], (8, SEQ))

    seq_tokens = lax.all_gather(tokens, "fsdp", axis=0, tiled=True, axis_index_groups=groups)
    part, normed_one, qkv, attn, lse = attn_forward(
        seq_tokens, gain_one[None, :], w, wo, cosine, sine, segq, segk
    )
    projected = lax.psum_scatter(part, "fsdp", scatter_dimension=0, tiled=True, axis_index_groups=groups)
    inputs = tokens.astype(F32)
    mixed = inputs + projected.astype(F32)
    scale_two = rms_scale(mixed)
    normal_two = mixed * scale_two
    normed_two = (normal_two * gain_two).astype(BF16)
    all_normed = lax.all_gather(normed_two, both, axis=0, tiled=True)
    all_grad = lax.all_gather(out_grad, both, axis=0, tiled=True)
    out_part, gx_part, geup, gtail, gedown, gsdown = ffn(
        all_normed, all_grad, marks, own, eup, tail, w_expert_down.reshape(2 * hidden, width), w_shared_down
    )
    gx = lax.psum_scatter(gx_part, both, scatter_dimension=0, tiled=True).astype(F32)
    ffn_out = lax.psum_scatter(out_part, both, scatter_dimension=0, tiled=True).astype(F32)
    block_out = (mixed + ffn_out).astype(BF16)

    logits = jnp.where(chosen, dot(normed_two, router), NEG)
    probs = jax.nn.softmax(logits, axis=-1)
    grad_gates = gx[:, width + at : width + at + experts]
    grad_logits = (
        probs * (grad_gates - jnp.sum(probs * grad_gates, axis=-1, keepdims=True))
    ).astype(BF16)
    grad_router = dot_tn(normed_two, grad_logits)
    grad_normed = gx[:, :width] + dot_nt(grad_logits, router)
    grad_gain_two = jnp.sum(grad_normed * normal_two, axis=0)
    grad_mixed = out_grad.astype(F32) + norm_back(grad_normed, normal_two, scale_two, gain_two)

    seq_gm = lax.all_gather(grad_mixed.astype(BF16), "fsdp", axis=0, tiled=True, axis_index_groups=groups)
    part_back, gw, gwo = attn_backward(
        seq_gm, wo, w, normed_one, qkv, attn, lse, cosine, sine, segq, segk
    )
    grad_normed_one = lax.psum_scatter(
        part_back, "fsdp", scatter_dimension=0, tiled=True, axis_index_groups=groups
    ).astype(F32)
    scale_one = rms_scale(inputs)
    normal_one = inputs * scale_one
    grad_gain_one = jnp.sum(grad_normed_one * normal_one, axis=0)
    tokens_grad = (grad_mixed + norm_back(grad_normed_one, normal_one, scale_one, gain_one)).astype(BF16)

    gw = lax.psum_scatter(gw, "dp", scatter_dimension=1, tiled=True)
    gw = lax.all_to_all(gw.reshape(SLOTS, nf, dense, 3 * HD), "fsdp", 1, 1, tiled=True).astype(F32)
    gw = jnp.sum(gw.reshape(SLOTS, nf // group, group, dense, 3, HD), axis=1)
    picked = [gw[i % SLOTS, i // SLOTS] for i in range(group * SLOTS) if real[i]]
    grad_wqkv = jnp.stack(picked, axis=2).reshape(dense, 3 * width)
    gwo = gwo * jnp.repeat(own_real, HD)[:, None]
    all_gwo = jnp.zeros(((HEADS + SLOTS - 1) * HD, width), BF16)
    all_gwo = lax.dynamic_update_slice(all_gwo, gwo, (first * HD, 0))[: HEADS * HD]
    grad_wout = lax.psum_scatter(all_gwo, both, scatter_dimension=0, tiled=True).astype(F32)
    small = jnp.concatenate([grad_router, grad_gain_one[:, None], grad_gain_two[:, None]], axis=1)
    small = lax.psum_scatter(small, both, scatter_dimension=0, tiled=True)
    gsup = jnp.stack([gtail[:, :shared], gtail[:, TAIL : TAIL + shared]], axis=1)
    gsup = lax.all_to_all(gsup.reshape(nd, dense, 2 * shared).astype(BF16), both, 0, 0, tiled=True)
    grad_sup = gsup.reshape(nd, dense, 2, shared).transpose(1, 2, 0, 3).reshape(dense, 2 * nd * shared).astype(F32)
    geup = lax.all_to_all(geup.reshape(nz, up_rows, 2, 2, hidden), "dp", 0, 0, tiled=True)
    grad_eup = geup.transpose(3, 1, 2, 0, 4).reshape(2, up_rows, 2 * nz * hidden).astype(F32)
    return (
        block_out, tokens_grad, small[:, experts], small[:, experts + 1], grad_wqkv, grad_wout,
        small[:, :experts], grad_sup, gsdown, grad_eup, gedown.reshape(2, hidden, width),
    )


def solution(mesh):
    one, two = P(("dp", "fsdp")), P(("dp", "fsdp"), None)
    three = P("fsdp", "dp", None)

    def local(tokens, *rest):
        near = mesh.shape["fsdp"] == 8 == SEQ // tokens.shape[0] and mesh.shape["dp"] <= 4
        return (local_near if near else local_far)(mesh, tokens, *rest)

    return jax.shard_map(
        local,
        mesh=mesh,
        in_specs=(two, two, one, two, one, one, two, two, two, two, two, three, three),
        out_specs=(two, two, one, one, two, two, two, two, two, three, three),
        check_vma=False,
    )
```

```python
import functools

import jax
import jax.numpy as jnp
import numpy as np
from jax import lax
from jax.experimental import pallas as pl
from jax.experimental.pallas import tpu as pltpu
from jax.sharding import PartitionSpec as P

HEADS = 10
HD = 128
SEQ = 1024
SLOTS = 2
EPS = 1e-06
ROPE = 10000.0
NEG = -1e30
TAIL = 64
F32 = jnp.float32
BF16 = jnp.bfloat16


MESH = pl.DeviceIdType.MESH
VMEM = pl.BlockSpec(memory_space=pltpu.VMEM)
ANY = pl.BlockSpec(memory_space=pl.ANY)


def up_to(value, step):
    return -(-value // step) * step


def rms_scale(values):
    return lax.rsqrt(jnp.mean(values * values, axis=-1, keepdims=True) + EPS)


def norm_back(grad_normed, normal_rows, scale_rows, gain_rows):
    scaled = grad_normed * gain_rows
    return scale_rows * (
        scaled - normal_rows * jnp.mean(scaled * normal_rows, axis=-1, keepdims=True)
    )


def head_table(group):
    heads, real = [], []
    for i in range(group):
        own = list(range(HEADS * i // group, HEADS * (i + 1) // group))
        assert len(own) <= SLOTS
        heads += own + [0] * (SLOTS - len(own))
        real += [1] * len(own) + [0] * (SLOTS - len(own))
    return heads, real


def dot(a, b):
    return jnp.dot(a, b, preferred_element_type=F32)


def dot_nt(a, b):
    return lax.dot_general(a, b, (((1,), (1,)), ((), ())), preferred_element_type=F32)


def dot_tn(a, b):
    return lax.dot_general(a, b, (((0,), (0,)), ((), ())), preferred_element_type=F32)


def attn_project(i, block, x, gain, w_ref, cos_ref, sin_ref, normed_ref, qkv_ref):
    rows = pl.ds(pl.multiple_of(i * block, block), block)
    x = x.astype(F32)
    normed = (x * rms_scale(x) * gain).astype(BF16)
    normed_ref[rows, :] = normed
    cosine, sine = cos_ref[rows, :], sin_ref[rows, :]
    for s in range(SLOTS):
        proj = dot(normed, w_ref[s])
        for c in range(3):
            piece = proj[:, c * HD : (c + 1) * HD]
            if c < 2:
                piece = piece * cosine + pltpu.roll(piece, HD // 2, 1) * sine
            at = (3 * s + c) * HD
            qkv_ref[rows, at : at + HD] = piece.astype(BF16)


def attn_block(i, block, segq_ref, segk_ref, qkv_ref, attn_ref, lse_ref):
    scale = HD**-0.5
    rows = slice(i * block, (i + 1) * block)
    keys = (i + 1) * block
    row_pos = i * block + lax.broadcasted_iota(jnp.int32, (block, keys), 0)
    key_pos = lax.broadcasted_iota(jnp.int32, (block, keys), 1)
    allowed = (key_pos <= row_pos) & (segq_ref[rows, :1] == segk_ref[:1, :keys])
    outs = []
    for s in range(SLOTS):
        at = 3 * s * HD
        q = qkv_ref[rows, at : at + HD]
        k = qkv_ref[:keys, at + HD : at + 2 * HD]
        v = qkv_ref[:keys, at + 2 * HD : at + 3 * HD]
        scores = jnp.where(allowed, dot_nt(q, k) * scale, NEG)
        top = jnp.max(scores, axis=-1, keepdims=True)
        weights = jnp.exp(scores - top)
        total = jnp.sum(weights, axis=-1, keepdims=True)
        out = dot(weights.astype(BF16), v) / total
        lse_ref[rows, s * HD : (s + 1) * HD] = jnp.broadcast_to(top + jnp.log(total), (block, HD))
        low = out.astype(BF16)
        attn_ref[rows, s * HD : (s + 1) * HD] = low
        outs.append(low)
    return jnp.concatenate(outs, axis=-1)


def attn_forward_kernel(
    tok_ref, gain_ref, w_ref, wo_ref, cos_ref, sin_ref, segq_ref, segk_ref,
    part_ref, normed_ref, qkv_ref, attn_ref, lse_ref,
    *, block,
):
    count = tok_ref.shape[0] // block

    def project(i, _):
        x = tok_ref[pl.ds(pl.multiple_of(i * block, block), block), :]
        attn_project(i, block, x, gain_ref[...], w_ref, cos_ref, sin_ref, normed_ref, qkv_ref)
        return 0

    lax.fori_loop(0, count, project, 0)
    for i in range(count):
        outs = attn_block(i, block, segq_ref, segk_ref, qkv_ref, attn_ref, lse_ref)
        part_ref[i * block : (i + 1) * block, :] = dot(outs, wo_ref[...]).astype(BF16)


def attn_forward(tok, gain, w, wo, cosine, sine, segq, segk):
    length, width = tok.shape
    return pl.pallas_call(
        functools.partial(attn_forward_kernel, block=256),
        out_shape=(
            jax.ShapeDtypeStruct((length, width), BF16),
            jax.ShapeDtypeStruct((length, width), BF16),
            jax.ShapeDtypeStruct((length, 3 * SLOTS * HD), BF16),
            jax.ShapeDtypeStruct((length, SLOTS * HD), BF16),
            jax.ShapeDtypeStruct((length, SLOTS * HD), F32),
        ),
        in_specs=[VMEM] * 8,
        out_specs=(VMEM,) * 5,
        compiler_params=pltpu.CompilerParams(vmem_limit_bytes=56 * 2**20),
        cost_estimate=pl.CostEstimate(
            flops=2 * length * width * 4 * SLOTS * HD + 4 * SLOTS * HD * length * length,
            bytes_accessed=10 * length * width,
            transcendentals=SLOTS * length * length,
        ),
        name="attn_forward",
    )(tok, gain, w, wo, cosine, sine, segq, segk)


def attn_back_block(
    i, block, gm, wo_ref, qkv_ref, attn_ref, lse_ref, cos_ref, sin_ref, segq_ref, segk_ref, gkv_ref, gqkv_ref
):
    scale = HD**-0.5
    rows = slice(i * block, (i + 1) * block)
    keys = (i + 1) * block
    row_pos = i * block + lax.broadcasted_iota(jnp.int32, (block, keys), 0)
    key_pos = lax.broadcasted_iota(jnp.int32, (block, keys), 1)
    allowed = (key_pos <= row_pos) & (segq_ref[rows, :1] == segk_ref[:1, :keys])
    grad_attn = dot_nt(gm, wo_ref[...]).astype(BF16)
    for s in range(SLOTS):
        at = 3 * s * HD
        cut = slice(s * HD, (s + 1) * HD)
        q = qkv_ref[rows, at : at + HD]
        k = qkv_ref[:keys, at + HD : at + 2 * HD]
        v = qkv_ref[:keys, at + 2 * HD : at + 3 * HD]
        ga = grad_attn[:, cut]
        delta = jnp.sum(ga.astype(F32) * attn_ref[rows, cut].astype(F32), axis=-1, keepdims=True)
        scores = dot_nt(q, k) * scale
        probs = jnp.where(allowed, jnp.exp(scores - lse_ref[rows, s * HD : s * HD + 1]), 0.0)
        gs = (probs * (dot_nt(ga, v) - delta)).astype(BF16)
        gq = dot(gs, k) * scale
        gq = gq * cos_ref[rows, :] - pltpu.roll(gq, HD // 2, 1) * sin_ref[rows, :]
        gqkv_ref[rows, at : at + HD] = gq.astype(BF16)
        gkv_ref[:keys, 2 * s * HD : (2 * s + 1) * HD] += dot_tn(gs, q)
        gkv_ref[:keys, (2 * s + 1) * HD : (2 * s + 2) * HD] += dot_tn(probs.astype(BF16), ga)


def attn_back_keys(w_ref, cos_ref, sin_ref, gkv_ref, gqkv_ref, wt_ref):
    step = 3 * HD
    for s in range(SLOTS):
        at = s * step
        gk = gkv_ref[:, 2 * s * HD : (2 * s + 1) * HD] * HD**-0.5
        gk = gk * cos_ref[...] - pltpu.roll(gk, HD // 2, 1) * sin_ref[...]
        gqkv_ref[:, at + HD : at + 2 * HD] = gk.astype(BF16)
        gqkv_ref[:, at + 2 * HD : at + 3 * HD] = gkv_ref[:, (2 * s + 1) * HD : (2 * s + 2) * HD].astype(BF16)
        wt_ref[s * step : (s + 1) * step, :] = w_ref[s].T


def attn_backward_kernel(
    gm_ref, wo_ref, w_ref, normed_ref, qkv_ref, attn_ref, lse_ref, cos_ref, sin_ref,
    segq_ref, segk_ref,
    part_ref, gw_ref, gwo_ref,
    gkv_ref, gqkv_ref, wt_ref,
    *, block,
):
    count = gm_ref.shape[0] // block
    step = 3 * HD
    gkv_ref[...] = jnp.zeros_like(gkv_ref)
    for i in range(count):
        attn_back_block(
            i, block, gm_ref[i * block : (i + 1) * block, :], wo_ref, qkv_ref, attn_ref, lse_ref, cos_ref, sin_ref, segq_ref, segk_ref, gkv_ref, gqkv_ref
        )
    attn_back_keys(w_ref, cos_ref, sin_ref, gkv_ref, gqkv_ref, wt_ref)
    for i in range(count):
        rows = slice(i * block, (i + 1) * block)
        part_ref[rows, :] = dot(gqkv_ref[rows, :], wt_ref[...]).astype(BF16)
    for s in range(SLOTS):
        gw_ref[s] = dot_tn(normed_ref[...], gqkv_ref[:, s * step : (s + 1) * step]).astype(BF16)
    gwo_ref[...] = dot_tn(attn_ref[...], gm_ref[...]).astype(BF16)


def attn_backward(gm, wo, w, normed, qkv, attn, lse, cosine, sine, segq, segk):
    length, width = gm.shape
    return pl.pallas_call(
        functools.partial(attn_backward_kernel, block=256),
        out_shape=(
            jax.ShapeDtypeStruct((length, width), BF16),
            jax.ShapeDtypeStruct((SLOTS, width, 3 * HD), BF16),
            jax.ShapeDtypeStruct((SLOTS * HD, width), BF16),
        ),
        in_specs=[VMEM] * 11,
        out_specs=(VMEM,) * 3,
        scratch_shapes=[
            pltpu.VMEM((length, 2 * SLOTS * HD), F32),
            pltpu.VMEM((length, 3 * SLOTS * HD), BF16),
            pltpu.VMEM((3 * SLOTS * HD, width), BF16),
        ],
        compiler_params=pltpu.CompilerParams(vmem_limit_bytes=56 * 2**20),
        cost_estimate=pl.CostEstimate(
            flops=4 * length * width * 4 * SLOTS * HD + 10 * SLOTS * HD * length * length,
            bytes_accessed=10 * length * width,
            transcendentals=SLOTS * length * length,
        ),
        name="attn_backward",
    )(gm, wo, w, normed, qkv, attn, lse, cosine, sine, segq, segk)


def ffn_weights(eup_ref, tail_ref, edown_ref, sdown_ref, up_ref, upt_ref, down_ref, downt_ref):
    width, half = downt_ref.shape
    pair, shared = edown_ref.shape[0], sdown_ref.shape[0]
    gap = half - pair - TAIL
    between = [jnp.zeros((width, gap), BF16)] if gap else []
    up_ref[...] = jnp.concatenate(
        [eup_ref[:, :pair], *between, tail_ref[:, :TAIL], eup_ref[:, pair:], *between, tail_ref[:, TAIL:]], axis=1
    )
    between = [jnp.zeros((gap, width), BF16)] if gap else []
    down_ref[...] = jnp.concatenate(
        [edown_ref[...], *between, sdown_ref[...], jnp.zeros((TAIL - shared, width), BF16)], axis=0
    )
    upt_ref[...] = up_ref[...].T
    downt_ref[...] = down_ref[...].T


def ffn_rows(x, g, marks, own, up_ref, upt_ref, down_ref, downt_ref, hidden, shared):
    half = down_ref.shape[0]
    pair = 2 * hidden
    pre = dot(x, up_ref[...])
    gate, up = pre[:, :half], pre[:, half:]
    logits = jnp.where(marks.astype(F32) > 0.5, gate[:, half - HD :], NEG)
    weights = jnp.exp(logits - jnp.max(logits, axis=-1, keepdims=True))
    probs = weights / jnp.sum(weights, axis=-1, keepdims=True)
    p0 = jnp.sum(probs * own[0:1, :], axis=-1, keepdims=True)
    p1 = jnp.sum(probs * own[1:2, :], axis=-1, keepdims=True)
    lane = lax.broadcasted_iota(jnp.int32, (1, half), 1)
    in0 = lane < hidden
    in1 = (lane >= hidden) & (lane < pair)
    rest = jnp.where((lane >= half - TAIL) & (lane < half - TAIL + shared), 1.0, 0.0)
    weight = jnp.where(in0, p0, jnp.where(in1, p1, rest))
    sig = jax.nn.sigmoid(gate)
    silu = gate * sig
    act = silu * up
    acts = (act * weight).astype(BF16)
    out = dot(acts, down_ref[...]).astype(BF16)
    grad = dot(g, downt_ref[...])
    both = act * grad
    d0 = jnp.sum(jnp.where(in0, both, 0.0), axis=-1, keepdims=True)
    d1 = jnp.sum(jnp.where(in1, both, 0.0), axis=-1, keepdims=True)
    grad = grad * weight
    grad_gate = grad * up * sig * (1.0 + gate * (1.0 - sig))
    grad_up = grad * silu
    grad_pre = jnp.concatenate([grad_gate, grad_up], axis=-1).astype(BF16)
    gates = (d0 * own[0:1, :] + d1 * own[1:2, :]).astype(BF16)
    gx = jnp.concatenate([dot(grad_pre, upt_ref[...]).astype(BF16), gates], axis=-1)
    return out, gx, grad_pre, acts


def ffn_kernel(
    x_ref, g_ref, mark_ref, own_ref, eup_ref, tail_ref, edown_ref, sdown_ref,
    out_ref, gx_ref, geup_ref, gtail_ref, gedown_ref, gsdown_ref,
    up_ref, upt_ref, down_ref, downt_ref, gup_ref, gdown_ref,
    *, hidden, shared,
):
    step = pl.program_id(0)
    half = down_ref.shape[0]
    pair = 2 * hidden

    @pl.when(step == 0)
    def _():
        gup_ref[...] = jnp.zeros_like(gup_ref)
        gdown_ref[...] = jnp.zeros_like(gdown_ref)
        ffn_weights(eup_ref, tail_ref, edown_ref, sdown_ref, up_ref, upt_ref, down_ref, downt_ref)

    out, gx, grad_pre, acts = ffn_rows(
        x_ref[...], g_ref[...], mark_ref[...], own_ref[...], up_ref, upt_ref, down_ref, downt_ref, hidden, shared
    )
    out_ref[...] = out
    gx_ref[...] = gx
    gup_ref[...] += dot_tn(x_ref[...], grad_pre)
    gdown_ref[...] += dot_tn(acts, g_ref[...])

    @pl.when(step == pl.num_programs(0) - 1)
    def _():
        geup_ref[...] = jnp.concatenate([gup_ref[:, :pair], gup_ref[:, half : half + pair]], axis=1).astype(BF16)
        gtail_ref[...] = jnp.concatenate([gup_ref[:, half - TAIL : half], gup_ref[:, 2 * half - TAIL :]], axis=1)
        gedown_ref[...] = gdown_ref[:pair, :]
        gsdown_ref[...] = gdown_ref[half - TAIL : half - TAIL + shared, :]


def ffn(x, g, marks, own, eup, tail, edown, sdown):
    total, width = x.shape
    pair, shared = edown.shape[0], sdown.shape[0]
    half = up_to(pair + TAIL, HD)
    tile = 512
    row = lambda n: pl.BlockSpec((tile, n), lambda i: (i, 0))
    return pl.pallas_call(
        functools.partial(ffn_kernel, hidden=pair // 2, shared=shared),
        out_shape=(
            jax.ShapeDtypeStruct((total, width), BF16),
            jax.ShapeDtypeStruct((total, width + HD), BF16),
            jax.ShapeDtypeStruct((width, 2 * pair), BF16),
            jax.ShapeDtypeStruct((width, HD), F32),
            jax.ShapeDtypeStruct((pair, width), F32),
            jax.ShapeDtypeStruct((shared, width), F32),
        ),
        grid=(total // tile,),
        in_specs=[row(width), row(width), row(HD)] + [VMEM] * 5,
        out_specs=(row(width), row(width + HD), VMEM, VMEM, VMEM, VMEM),
        scratch_shapes=[
            pltpu.VMEM((width, 2 * half), BF16),
            pltpu.VMEM((2 * half, width), BF16),
            pltpu.VMEM((half, width), BF16),
            pltpu.VMEM((width, half), BF16),
            pltpu.VMEM((width, 2 * half), F32),
            pltpu.VMEM((half, width), F32),
        ],
        compiler_params=pltpu.CompilerParams(vmem_limit_bytes=60 * 2**20),
        cost_estimate=pl.CostEstimate(
            flops=2 * total * width * 9 * half,
            bytes_accessed=8 * total * width,
            transcendentals=total * half,
        ),
        name="ffn",
    )(x, g, marks, own, eup, tail, edown, sdown)


def flip(f, bits):
    for b in (1, 2, 4):
        if bits & b:
            f = f + b - 2 * b * (f // b % 2)
    return f


def place():
    return lax.axis_index("dp"), lax.axis_index("fsdp")


def greet(devices):
    barrier = pltpu.get_barrier_semaphore()
    for device in devices:
        pl.semaphore_signal(barrier, inc=1, device_id=device, device_id_type=MESH)
    pl.semaphore_wait(barrier, len(devices))


def greet_all(nz, nf):
    barrier = pltpu.get_barrier_semaphore()
    z, f = place()
    me, count = z * nf + f, nz * nf

    def hail(i, _):
        d = (me + i) % count
        pl.semaphore_signal(barrier, inc=1, device_id=(d // nf, d % nf), device_id_type=MESH)
        return 0

    lax.fori_loop(1, count, hail, 0)
    pl.semaphore_wait(barrier, count - 1)


def send(src, dst, sems, index, device):
    return pltpu.make_async_remote_copy(
        src, dst, sems[0].at[index], sems[1].at[index], device_id=device, device_id_type=MESH
    )


ORDER = ((2, 4), (4, 2))


def halves(rows):
    return ((0, rows // 2), (rows // 2, rows - rows // 2))


def away(j, nz):
    if nz < 3:
        return j
    if isinstance(j, int):
        return j if j < 2 else nz - 1 if j == 2 else j - 1
    return jnp.where(j < 2, j, jnp.where(j == 2, nz - 1, j - 1))


def spot(ref, piece, f):
    return ref.at[piece, f // 4, f // 2 % 2, f % 2] if len(ref.shape) == 6 else ref.at[piece, f]


class Gather:
    @staticmethod
    def copies(nz):
        return 11 * nz

    def __init__(self, buf, sems, nz, z, f, own=None):
        self.own = own
        self.buf, self.sems, self.nz, self.z, self.f = buf, sems, nz, z, f

    def slot(self, j, r, h=None):
        piece = lax.rem(self.z - away(j, self.nz) + self.nz, self.nz) if self.nz > 1 else 0
        ref = spot(self.buf, piece, flip(self.f, r))
        return ref if h is None else ref.at[pl.ds(*halves(self.buf.shape[-2])[h])]

    def here(self, j, r, h, index, device):
        ref = self.slot(j, r, h)
        src = ref
        if self.own is not None and isinstance(j, int) and j == 0 and r == 0:
            src = self.own if h is None else self.own.at[pl.ds(*halves(self.own.shape[-2])[h])]
        return send(src, ref, self.sems, index, device)

    def by_z(self, j):
        own = self.slot(0, 0)
        src = own if self.own is None else self.own
        return send(src, own, self.sems, j, (lax.rem(self.z + away(j, self.nz), self.nz), self.f))

    def near(self, j, h):
        return self.here(j, 0, h, self.nz + 2 * j + h, (self.z, flip(self.f, ORDER[h][0])))

    def far(self, j, h, i):
        r = ORDER[h][0] if i else 0
        return self.here(j, r, h, 3 * self.nz + 4 * j + 2 * h + i, (self.z, flip(self.f, ORDER[h][1])))

    def core(self, j, i):
        return self.here(j, 2 * i, None, 7 * self.nz + 4 * j + i, (self.z, flip(self.f, 1)))

    def along_z(self, j):
        if 1 < j <= self.nz:
            self.by_z(j - 1).wait_send()
        if j < self.nz:
            self.by_z(j).start()

    def first(self, j, own=False):
        if not own:
            self.by_z(j).wait_recv()
        for h in range(2):
            self.near(j, h).start()
        self.core(j, 0).start()

    def second(self, j):
        for h in range(2):
            self.near(j, h).wait_recv()
            for i in range(2):
                self.far(j, h, i).start()

    def third(self, j):
        for h in range(2):
            for i in range(2):
                self.far(j, h, i).wait_recv()
        for i in range(1, 4):
            self.core(j, i).start()

    def fourth(self, j):
        for i in range(4):
            self.core(j, i).wait_recv()

    def end(self, first=0):
        for j in range(first, self.nz):
            for h in range(2):
                self.near(j, h).wait_send()
                for i in range(2):
                    self.far(j, h, i).wait_send()
            for i in range(4):
                self.core(j, i).wait_send()


class Reduce:
    @staticmethod
    def copies(nz):
        return 11 * nz

    @staticmethod
    def scratch(nz, rows, width):
        return [
            pltpu.VMEM((nz, 4, rows, width), BF16),
            pltpu.VMEM((nz, 2, rows, width), BF16),
            pltpu.VMEM((nz, rows, width), BF16),
            pltpu.VMEM((nz, rows, width), BF16),
        ]

    def __init__(self, bufs, sems, nz, z, f):
        self.by_core, self.by_near, self.by_far, self.by_z = bufs
        self.sems, self.nz, self.z, self.f = sems, nz, z, f
        self.parts = halves(self.by_core.shape[-2])

    def core(self, j, i, src):
        to = self.by_core.at[j, i]
        return send(to if src is None else src, to, self.sems, 4 * j + i, (self.z, flip(self.f, 1)))

    def near(self, j, h, i):
        last = ORDER[1 - h][1]
        rows = pl.ds(*self.parts[h])
        return send(
            self.by_core.at[j, 3 if i else last // 2, rows], self.by_near.at[j, i, rows], self.sems,
            4 * self.nz + 4 * j + 2 * h + i, (self.z, flip(self.f, last)),
        )

    def far_copy(self, j, h):
        rows = pl.ds(*self.parts[h])
        return send(
            self.by_near.at[j, 1, rows], self.by_far.at[j, rows], self.sems,
            8 * self.nz + 2 * j + h, (self.z, flip(self.f, ORDER[1 - h][0])),
        )

    def z_copy(self, j):
        there = lax.rem(self.z - away(j, self.nz) + self.nz, self.nz)
        return send(self.by_far.at[j], self.by_z.at[j], self.sems, 10 * self.nz + j, (there, self.f))

    def send_near(self, j):
        for h in range(2):
            for i in range(2):
                self.near(j, h, i).start()

    def far(self, j):
        for h in range(2):
            at, size = self.parts[h]
            rows = slice(at, at + size)
            for i, r in enumerate((0, ORDER[1 - h][0])):
                self.near(j, h, i).wait_recv()
                self.by_near[j, i, rows] = self.by_near[j, i, rows] + self.by_core[j, r // 2, rows]
            self.far_copy(j, h).start()

    def along_z(self, j):
        for h in range(2):
            at, size = self.parts[h]
            rows = slice(at, at + size)
            self.far_copy(j, h).wait_recv()
            self.by_far[j, rows] = self.by_far[j, rows] + self.by_near[j, 0, rows]
        if isinstance(j, int):
            if j:
                self.z_copy(j).start()
        else:

            @pl.when(j > 0)
            def _():
                self.z_copy(j).start()

    def total(self):
        result = self.by_far[0].astype(F32)
        for j in range(1, self.nz):
            self.z_copy(j).wait_recv()
            result = result + self.by_z[j].astype(F32)
        return result

    def end(self):
        for j in range(self.nz):
            for h in range(2):
                for i in range(2):
                    self.near(j, h, i).wait_send()
                self.far_copy(j, h).wait_send()
            if j:
                self.z_copy(j).wait_send()


def near_devices(z, f):
    return [(z, flip(f, 1)), (z, flip(f, 2)), (z, flip(f, 4))]


def z_devices(z, f, nz):
    return [(lax.rem(z + zr, nz), f) for zr in range(1, nz)]


def pair_of(count):
    return [pltpu.SemaphoreType.DMA((count,))] * 2


def first_head(member):
    return HEADS * member // 8


def out_blocks(member, dense):
    return first_head(member) * HD // dense, (first_head(member + 1) * HD - 1) // dense


def head_owner(head):
    return (8 * head + 7) // HEADS


def front_kernel(
    tok_ref, wqkv_ref, wout_ref, router_ref, sup_ref, again_ref, fgain_ref, eids_ref, seg_ref, cos_in, sin_in, og_ref,
    eup_in,
    w_out, wo_ref, tail_out, router_out, gain_one_ref, gain_two_ref, mark_out, own_mark_ref, segq_ref, segk_ref,
    normed_out, qkv_out, attn_out, lse_out, mixed_ref, low_ref, plane_ref, all_grad_ref, pieces_ref,
    w_ref, tail_ref, mark_ref, normed_ref, qkv_ref, attn_ref, lse_ref, ids_ref, cos_ref, sin_ref, eup_ref, out_sems,
    seq, wq, wo_in, wz, wzo, all_ids, qpack, tpack, part, wide, pack, *refs, nz, nf, hidden, shared, heads, real,
):
    bufs, refs = refs[:4], refs[4:]
    (
        tok_s, tok_r, all_s, all_r, q_s, q_r, wo_s, wo_r, zq_s, zq_r, zo_s, zo_r, rs, rr, gs, gr, xs, xr, es, er,
        own_sems,
    ) = refs
    z, f = place()
    me, count = z * nf + f, nz * nf
    rows, width = tok_ref.shape
    dense = wqkv_ref.shape[0]
    experts = router_ref.shape[0]
    full = shared * count
    loads = [
        pltpu.make_async_copy(src, dst, out_sems.at[7 + k])
        for k, (src, dst) in enumerate(((eup_in, eup_ref), (cos_in, cos_ref), (sin_in, sin_ref)))
    ]
    for copy in loads:
        copy.start()
    greet_all(nz, nf)

    toks = (tok_s, tok_r)
    to_near = [send(tok_ref, seq.at[f], toks, i, (z, flip(f, r))) for i, r in enumerate((2, 4, 6))]
    to_core = [send(tok_ref, seq.at[f], toks, 3, (z, flip(f, 1)))]
    own = pltpu.make_async_copy(og_ref, all_grad_ref.at[z, f], own_sems.at[0])
    own.start()
    for copy in to_near + to_core:
        copy.start()
    seq[f] = tok_ref[...]
    ids_ref[...] = jnp.concatenate([eids_ref[...], seg_ref[...]], axis=0)
    all_ids[me] = ids_ref[...]
    router = router_ref[...].astype(F32).T.astype(BF16)
    both_gains = jnp.concatenate([again_ref[...].astype(F32).T, fgain_ref[...].astype(F32).T], axis=1).astype(BF16)

    def leave(k, src, dst):
        return pltpu.make_async_copy(src, dst, out_sems.at[k])

    outgoing = [
        leave(k, src, dst)
        for k, (src, dst) in enumerate(
            (
                (w_ref, w_out), (tail_ref, tail_out), (mark_ref, mark_out), (normed_ref, normed_out),
                (qkv_ref, qkv_out), (attn_ref, attn_out), (lse_ref, lse_out),
            )
        )
    ]
    own.wait()
    grads = Gather(all_grad_ref, (gs, gr), nz, z, f)
    grads.first(0, own=True)

    def two(m):
        return first_head(m + 1) - first_head(m) == 2

    def wanted(m, block):
        low, high = out_blocks(m, dense)
        return (low <= block) & (block <= high)

    low, high = out_blocks(f, dense)

    def piece(j):
        return lax.rem(z - away(j, nz) + nz, nz) if j else z

    def along(src, dst, sems, j):
        return send(src, dst.at[z], sems, j, (lax.rem(z + away(j, nz), nz), f))

    zq = [None] + [along(wqkv_ref, wz, (zq_s, zq_r), j) for j in range(1, nz)]
    zo = [None] + [along(wout_ref, wzo, (zo_s, zo_r), j) for j in range(1, nz)]
    for copy in zq[1:] + zo[1:]:
        copy.start()

    pad = jnp.zeros((dense, TAIL - shared - experts), BF16)
    pad_two = jnp.zeros((dense, TAIL - shared - 2), BF16)
    for d in range(count):
        tpack[d] = jnp.concatenate(
            [
                sup_ref[:, d * shared : (d + 1) * shared], router, pad,
                sup_ref[:, full + d * shared : full + (d + 1) * shared], both_gains, pad_two,
            ],
            axis=1,
        )

    def copies(d, k):
        src, dst = ((tpack.at[d], tail_ref.at[me]), (ids_ref, all_ids.at[me]))[k]
        return pltpu.make_async_remote_copy(
            src, dst, all_s.at[k, d], all_r.at[k, me], device_id=(d // nf, d % nf), device_id_type=MESH
        )

    def came(d, k):
        dst = (tail_ref.at[d], all_ids.at[d])[k]
        return pltpu.make_async_remote_copy(
            dst, dst, all_s.at[k, d], all_r.at[k, d], device_id=(d // nf, d % nf), device_id_type=MESH
        )

    def start(i, _):
        d = (me + i) % count
        copies(d, 0).start()
        copies(d, 1).start()
        return 0

    whole = nz * hidden
    for copy in loads:
        copy.wait()
    for t in range(nz):
        pack[t] = jnp.concatenate(
            [
                eup_ref[e, :, g * whole + t * hidden : g * whole + (t + 1) * hidden]
                for g in range(2)
                for e in range(2)
            ],
            axis=1,
        )
    tail_ref[me] = tpack[me]
    lax.fori_loop(1, count, start, 0)

    def q_copy(j, m, s):
        return pltpu.make_async_remote_copy(
            qpack.at[j, m, s], wq.at[s, piece(j) * nf + f], q_s.at[j, m, s], q_r.at[j, f, s],
            device_id=(z, m), device_id_type=MESH,
        )

    def q_came(j, m, s):
        dst = wq.at[s, piece(j) * nf + m]
        return pltpu.make_async_remote_copy(
            dst, dst, q_s.at[j, m, s], q_r.at[j, m, s], device_id=(z, m), device_id_type=MESH
        )

    def q_own(j, s):
        wq[s, piece(j) * nf + f] = qpack[j, f, s]

    def q_each(act, m):
        act(0)

        @pl.when(two(m))
        def _():
            act(1)

    def q_send(j):
        ref = wz.at[piece(j)] if j else wqkv_ref
        for m in range(8):
            for s in range(SLOTS):
                h = heads[m * SLOTS + s]
                if real[m * SLOTS + s]:
                    qpack[j, m, s] = jnp.concatenate(
                        [ref[:, c * width + h * HD : c * width + (h + 1) * HD] for c in range(3)], axis=1
                    )

        def go(i, _):
            m = (f + i) % nf
            q_each(lambda s: q_copy(j, m, s).start(), m)
            return 0

        lax.fori_loop(1, nf, go, 0)
        q_each(lambda s: q_own(j, s), f)

    grads.second(0)
    for i, r in enumerate((2, 4, 6)):
        to_near[i].wait_recv()
        slot = seq.at[flip(f, r)]
        copy = send(slot, slot, toks, 4 + i, (z, flip(f, 1)))
        copy.start()
        to_core.append(copy)
    q_send(0)
    grads.third(0)
    for copy in zq[1:]:
        copy.wait_send()
    for j in range(1, nz):
        grads.by_z(j).start()
    for j in range(1, nz):
        zq[j].wait_recv()
        q_send(j)

    def arrive(i, _):
        d = (me + i) % count
        came(d, 0).wait_recv()
        came(d, 1).wait_recv()
        return 0

    lax.fori_loop(1, count, arrive, 0)

    def q_arrive(i, _):
        m = (f + i) % nf
        for j in range(nz):
            q_each(lambda s: q_came(j, m, s).wait_recv(), f)
        return 0

    lax.fori_loop(1, nf, q_arrive, 0)
    for copy in to_core:
        copy.wait_recv()

    w_ref[0] = wq[0].reshape(width, 3 * HD)
    w_ref[1] = jnp.where(two(f), wq[1].astype(F32), 0.0).reshape(width, 3 * HD).astype(BF16)
    outgoing[0].start()
    outgoing[1].start()
    tails = tail_ref[...].reshape(width, 2 * TAIL)
    gains = tails[:, TAIL + shared : TAIL + shared + 2].astype(F32).T
    gain_one_ref[...] = gains[0:1]
    gain_two_ref[...] = gains[1:2]
    router_out[...] = jnp.concatenate(
        [
            jnp.zeros((width, TAIL + shared), BF16), tails[:, shared : shared + experts],
            jnp.zeros((width, TAIL - shared - experts), BF16),
        ],
        axis=1,
    )
    for m in range(8):
        ids = all_ids[z * nf + m]
        segk_ref[:, m * rows : (m + 1) * rows] = jnp.broadcast_to(ids[-1:], (8, rows))
        segq_ref[m * rows : (m + 1) * rows, :] = jnp.broadcast_to(ids.T[:, -1:], (rows, HD))
    block = 256
    gain_one = gain_one_ref[...]

    def project(i, _):
        x = seq[pl.ds(i * (block // rows), block // rows)].reshape(block, width)
        attn_project(i, block, x, gain_one, w_ref, cos_ref, sin_ref, normed_ref, qkv_ref)
        return 0

    lax.fori_loop(0, 8 * rows // block, project, 0)
    outgoing[3].start()
    outgoing[4].start()
    def out_block(j):
        return piece(j) * nf + f

    def out_src(j):
        return wzo.at[piece(j)] if j else wout_ref

    def out_copy(j, m):
        first, _ = out_blocks(m, dense)
        slot = out_block(j) - first
        return pltpu.make_async_remote_copy(
            out_src(j), wo_in.at[slot], wo_s.at[j, m], wo_r.at[slot], device_id=(z, m), device_id_type=MESH
        )

    def out_own(j):
        wo_in[out_block(j) - low] = wzo[piece(j)] if j else wout_ref[...]

    def out_each(act, act_own):
        for j in range(nz):

            def one(i, _):
                m = (f + i) % nf

                @pl.when(wanted(m, out_block(j)))
                def _():
                    act(j, m)

                return 0

            lax.fori_loop(1, nf, one, 0)

            @pl.when(wanted(f, out_block(j)))
            def _():
                act_own(j)

    for j in range(1, nz):
        zo[j].wait()
    out_each(lambda j, m: out_copy(j, m).start(), out_own)

    reduce = Reduce(bufs, (rs, rr), 1, z, f)
    for i in range(8 * rows // block):
        attn_block(i, block, segq_ref, segk_ref, qkv_ref, attn_ref, lse_ref)

    outgoing[5].start()
    outgoing[6].start()

    def arrive_out(j, _):
        @pl.when((low + j <= high) & (lax.rem(low + j, nf) != f))
        def _():
            pltpu.make_async_remote_copy(
                wo_in.at[j], wo_in.at[j], wo_s.at[0, j], wo_r.at[j], device_id=(z, flip(f, 1)), device_id_type=MESH
            ).wait_recv()

        return 0

    lax.fori_loop(0, wo_in.shape[0], arrive_out, 0)
    wide[...] = wo_in[...].astype(F32).reshape(wide.shape)
    offset = pl.multiple_of(first_head(f) * HD - low * dense, 8)
    wo_ref[:HD, :] = wide[pl.ds(offset, HD), :].astype(BF16)
    wo_ref[HD:, :] = jnp.where(two(f), wide[pl.ds(offset + HD, HD), :], 0.0).astype(BF16)
    for i in range(8 * rows // block):
        at = i * (block // rows)
        part[at : at + block // rows] = (
            dot(attn_ref[i * block : (i + 1) * block, :], wo_ref[...]).astype(BF16).reshape(block // rows, rows, width)
        )
    for i in range(4):
        reduce.core(0, i, part.at[flip(f, 1 | 2 * i)]).start()
    ups = []
    for j in range(1, nz):
        there = lax.rem(z + j, nz)
        copy = send(pack.at[there], pieces_ref.at[z], (es, er), j, (there, f))
        copy.start()
        ups.append(copy)
    ups.append(pltpu.make_async_copy(pack.at[z], pieces_ref.at[z], own_sems.at[2]))
    ups[-1].start()
    for i in range(4):
        reduce.core(0, i, None).wait_recv()
        reduce.by_core[0, i] = reduce.by_core[0, i] + part[flip(f, 2 * i)]
    reduce.send_near(0)
    reduce.far(0)
    reduce.along_z(0)
    mixed = tok_ref[...].astype(F32) + reduce.by_far[0].astype(F32)
    mixed_ref[...] = mixed
    low_ref[...] = (mixed * rms_scale(mixed) * gain_two_ref[...]).astype(BF16)
    near_own = pltpu.make_async_copy(low_ref, plane_ref.at[0, f], own_sems.at[1])
    near_own.start()
    near = Gather(plane_ref, (xs, xr), 1, z, f, own=low_ref)
    near.first(0, own=True)
    for j in range(1, nz):
        grads.first(j)
    near.second(0)
    for j in range(1, nz):
        grads.second(j)
    lane = lax.broadcasted_iota(jnp.int32, (rows, HD), 1) - TAIL - shared

    def mark(d, _):
        ids = all_ids[d].T
        found = ids[:, 0:1] == lane
        for k in range(1, ids.shape[1] - 1):
            found = found | (ids[:, k : k + 1] == lane)
        value = jnp.where(found, 1.0, 0.0)
        mark_ref[d] = value.astype(BF16)

        @pl.when(d == me)
        def _():
            own_mark_ref[...] = value

        return 0

    lax.fori_loop(0, count, mark, 0)
    outgoing[2].start()
    near.third(0)
    for j in range(1, nz):
        grads.third(j)
    for j in range(nz):
        grads.fourth(j)
    near.fourth(0)

    def left(i, _):
        d = (me + i) % count
        copies(d, 0).wait_send()
        copies(d, 1).wait_send()
        return 0

    lax.fori_loop(1, count, left, 0)

    def q_left(i, _):
        m = (f + i) % nf
        for j in range(nz):
            q_each(lambda s: q_copy(j, m, s).wait_send(), m)
        return 0

    lax.fori_loop(1, nf, q_left, 0)
    out_each(lambda j, m: out_copy(j, m).wait_send(), lambda j: None)
    for copy in to_near + to_core:
        copy.wait_send()
    for i in range(4):
        reduce.core(0, i, part.at[0]).wait_send()
    reduce.end()
    for j in range(1, nz):
        grads.by_z(j).wait_send()
    grads.end()
    near.end()
    for copy in ups + outgoing + [near_own]:
        copy.wait()


def front(tok, wqkv, wout, router, sup, again, fgain, eids, seg, cosine, sine, og, eup, nz, nf, shared):
    rows, width = tok.shape
    dense, count = wqkv.shape[0], nz * nf
    length = 8 * rows
    hidden, up_rows = eup.shape[2] // (2 * nz), eup.shape[1]
    heads, real = head_table(8)
    shape = jax.ShapeDtypeStruct
    return pl.pallas_call(
        functools.partial(front_kernel, nz=nz, nf=nf, hidden=hidden, shared=shared, heads=heads, real=real),
        out_shape=(
            shape((SLOTS, width, 3 * HD), BF16),
            shape((SLOTS * HD, width), BF16),
            shape((count, dense, 2 * TAIL), BF16),
            shape((width, HD), BF16),
            shape((1, width), F32),
            shape((1, width), F32),
            shape((count, rows, HD), BF16),
            shape((rows, HD), F32),
            shape((length, HD), jnp.int32),
            shape((8, length), jnp.int32),
            shape((length, width), BF16),
            shape((length, 3 * SLOTS * HD), BF16),
            shape((length, SLOTS * HD), BF16),
            shape((length, SLOTS * HD), F32),
            shape((rows, width), F32),
            shape((rows, width), BF16),
            shape((1, 8, rows, width), BF16),
            shape((nz, 8, rows, width), BF16),
            shape((nz, up_rows, 4 * hidden), BF16),
        ),
        in_specs=[VMEM] * 9 + [ANY] * 2 + [VMEM, ANY],
        out_specs=(ANY, VMEM, ANY, VMEM, VMEM, VMEM, ANY, VMEM, VMEM, VMEM) + (ANY,) * 4 + (VMEM,) * 2 + (ANY,) * 3,
        scratch_shapes=[
            pltpu.VMEM((SLOTS, width, 3 * HD), BF16),
            pltpu.VMEM((count, dense, 2 * TAIL), BF16),
            pltpu.VMEM((count, rows, HD), BF16),
            pltpu.VMEM((length, width), BF16),
            pltpu.VMEM((length, 3 * SLOTS * HD), BF16),
            pltpu.VMEM((length, SLOTS * HD), BF16),
            pltpu.VMEM((length, SLOTS * HD), F32),
            pltpu.VMEM((eids.shape[0] + 1, rows), jnp.int32),
            pltpu.VMEM(cosine.shape, F32),
            pltpu.VMEM(sine.shape, F32),
            pltpu.VMEM(eup.shape, BF16),
            pltpu.SemaphoreType.DMA((10,)),
            pltpu.VMEM((8, rows, width), BF16),
            pltpu.VMEM((SLOTS, count, dense, 3 * HD), BF16),
            pltpu.VMEM((8, dense, width), BF16),
            pltpu.VMEM((nz, dense, 3 * width), BF16),
            pltpu.VMEM((nz, dense, width), BF16),
            pltpu.VMEM((count, eids.shape[0] + 1, rows), jnp.int32),
            pltpu.VMEM((nz, 8, SLOTS, dense, 3 * HD), BF16),
            pltpu.VMEM((count, dense, 2 * TAIL), BF16),
            pltpu.VMEM((8, rows, width), BF16),
            pltpu.VMEM((8 * dense, width), F32),
            pltpu.VMEM((nz, up_rows, 4 * hidden), BF16),
            *Reduce.scratch(1, rows, width),
            *pair_of(7),
            pltpu.SemaphoreType.DMA((2, count)),
            pltpu.SemaphoreType.DMA((2, count)),
            pltpu.SemaphoreType.DMA((nz, 8, SLOTS)),
            pltpu.SemaphoreType.DMA((nz, 8, SLOTS)),
            pltpu.SemaphoreType.DMA((nz, 8)),
            pltpu.SemaphoreType.DMA((8,)),
            *pair_of(nz),
            *pair_of(nz),
            *pair_of(Reduce.copies(1)),
            *pair_of(Gather.copies(nz)),
            *pair_of(Gather.copies(1)),
            *pair_of(nz),
            pltpu.SemaphoreType.DMA((3,)),
        ],
        compiler_params=pltpu.CompilerParams(
            collective_id=1, has_side_effects=True, vmem_limit_bytes=58 * 2**20
        ),
        name="front",
    )(tok, wqkv, wout, router, sup, again, fgain, eids, seg, cosine, sine, og, eup)


def route_grads(gx, og, mixed, normed, router, marks, gain):
    width = mixed.shape[1]
    scale = rms_scale(mixed)
    normal = mixed * scale
    logits = jnp.where(marks > 0.5, dot(normed, router), NEG)
    weights = jnp.exp(logits - jnp.max(logits, axis=-1, keepdims=True))
    probs = weights / jnp.sum(weights, axis=-1, keepdims=True)
    grad_gates = gx[:, width:]
    grad_logits = (probs * (grad_gates - jnp.sum(probs * grad_gates, axis=-1, keepdims=True))).astype(BF16)
    grad_router = dot_tn(normed, grad_logits)
    grad_normed = gx[:, :width] + dot_nt(grad_logits, router)
    ones = jnp.where(lax.broadcasted_iota(jnp.int32, (mixed.shape[0], HD), 1) == TAIL - 1, 1.0, 0.0)
    grad_gain = lax.dot_general(
        grad_normed * normal, ones, (((0,), (0,)), ((), ())),
        precision=lax.Precision.HIGHEST, preferred_element_type=F32,
    )
    grad_mixed = og.astype(F32) + norm_back(grad_normed, normal, scale, gain)
    return grad_mixed, pltpu.roll(grad_router + grad_gain, TAIL, 1)


def experts_kernel(
    normed_ref, plane_ref, all_grad_ref, mark_in, own_ref, eup_in, tail_ref, edown_in, sdown_ref,
    og_ref, mixed_ref, router_ref, own_mark_ref, gain_ref,
    out_any, low_ref, gm_ref, small_ref, geup_ref, gedown_ref, gsdown_ref, all_normed_ref,
    out_ref,
    up_ref, upt_ref, down_ref, downt_ref, gup_ref, gdown_ref,
    xt, gt, px, po, mark_ref, eup_ref, edown_ref, *refs, nz, hidden, shared,
):
    bufs, (tile_sems, rs, rr, os_, or_, xs, xr, own_sems) = refs[:4], refs[4:]
    z, f = place()
    rows, width = mixed_ref.shape
    half = down_ref.shape[0]
    pair = 2 * hidden
    starts = [
        pltpu.make_async_copy(src, dst, own_sems.at[k])
        for k, (src, dst) in enumerate(((eup_in, eup_ref), (edown_in, edown_ref), (mark_in, mark_ref)))
    ]
    for copy in starts:
        copy.start()
    greet(near_devices(z, f) + z_devices(z, f, nz))
    gather = Gather(all_normed_ref, (xs, xr), nz, z, f, own=normed_ref)
    gather.along_z(1)
    reduce = Reduce(bufs, (rs, rr), nz, z, f)
    outs = Reduce([out_ref, out_ref, out_ref, out_ref], (os_, or_), nz, z, f)
    for copy in starts:
        copy.wait()
    ffn_weights(eup_ref, tail_ref, edown_ref, sdown_ref, up_ref, upt_ref, down_ref, downt_ref)
    gup_ref[...] = jnp.zeros_like(gup_ref)
    gdown_ref[...] = jnp.zeros_like(gdown_ref)
    gather.along_z(2)
    if nz > 1:
        gather.first(1)

    def where(i):
        j, t = i // 4, i % 4
        base = f + (1 - 2 * (f % 2)) * (1 - t // 2) + (4 - 8 * (f // 4 % 2)) * (t % 2)
        return lax.rem(z - away(j, nz) + nz, nz), base // 4, base % 2

    def loads(i, rows_ref=all_normed_ref):
        piece, y, core = where(i)
        there = piece if rows_ref is all_normed_ref else 0
        slot = i % 2
        return [
            pltpu.make_async_copy(rows_ref.at[there, y, :, core], xt.at[slot], tile_sems.at[slot, 0]),
            pltpu.make_async_copy(all_grad_ref.at[piece, y, :, core], gt.at[slot], tile_sems.at[slot, 1]),
        ]

    for copy in loads(0, plane_ref):
        copy.start()
    last = 4 * nz - 1

    def tile(i, _):
        j, t = i // 4, i % 4
        more = j < nz - 1

        @pl.when((t == 0) & more)
        def _():
            gather.second(j + 1)

        @pl.when(i == 1)
        def _():
            gather.along_z(3)

        @pl.when((t == 2) & more)
        def _():
            gather.third(j + 1)

        @pl.when((t == 2) & (j < nz - 2))
        def _():
            gather.first(j + 2)

        @pl.when((t == 3) & more)
        def _():
            gather.fourth(j + 1)

        @pl.when((t == 0) & (j > 0))
        def _():
            for k in range(4):
                reduce.core(j - 1, k, px.at[k]).wait_send()
                outs.core(j - 1, k, po.at[k]).wait_send()

        for copy in loads(i):
            copy.wait()

        @pl.when(i < 3)
        def _():
            for copy in loads(i + 1, plane_ref):
                copy.start()

        @pl.when((i >= 3) & (i < last))
        def _():
            for copy in loads(i + 1):
                copy.start()

        piece, y, core = where(i)
        marks = jnp.concatenate([mark_ref[piece, 4 * y + core], mark_ref[piece, 4 * y + 2 + core]], axis=0)
        x, g = xt[i % 2].reshape(2 * rows, width), gt[i % 2].reshape(2 * rows, width)
        out, gx, grad_pre, acts = ffn_rows(
            x, g, marks, own_ref[...], up_ref, upt_ref, down_ref, downt_ref, hidden, shared
        )
        x_at = f // 2 % 2
        for b in range(2):
            at = 2 * t + (1 - x_at if b else x_at)
            po[at] = out[b * rows : (b + 1) * rows]
            px[at] = gx[b * rows : (b + 1) * rows]
        gup_ref[...] += dot_tn(x, grad_pre)
        gdown_ref[...] += dot_tn(acts, g)

        @pl.when(t == 1)
        def _():
            for k in range(4):
                reduce.core(j, k, px.at[k]).start()
            for k in range(4):
                outs.core(j, k, po.at[k]).start()

        @pl.when((t == 1) & (j > 0))
        def _():
            reduce.far(j - 1)

        @pl.when((t == 2) & (j > 0))
        def _():
            reduce.along_z(j - 1)

        @pl.when(t == 3)
        def _():
            for k in range(4):
                reduce.core(j, k, None).wait_recv()
                reduce.by_core[j, k] = reduce.by_core[j, k] + px[4 + k]
            reduce.send_near(j)
            for k in range(4):
                outs.core(j, k, None).wait_recv()
                out_ref[j, k] = out_ref[j, k] + po[4 + k]

        return 0

    lax.fori_loop(0, 4 * nz, tile, 0)
    up_ref[:, : 2 * pair] = jnp.concatenate([gup_ref[:, :pair], gup_ref[:, half : half + pair]], axis=1).astype(BF16)
    up_rows = width // nz
    ends = [
        pltpu.make_async_copy(up_ref.at[pl.ds(p * up_rows, up_rows), pl.ds(0, 2 * pair)], geup_ref.at[p], own_sems.at[p])
        for p in range(nz)
    ]
    ends.append(pltpu.make_async_copy(gdown_ref.at[pl.ds(0, pair)], gedown_ref, own_sems.at[nz]))
    ends.append(pltpu.make_async_copy(out_ref, out_any, own_sems.at[nz + 1]))
    for copy in ends:
        copy.start()
    reduce.far(nz - 1)
    gtail = jnp.concatenate([gup_ref[:, half - TAIL : half], gup_ref[:, 2 * half - TAIL :]], axis=1)
    gsdown_ref[...] = gdown_ref[half - TAIL : half - TAIL + shared, :]
    reduce.along_z(nz - 1)
    grad_mixed, small = route_grads(
        reduce.total(), og_ref[...], mixed_ref[...], normed_ref[...], router_ref[...], own_mark_ref[...], gain_ref[...]
    )
    gm_ref[...] = grad_mixed
    low_ref[...] = grad_mixed.astype(BF16)
    small_ref[...] = (small + gtail).astype(BF16)
    for k in range(4):
        reduce.core(nz - 1, k, px.at[k]).wait_send()
        outs.core(nz - 1, k, po.at[k]).wait_send()
    for copy in ends:
        copy.wait()
    for j in range(4, nz + 1):
        gather.along_z(j)
    gather.end(1)
    reduce.end()


def experts_turn(
    normed, plane, all_grad, marks, own, eup, tail, edown, sdown, og, mixed, router, own_marks, gain, nz, nf
):
    rows, width = mixed.shape
    pair, shared = edown.shape[0], sdown.shape[0]
    half = up_to(pair + TAIL, HD)
    wide = width + HD
    return pl.pallas_call(
        functools.partial(experts_kernel, nz=nz, hidden=pair // 2, shared=shared),
        out_shape=(
            jax.ShapeDtypeStruct((nz, 4, rows, width), BF16),
            jax.ShapeDtypeStruct((rows, width), BF16),
            jax.ShapeDtypeStruct((rows, width), F32),
            jax.ShapeDtypeStruct((width, HD), BF16),
            jax.ShapeDtypeStruct((nz, width // nz, 2 * pair), BF16),
            jax.ShapeDtypeStruct((pair, width), F32),
            jax.ShapeDtypeStruct((shared, width), F32),
            jax.ShapeDtypeStruct((nz, 2, 2, 2, rows, width), BF16),
        ),
        in_specs=[VMEM, ANY, ANY, ANY, VMEM, ANY, VMEM, ANY] + [VMEM] * 6,
        out_specs=(ANY, VMEM, VMEM, VMEM, ANY, ANY, VMEM, ANY),
        scratch_shapes=[
            pltpu.VMEM((nz, 4, rows, width), BF16),
            pltpu.VMEM((width, 2 * half), BF16),
            pltpu.VMEM((2 * half, width), BF16),
            pltpu.VMEM((half, width), BF16),
            pltpu.VMEM((width, half), BF16),
            pltpu.VMEM((width, 2 * half), F32),
            pltpu.VMEM((half, width), F32),
            pltpu.VMEM((2, 2, rows, width), BF16),
            pltpu.VMEM((2, 2, rows, width), BF16),
            pltpu.VMEM((8, rows, wide), BF16),
            pltpu.VMEM((8, rows, width), BF16),
            pltpu.VMEM((nz, 8, rows, HD), BF16),
            pltpu.VMEM(eup.shape, BF16),
            pltpu.VMEM(edown.shape, BF16),
            *Reduce.scratch(nz, rows, wide),
            pltpu.SemaphoreType.DMA((2, 2)),
            *pair_of(Reduce.copies(nz)),
            *pair_of(Reduce.copies(nz)),
            *pair_of(Gather.copies(nz)),
            pltpu.SemaphoreType.DMA((nz + 3,)),
        ],
        compiler_params=pltpu.CompilerParams(
            collective_id=3, has_side_effects=True, vmem_limit_bytes=60 * 2**20
        ),
        name="experts_turn",
    )(
        normed, plane.reshape(1, 2, 2, 2, rows, width), all_grad.reshape(nz, 2, 2, 2, rows, width),
        marks.reshape(nz, 8, rows, HD), own, eup, tail, edown, sdown, og, mixed, router, own_marks, gain
    )[:7]


def back_kernel(
    low_ref, geup_ref, *refs, nz, nf, heads, real,
):
    sources, refs = refs[:11], refs[11:]
    (wo_ref, w_ref, normed_ref, qkv_ref, attn_ref, lse_ref, cos_ref, sin_ref, segq_ref, segk_ref, out_ref), refs = (
        refs[-12:-1],
        refs[:-12] + refs[-1:],
    )
    back_body(sources, low_ref, geup_ref, wo_ref, w_ref, normed_ref, qkv_ref, attn_ref, lse_ref, cos_ref, sin_ref,
              segq_ref, segk_ref, out_ref, *refs, nz=nz, nf=nf, heads=heads, real=real)


def back_body(
    sources, low_ref, geup_ref, wo_ref, w_ref, normed_ref, qkv_ref, attn_ref, lse_ref, cos_ref, sin_ref, segq_ref, segk_ref,
    out_ref, small_ref, tok_ref, mixed_ref, own_gm_ref, gain_ref,
    block_ref, gtok_ref, gwqkv_ref, gwout_ref, all_small_ref, pieces_ref,
    seq, gkv_ref, gqkv_ref, wt_ref, part_ref, gw_ref, gwo_ref, gq, gob, gpk, gz, smalls, *refs, nz, nf, heads, real,
):
    bufs, refs = refs[:7], refs[7:]
    rs, rr, os_, or_, all_s, all_r, q_s, q_r, wo_s, wo_r, zs, zr, gs, gr, es, er, own_sems, in_sems = refs
    local = (wo_ref, w_ref, normed_ref, qkv_ref, attn_ref, lse_ref, cos_ref, sin_ref, segq_ref, segk_ref, out_ref)
    loads = [pltpu.make_async_copy(src, dst, in_sems.at[k]) for k, (src, dst) in enumerate(zip(sources, local))]
    for copy in loads:
        copy.start()
    z, f = place()
    me, count = z * nf + f, nz * nf
    dense = gw_ref.shape[2]
    rows, width = tok_ref.shape
    length = 8 * rows
    greet_all(nz, nf)
    seq[0, f] = low_ref[...]
    turned = Gather(seq, (gs, gr), 1, z, f)
    turned.first(0, own=True)
    ups = []
    for j in range(1, nz):
        there = lax.rem(z + j, nz)
        ups.append(send(geup_ref.at[there], pieces_ref.at[z], (es, er), j, (there, f)))
    ups.append(pltpu.make_async_copy(geup_ref.at[z], pieces_ref.at[z], own_sems.at[0]))
    for copy in ups:
        copy.start()
    turned.second(0)
    outs = Reduce([out_ref, *bufs[4:]], (os_, or_), nz, z, f)
    order = list(range(1, nz)) + [0]
    loads[10].wait()
    outs.send_near(order[0])
    turned.third(0)

    def two(m):
        return first_head(m + 1) - first_head(m) == 2

    def small_copy(d):
        return pltpu.make_async_remote_copy(
            small_ref.at[d], smalls.at[me], all_s.at[d], all_r.at[me], device_id=(d // nf, d % nf), device_id_type=MESH
        )

    def small_came(d):
        return pltpu.make_async_remote_copy(
            smalls.at[d], smalls.at[d], all_s.at[d], all_r.at[d], device_id=(d // nf, d % nf), device_id_type=MESH
        )

    def q_copy(p, m, s):
        return pltpu.make_async_remote_copy(
            gw_ref.at[s, p * nf + m], gq.at[p, f, s], q_s.at[p, m, s], q_r.at[p, f, s],
            device_id=(z, m), device_id_type=MESH,
        )

    def q_came(p, m, s):
        dst = gq.at[p, m, s]
        return pltpu.make_async_remote_copy(
            dst, dst, q_s.at[p, m, s], q_r.at[p, m, s], device_id=(z, m), device_id_type=MESH
        )

    def owner_of(block):
        return head_owner(block * dense // HD)

    low, high = out_blocks(f, dense)

    def out_copy(i):
        d = low + i
        k = 2 * (d // nf) + f - owner_of(d)
        return pltpu.make_async_remote_copy(
            gwo_ref.at[i], gob.at[k], wo_s.at[i], wo_r.at[k], device_id=(z, d % nf), device_id_type=MESH
        )

    for copy in loads[:10]:
        copy.wait()
    turned.fourth(0)
    spare = gwo_ref.shape[0] * dense
    wide = up_to(spare, HD)
    shift = first_head(f) * HD - low * dense
    moved = jnp.concatenate([attn_ref[...].astype(F32), jnp.zeros((length, wide - SLOTS * HD), F32)], axis=1)
    moved = pltpu.roll(moved, shift, 1).astype(BF16)
    gwo_ref[...] = dot_tn(moved, seq[0].reshape(length, width))[:spare].reshape(gwo_ref.shape).astype(BF16)

    def start_small(i, _):
        small_copy((me + i) % count).start()
        return 0

    lax.fori_loop(1, count, start_small, 0)
    smalls[me] = small_ref[me]

    def start_out(i, _):
        d = low + i

        @pl.when((d <= high) & (d % nf != f))
        def _():
            out_copy(i).start()

        @pl.when((d <= high) & (d % nf == f))
        def _():
            gob[2 * (d // nf) + f - owner_of(d)] = gwo_ref[i]

        return 0

    lax.fori_loop(0, gwo_ref.shape[0], start_out, 0)
    gkv_ref[...] = jnp.zeros_like(gkv_ref)
    block = 256
    for i in range(length // block):
        attn_back_block(
            i, block, seq[0, i * block // rows : (i + 1) * block // rows].reshape(block, width), wo_ref, qkv_ref, attn_ref, lse_ref, cos_ref, sin_ref, segq_ref, segk_ref, gkv_ref, gqkv_ref
        )
        if i + 1 < nz:
            outs.send_near(order[i + 1])
    attn_back_keys(w_ref, cos_ref, sin_ref, gkv_ref, gqkv_ref, wt_ref)
    if nz > 0:
        outs.far(order[0])
    if nz > 1:
        outs.far(order[1])
    step = 3 * HD
    reduce = Reduce(bufs[:4], (rs, rr), 1, z, f)
    for i in range(length // block):
        mine = slice(i * block, (i + 1) * block)
        at = i * block // rows
        part_ref[at : at + block // rows] = (
            dot(gqkv_ref[mine, :], wt_ref[...]).astype(BF16).reshape(block // rows, rows, width)
        )
    for i in range(4):
        reduce.core(0, i, part_ref.at[flip(f, 1 | 2 * i)]).start()
    if nz > 2:
        outs.far(order[2])
    if nz > 3:
        outs.far(order[3])

    def weights(s):
        value = dot_tn(normed_ref[...], gqkv_ref[:, s * step : (s + 1) * step])
        gw_ref[s] = value.reshape(count, dense, step).astype(BF16)

        def start(i, _):
            for p in range(nz):
                q_copy(p, (f + i) % nf, s).start()
            return 0

        lax.fori_loop(1, nf, start, 0)
        for p in range(nz):
            gq[p, f, s] = gw_ref[s, p * nf + f]

    weights(0)
    for i in range(4):
        reduce.core(0, i, None).wait_recv()
        reduce.by_core[0, i] = reduce.by_core[0, i] + part_ref[flip(f, 2 * i)]
    reduce.send_near(0)
    if nz > 0:
        outs.along_z(order[0])
    if nz > 1:
        outs.along_z(order[1])

    @pl.when(two(f))
    def _():
        weights(1)

    if nz > 2:
        outs.along_z(order[2])
    reduce.far(0)
    if nz > 3:
        outs.along_z(order[3])

    def q_arrive(i, _):
        m = (f + i) % nf
        for p in range(nz):
            q_came(p, m, 0).wait_recv()

        @pl.when(two(m))
        def _():
            for p in range(nz):
                q_came(p, m, 1).wait_recv()

        return 0

    lax.fori_loop(1, nf, q_arrive, 0)

    def arrive_out(k, _):
        d = (k // 2) * nf + f
        source = owner_of(d) + k % 2
        last = head_owner((d * dense + dense - 1) // HD)

        @pl.when((source <= last) & (source != f))
        def _():
            pltpu.make_async_remote_copy(
                gob.at[k], gob.at[k], wo_s.at[0], wo_r.at[k], device_id=(z, flip(f, 1)), device_id_type=MESH
            ).wait_recv()

        return 0

    lax.fori_loop(0, 2 * nz, arrive_out, 0)
    for p in range(nz):
        for m in range(8):
            for s in range(SLOTS):
                if real[m * SLOTS + s]:
                    at = heads[m * SLOTS + s] * HD
                    for c in range(3):
                        gpk[p, :, c * width + at : c * width + at + HD] = gq[p, m, s, :, c * HD : (c + 1) * HD]
        d = p * nf + f
        gpk[p, :, 3 * width :] = gob[2 * p]

        @pl.when(head_owner((d * dense + dense - 1) // HD) != owner_of(d))
        def _():
            gpk[p, :, 3 * width :] = gob[2 * p] + gob[2 * p + 1]

    alongs = []
    for j in range(1, nz):
        there = lax.rem(z + j, nz)
        copy = send(gpk.at[there], gz.at[z], (zs, zr), j, (there, f))
        copy.start()
        alongs.append(copy)
    gz[z] = gpk[z]
    reduce.along_z(0)
    x = tok_ref[...].astype(F32)
    scale = rms_scale(x)
    gtok_ref[...] = (
        own_gm_ref[...] + norm_back(reduce.by_far[0].astype(F32), x * scale, scale, gain_ref[...])
    ).astype(BF16)
    block_ref[...] = (mixed_ref[...] + outs.total()).astype(BF16)

    def finish(i, _):
        d = (me + i) % count
        small_came(d).wait_recv()
        small_copy(d).wait_send()
        return 0

    lax.fori_loop(1, count, finish, 0)

    def q_left(i, _):
        m = (f + i) % nf
        for p in range(nz):
            q_copy(p, m, 0).wait_send()

        @pl.when(two(f))
        def _():
            for p in range(nz):
                q_copy(p, m, 1).wait_send()

        return 0

    lax.fori_loop(1, nf, q_left, 0)

    def out_left(i, _):
        @pl.when((low + i <= high) & ((low + i) % nf != f))
        def _():
            out_copy(i).wait_send()

        return 0

    lax.fori_loop(0, gwo_ref.shape[0], out_left, 0)
    for copy in alongs:
        copy.wait()
    gwqkv_ref[...] = sum(gz[p, :, : 3 * width].astype(F32) for p in range(nz))
    gwout_ref[...] = sum(gz[p, :, 3 * width :].astype(F32) for p in range(nz))
    all_small_ref[...] = smalls[...]
    for i in range(4):
        reduce.core(0, i, part_ref.at[0]).wait_send()
    reduce.end()
    outs.end()
    turned.end()
    for copy in ups:
        copy.wait()


def back(
    low, geup, wo, w, normed, qkv, attn, lse, cosine, sine, segq, segk, out_part, small, tok, mixed, own_gm, gain, nz, nf
):
    rows, width = tok.shape
    length, count = 8 * rows, nz * nf
    dense = width // count
    heads, real = head_table(8)
    return pl.pallas_call(
        functools.partial(back_kernel, nz=nz, nf=nf, heads=heads, real=real),
        out_shape=(
            jax.ShapeDtypeStruct((rows, width), BF16),
            jax.ShapeDtypeStruct((rows, width), BF16),
            jax.ShapeDtypeStruct((dense, 3 * width), F32),
            jax.ShapeDtypeStruct((dense, width), F32),
            jax.ShapeDtypeStruct((count, dense, HD), BF16),
            jax.ShapeDtypeStruct(geup.shape, BF16),
        ),
        in_specs=[VMEM] + [ANY] * 12 + [VMEM] * 5,
        out_specs=(VMEM,) * 5 + (ANY,),
        scratch_shapes=[
            pltpu.VMEM((1, 8, rows, width), BF16),
            pltpu.VMEM((length, 2 * SLOTS * HD), F32),
            pltpu.VMEM((length, 3 * SLOTS * HD), BF16),
            pltpu.VMEM((3 * SLOTS * HD, width), BF16),
            pltpu.VMEM((8, rows, width), BF16),
            pltpu.VMEM((SLOTS, count, dense, 3 * HD), BF16),
            pltpu.VMEM((8, dense, width), BF16),
            pltpu.VMEM((nz, 8, SLOTS, dense, 3 * HD), BF16),
            pltpu.VMEM((2 * nz, dense, width), BF16),
            pltpu.VMEM((nz, dense, 4 * width), BF16),
            pltpu.VMEM((nz, dense, 4 * width), BF16),
            pltpu.VMEM((count, dense, HD), BF16),
            *Reduce.scratch(1, rows, width),
            *Reduce.scratch(nz, rows, width)[1:],
            *pair_of(Reduce.copies(1)),
            *pair_of(Reduce.copies(nz)),
            *pair_of(count),
            pltpu.SemaphoreType.DMA((nz, 8, SLOTS)),
            pltpu.SemaphoreType.DMA((nz, 8, SLOTS)),
            pltpu.SemaphoreType.DMA((8,)),
            pltpu.SemaphoreType.DMA((2 * nz,)),
            *pair_of(nz),
            *pair_of(Gather.copies(1)),
            *pair_of(nz),
            pltpu.SemaphoreType.DMA((1,)),
            *[pltpu.VMEM(a.shape, a.dtype) for a in (wo, w, normed, qkv, attn, lse, cosine, sine, segq, segk, out_part)],
            pltpu.SemaphoreType.DMA((11,)),
        ],
        compiler_params=pltpu.CompilerParams(
            collective_id=4, has_side_effects=True, vmem_limit_bytes=60 * 2**20
        ),
        name="back",
    )(
        low, geup, wo, w, normed, qkv, attn, lse, cosine, sine, segq, segk, out_part,
        small.reshape(count, dense, HD), tok, mixed, own_gm, gain,
    )


def unpack_kernel(
    pieces_ref, small_ref, wqkv_ref, gwqkv_ref, gain_ref, block_in, tok_in, wout_in, edown_in, sdown_in,
    geup_ref, gsup_ref, grouter_ref, gone_ref, gtwo_ref, block_ref, tok_ref, gqkv_ref, wout_ref, edown_ref, sdown_ref,
    *, shared, experts,
):
    for src, dst in (
        (block_in, block_ref), (tok_in, tok_ref), (gwqkv_ref, gqkv_ref), (wout_in, wout_ref), (edown_in, edown_ref),
        (sdown_in, sdown_ref),
    ):
        dst[...] = src[...]
    nz = pieces_ref.shape[0]
    hidden = pieces_ref.shape[2] // 4
    for t in range(nz):
        for g in range(2):
            for e in range(2):
                at = (2 * g + e) * hidden
                to = (g * nz + t) * hidden
                geup_ref[e, :, to : to + hidden] = pieces_ref[t, :, at : at + hidden].astype(F32)
    count = small_ref.shape[0]
    total = small_ref[0].astype(F32)
    for d in range(count):
        if d:
            total = total + small_ref[d].astype(F32)
        for g in range(2):
            to = (g * count + d) * shared
            gsup_ref[:, to : to + shared] = small_ref[d, :, g * TAIL : g * TAIL + shared].astype(F32)
    grouter_ref[...] = total[:, shared : shared + experts].T
    one = jnp.sum(wqkv_ref[...].astype(F32) * gwqkv_ref[...], axis=-1, keepdims=True) / gain_ref[...].astype(F32).T
    gone_ref[...] = one.T
    gtwo_ref[...] = total[:, HD - 1 :].T


def unpack(pieces, small, wqkv, gwqkv, gain, rest, shared, experts):
    nz, up_rows, packed = pieces.shape
    count, dense, _ = small.shape
    return pl.pallas_call(
        functools.partial(unpack_kernel, shared=shared, experts=experts),
        out_shape=(
            jax.ShapeDtypeStruct((2, up_rows, nz * packed // 2), F32),
            jax.ShapeDtypeStruct((dense, 2 * count * shared), F32),
            jax.ShapeDtypeStruct((experts, dense), F32),
            jax.ShapeDtypeStruct((1, dense), F32),
            jax.ShapeDtypeStruct((1, dense), F32),
            *[jax.ShapeDtypeStruct(a.shape, a.dtype) for a in (*rest[:2], gwqkv, *rest[2:])],
        ),
        in_specs=[VMEM] * 10,
        out_specs=(VMEM,) * 11,
        compiler_params=pltpu.CompilerParams(vmem_limit_bytes=60 * 2**20),
        name="unpack",
    )(pieces, small, wqkv, gwqkv, gain, *rest)


def tables():
    pos = np.arange(SEQ, dtype=np.float32)
    freqs = np.float32(ROPE) ** (-np.arange(HD // 2, dtype=np.float32) * np.float32(2.0 / HD))
    angles = (pos[:, None] * freqs[None, :]).astype(np.float32)
    cosine = np.concatenate([np.cos(angles)] * 2, axis=1).astype(np.float32)
    sine = np.concatenate([-np.sin(angles), np.sin(angles)], axis=1).astype(np.float32)
    return jnp.asarray(cosine), jnp.asarray(sine)


def local_near(
    mesh, tokens, out_grad, segment_ids, expert_ids, attn_gain, ffn_gain, w_qkv, w_out,
    w_router, w_shared_up, w_shared_down, w_expert_up, w_expert_down,
):
    nz, nf = mesh.shape["dp"], mesh.shape["fsdp"]
    rows, width = tokens.shape
    experts = w_router.shape[1]
    hidden, shared = w_expert_down.shape[1], w_shared_down.shape[0]
    f = lax.axis_index("fsdp")
    cosine, sine = tables()
    (
        w, wo, tail, router, gain_one, gain_two, marks, own_marks, segq, segk, normed_one, qkv, attn, lse, mixed, normed,
        plane, all_grad, pieces,
    ) = front(
        tokens, w_qkv, w_out, w_router.T, w_shared_up, attn_gain[None], ffn_gain[None], expert_ids.T,
        segment_ids[None], cosine, sine, out_grad, w_expert_up, nz, nf, shared,
    )
    tail = tail.reshape(width, 2 * TAIL)
    lane = jnp.arange(HD, dtype=jnp.int32) - TAIL - shared
    own = (lane[None, :] == (2 * f + jnp.arange(2, dtype=jnp.int32))[:, None]).astype(F32)
    out_part, low, grad_mixed, small, geup, gedown, gsdown = experts_turn(
        normed, plane, all_grad, marks, own, pieces.reshape(width, 4 * hidden), tail,
        w_expert_down.reshape(2 * hidden, width), w_shared_down, out_grad, mixed, router, own_marks, gain_two, nz, nf,
    )
    block_out, tokens_grad, grad_wqkv, grad_wout, smalls, gpieces = back(
        low, geup, wo, w, normed_one, qkv, attn, lse, cosine, sine, segq, segk, out_part, small,
        tokens, mixed, grad_mixed, gain_one, nz, nf,
    )
    (
        grad_eup, grad_sup, grad_router, grad_one, grad_two, block_out, tokens_grad, grad_wqkv, grad_wout, gedown, gsdown,
    ) = unpack(
        gpieces, smalls, w_qkv, grad_wqkv, attn_gain[None], (block_out, tokens_grad, grad_wout, gedown, gsdown),
        shared, experts,
    )
    return (
        block_out, tokens_grad, grad_one[0], grad_two[0], grad_wqkv, grad_wout, grad_router.T, grad_sup,
        gsdown, grad_eup, gedown.reshape(2, hidden, width),
    )


def local_far(
    mesh, tokens, out_grad, segment_ids, expert_ids, attn_gain, ffn_gain, w_qkv, w_out,
    w_router, w_shared_up, w_shared_down, w_expert_up, w_expert_down,
):
    nz, nf = mesh.shape["dp"], mesh.shape["fsdp"]
    nd = nz * nf
    rows, width = tokens.shape
    group = SEQ // rows
    experts = w_router.shape[1]
    dense = w_qkv.shape[0]
    hidden, shared = w_expert_down.shape[1], w_shared_down.shape[0]
    up_rows = w_expert_up.shape[1]
    both = ("dp", "fsdp")
    groups = None if nf == group else [[a + i for i in range(group)] for a in range(0, nf, group)]
    f = lax.axis_index("fsdp")
    member = lax.rem(f, group)
    heads, real = head_table(group)

    by_head = w_qkv.reshape(dense, 3, HEADS, HD)
    empty = jnp.zeros((dense, 3, HD), BF16)
    cols = jnp.stack([by_head[:, :, h] if r else empty for h, r in zip(heads, real)], axis=0)
    cols = cols.reshape(group, SLOTS, dense, 3 * HD)
    cols = jnp.tile(cols, (nf // group, 1, 1, 1))
    cols = lax.all_to_all(cols, "fsdp", 0, 0, tiled=True)
    w = lax.all_gather(cols, "dp", axis=0, tiled=True).transpose(1, 0, 2, 3).reshape(SLOTS, width, 3 * HD)
    full_out = lax.all_gather(w_out, both, axis=0, tiled=True)
    first = HEADS * member // group
    own_real = (first + jnp.arange(SLOTS) < HEADS * (member + 1) // group).astype(BF16)
    padded = jnp.pad(full_out, ((0, (SLOTS - 1) * HD), (0, 0)))
    wo = lax.dynamic_slice(padded, (first * HD, 0), (SLOTS * HD, width))
    wo = wo * jnp.repeat(own_real, HD)[:, None]
    gains = lax.all_gather(jnp.stack([attn_gain, ffn_gain], axis=1).astype(F32), both, axis=0, tiled=True)
    gain_one, gain_two = gains[:, 0], gains[:, 1]
    router = lax.all_gather(w_router, both, axis=0, tiled=True)
    sup = w_shared_up.reshape(dense, 2, nd, shared).transpose(2, 0, 1, 3).reshape(nd, dense, 2 * shared)
    sup = lax.all_to_all(sup, both, 0, 0, tiled=True).reshape(width, 2, shared)
    eup = w_expert_up.reshape(2, up_rows, 2, nz, hidden).transpose(3, 1, 2, 0, 4)
    eup = lax.all_to_all(eup, "dp", 0, 0, tiled=True).reshape(width, 4 * hidden)
    rest = jnp.zeros((width, TAIL - shared), BF16)
    tail = jnp.concatenate([sup[:, 0], router, rest[:, experts:], sup[:, 1], rest], axis=1)
    chosen = jnp.any(expert_ids[:, :, None] == jnp.arange(experts, dtype=jnp.int32), axis=1)
    at = TAIL + shared
    marks = jnp.pad(chosen.astype(BF16), ((0, 0), (at, HD - experts - at)))
    marks = lax.all_gather(marks, both, axis=0, tiled=True)
    lane = jnp.arange(HD, dtype=jnp.int32)
    own = (lane[None, :] == (at + 2 * f + jnp.arange(2, dtype=jnp.int32))[:, None]).astype(F32)
    cosine, sine = tables()
    seg = lax.all_gather(segment_ids, "fsdp", axis=0, tiled=True, axis_index_groups=groups)
    segq = jnp.broadcast_to(seg[:, None], (SEQ, HD))
    segk = jnp.broadcast_to(seg[None, :], (8, SEQ))

    seq_tokens = lax.all_gather(tokens, "fsdp", axis=0, tiled=True, axis_index_groups=groups)
    part, normed_one, qkv, attn, lse = attn_forward(
        seq_tokens, gain_one[None, :], w, wo, cosine, sine, segq, segk
    )
    projected = lax.psum_scatter(part, "fsdp", scatter_dimension=0, tiled=True, axis_index_groups=groups)
    inputs = tokens.astype(F32)
    mixed = inputs + projected.astype(F32)
    scale_two = rms_scale(mixed)
    normal_two = mixed * scale_two
    normed_two = (normal_two * gain_two).astype(BF16)
    all_normed = lax.all_gather(normed_two, both, axis=0, tiled=True)
    all_grad = lax.all_gather(out_grad, both, axis=0, tiled=True)
    out_part, gx_part, geup, gtail, gedown, gsdown = ffn(
        all_normed, all_grad, marks, own, eup, tail, w_expert_down.reshape(2 * hidden, width), w_shared_down
    )
    gx = lax.psum_scatter(gx_part, both, scatter_dimension=0, tiled=True).astype(F32)
    ffn_out = lax.psum_scatter(out_part, both, scatter_dimension=0, tiled=True).astype(F32)
    block_out = (mixed + ffn_out).astype(BF16)

    logits = jnp.where(chosen, dot(normed_two, router), NEG)
    probs = jax.nn.softmax(logits, axis=-1)
    grad_gates = gx[:, width + at : width + at + experts]
    grad_logits = (
        probs * (grad_gates - jnp.sum(probs * grad_gates, axis=-1, keepdims=True))
    ).astype(BF16)
    grad_router = dot_tn(normed_two, grad_logits)
    grad_normed = gx[:, :width] + dot_nt(grad_logits, router)
    grad_gain_two = jnp.sum(grad_normed * normal_two, axis=0)
    grad_mixed = out_grad.astype(F32) + norm_back(grad_normed, normal_two, scale_two, gain_two)

    seq_gm = lax.all_gather(grad_mixed.astype(BF16), "fsdp", axis=0, tiled=True, axis_index_groups=groups)
    part_back, gw, gwo = attn_backward(
        seq_gm, wo, w, normed_one, qkv, attn, lse, cosine, sine, segq, segk
    )
    grad_normed_one = lax.psum_scatter(
        part_back, "fsdp", scatter_dimension=0, tiled=True, axis_index_groups=groups
    ).astype(F32)
    scale_one = rms_scale(inputs)
    normal_one = inputs * scale_one
    grad_gain_one = jnp.sum(grad_normed_one * normal_one, axis=0)
    tokens_grad = (grad_mixed + norm_back(grad_normed_one, normal_one, scale_one, gain_one)).astype(BF16)

    gw = lax.psum_scatter(gw, "dp", scatter_dimension=1, tiled=True)
    gw = lax.all_to_all(gw.reshape(SLOTS, nf, dense, 3 * HD), "fsdp", 1, 1, tiled=True).astype(F32)
    gw = jnp.sum(gw.reshape(SLOTS, nf // group, group, dense, 3, HD), axis=1)
    picked = [gw[i % SLOTS, i // SLOTS] for i in range(group * SLOTS) if real[i]]
    grad_wqkv = jnp.stack(picked, axis=2).reshape(dense, 3 * width)
    gwo = gwo * jnp.repeat(own_real, HD)[:, None]
    all_gwo = jnp.zeros(((HEADS + SLOTS - 1) * HD, width), BF16)
    all_gwo = lax.dynamic_update_slice(all_gwo, gwo, (first * HD, 0))[: HEADS * HD]
    grad_wout = lax.psum_scatter(all_gwo, both, scatter_dimension=0, tiled=True).astype(F32)
    small = jnp.concatenate([grad_router, grad_gain_one[:, None], grad_gain_two[:, None]], axis=1)
    small = lax.psum_scatter(small, both, scatter_dimension=0, tiled=True)
    gsup = jnp.stack([gtail[:, :shared], gtail[:, TAIL : TAIL + shared]], axis=1)
    gsup = lax.all_to_all(gsup.reshape(nd, dense, 2 * shared).astype(BF16), both, 0, 0, tiled=True)
    grad_sup = gsup.reshape(nd, dense, 2, shared).transpose(1, 2, 0, 3).reshape(dense, 2 * nd * shared).astype(F32)
    geup = lax.all_to_all(geup.reshape(nz, up_rows, 2, 2, hidden), "dp", 0, 0, tiled=True)
    grad_eup = geup.transpose(3, 1, 2, 0, 4).reshape(2, up_rows, 2 * nz * hidden).astype(F32)
    return (
        block_out, tokens_grad, small[:, experts], small[:, experts + 1], grad_wqkv, grad_wout,
        small[:, :experts], grad_sup, gsdown, grad_eup, gedown.reshape(2, hidden, width),
    )


def solution(mesh):
    one, two = P(("dp", "fsdp")), P(("dp", "fsdp"), None)
    three = P("fsdp", "dp", None)

    def local(tokens, *rest):
        near = mesh.shape["fsdp"] == 8 == SEQ // tokens.shape[0] and mesh.shape["dp"] <= 4
        return (local_near if near else local_far)(mesh, tokens, *rest)

    return jax.shard_map(
        local,
        mesh=mesh,
        in_specs=(two, two, one, two, one, one, two, two, two, two, two, three, three),
        out_specs=(two, two, one, one, two, two, two, two, two, three, three),
        check_vma=False,
    )
```
